32 devices in a mesh: group: 4 (over x, core), dp: 2 (over y), mp: 4 (over z).
Axes of the slice: x: 2, y: 2, z: 4, core: 2. Of those that a mesh axis runs over, the one named last changes fastest.
Arguments:
- patches: float32 [4, 96, 196, 768], P('group', 'dp', None, 'mp'), may hold values from -6 to 6
- labels: int32 [4, 96], P('group', 'dp'), may hold values from 0 to 999
- partner: int32 [4, 96], P('group', 'dp'), may hold values from 0 to 47
- class_weight: float32 [1000], replicated, may hold values from 0.3 to 3
- embedding: float32 [768, 384], P('mp'), may hold values from -0.21875 to 0.21875
- mixing: float32 [1, 196, 197], replicated, may hold values from -0.4375 to 0.4375
- expand: float32 [1, 385, 1536], P(None, None, 'mp'), may hold values from -0.3125 to 0.3125
- shrink: float32 [1, 1536, 384], P(None, 'mp'), may hold values from -0.15625 to 0.15625
- classifier: float32 [385, 1000], P(None, 'mp'), may hold values from -6 to 6
- scales: float32 [5, 384], P(None, 'mp'), may hold values from 0.5 to 1.5
- shifts: float32 [5, 384], P(None, 'mp'), may hold values from -2 to 2
- embedding_first: float32 [4, 768, 384], P('group', 'mp'), may hold values from -1 to 1, as said below
- mixing_first: float32 [4, 1, 196, 197], P('group'), may hold values from -1 to 1, as said below
- expand_first: float32 [4, 1, 385, 1536], P('group', None, None, 'mp'), may hold values from -1 to 1, as said below
- shrink_first: float32 [4, 1, 1536, 384], P('group', None, 'mp'), may hold values from -1 to 1, as said below
- classifier_first: float32 [4, 385, 1000], P('group', None, 'mp'), may hold values from -1 to 1, as said below
- scale_first_moments: float32 [4, 5, 384], P('group', None, 'mp'), may hold values from -1 to 1, as said below
- shifts_first: float32 [4, 5, 384], P('group', None, 'mp'), may hold values from -1 to 1, as said below
- embedding_second: float32 [4, 768, 384], P('group', 'mp'), may hold values from 0 to 1, as said below
- mixing_second: float32 [4, 1, 196, 197], P('group'), may hold values from 0 to 1, as said below
- expand_second: float32 [4, 1, 385, 1536], P('group', None, None, 'mp'), may hold values from 0 to 1, as said below
- shrink_second: float32 [4, 1, 1536, 384], P('group', None, 'mp'), may hold values from 0 to 1, as said below
- classifier_second: float32 [4, 385, 1000], P('group', None, 'mp'), may hold values from 0 to 1, as said below
- scales_second: float32 [4, 5, 384], P('group', None, 'mp'), may hold values from 0 to 1, as said below
- shifts_second: float32 [4, 5, 384], P('group', None, 'mp'), may hold values from 0 to 1, as said below
- embedding_outer: float32 [768, 384], P('mp'), may hold values from -0.12 to 0.12
- mixing_outer: float32 [1, 196, 197], replicated, may hold values from -0.12 to 0.12
- expand_outer: float32 [1, 385, 1536], P(None, None, 'mp'), may hold values from -0.12 to 0.12
- shrink_outer: float32 [1, 1536, 384], P(None, 'mp'), may hold values from -0.12 to 0.12
- classifier_outer: float32 [385, 1000], P(None, 'mp'), may hold values from -0.12 to 0.12
- scales_outer: float32 [5, 384], P(None, 'mp'), may hold values from -0.12 to 0.12
- shifts_outer: float32 [5, 384], P(None, 'mp'), may hold values from -0.12 to 0.12
Outputs:
- losses: float32 [4, 2], P('group')
- grad_norm: float32 [4], P('group')
- embedding_update: float32 [768, 384], P('mp')
- mixing_update: float32 [1, 196, 197], replicated
- expand_update: float32 [1, 385, 1536], P(None, None, 'mp')
- shrink_update: float32 [1, 1536, 384], P(None, 'mp')
- classifier_update: float32 [385, 1000], P(None, 'mp')
- scales_update: float32 [5, 384], P(None, 'mp')
- shifts_update: float32 [5, 384], P(None, 'mp')
- embedding_mean: float32 [4, 768, 384], P('group', 'mp')
- mixing_mean: float32 [4, 1, 196, 197], P('group')
- expand_mean: float32 [4, 1, 385, 1536], P('group', None, None, 'mp')
- shrink_mean: float32 [4, 1, 1536, 384], P('group', None, 'mp')
- classifier_mean: float32 [4, 385, 1000], P('group', None, 'mp')
- scales_mean: float32 [4, 5, 384], P('group', None, 'mp')
- shifts_mean: float32 [4, 5, 384], P('group', None, 'mp')
- embedding_square: float32 [4, 768, 384], P('group', 'mp')
- mixing_square: float32 [4, 1, 196, 197], P('group')
- expand_square: float32 [4, 1, 385, 1536], P('group', None, None, 'mp')
- shrink_square: float32 [4, 1, 1536, 384], P('group', None, 'mp')
- classifier_square: float32 [4, 385, 1000], P('group', None, 'mp')
- scales_square: float32 [4, 5, 384], P('group', None, 'mp')
- shifts_square: float32 [4, 5, 384], P('group', None, 'mp')
- embedding_velocity: float32 [768, 384], P('mp')
- mixing_velocity: float32 [1, 196, 197], replicated
- expand_velocity: float32 [1, 385, 1536], P(None, None, 'mp')
- shrink_velocity: float32 [1, 1536, 384], P(None, 'mp')
- classifier_velocity: float32 [385, 1000], P(None, 'mp')
- scales_velocity: float32 [5, 384], P(None, 'mp')
- shifts_velocity: float32 [5, 384], P(None, 'mp')
The draws below stay inside these ranges and needn't reach their ends.
Inputs may be any that keep to these rules, and one draw needn't show every extreme that they name: partner names an image of the same aligned block of 48 images, by its place in that block. `embedding_first`: first moments of both signs. `mixing_first`: first moments of both signs. `expand_first`: first moments of both signs. `shrink_first`: first moments of both signs. `classifier_first`: first moments of both signs. `scale_first_moments`: first moments of both signs. `shifts_first`: first moments of both signs. `embedding_second`: positive. `mixing_second`: positive. `expand_second`: positive. `shrink_second`: positive. `classifier_second`: positive. `scales_second`: positive. `shifts_second`: positive.
All inputs are finite; a program needn't handle non-finite values.
Results may differ from the reference program's by a relative error of at most 0.0024.
The reference program's roundings to bfloat16 on the way count: a program that leaves them out, or rounds other values in their place, can miss the bound.
Values may be sent and summed in bfloat16 or wider, within the bound.
A program may use at most 256 MiB of HBM per device.

```python
import math
import jax
import jax.numpy as jnp
from jax import lax

D = 384
HID = 1536
PATCH_EDGE = 196
PD = 768
C = 1000
LAYERS = 1
STEP = 10
IMG_DEV = 48
GROUPS = 4
IMAGES = 96
N_DP = 2


def gradient_scale():
    parameters = PD * D + LAYERS * (PATCH_EDGE * (PATCH_EDGE + 1) + (D + 1) * HID + HID * D) + (D + 1) * C + (7 * LAYERS + 3) * D
    return 0.01 / parameters ** 0.5


def first_moment(key, shape, relative):
    return 0.11 * relative * gradient_scale() * jax.random.normal(key, shape, jnp.float32)


def second_moment(key, shape, relative):
    spread = jax.random.uniform(key, shape, jnp.float32, 1.0, 4.0)
    return 0.001 * (relative * gradient_scale()) ** 2 * spread


def draw_embedding_first(key, part):
    key = jax.random.fold_in(key, 1)
    return first_moment(key, (GROUPS, PD, D), 0.3)


def draw_mixing_first(key, part):
    key = jax.random.fold_in(key, 2)
    return first_moment(key, (GROUPS, LAYERS, PATCH_EDGE, PATCH_EDGE + 1), 0.3)


def draw_expand_first(key, part):
    key = jax.random.fold_in(key, 3)
    return first_moment(key, (GROUPS, LAYERS, D + 1, HID), 1.0)


def draw_shrink_first(key, part):
    key = jax.random.fold_in(key, 4)
    return first_moment(key, (GROUPS, LAYERS, HID, D), 1.0)


def draw_classifier_first(key, part):
    key = jax.random.fold_in(key, 5)
    return first_moment(key, (GROUPS, D + 1, C), 1.0)


def draw_scale_first_moments(key, part):
    key = jax.random.fold_in(key, 6)
    return first_moment(key, (GROUPS, 4 * LAYERS + 1, D), 1.0)


def draw_shifts_first(key, part):
    key = jax.random.fold_in(key, 7)
    return first_moment(key, (GROUPS, 3 * LAYERS + 2, D), 1.0)


def draw_embedding_second(key, part):
    key = jax.random.fold_in(key, 11)
    return second_moment(key, (GROUPS, PD, D), 0.3)


def draw_mixing_second(key, part):
    key = jax.random.fold_in(key, 12)
    return second_moment(key, (GROUPS, LAYERS, PATCH_EDGE, PATCH_EDGE + 1), 0.3)


def draw_expand_second(key, part):
    key = jax.random.fold_in(key, 13)
    return second_moment(key, (GROUPS, LAYERS, D + 1, HID), 1.0)


def draw_shrink_second(key, part):
    key = jax.random.fold_in(key, 14)
    return second_moment(key, (GROUPS, LAYERS, HID, D), 1.0)


def draw_classifier_second(key, part):
    key = jax.random.fold_in(key, 15)
    return second_moment(key, (GROUPS, D + 1, C), 1.0)


def draw_scales_second(key, part):
    key = jax.random.fold_in(key, 16)
    return second_moment(key, (GROUPS, 4 * LAYERS + 1, D), 1.0)


def draw_shifts_second(key, part):
    key = jax.random.fold_in(key, 17)
    return second_moment(key, (GROUPS, 3 * LAYERS + 2, D), 1.0)


def set_ends(values, own_key, low, top_value):
    longest = values.shape.index(max(values.shape))
    spots = []
    for shift in (0, 1):
        where = [jax.random.randint(jax.random.fold_in(own_key, axis), (), 0, length) for axis, length in enumerate(values.shape)]
        where[longest] = (where[longest] + shift) % values.shape[longest]
        spots.append(tuple(where))
    return values.at[spots[0]].set(low).at[spots[1]].set(top_value)


def shard_levels(key, extent, pieces, smallest, high):
    factor_of = 1.0
    for position, parts in pieces:
        steps = jax.random.uniform(jax.random.fold_in(jax.random.fold_in(key, 6), position), (parts,), jnp.float32, smallest / len(pieces), high / len(pieces))
        factor_of = factor_of * jnp.repeat(jnp.exp(steps), extent[position] // parts).reshape((-1,) + (1,) * (len(extent) - 1 - position))
    return factor_of


def centred(key, extent, scale, limit, cuts=(), kind=jnp.bfloat16):
    values = jax.random.normal(key, extent, jnp.float32) * scale
    if len(cuts) > 0:
        values = shard_levels(key, extent, cuts, -0.22, 0.18) * values
    return jnp.clip(values, min=-limit, max=limit).astype(kind)


def setup_inputs(seed: int = 0) -> dict:
    splits = jax.random.split(jax.random.key(seed), 33)
    return {
        "patches": centred(splits[0], (GROUPS, IMAGES, PATCH_EDGE, PD), 1.0, 6.0, ((0, 4), (1, 2), (3, 4)), jnp.float32),
        "labels": set_ends(jax.random.randint(splits[1], (GROUPS, IMAGES), 0, C), jax.random.fold_in(splits[1], 1), 0, C - 1).astype(jnp.int32),
        "partner": set_ends(jax.random.randint(splits[2], (GROUPS, IMAGES), 0, IMG_DEV), jax.random.fold_in(splits[2], 1), 0, IMG_DEV - 1).astype(jnp.int32),
        "class_weight": jnp.clip(jnp.exp(jax.random.uniform(splits[3], (C,), jnp.float32, math.log(0.3), math.log(3.0))), 0.3, 3.0),
        "embedding": centred(splits[4], (PD, D), PD ** -0.5, 0.21875, ((0, 4),), jnp.float32),
        "mixing": centred(splits[5], (LAYERS, PATCH_EDGE, PATCH_EDGE + 1), PATCH_EDGE ** -0.5, 0.4375, (), jnp.float32),
        "expand": centred(splits[6], (LAYERS, D + 1, HID), D ** -0.5, 0.3125, ((2, 4),), jnp.float32),
        "shrink": centred(splits[7], (LAYERS, HID, D), HID ** -0.5, 0.15625, ((1, 4),), jnp.float32),
        "classifier": centred(splits[8], (D + 1, C), 1.0, 6.0, ((1, 4),), jnp.float32),
        "scales": jnp.clip(1.0 + 0.1 * jax.random.normal(splits[9], (4 * LAYERS + 1, D), jnp.float32), 0.5, 1.5),
        "shifts": centred(splits[10], (3 * LAYERS + 2, D), 0.3, 2.0, ((1, 4),), jnp.float32),
        "embedding_first": draw_embedding_first(jax.random.fold_in(splits[32], 71), 0),
        "mixing_first": draw_mixing_first(jax.random.fold_in(splits[32], 71), 0),
        "expand_first": draw_expand_first(jax.random.fold_in(splits[32], 71), 0),
        "shrink_first": draw_shrink_first(jax.random.fold_in(splits[32], 71), 0),
        "classifier_first": draw_classifier_first(jax.random.fold_in(splits[32], 71), 0),
        "scale_first_moments": draw_scale_first_moments(jax.random.fold_in(splits[32], 71), 0),
        "shifts_first": draw_shifts_first(jax.random.fold_in(splits[32], 71), 0),
        "embedding_second": draw_embedding_second(jax.random.fold_in(splits[32], 71), 0),
        "mixing_second": draw_mixing_second(jax.random.fold_in(splits[32], 71), 0),
        "expand_second": draw_expand_second(jax.random.fold_in(splits[32], 71), 0),
        "shrink_second": draw_shrink_second(jax.random.fold_in(splits[32], 71), 0),
        "classifier_second": draw_classifier_second(jax.random.fold_in(splits[32], 71), 0),
        "scales_second": draw_scales_second(jax.random.fold_in(splits[32], 71), 0),
        "shifts_second": draw_shifts_second(jax.random.fold_in(splits[32], 71), 0),
        "embedding_outer": centred(splits[25], (PD, D), 0.02, 0.12, ((0, 4),), jnp.float32),
        "mixing_outer": centred(splits[26], (LAYERS, PATCH_EDGE, PATCH_EDGE + 1), 0.02, 0.12, (), jnp.float32),
        "expand_outer": centred(splits[27], (LAYERS, D + 1, HID), 0.02, 0.12, ((2, 4),), jnp.float32),
        "shrink_outer": centred(splits[28], (LAYERS, HID, D), 0.02, 0.12, ((1, 4),), jnp.float32),
        "classifier_outer": centred(splits[29], (D + 1, C), 0.02, 0.12, ((1, 4),), jnp.float32),
        "scales_outer": centred(splits[30], (4 * LAYERS + 1, D), 0.02, 0.12, ((1, 4),), jnp.float32),
        "shifts_outer": centred(splits[31], (3 * LAYERS + 2, D), 0.02, 0.12, ((1, 4),), jnp.float32),
    }


@jax.custom_vjp
def low(v):
    return lax.optimization_barrier(v.astype(jnp.bfloat16)).astype(jnp.float32)

@jax.custom_vjp
def low_back(v):
    return v

def low_keep(v):
    return (low(v), None)

def low_pass(kept, grad):
    return (grad,)

def back_keep(v):
    return (v, None)

def back_low(kept, grad):
    return (low(grad),)
low.defvjp(low_keep, low_pass)
low_back.defvjp(back_keep, back_low)
HIGH_ACCURACY = lax.Precision.HIGHEST
mix_share = 0.7
clip_limit = 0.01
beta_one = 0.9
beta_two = 0.999
adam_eps = 1e-08
weight_decay = 0.05
matrix_rate = 0.05
head_rate = 0.5
vector_rate = 0.4
outer_rate = 0.7
outer_momentum = 0.9

def forward(weights, images, pair_index, label_hot, mate_hot, first_mix_weight, weight_b):
    embedding, mixing, expand, shrink, classifier, scales, shifts = weights
    image_count = images.shape[0]
    blended = mix_share * images + (1.0 - mix_share) * images[pair_index]
    pixel_rows = low(blended).reshape(image_count * PATCH_EDGE, PD)
    stream = low_back(jnp.dot(pixel_rows, low(embedding), precision=HIGH_ACCURACY)) + shifts[3 * LAYERS]
    for layer_index in range(LAYERS):
        mixing_block_input = low(scales[4 * layer_index] * stream + shifts[3 * layer_index]).reshape(image_count, PATCH_EDGE, D)
        lookup_table = low(mixing[layer_index])
        mixed_images = jnp.einsum('et,atx->aex', lookup_table[:, :PATCH_EDGE], mixing_block_input, precision=HIGH_ACCURACY) + lookup_table[:, PATCH_EDGE][None, :, None]
        mixed_images = low_back(mixed_images).reshape(image_count * PATCH_EDGE, D)
        stream = stream + scales[4 * layer_index + 1] * mixed_images
        ffn_input = low(scales[4 * layer_index + 2] * stream + shifts[3 * layer_index + 1])
        up_table = low(expand[layer_index])
        hidden = low_back(jnp.dot(ffn_input, up_table[:D], precision=HIGH_ACCURACY) + up_table[D])
        active = low(jax.nn.gelu(hidden))
        output = low_back(jnp.dot(active, low(shrink[layer_index]), precision=HIGH_ACCURACY))
        stream = stream + scales[4 * layer_index + 3] * (output + shifts[3 * layer_index + 2])
    final = scales[4 * LAYERS] * stream + shifts[3 * LAYERS + 1]
    pooled = low(lax.optimization_barrier(jnp.mean(final.reshape(image_count, PATCH_EDGE, D), axis=1)))
    head_table = low(classifier)
    logits = low_back(jnp.dot(pooled, head_table[:D], precision=HIGH_ACCURACY) + head_table[D])
    maximum = lax.optimization_barrier(jnp.max(logits, axis=1, keepdims=True))
    log_total = maximum[:, 0] + jnp.log(lax.optimization_barrier(jnp.sum(jnp.exp(logits - maximum), axis=1)))
    target_a = lax.optimization_barrier(jnp.sum(label_hot * logits, axis=1))
    target_b = lax.optimization_barrier(jnp.sum(mate_hot * logits, axis=1))
    return jnp.sum(first_mix_weight * (log_total - target_a) + weight_b * (log_total - target_b))

def adamw(weight, gradient, moment_one, moment_two, step_rate):
    mean_new = beta_one * moment_one + (1.0 - beta_one) * gradient
    square_new = beta_two * moment_two + (1.0 - beta_two) * gradient * gradient
    mean_hat = mean_new / (1.0 - beta_one ** STEP)
    square_hat = square_new / (1.0 - beta_two ** STEP)
    inner = weight - step_rate * (mean_hat / (jnp.sqrt(square_hat) + adam_eps) + weight_decay * weight)
    return (inner, mean_new, square_new)

def reference(patches, labels, partner, class_weight, embedding, mixing, expand, shrink, classifier, scales, shifts, embedding_first, mixing_first, expand_first, shrink_first, classifier_first, scale_first_moments, shifts_first, embedding_second, mixing_second, expand_second, shrink_second, classifier_second, scales_second, shifts_second, embedding_outer, mixing_outer, expand_outer, shrink_outer, classifier_outer, scales_outer, shifts_outer):
    weights = (embedding, mixing, expand, shrink, classifier, scales, shifts)
    firsts = (embedding_first, mixing_first, expand_first, shrink_first, classifier_first, scale_first_moments, shifts_first)
    seconds = (embedding_second, mixing_second, expand_second, shrink_second, classifier_second, scales_second, shifts_second)
    outers = (embedding_outer, mixing_outer, expand_outer, shrink_outer, classifier_outer, scales_outer, shifts_outer)
    step_rates = (matrix_rate,) * 4 + (head_rate,) + (vector_rate,) * 2
    classes = jnp.arange(C, dtype=jnp.int32)
    loss_rows = []
    norm_rows = []
    means = [[] for member in range(7)]
    squares = [[] for member in range(7)]
    moved = [jnp.zeros_like(weight) for weight in weights]
    for group_index in range(GROUPS):
        blocks = patches[group_index].reshape(N_DP, IMG_DEV, PATCH_EDGE, PD)
        own_labels = labels[group_index].reshape(N_DP, IMG_DEV)
        pair_blocks = partner[group_index].reshape(N_DP, IMG_DEV)
        mate_labels = jnp.take_along_axis(own_labels, pair_blocks, axis=1)

        def block_step(running, block):
            gradients, loss_sum, weight_total = running
            images, labels_a, pair_index, second_labels = block
            label_hot = (labels_a[:, None] == classes[None, :]).astype(jnp.float32)
            mate_hot = (second_labels[:, None] == classes[None, :]).astype(jnp.float32)
            first_mix_weight = mix_share * lax.optimization_barrier(jnp.sum(label_hot * class_weight[None, :], axis=1))
            weight_b = (1.0 - mix_share) * lax.optimization_barrier(jnp.sum(mate_hot * class_weight[None, :], axis=1))
            block_loss, pullback = jax.vjp(lambda current: forward(current, images, pair_index, label_hot, mate_hot, first_mix_weight, weight_b), weights)
            block_grads, = pullback(jnp.ones_like(block_loss))
            gradients = jax.tree.map(jnp.add, gradients, block_grads)
            return ((gradients, loss_sum + block_loss, weight_total + jnp.sum(first_mix_weight + weight_b)), None)
        zeros_start = (tuple((jnp.zeros_like(weight) for weight in weights)), jnp.zeros((), jnp.float32), jnp.zeros((), jnp.float32))
        (gradients, loss_sum, weight_total), unused = lax.scan(block_step, zeros_start, (blocks, own_labels, pair_blocks, mate_labels))
        gradients = tuple((gradient / weight_total for gradient in gradients))
        grad_size = jnp.sqrt(sum((jnp.sum(gradient * gradient) for gradient in gradients)))
        factor = clip_limit / jnp.maximum(grad_size, clip_limit)
        for member in range(7):
            inner, mean_new, square_new = adamw(weights[member], factor * gradients[member], firsts[member][group_index], seconds[member][group_index], step_rates[member])
            moved[member] = moved[member] + (weights[member] - inner)
            means[member].append(mean_new)
            squares[member].append(square_new)
        loss_rows.append(jnp.stack([loss_sum, weight_total]))
        norm_rows.append(grad_size)
    updates = []
    velocities = []
    for member in range(7):
        average = moved[member] / GROUPS
        velocity = outer_momentum * outers[member] + average
        velocities.append(velocity)
        updates.append(weights[member] - outer_rate * (average + outer_momentum * velocity))
    mean_out = [jnp.stack(entry) for entry in means]
    square_out = [jnp.stack(entry) for entry in squares]
    return (jnp.stack(loss_rows), jnp.stack(norm_rows), updates[0], updates[1], updates[2], updates[3], updates[4], updates[5], updates[6], mean_out[0], mean_out[1], mean_out[2], mean_out[3], mean_out[4], mean_out[5], mean_out[6], square_out[0], square_out[1], square_out[2], square_out[3], square_out[4], square_out[5], square_out[6], velocities[0], velocities[1], velocities[2], velocities[3], velocities[4], velocities[5], velocities[6])
```

```python
import functools

import jax
import jax.numpy as jnp
from jax import lax
from jax.experimental import pallas as pl
from jax.experimental.pallas import tpu as pltpu
from jax.sharding import PartitionSpec as P

F32 = jnp.float32
BF16 = jnp.bfloat16
MESH = pl.DeviceIdType.MESH
VMEM = pltpu.VMEM
SMEM = pltpu.SMEM

D = 384
PATCHES = 196
ROWS = 208
STEP = 10
LANE = 128

mix_share = 0.7
clip_limit = 0.01
beta_one = 0.9
beta_two = 0.999
adam_eps = 1e-08
weight_decay = 0.05
matrix_rate = 0.05
head_rate = 0.5
vector_rate = 0.4
outer_rate = 0.7
outer_momentum = 0.9

GELU_A = 0.7978845608028654
GELU_B = GELU_A * 0.044715

B_EXP, B_EMB, B_MIX, B_SMALL, B_ACT, B_ROWS = 0, 392, 584, 640, 656, 672
MIX_BLOCK = 56
A_EMB, A_EXP, A_SHR, A_ROWS = 0, 192, 584, 976
C_CLS, C_MIX, C_SCA, C_SHI, C_ROWS = 0, 392, 592, 600, 624


def dot(a, b, dims=((1,), (0,)), precision=None):
    return lax.dot_general(
        a, b, (dims, ((), ())), preferred_element_type=F32, precision=precision
    )


def exact(a, b, dims=((1,), (0,))):
    return dot(a, b, dims, lax.Precision.HIGHEST)


def rounded(a):
    return a.astype(BF16).astype(F32)


def greet(peers):
    barrier = pltpu.get_barrier_semaphore()
    for peer in peers:
        pl.semaphore_signal(barrier, inc=1, device_id=peer, device_id_type=MESH)
    pl.semaphore_wait(barrier, len(peers))


def remote(src, dst, send_sem, recv_sem, peer):
    return pltpu.make_async_remote_copy(
        src_ref=src, dst_ref=dst, send_sem=send_sem, recv_sem=recv_sem,
        device_id=peer, device_id_type=MESH,
    )


def move_kernel(
    G, MP, NI,
    partner, patches, emb, expa, shr, cls, sca, shi,
    rows, e_all, w1, w2, wc, small,
    stage, rs_send, rs_recv, wz_send, wz_recv, wg_send, wg_recv, sm_send, sm_recv,
):
    z = lax.axis_index("mp")
    g = lax.axis_index("group")
    NP = NI // 2
    zpeer = [lax.rem(z + d, MP) for d in range(1, MP)]
    gpeer = [lax.rem(g + d, G) for d in range(1, G)]
    greet([{"mp": t} for t in zpeer] + [{"group": t} for t in gpeer])

    hid = expa.shape[1]
    ncls = cls.shape[1]
    cpad = wc.shape[1] // MP

    e_all[z] = emb[...].astype(BF16)
    w1[:, pl.ds(pl.multiple_of(z * hid, LANE), hid)] = expa[0:D, :].astype(BF16)
    w2[pl.ds(pl.multiple_of(z * hid, 16), hid), :] = shr[...].astype(BF16)
    head = jnp.concatenate([cls[0:D, :], jnp.zeros((D, cpad - ncls), F32)], axis=1)
    wc[:, pl.ds(pl.multiple_of(z * cpad, LANE), cpad)] = head.astype(BF16)
    small[z] = jnp.zeros(small.shape[1:], F32)
    small[z, 0:5, 0 : D // MP] = sca[...]
    small[z, 5:10, 0 : D // MP] = shi[...]
    small[z, 10:11, :] = rounded(expa[D : D + 1, :])
    small[z, 11:12, 0:ncls] = rounded(cls[D : D + 1, :])

    er, hr, dr = emb.shape[0] // G, hid // G, D // G

    def pieces(t, j):
        return (
            e_all.at[t, pl.ds(pl.multiple_of(j * er, 16), er), :],
            w1.at[pl.ds(pl.multiple_of(j * dr, 16), dr), pl.ds(pl.multiple_of(t * hid, LANE), hid)],
            w2.at[pl.ds(pl.multiple_of(t * hid + j * hr, 16), hr), :],
            wc.at[pl.ds(pl.multiple_of(j * dr, 16), dr), pl.ds(pl.multiple_of(t * cpad, LANE), cpad)],
        )

    started = []
    for d, t in enumerate(zpeer):
        c = remote(small.at[z], small.at[z], sm_send.at[d], sm_recv.at[z], {"mp": t})
        c.start()
        started.append(c)
        for k, part in enumerate(pieces(z, g)):
            c = remote(part, part, wz_send.at[d, k], wz_recv.at[z, k], {"mp": t})
            c.start()
            started.append(c)

    share = F32(mix_share)
    other = F32(1.0 - mix_share)

    def blend(i):
        return share * patches[i] + other * patches[partner[i]]

    tail = rows.shape[-2] - 192

    def put(ref, lead, value):
        ref[lead + (slice(0, 192), slice(None))] = value[0:192].astype(BF16)
        last = jnp.concatenate([value[192:], jnp.zeros((tail - (PATCHES - 192), LANE), F32)], axis=0)
        ref[lead + (slice(192, 192 + tail), slice(None))] = last.astype(BF16)

    def blend_pair(t, p, ref, lead):
        a = blend(t * NI + 2 * p)
        b = blend(t * NI + 2 * p + 1)
        put(ref, lead + (0,), a[:, 0:LANE])
        put(ref, lead + (1,), b[:, 0:LANE])
        put(ref, lead + (2,), jnp.concatenate([a[:, LANE:], b[:, LANE:]], axis=1))

    def send(p, d):
        return remote(stage.at[d, p], rows.at[z, p], rs_send.at[d, p], rs_recv.at[z, p], {"mp": zpeer[d]})

    def each_pair(p, carry):
        for d in range(MP - 1):
            blend_pair(zpeer[d], p, stage, (d, p))
            send(p, d).start()
        return carry

    lax.fori_loop(0, NP, each_pair, 0)

    for d in range(1, MP):
        t = lax.rem(z + MP - d, MP)
        for k, part in enumerate(pieces(t, g)):
            remote(part, part, wz_send.at[d - 1, k], wz_recv.at[t, k], {"mp": t}).wait_recv()
            for e, j in enumerate(gpeer):
                c = remote(part, part, wg_send.at[d - 1, e, k], wg_recv.at[t, g, k], {"group": j})
                c.start()
                started.append(c)

    def own_pair(p, carry):
        blend_pair(z, p, rows, (z, p))
        return carry

    lax.fori_loop(0, NP, own_pair, 0)

    def drain(p, carry):
        for d in range(MP - 1):
            send(p, d).wait_send()
            t = zpeer[d]
            remote(stage.at[d, p], rows.at[t, p], rs_send.at[d, p], rs_recv.at[t, p], {"mp": t}).wait_recv()
        return carry

    lax.fori_loop(0, NP, drain, 0)
    for c in started:
        c.wait_send()
    for t in zpeer:
        remote(small.at[t], small.at[t], sm_send.at[0], sm_recv.at[t], {"mp": t}).wait_recv()
        for j in gpeer:
            for k, part in enumerate(pieces(t, j)):
                remote(part, part, wg_send.at[0, 0, k], wg_recv.at[t, j, k], {"group": j}).wait_recv()


def move(G, MP, partner, patches, emb, expa, shr, cls, sca, shi):
    NI = patches.shape[0] // MP
    NP = NI // 2
    hid = expa.shape[1]
    cpad = -(-cls.shape[1] // LANE) * LANE
    dma = pltpu.SemaphoreType.DMA
    vm = pl.BlockSpec(memory_space=VMEM)
    ge = max(G - 1, 1)
    return pl.pallas_call(
        functools.partial(move_kernel, G, MP, NI),
        out_shape=(
            jax.ShapeDtypeStruct((MP, NP, 3, ROWS, LANE), BF16),
            jax.ShapeDtypeStruct((MP, emb.shape[0], D), BF16),
            jax.ShapeDtypeStruct((D, hid * MP), BF16),
            jax.ShapeDtypeStruct((hid * MP, D), BF16),
            jax.ShapeDtypeStruct((D, cpad * MP), BF16),
            jax.ShapeDtypeStruct((MP, 16, hid), F32),
        ),
        in_specs=[pl.BlockSpec(memory_space=SMEM)] + [vm] * 7,
        out_specs=(vm,) * 6,
        scratch_shapes=[
            pltpu.VMEM((MP - 1, NP, 3, ROWS, LANE), BF16),
            dma((MP - 1, NP)),
            dma((MP, NP)),
            dma((MP - 1, 4)),
            dma((MP, 4)),
            dma((MP - 1, ge, 4)),
            dma((MP, G, 4)),
            dma((MP - 1,)),
            dma((MP,)),
        ],
        compiler_params=pltpu.CompilerParams(
            collective_id=0, has_side_effects=True, vmem_limit_bytes=56 << 20
        ),
    )(partner, patches, emb, expa, shr, cls, sca, shi)


def step_kernel(
    MP, NI, ncls,
    labels, partner, rows, e_all, w1, w2, wc, small, mixing, class_weight,
    bundle, factors,
    xs, gp, s0, s1, mx, mi, fi, ep, mm, mt, mbias, vec, b1, asum, s1sum, la, lb,
    dact, ds2, dh, csum, gw, ge, gm, gmb, gvec,
):
    z = lax.axis_index("mp")
    NP = NI // 2
    PR = 2 * ROWS
    hid_all = w1.shape[1]
    hid = hid_all // MP
    cpad = wc.shape[1] // MP
    CH = 256
    NCH = hid_all // CH
    er = e_all.shape[1]

    full = jnp.zeros((16, D), F32)
    for t in range(MP):
        block = small[t]
        full = full + (pltpu.roll(block, t * (D // MP), 1) if t else block)
    vec[...] = full
    for t in range(MP):
        b1[:, t * hid : (t + 1) * hid] = small[t, 10:11, :]
        ep[t * LANE : (t + 1) * LANE, :] = e_all[t, 0:LANE, :]
        half = er - LANE
        ep[MP * LANE + t * half : MP * LANE + (t + 1) * half, :] = e_all[t, LANE:er, :]

    wide = jnp.concatenate([mixing[...], jnp.zeros((PATCHES, 256 - PATCHES - 1), F32)], axis=1)
    wide = jnp.concatenate([wide, jnp.zeros((256 - PATCHES, 256), F32)], axis=0)
    column = lax.broadcasted_iota(jnp.int32, (256, 256), 1)
    square = jnp.where(column < PATCHES, wide, 0.0)
    mm[...] = square[0:ROWS, 0:ROWS].astype(BF16)
    mt[...] = jnp.transpose(square)[0:ROWS, 0:ROWS].astype(BF16)
    mbias[...] = rounded(jnp.sum(jnp.where(column == PATCHES, wide, 0.0), axis=1, keepdims=True)[0:ROWS])

    asum[...] = jnp.zeros_like(asum)
    s1sum[...] = jnp.zeros_like(s1sum)
    csum[...] = jnp.zeros_like(csum)
    gw[...] = jnp.zeros_like(gw)
    ge[...] = jnp.zeros_like(ge)
    gm[...] = jnp.zeros_like(gm)
    gmb[...] = jnp.zeros_like(gmb)
    gvec[...] = jnp.zeros_like(gvec)

    def scale(k):
        return vec[k : k + 1, :]

    def shift(k):
        return vec[5 + k : 6 + k, :]

    def forward(p, carry):
        for t in range(MP):
            xs[p, 0:ROWS, t * LANE : (t + 1) * LANE] = rows[t, p, 0]
            xs[p, ROWS:PR, t * LANE : (t + 1) * LANE] = rows[t, p, 1]
        for t in range(0, MP, 2):
            left, right = rows[t, p, 2], rows[t + 1, p, 2]
            at = MP * LANE + t * 64
            xs[p, 0:ROWS, at : at + LANE] = jnp.concatenate([left[:, 0:64], right[:, 0:64]], axis=1)
            xs[p, ROWS:PR, at : at + LANE] = jnp.concatenate([left[:, 64:], right[:, 64:]], axis=1)
        stream0 = dot(xs[p], ep[...]) + shift(3)
        s0[p] = stream0
        mi[p] = (scale(0) * stream0 + shift(0)).astype(BF16)
        for b in range(2):
            r = slice(b * ROWS, (b + 1) * ROWS)
            mixed = dot(mm[...], mi[p, r, :]) + mbias[...]
            mx[p, r, :] = mixed
            stream1 = s0[p, r, :] + scale(1) * mixed
            s1[p, r, :] = stream1
            fi[p, r, :] = (scale(2) * stream1 + shift(1)).astype(BF16)
            s1sum[pl.ds(2 * p + b, 1), :] = jnp.sum(stream1[0:PATCHES], axis=0, keepdims=True)

        def chunk(c, carry):
            cols = pl.ds(pl.multiple_of(c * CH, CH), CH)
            for b in range(2):
                r = slice(b * ROWS, (b + 1) * ROWS)
                h = dot(fi[p, r, :], w1[:, cols]) + b1[:, cols]
                sq = h * h
                s = 0.5 * jnp.tanh(h * (GELU_A + GELU_B * sq)) + 0.5
                act = rounded(h * s)
                asum[pl.ds(2 * p + b, 1), cols] = jnp.sum(act[0:PATCHES], axis=0, keepdims=True)
                gp[p, r, cols] = s + s * (1.0 - s) * (h * (2.0 * GELU_A + 6.0 * GELU_B * sq))
                gp[p, b * ROWS + PATCHES : (b + 1) * ROWS, cols] = jnp.zeros((ROWS - PATCHES, CH), F32)
            return carry

        lax.fori_loop(0, NCH, chunk, 0)
        return carry

    lax.fori_loop(0, NP, forward, 0)

    la[...] = jnp.full(la.shape, -1, jnp.int32)
    lb[...] = jnp.full(lb.shape, -1, jnp.int32)
    for i in range(NI):
        own = labels[z * NI + i]
        mate = labels[partner[z * NI + i]]
        la[i : i + 1, :] = jnp.full((1, LANE), own, jnp.int32)
        lb[i : i + 1, :] = jnp.full((1, LANE), mate, jnp.int32)
    outsum = exact(asum[...], w2[...].astype(F32)) + PATCHES * shift(2)
    stream2 = s1sum[...] + scale(3) * outsum
    pooled = (scale(4) * (stream2 * (1.0 / PATCHES)) + shift(4)).astype(BF16)
    bias = jnp.concatenate([small[t, 11:12, 0:cpad] for t in range(MP)], axis=1)
    lane = lax.broadcasted_iota(jnp.int32, (16, cpad * MP), 1)
    inside = lax.rem(lane, cpad)
    valid = inside < ncls
    class_id = (lane // cpad) * ncls + inside
    logits = jnp.where(valid, dot(pooled, wc[...]) + bias, -1e30)
    hot_a = jnp.where(valid & (class_id == la[:, 0:1]), 1.0, 0.0)
    hot_b = jnp.where(valid & (class_id == lb[:, 0:1]), 1.0, 0.0)
    weight_a = mix_share * jnp.sum(hot_a * class_weight[...], axis=1, keepdims=True)
    weight_b = (1.0 - mix_share) * jnp.sum(hot_b * class_weight[...], axis=1, keepdims=True)
    top = jnp.max(logits, axis=1, keepdims=True)
    exps = jnp.where(valid, jnp.exp(logits - top), 0.0)
    exp_sum = jnp.sum(exps, axis=1, keepdims=True)
    log_total = top + jnp.log(exp_sum)
    target_a = jnp.sum(hot_a * logits, axis=1, keepdims=True)
    target_b = jnp.sum(hot_b * logits, axis=1, keepdims=True)
    loss = jnp.sum(weight_a * (log_total - target_a) + weight_b * (log_total - target_b), axis=0, keepdims=True)
    total = jnp.sum(weight_a + weight_b, axis=0, keepdims=True)
    dlog = ((weight_a + weight_b) * (exps / exp_sum) - weight_a * hot_a - weight_b * hot_b).astype(BF16)
    dfinal = dot(dlog, wc[...], ((1,), (1,))) * (1.0 / PATCHES)
    dstream2 = scale(4) * dfinal
    ds2[...] = dstream2
    dout = scale(3) * dstream2
    low = dout.astype(BF16)
    dact[...] = dot(low, w2[...], ((1,), (1,)))
    factors[:, 0:16, :] = jnp.broadcast_to(low[None], (MP, 16, D))
    factors[:, 16:32, :] = jnp.broadcast_to(pooled[None], (MP, 16, D))
    for t in range(MP):
        factors[t, 32:48, 0:cpad] = dlog[:, t * cpad : (t + 1) * cpad]
        factors[t, 32:48, cpad:] = jnp.zeros((16, D - cpad), BF16)

    def backward(p, carry):
        def chunk(c, carry):
            cols = pl.ds(pl.multiple_of(c * CH, CH), CH)
            for b in range(2):
                r = slice(b * ROWS, (b + 1) * ROWS)
                dh[r, cols] = (gp[p, r, cols] * dact[pl.ds(2 * p + b, 1), cols]).astype(BF16)
            value = dh[:, cols]
            csum[0:1, cols] += jnp.sum(value.astype(F32), axis=0, keepdims=True)
            gw[:, cols] += dot(fi[p], value, ((0,), (0,)))
            return carry

        lax.fori_loop(0, NCH, chunk, 0)
        dffn = dot(dh[...], w1[...], ((1,), (1,)))
        gvec[2:3, :] += jnp.sum(dffn * s1[p], axis=0, keepdims=True)
        gvec[6:7, :] += jnp.sum(dffn, axis=0, keepdims=True)
        for b in range(2):
            r = slice(b * ROWS, (b + 1) * ROWS)
            d1 = ds2[pl.ds(2 * p + b, 1), :] + scale(2) * dffn[r]
            gvec[1:2, :] += jnp.sum(mx[p, r, :] * d1, axis=0, keepdims=True)
            dmixed = (scale(1) * d1).astype(BF16)
            gm[...] += dot(dmixed, mi[p, r, :], ((1,), (1,)))
            gmb[...] += dmixed.astype(F32)
            dmixer = dot(mt[...], dmixed)
            gvec[0:1, :] += jnp.sum(dmixer * s0[p, r, :], axis=0, keepdims=True)
            gvec[5:6, :] += jnp.sum(dmixer, axis=0, keepdims=True)
            d0 = (d1 + scale(0) * dmixer).astype(BF16)
            ge[...] += dot(xs[p, r, :], d0, ((0,), (0,)))
        return carry

    lax.fori_loop(0, NP, backward, 0)

    gvec[3:4, :] = jnp.sum(outsum * dstream2, axis=0, keepdims=True)
    gvec[4:5, :] = jnp.sum(dfinal * stream2, axis=0, keepdims=True)
    gvec[7:8, :] = PATCHES * jnp.sum(dout, axis=0, keepdims=True)
    gvec[8:9, :] = (
        PATCHES * jnp.sum(dstream2, axis=0, keepdims=True) + scale(2) * gvec[6:7, :] + scale(0) * gvec[5:6, :]
    )
    gvec[9:10, :] = PATCHES * jnp.sum(dfinal, axis=0, keepdims=True)
    lane = lax.broadcasted_iota(jnp.int32, (1, D), 1)
    gvec[10:11, :] = jnp.where(lane == 0, loss, jnp.where(lane == 1, total, 0.0))

    row = lax.broadcasted_iota(jnp.int32, (ROWS, 256), 0)
    column = lax.broadcasted_iota(jnp.int32, (ROWS, 256), 1)
    bias_grad = jnp.sum(gmb[...], axis=1, keepdims=True)
    grad = jnp.concatenate([gm[...], jnp.zeros((ROWS, 256 - ROWS), F32)], axis=1)
    grad = jnp.where(column < PATCHES, grad, jnp.where(column == PATCHES, bias_grad, 0.0))
    grad = jnp.where(row < PATCHES, grad, 0.0)
    for t in range(MP):
        bundle[t, B_EXP : B_EXP + D, :] = gw[:, t * hid : (t + 1) * hid]
        bundle[t, B_EXP + D : B_EMB, :] = jnp.concatenate(
            [csum[:, t * hid : (t + 1) * hid], jnp.zeros((B_EMB - B_EXP - D - 1, hid), F32)], axis=0
        )
        bundle[t, B_EMB : B_EMB + LANE, :] = ge[t * LANE : (t + 1) * LANE, :]
        half = er - LANE
        bundle[t, B_EMB + LANE : B_EMB + er, :] = ge[MP * LANE + t * half : MP * LANE + (t + 1) * half, :]
        bundle[t, B_MIX:B_SMALL, :] = jnp.zeros((MIX_BLOCK, D), F32)
        n = min(MIX_BLOCK, ROWS - t * MIX_BLOCK)
        bundle[t, B_MIX : B_MIX + n, 0:256] = grad[t * MIX_BLOCK : t * MIX_BLOCK + n]
        bundle[t, B_SMALL:B_ACT, :] = gvec[...]
        bundle[t, B_ACT:B_ROWS, :] = asum[:, t * hid : (t + 1) * hid]


def local_step(MP, ncls, labels, partner, rows, e_all, w1, w2, wc, small, mixing, class_weight):
    NP = rows.shape[1]
    NI = 2 * NP
    PR = 2 * ROWS
    hid_all = w1.shape[1]
    pd = e_all.shape[0] * e_all.shape[1]
    vm = pl.BlockSpec(memory_space=VMEM)
    sm = pl.BlockSpec(memory_space=SMEM)
    return pl.pallas_call(
        functools.partial(step_kernel, MP, NI, ncls),
        out_shape=(
            jax.ShapeDtypeStruct((MP, B_ROWS, D), F32),
            jax.ShapeDtypeStruct((MP, 48, D), BF16),
        ),
        in_specs=[sm, sm] + [vm] * 8,
        out_specs=(vm, vm),
        scratch_shapes=[
            VMEM((NP, PR, pd), BF16),
            VMEM((NP, PR, hid_all), F32),
            VMEM((NP, PR, D), F32),
            VMEM((NP, PR, D), F32),
            VMEM((NP, PR, D), F32),
            VMEM((NP, PR, D), BF16),
            VMEM((NP, PR, D), BF16),
            VMEM((pd, D), BF16),
            VMEM((ROWS, ROWS), BF16),
            VMEM((ROWS, ROWS), BF16),
            VMEM((ROWS, 1), F32),
            VMEM((16, D), F32),
            VMEM((1, hid_all), F32),
            VMEM((16, hid_all), F32),
            VMEM((16, D), F32),
            VMEM((16, LANE), jnp.int32),
            VMEM((16, LANE), jnp.int32),
            VMEM((16, hid_all), F32),
            VMEM((16, D), F32),
            VMEM((PR, hid_all), BF16),
            VMEM((1, hid_all), F32),
            VMEM((D, hid_all), F32),
            VMEM((pd, D), F32),
            VMEM((ROWS, ROWS), F32),
            VMEM((ROWS, D), F32),
            VMEM((16, D), F32),
        ],
        compiler_params=pltpu.CompilerParams(vmem_limit_bytes=62 << 20),
    )(labels, partner, rows, e_all, w1, w2, wc, small, mixing, class_weight)


def adamw(weight, gradient, moment_one, moment_two, rate):
    mean_new = beta_one * moment_one + (1.0 - beta_one) * gradient
    square_new = beta_two * moment_two + (1.0 - beta_two) * gradient * gradient
    mean_hat = mean_new * (1.0 / (1.0 - beta_one**STEP))
    square_hat = square_new * (1.0 / (1.0 - beta_two**STEP))
    moved = rate * (mean_hat / (jnp.sqrt(square_hat) + adam_eps) + weight_decay * weight)
    return moved, mean_new, square_new


def sum_kernel(
    G, DP, MP,
    bundle, factors,
    emb, mixing, expa, shr, cls, sca, shi,
    emb1, mixing1, expa1, shr1, cls1, sca1, shi1,
    emb2, mixing2, expa2, shr2, cls2, sca2, shi2,
    g_emb, g_mix, g_exp, g_shr, g_cls, g_vec, sum_a, sum_c, info,
    rb, rc, yb, yc, nz, mva, mvc, h1a, h1c, h2a, h2c,
    zs, zr, ys, yr, ns, nr, gs, gr,
):
    z = lax.axis_index("mp")
    y = lax.axis_index("dp")
    g = lax.axis_index("group")
    zpeer = [lax.rem(z + d, MP) for d in range(1, MP)]
    ypeer = [lax.rem(y + d, DP) for d in range(1, DP)]
    gstep = []
    if G > 1:
        gstep.append(g + 1 - 2 * lax.rem(g, 2))
    if G > 2:
        gstep.append(lax.rem(g + 2, 4))
    greet([{"mp": t} for t in zpeer] + [{"dp": t} for t in ypeer] + [{"group": t} for t in gstep])

    started = []

    def go(*args):
        c = remote(*args)
        c.start()
        started.append(c)

    for d, t in enumerate(zpeer):
        go(factors.at[t], rc.at[z], zs.at[d, 0], zr.at[z, 0], {"mp": t})
        go(bundle.at[t], rb.at[z], zs.at[d, 1], zr.at[z, 1], {"mp": t})
    rc[z] = factors[z]
    rb[z, B_SMALL:, :] = bundle[z, B_SMALL:, :]
    for t in zpeer:
        remote(factors.at[t], rc.at[t], zs.at[0, 0], zr.at[t, 0], {"mp": t}).wait_recv()
        remote(bundle.at[t], rb.at[t], zs.at[0, 1], zr.at[t, 1], {"mp": t}).wait_recv()

    total = bundle[z, 0:B_SMALL, :]
    for t in zpeer:
        total = total + rb[t, 0:B_SMALL, :]
    yb[y, 0:B_SMALL, :] = total
    vector = rb[0, B_SMALL:B_ACT, :]
    for t in range(1, MP):
        vector = vector + rb[t, B_SMALL:B_ACT, :]
    yb[y, B_SMALL:B_ACT, :] = vector
    for t in range(MP):
        yb[y, B_ACT + 16 * t : B_ACT + 16 * (t + 1), :] = rb[t, B_ACT:B_ROWS, :]
        for k in range(3):
            at = (k * MP + t) * 16
            yc[y, at : at + 16, :] = rc[t, 16 * k : 16 * (k + 1), :]
    for d, t in enumerate(ypeer):
        go(yb.at[y], yb.at[y], ys.at[d, 0], yr.at[y, 0], {"dp": t})
        go(yc.at[y], yc.at[y], ys.at[d, 1], yr.at[y, 1], {"dp": t})
    for t in ypeer:
        remote(yb.at[t], yb.at[t], ys.at[0, 0], yr.at[t, 0], {"dp": t}).wait_recv()
        remote(yc.at[t], yc.at[t], ys.at[0, 1], yr.at[t, 1], {"dp": t}).wait_recv()

    def over_dp(lo, hi):
        value = yb[0, lo:hi, :]
        for t in range(1, DP):
            value = value + yb[t, lo:hi, :]
        return value

    n = 16 * MP
    cpad = g_cls.shape[1]
    grad_shr = jnp.zeros((D, D), F32)
    grad_cls = jnp.zeros((D, cpad), F32)
    cls_bias = jnp.zeros((1, cpad), F32)
    for t in range(DP):
        acts = yb[t, B_ACT : B_ACT + n, :]
        dout, pooled, dlog = yc[t, 0:n, :], yc[t, n : 2 * n, :], yc[t, 2 * n : 3 * n, 0:cpad]
        grad_shr = grad_shr + exact(acts, dout.astype(F32), ((0,), (0,)))
        grad_cls = grad_cls + dot(pooled, dlog, ((0,), (0,)))
        cls_bias = cls_bias + jnp.sum(dlog.astype(F32), axis=0, keepdims=True)
    g_shr[...] = grad_shr
    g_cls[0:D, :] = grad_cls
    g_cls[D:, :] = jnp.concatenate([cls_bias, jnp.zeros((g_cls.shape[0] - D - 1, cpad), F32)], axis=0)
    g_exp[...] = over_dp(B_EXP, B_EMB)
    g_emb[...] = over_dp(B_EMB, B_MIX)
    vector = over_dp(B_SMALL, B_ACT)
    mix = over_dp(B_MIX, B_SMALL)[:, 0:256]

    def squares(v):
        return jnp.sum(jnp.sum(v * v, axis=1, keepdims=True), axis=0, keepdims=True)

    part = (
        squares(g_exp[...]) + squares(g_emb[...]) + squares(g_shr[...]) + squares(g_cls[...]) + squares(mix)
    )
    nz[z, 0:MIX_BLOCK, :] = mix
    nz[z, MIX_BLOCK:, :] = jnp.broadcast_to(part, (8, 256))
    for d, t in enumerate(zpeer):
        go(nz.at[z], nz.at[z], ns.at[d], nr.at[z], {"mp": t})
    for t in zpeer:
        remote(nz.at[t], nz.at[t], ns.at[0], nr.at[t], {"mp": t}).wait_recv()
    square = nz[0, MIX_BLOCK : MIX_BLOCK + 1, 0:1]
    for t in range(1, MP):
        square = square + nz[t, MIX_BLOCK : MIX_BLOCK + 1, 0:1]
    square = square + squares(vector[0:10])
    loss_sum = vector[10:11, 0:1]
    weight_total = vector[10:11, 1:2]
    size = jnp.sqrt(square) / weight_total
    factor = clip_limit / jnp.maximum(size, clip_limit)
    scaled = factor / weight_total
    lane = lax.broadcasted_iota(jnp.int32, (8, LANE), 1)
    info[...] = jnp.where(lane == 0, loss_sum, jnp.where(lane == 1, weight_total, size))

    g_exp[...] = g_exp[...] * scaled
    g_emb[...] = g_emb[...] * scaled
    g_shr[...] = g_shr[...] * scaled
    g_cls[...] = g_cls[...] * scaled
    for t in range(MP):
        g_mix[t * MIX_BLOCK : (t + 1) * MIX_BLOCK, :] = nz[t, 0:MIX_BLOCK, :] * scaled
    own = D // MP
    g_vec[...] = pltpu.roll(vector, lax.rem((MP - z) * own, D), 1)[:, 0:LANE] * scaled

    ncls = cls.shape[1]
    mva[A_EXP + D : A_SHR, :] = jnp.zeros((A_SHR - A_EXP - D, D), F32)
    mva[A_SHR + D :, :] = jnp.zeros((A_ROWS - A_SHR - D, D), F32)
    mvc[...] = jnp.zeros_like(mvc)
    mva[A_EMB : A_EMB + emb.shape[0], :] = adamw(emb[...], g_emb[...], emb1[...], emb2[...], matrix_rate)[0]
    mva[A_EXP : A_EXP + D + 1, :] = adamw(expa[...], g_exp[0 : D + 1, :], expa1[...], expa2[...], matrix_rate)[0]
    mva[A_SHR : A_SHR + shr.shape[0], :] = adamw(shr[...], g_shr[...], shr1[...], shr2[...], matrix_rate)[0]
    mvc[C_CLS : C_CLS + D + 1, 0:ncls] = adamw(cls[...], g_cls[0 : D + 1, 0:ncls], cls1[...], cls2[...], head_rate)[0]
    mvc[C_MIX : C_MIX + PATCHES, 0 : PATCHES + 1] = adamw(
        mixing[...], g_mix[0:PATCHES, 0 : PATCHES + 1], mixing1[...], mixing2[...], matrix_rate
    )[0]
    mvc[C_SCA : C_SCA + 5, 0:own] = adamw(sca[...], g_vec[0:5, 0:own], sca1[...], sca2[...], vector_rate)[0]
    mvc[C_SHI : C_SHI + 5, 0:own] = adamw(shi[...], g_vec[5:10, 0:own], shi1[...], shi2[...], vector_rate)[0]

    if G == 1:
        sum_a[...] = mva[...]
        sum_c[...] = mvc[...]
    else:
        ha, hc = A_ROWS // 2, C_ROWS // 2
        mine, theirs = lax.rem(g, 2), 1 - lax.rem(g, 2)

        def half(ref, k, n):
            return ref.at[pl.ds(pl.multiple_of(k * n, 8), n), :]

        peer = {"group": gstep[0]}
        go(half(mva, theirs, ha), h1a, gs.at[0], gr.at[0], peer)
        go(half(mvc, theirs, hc), h1c, gs.at[1], gr.at[1], peer)
        remote(h1a, h1a, gs.at[0], gr.at[0], peer).wait_recv()
        remote(h1c, h1c, gs.at[1], gr.at[1], peer).wait_recv()
        own_a = pl.ds(pl.multiple_of(mine * ha, 8), ha)
        own_c = pl.ds(pl.multiple_of(mine * hc, 8), hc)
        pa = mva[own_a, :] + h1a[...]
        pc = mvc[own_c, :] + h1c[...]
        if G > 2:
            h2a[0] = pa
            h2c[0] = pc
            far = {"group": gstep[1]}
            go(h2a.at[0], h2a.at[1], gs.at[2], gr.at[2], far)
            go(h2c.at[0], h2c.at[1], gs.at[3], gr.at[3], far)
            remote(h2a.at[0], h2a.at[1], gs.at[2], gr.at[2], far).wait_recv()
            remote(h2c.at[0], h2c.at[1], gs.at[3], gr.at[3], far).wait_recv()
            pa = h2a[0] + h2a[1]
            pc = h2c[0] + h2c[1]
        sum_a[own_a, :] = pa
        sum_c[own_c, :] = pc
        go(half(sum_a, mine, ha), half(sum_a, mine, ha), gs.at[4], gr.at[4], peer)
        go(half(sum_c, mine, hc), half(sum_c, mine, hc), gs.at[5], gr.at[5], peer)
        remote(h1a, half(sum_a, theirs, ha), gs.at[4], gr.at[4], peer).wait_recv()
        remote(h1c, half(sum_c, theirs, hc), gs.at[5], gr.at[5], peer).wait_recv()

    for c in started:
        c.wait_send()


def gradient_sums(G, DP, MP, bundle, factors, weights, firsts, seconds):
    dma = pltpu.SemaphoreType.DMA
    vm = pl.BlockSpec(memory_space=VMEM)
    cpad = -(-weights[4].shape[1] // LANE) * LANE
    s = jax.ShapeDtypeStruct
    rows_y = B_ACT + 16 * MP
    return pl.pallas_call(
        functools.partial(sum_kernel, G, DP, MP),
        out_shape=(
            s((weights[0].shape[0], D), F32),
            s((MP * MIX_BLOCK, 256), F32),
            s((B_EMB, D), F32),
            s((D, D), F32),
            s((392, cpad), F32),
            s((16, LANE), F32),
            s((A_ROWS, D), F32),
            s((C_ROWS, 256), F32),
            s((8, LANE), F32),
        ),
        in_specs=[vm] * 23,
        out_specs=(vm,) * 9,
        scratch_shapes=[
            VMEM((MP, B_ROWS, D), F32),
            VMEM((MP, 48, D), BF16),
            VMEM((DP, rows_y, D), F32),
            VMEM((DP, 48 * MP, D), BF16),
            VMEM((MP, MIX_BLOCK + 8, 256), F32),
            VMEM((A_ROWS, D), F32),
            VMEM((C_ROWS, 256), F32),
            VMEM((A_ROWS // 2, D), F32),
            VMEM((C_ROWS // 2, 256), F32),
            VMEM((2, A_ROWS // 2, D), F32),
            VMEM((2, C_ROWS // 2, 256), F32),
            dma((MP - 1, 2)),
            dma((MP, 2)),
            dma((max(DP - 1, 1), 2)),
            dma((DP, 2)),
            dma((MP - 1,)),
            dma((MP,)),
            dma((6,)),
            dma((6,)),
        ],
        compiler_params=pltpu.CompilerParams(
            collective_id=1, has_side_effects=True, vmem_limit_bytes=60 << 20
        ),
    )(bundle, factors, *weights, *firsts, *seconds)


def finish_kernel(groups, *refs):
    g_emb, g_mix, g_exp, g_shr, g_cls, g_vec, sum_a, sum_c = refs[:8]
    weights, firsts, seconds, outers = (refs[8 + 7 * k : 15 + 7 * k] for k in range(4))
    updates, means, squares, velocities = (refs[36 + 7 * k : 43 + 7 * k] for k in range(4))
    own = weights[5].shape[1]
    ncls = weights[4].shape[1]
    grads = (
        g_emb[...], g_mix[0:PATCHES, 0 : PATCHES + 1], g_exp[0 : D + 1, :], g_shr[...],
        g_cls[0 : D + 1, 0:ncls], g_vec[0:5, 0:own], g_vec[5:10, 0:own],
    )
    sums = (
        sum_a[A_EMB : A_EMB + weights[0].shape[0], :],
        sum_c[C_MIX : C_MIX + PATCHES, 0 : PATCHES + 1],
        sum_a[A_EXP : A_EXP + D + 1, :],
        sum_a[A_SHR : A_SHR + D, :],
        sum_c[C_CLS : C_CLS + D + 1, 0:ncls],
        sum_c[C_SCA : C_SCA + 5, 0:own],
        sum_c[C_SHI : C_SHI + 5, 0:own],
    )
    for k in range(7):
        gradient = grads[k]
        means[k][...] = beta_one * firsts[k][...] + (1.0 - beta_one) * gradient
        squares[k][...] = beta_two * seconds[k][...] + (1.0 - beta_two) * gradient * gradient
        average = sums[k] * (1.0 / groups)
        velocity = outer_momentum * outers[k][...] + average
        velocities[k][...] = velocity
        updates[k][...] = weights[k][...] - outer_rate * (average + outer_momentum * velocity)


def finish(G, grads, sums, weights, firsts, seconds, outers):
    vm = pl.BlockSpec(memory_space=VMEM)
    shapes = tuple(jax.ShapeDtypeStruct(w.shape, F32) for w in weights) * 4
    return pl.pallas_call(
        functools.partial(finish_kernel, G),
        out_shape=shapes,
        in_specs=[vm] * 36,
        out_specs=(vm,) * 28,
        compiler_params=pltpu.CompilerParams(vmem_limit_bytes=60 << 20),
    )(*grads, *sums, *weights, *firsts, *seconds, *outers)


def per_device(
    G, DP, MP,
    patches, labels, partner, class_weight,
    embedding, mixing, expand, shrink, classifier, scales, shifts, *state,
):
    weights = (embedding, mixing[0], expand[0], shrink[0], classifier, scales, shifts)
    flat = lambda group, lead: tuple(a.reshape(w.shape) for a, w in zip(group, weights, strict=True))
    firsts, seconds, outers = flat(state[0:7], 0), flat(state[7:14], 0), flat(state[14:21], 0)
    ncls = classifier.shape[1]
    cpad = -(-ncls // LANE) * LANE
    padded = jnp.pad(class_weight.reshape(MP, ncls), ((0, 0), (0, cpad - ncls))).reshape(1, MP * cpad)
    rows, e_all, w1, w2, wc, small = move(
        G, MP, partner[0], patches[0], embedding, expand[0], shrink[0], classifier, scales, shifts
    )
    bundle, factors = local_step(
        MP, ncls, labels[0], partner[0], rows, e_all, w1, w2, wc, small, mixing[0], padded
    )
    *grads, sum_a, sum_c, info = gradient_sums(G, DP, MP, bundle, factors, weights, firsts, seconds)
    done = finish(G, grads, (sum_a, sum_c), weights, firsts, seconds, outers)
    updates, means, squares, velocities = (list(done[7 * k : 7 * k + 7]) for k in range(4))
    for k in (1, 2, 3):
        updates[k], velocities[k] = updates[k][None], velocities[k][None]
        means[k], squares[k] = means[k][None], squares[k][None]
    means = [a[None] for a in means]
    squares = [a[None] for a in squares]
    return (info[0:1, 0:2], info[0, 2:3], *updates, *means, *squares, *velocities)


WEIGHT_SPECS = (
    P("mp", None),
    P(),
    P(None, None, "mp"),
    P(None, "mp", None),
    P(None, "mp"),
    P(None, "mp"),
    P(None, "mp"),
)
STATE_SPECS = (
    P("group", "mp", None),
    P("group", None, None, None),
    P("group", None, None, "mp"),
    P("group", None, "mp", None),
    P("group", None, "mp"),
    P("group", None, "mp"),
    P("group", None, "mp"),
)


def solution(mesh):
    G, DP, MP = mesh.shape["group"], mesh.shape["dp"], mesh.shape["mp"]
    return jax.shard_map(
        functools.partial(per_device, G, DP, MP),
        mesh=mesh,
        in_specs=(
            P("group", "dp", None, "mp"),
            P("group", "dp"),
            P("group", "dp"),
            P(),
            *WEIGHT_SPECS,
            *STATE_SPECS,
            *STATE_SPECS,
            *WEIGHT_SPECS,
        ),
        out_specs=(
            P("group", None),
            P("group"),
            *WEIGHT_SPECS,
            *STATE_SPECS,
            *STATE_SPECS,
            *WEIGHT_SPECS,
        ),
        check_vma=False,
    )
```

```python
import functools

import jax
import jax.numpy as jnp
from jax import lax
from jax.experimental import pallas as pl
from jax.experimental.pallas import tpu as pltpu
from jax.sharding import PartitionSpec as P

F32 = jnp.float32
BF16 = jnp.bfloat16
MESH = pl.DeviceIdType.MESH
VMEM = pltpu.VMEM
SMEM = pltpu.SMEM

D = 384
PATCHES = 196
ROWS = 208
STEP = 10
LANE = 128

mix_share = 0.7
clip_limit = 0.01
beta_one = 0.9
beta_two = 0.999
adam_eps = 1e-08
weight_decay = 0.05
matrix_rate = 0.05
head_rate = 0.5
vector_rate = 0.4
outer_rate = 0.7
outer_momentum = 0.9

GELU_A = 0.7978845608028654
GELU_B = GELU_A * 0.044715

S_VEC, S_ROWS = 56, 72
A_EMB, A_EXP, A_SHR, A_ROWS = 0, 192, 584, 992
C_CLS, C_MIX, C_SCA, C_SHI, C_ROWS = 0, 392, 592, 600, 624


def dot(a, b, dims=((1,), (0,)), precision=None):
    return lax.dot_general(
        a, b, (dims, ((), ())), preferred_element_type=F32, precision=precision
    )


def exact(a, b, dims=((1,), (0,))):
    return dot(a, b, dims, lax.Precision.HIGHEST)


def rounded(a):
    return a.astype(BF16).astype(F32)


def greet(peers):
    barrier = pltpu.get_barrier_semaphore()
    for peer in peers:
        pl.semaphore_signal(barrier, inc=1, device_id=peer, device_id_type=MESH)
    pl.semaphore_wait(barrier, len(peers))


def remote(src, dst, send_sem, recv_sem, peer):
    return pltpu.make_async_remote_copy(
        src_ref=src, dst_ref=dst, send_sem=send_sem, recv_sem=recv_sem,
        device_id=peer, device_id_type=MESH,
    )


def move_kernel(
    G, MP, NI,
    partner, patches, emb, expa, shr, cls, sca, shi,
    rows, e_all, w1, w2, wc, small,
    stage, rs_send, rs_recv, wz_send, wz_recv, wg_send, wg_recv, sm_send, sm_recv,
):
    z = lax.axis_index("mp")
    g = lax.axis_index("group")
    NP = NI // 2
    zpeer = [lax.rem(z + d, MP) for d in range(1, MP)]
    gpeer = [lax.rem(g + d, G) for d in range(1, G)]
    greet([{"mp": t} for t in zpeer] + [{"group": t} for t in gpeer])

    hid = expa.shape[1]
    ncls = cls.shape[1]
    cpad = wc.shape[1] // MP

    e_all[z] = emb[...].astype(BF16)
    w1[:, pl.ds(pl.multiple_of(z * hid, LANE), hid)] = expa[0:D, :].astype(BF16)
    w2[pl.ds(pl.multiple_of(z * hid, 16), hid), :] = shr[...].astype(BF16)
    head = jnp.concatenate([cls[0:D, :], jnp.zeros((D, cpad - ncls), F32)], axis=1)
    wc[:, pl.ds(pl.multiple_of(z * cpad, LANE), cpad)] = head.astype(BF16)
    small[z] = jnp.zeros(small.shape[1:], F32)
    small[z, 0:5, 0 : D // MP] = sca[...]
    small[z, 5:10, 0 : D // MP] = shi[...]
    small[z, 10:11, :] = rounded(expa[D : D + 1, :])
    small[z, 11:12, 0:ncls] = rounded(cls[D : D + 1, :])

    er, hr, dr = emb.shape[0] // G, hid // G, D // G

    def pieces(t, j):
        return (
            e_all.at[t, pl.ds(pl.multiple_of(j * er, 16), er), :],
            w1.at[pl.ds(pl.multiple_of(j * dr, 16), dr), pl.ds(pl.multiple_of(t * hid, LANE), hid)],
            w2.at[pl.ds(pl.multiple_of(t * hid + j * hr, 16), hr), :],
            wc.at[pl.ds(pl.multiple_of(j * dr, 16), dr), pl.ds(pl.multiple_of(t * cpad, LANE), cpad)],
        )

    started = []
    for d, t in enumerate(zpeer):
        c = remote(small.at[z], small.at[z], sm_send.at[d], sm_recv.at[z], {"mp": t})
        c.start()
        started.append(c)
        for k, part in enumerate(pieces(z, g)):
            c = remote(part, part, wz_send.at[d, k], wz_recv.at[z, k], {"mp": t})
            c.start()
            started.append(c)

    share = F32(mix_share)
    other = F32(1.0 - mix_share)

    def blend(i):
        return share * patches[i] + other * patches[partner[i]]

    tail = rows.shape[-2] - 192

    def put(ref, lead, value):
        ref[lead + (slice(0, 192), slice(None))] = value[0:192].astype(BF16)
        last = jnp.concatenate([value[192:], jnp.zeros((tail - (PATCHES - 192), LANE), F32)], axis=0)
        ref[lead + (slice(192, 192 + tail), slice(None))] = last.astype(BF16)

    def blend_pair(t, p, ref, lead):
        a = blend(t * NI + 2 * p)
        b = blend(t * NI + 2 * p + 1)
        put(ref, lead + (0,), a[:, 0:LANE])
        put(ref, lead + (1,), b[:, 0:LANE])
        put(ref, lead + (2,), jnp.concatenate([a[:, LANE:], b[:, LANE:]], axis=1))

    def send(p, d):
        return remote(stage.at[d, p], rows.at[z, p], rs_send.at[d, p], rs_recv.at[z, p], {"mp": zpeer[d]})

    def each_pair(p, carry):
        for d in range(MP - 1):
            blend_pair(zpeer[d], p, stage, (d, p))
            send(p, d).start()
        return carry

    lax.fori_loop(0, NP, each_pair, 0)

    for d in range(1, MP):
        t = lax.rem(z + MP - d, MP)
        for k, part in enumerate(pieces(t, g)):
            remote(part, part, wz_send.at[d - 1, k], wz_recv.at[t, k], {"mp": t}).wait_recv()
            for e, j in enumerate(gpeer):
                c = remote(part, part, wg_send.at[d - 1, e, k], wg_recv.at[t, g, k], {"group": j})
                c.start()
                started.append(c)

    def own_pair(p, carry):
        blend_pair(z, p, rows, (z, p))
        return carry

    lax.fori_loop(0, NP, own_pair, 0)

    def drain(p, carry):
        for d in range(MP - 1):
            send(p, d).wait_send()
            t = zpeer[d]
            remote(stage.at[d, p], rows.at[t, p], rs_send.at[d, p], rs_recv.at[t, p], {"mp": t}).wait_recv()
        return carry

    lax.fori_loop(0, NP, drain, 0)
    for c in started:
        c.wait_send()
    for t in zpeer:
        remote(small.at[t], small.at[t], sm_send.at[0], sm_recv.at[t], {"mp": t}).wait_recv()
        for j in gpeer:
            for k, part in enumerate(pieces(t, j)):
                remote(part, part, wg_send.at[0, 0, k], wg_recv.at[t, j, k], {"group": j}).wait_recv()


def move(G, MP, partner, patches, emb, expa, shr, cls, sca, shi):
    NI = patches.shape[0] // MP
    NP = NI // 2
    hid = expa.shape[1]
    cpad = -(-cls.shape[1] // LANE) * LANE
    dma = pltpu.SemaphoreType.DMA
    vm = pl.BlockSpec(memory_space=VMEM)
    ge = max(G - 1, 1)
    return pl.pallas_call(
        functools.partial(move_kernel, G, MP, NI),
        out_shape=(
            jax.ShapeDtypeStruct((MP, NP, 3, ROWS, LANE), BF16),
            jax.ShapeDtypeStruct((MP, emb.shape[0], D), BF16),
            jax.ShapeDtypeStruct((D, hid * MP), BF16),
            jax.ShapeDtypeStruct((hid * MP, D), BF16),
            jax.ShapeDtypeStruct((D, cpad * MP), BF16),
            jax.ShapeDtypeStruct((MP, 16, hid), F32),
        ),
        in_specs=[pl.BlockSpec(memory_space=SMEM)] + [vm] * 7,
        out_specs=(vm,) * 6,
        scratch_shapes=[
            pltpu.VMEM((MP - 1, NP, 3, ROWS, LANE), BF16),
            dma((MP - 1, NP)),
            dma((MP, NP)),
            dma((MP - 1, 4)),
            dma((MP, 4)),
            dma((MP - 1, ge, 4)),
            dma((MP, G, 4)),
            dma((MP - 1,)),
            dma((MP,)),
        ],
        compiler_params=pltpu.CompilerParams(
            collective_id=0, has_side_effects=True, vmem_limit_bytes=56 << 20
        ),
    )(partner, patches, emb, expa, shr, cls, sca, shi)


def step_kernel(
    MP, NI, ncls,
    labels, partner, rows, e_all, w1, w2, wc, small, mixing, class_weight,
    big, sm, acts, factors,
    xs, gp, s0, s1, mx, mi, fi, ep, mm, mt, mbias, vec, b1, asum, s1sum, la, lb,
    dact, ds2, dh, csum, gw, ge, gm, gmb, gvec,
):
    z = lax.axis_index("mp")
    NP = NI // 2
    PR = 2 * ROWS
    hid_all = w1.shape[1]
    hid = hid_all // MP
    cpad = wc.shape[1] // MP
    CH = 256
    NCH = hid_all // CH
    er = e_all.shape[1]

    full = jnp.zeros((16, D), F32)
    for t in range(MP):
        block = small[t]
        full = full + (pltpu.roll(block, t * (D // MP), 1) if t else block)
    vec[...] = full
    for t in range(MP):
        b1[:, t * hid : (t + 1) * hid] = small[t, 10:11, :]
        ep[t * LANE : (t + 1) * LANE, :] = e_all[t, 0:LANE, :]
        half = er - LANE
        ep[MP * LANE + t * half : MP * LANE + (t + 1) * half, :] = e_all[t, LANE:er, :]

    wide = jnp.concatenate([mixing[...], jnp.zeros((PATCHES, 256 - PATCHES - 1), F32)], axis=1)
    wide = jnp.concatenate([wide, jnp.zeros((256 - PATCHES, 256), F32)], axis=0)
    column = lax.broadcasted_iota(jnp.int32, (256, 256), 1)
    square = jnp.where(column < PATCHES, wide, 0.0)
    mm[...] = square[0:ROWS, 0:ROWS].astype(BF16)
    mt[...] = jnp.transpose(square)[0:ROWS, 0:ROWS].astype(BF16)
    mbias[...] = rounded(jnp.sum(jnp.where(column == PATCHES, wide, 0.0), axis=1, keepdims=True)[0:ROWS])

    asum[...] = jnp.zeros_like(asum)
    s1sum[...] = jnp.zeros_like(s1sum)
    csum[...] = jnp.zeros_like(csum)
    gw[...] = jnp.zeros_like(gw)
    ge[...] = jnp.zeros_like(ge)
    gm[...] = jnp.zeros_like(gm)
    gmb[...] = jnp.zeros_like(gmb)
    gvec[...] = jnp.zeros_like(gvec)

    def scale(k):
        return vec[k : k + 1, :]

    def shift(k):
        return vec[5 + k : 6 + k, :]

    def forward(p, carry):
        for t in range(MP):
            xs[p, 0:ROWS, t * LANE : (t + 1) * LANE] = rows[t, p, 0]
            xs[p, ROWS:PR, t * LANE : (t + 1) * LANE] = rows[t, p, 1]
        for t in range(0, MP, 2):
            left, right = rows[t, p, 2], rows[t + 1, p, 2]
            at = MP * LANE + t * 64
            xs[p, 0:ROWS, at : at + LANE] = jnp.concatenate([left[:, 0:64], right[:, 0:64]], axis=1)
            xs[p, ROWS:PR, at : at + LANE] = jnp.concatenate([left[:, 64:], right[:, 64:]], axis=1)
        stream0 = dot(xs[p], ep[...]) + shift(3)
        s0[p] = stream0
        mi[p] = (scale(0) * stream0 + shift(0)).astype(BF16)
        for b in range(2):
            r = slice(b * ROWS, (b + 1) * ROWS)
            mixed = dot(mm[...], mi[p, r, :]) + mbias[...]
            mx[p, r, :] = mixed
            stream1 = s0[p, r, :] + scale(1) * mixed
            s1[p, r, :] = stream1
            fi[p, r, :] = (scale(2) * stream1 + shift(1)).astype(BF16)
            s1sum[pl.ds(2 * p + b, 1), :] = jnp.sum(stream1[0:PATCHES], axis=0, keepdims=True)

        def chunk(c, carry):
            cols = pl.ds(pl.multiple_of(c * CH, CH), CH)
            for b in range(2):
                r = slice(b * ROWS, (b + 1) * ROWS)
                h = dot(fi[p, r, :], w1[:, cols]) + b1[:, cols]
                sq = h * h
                s = 0.5 * jnp.tanh(h * (GELU_A + GELU_B * sq)) + 0.5
                act = rounded(h * s)
                asum[pl.ds(2 * p + b, 1), cols] = jnp.sum(act[0:PATCHES], axis=0, keepdims=True)
                gp[p, r, cols] = s + s * (1.0 - s) * (h * (2.0 * GELU_A + 6.0 * GELU_B * sq))
                gp[p, b * ROWS + PATCHES : (b + 1) * ROWS, cols] = jnp.zeros((ROWS - PATCHES, CH), F32)
            return carry

        lax.fori_loop(0, NCH, chunk, 0)
        return carry

    lax.fori_loop(0, NP, forward, 0)

    la[...] = jnp.full(la.shape, -1, jnp.int32)
    lb[...] = jnp.full(lb.shape, -1, jnp.int32)
    for i in range(NI):
        own = labels[z * NI + i]
        mate = labels[partner[z * NI + i]]
        la[i : i + 1, :] = jnp.full((1, LANE), own, jnp.int32)
        lb[i : i + 1, :] = jnp.full((1, LANE), mate, jnp.int32)
    outsum = exact(asum[...], w2[...].astype(F32)) + PATCHES * shift(2)
    stream2 = s1sum[...] + scale(3) * outsum
    pooled = (scale(4) * (stream2 * (1.0 / PATCHES)) + shift(4)).astype(BF16)
    bias = jnp.concatenate([small[t, 11:12, 0:cpad] for t in range(MP)], axis=1)
    lane = lax.broadcasted_iota(jnp.int32, (16, cpad * MP), 1)
    inside = lax.rem(lane, cpad)
    valid = inside < ncls
    class_id = (lane // cpad) * ncls + inside
    logits = jnp.where(valid, dot(pooled, wc[...]) + bias, -1e30)
    hot_a = jnp.where(valid & (class_id == la[:, 0:1]), 1.0, 0.0)
    hot_b = jnp.where(valid & (class_id == lb[:, 0:1]), 1.0, 0.0)
    weight_a = mix_share * jnp.sum(hot_a * class_weight[...], axis=1, keepdims=True)
    weight_b = (1.0 - mix_share) * jnp.sum(hot_b * class_weight[...], axis=1, keepdims=True)
    top = jnp.max(logits, axis=1, keepdims=True)
    exps = jnp.where(valid, jnp.exp(logits - top), 0.0)
    exp_sum = jnp.sum(exps, axis=1, keepdims=True)
    log_total = top + jnp.log(exp_sum)
    target_a = jnp.sum(hot_a * logits, axis=1, keepdims=True)
    target_b = jnp.sum(hot_b * logits, axis=1, keepdims=True)
    loss = jnp.sum(weight_a * (log_total - target_a) + weight_b * (log_total - target_b), axis=0, keepdims=True)
    total = jnp.sum(weight_a + weight_b, axis=0, keepdims=True)
    dlog = ((weight_a + weight_b) * (exps / exp_sum) - weight_a * hot_a - weight_b * hot_b).astype(BF16)
    dfinal = dot(dlog, wc[...], ((1,), (1,))) * (1.0 / PATCHES)
    dstream2 = scale(4) * dfinal
    ds2[...] = dstream2
    dout = scale(3) * dstream2
    low = dout.astype(BF16)
    dact[...] = dot(low, w2[...], ((1,), (1,)))
    factors[:, 0:16, :] = jnp.broadcast_to(low[None], (MP, 16, D))
    factors[:, 16:32, :] = jnp.broadcast_to(pooled[None], (MP, 16, D))
    for t in range(MP):
        factors[t, 32:48, 0:cpad] = dlog[:, t * cpad : (t + 1) * cpad]
        factors[t, 32:48, cpad:] = jnp.zeros((16, D - cpad), BF16)

    def backward(p, carry):
        def chunk(c, carry):
            cols = pl.ds(pl.multiple_of(c * CH, CH), CH)
            for b in range(2):
                r = slice(b * ROWS, (b + 1) * ROWS)
                dh[r, cols] = (gp[p, r, cols] * dact[pl.ds(2 * p + b, 1), cols]).astype(BF16)
            value = dh[:, cols]
            csum[0:1, cols] += jnp.sum(value.astype(F32), axis=0, keepdims=True)
            gw[:, cols] += dot(fi[p], value, ((0,), (0,)))
            return carry

        lax.fori_loop(0, NCH, chunk, 0)
        dffn = dot(dh[...], w1[...], ((1,), (1,)))
        gvec[2:3, :] += jnp.sum(dffn * s1[p], axis=0, keepdims=True)
        gvec[6:7, :] += jnp.sum(dffn, axis=0, keepdims=True)
        for b in range(2):
            r = slice(b * ROWS, (b + 1) * ROWS)
            d1 = ds2[pl.ds(2 * p + b, 1), :] + scale(2) * dffn[r]
            gvec[1:2, :] += jnp.sum(mx[p, r, :] * d1, axis=0, keepdims=True)
            dmixed = (scale(1) * d1).astype(BF16)
            gm[...] += dot(dmixed, mi[p, r, :], ((1,), (1,)))
            gmb[...] += dmixed.astype(F32)
            dmixer = dot(mt[...], dmixed)
            gvec[0:1, :] += jnp.sum(dmixer * s0[p, r, :], axis=0, keepdims=True)
            gvec[5:6, :] += jnp.sum(dmixer, axis=0, keepdims=True)
            d0 = (d1 + scale(0) * dmixer).astype(BF16)
            ge[...] += dot(xs[p, r, :], d0, ((0,), (0,)))
        return carry

    lax.fori_loop(0, NP, backward, 0)

    gvec[3:4, :] = jnp.sum(outsum * dstream2, axis=0, keepdims=True)
    gvec[4:5, :] = jnp.sum(dfinal * stream2, axis=0, keepdims=True)
    gvec[7:8, :] = PATCHES * jnp.sum(dout, axis=0, keepdims=True)
    gvec[8:9, :] = (
        PATCHES * jnp.sum(dstream2, axis=0, keepdims=True) + scale(2) * gvec[6:7, :] + scale(0) * gvec[5:6, :]
    )
    gvec[9:10, :] = PATCHES * jnp.sum(dfinal, axis=0, keepdims=True)
    lane = lax.broadcasted_iota(jnp.int32, (1, D), 1)
    gvec[10:11, :] = jnp.where(lane == 0, loss, jnp.where(lane == 1, total, 0.0))

    row = lax.broadcasted_iota(jnp.int32, (ROWS, 256), 0)
    column = lax.broadcasted_iota(jnp.int32, (ROWS, 256), 1)
    bias_grad = jnp.sum(gmb[...], axis=1, keepdims=True)
    grad = jnp.concatenate([gm[...], jnp.zeros((ROWS, 256 - ROWS), F32)], axis=1)
    grad = jnp.where(column < PATCHES, grad, jnp.where(column == PATCHES, bias_grad, 0.0))
    grad = jnp.where(row < PATCHES, grad, 0.0)
    half = er - LANE
    own = D // MP
    lane = lax.broadcasted_iota(jnp.int32, (16, LANE), 1)
    for t in range(MP):
        big[t, 0:D, :] = gw[:, t * hid : (t + 1) * hid]
        big[t, D : D + LANE, :] = ge[t * LANE : (t + 1) * LANE, :]
        big[t, D + LANE : D + er, :] = ge[MP * LANE + t * half : MP * LANE + (t + 1) * half, :]
        if D + er < big.shape[1]:
            big[t, D + er :, :] = jnp.zeros((big.shape[1] - D - er, D), F32)
        sm[t, 0:S_VEC, :] = jnp.zeros((S_VEC, 256), F32)
        n = min(S_VEC, ROWS - t * S_VEC)
        sm[t, 0:n, :] = grad[t * S_VEC : t * S_VEC + n]
        vector = gvec[...]
        if t:
            vector = pltpu.roll(vector, D - t * own, 1)
        sm[t, S_VEC:S_ROWS, 0:LANE] = jnp.where(lane < own, vector[:, 0:LANE], 0.0)
        sm[t, S_VEC:S_ROWS, LANE:] = jnp.zeros((16, LANE), F32)
        sm[t, S_VEC + 10 : S_VEC + 11, 0:LANE] = gvec[10:11, 0:LANE]
        for k in range(hid // LANE):
            at = t * hid + k * LANE
            sm[t, S_VEC + 11 + k : S_VEC + 12 + k, 0:LANE] = csum[:, at : at + LANE]
        acts[t] = asum[:, t * hid : (t + 1) * hid]


def local_step(DP, MP, ncls, labels, partner, rows, e_all, w1, w2, wc, small, mixing, class_weight):
    NP = rows.shape[1]
    NI = 2 * NP
    PR = 2 * ROWS
    hid_all = w1.shape[1]
    pd = e_all.shape[0] * e_all.shape[1]
    vm = pl.BlockSpec(memory_space=VMEM)
    sm = pl.BlockSpec(memory_space=SMEM)
    return pl.pallas_call(
        functools.partial(step_kernel, MP, NI, ncls),
        out_shape=(
            jax.ShapeDtypeStruct((MP, DP * part_rows(DP, e_all.shape[1]), D), F32),
            jax.ShapeDtypeStruct((MP, S_ROWS, 256), F32),
            jax.ShapeDtypeStruct((MP, 16, hid_all // MP), F32),
            jax.ShapeDtypeStruct((MP, 48, D), BF16),
        ),
        in_specs=[sm, sm] + [vm] * 8,
        out_specs=(vm,) * 4,
        scratch_shapes=[
            VMEM((NP, PR, pd), BF16),
            VMEM((NP, PR, hid_all), F32),
            VMEM((NP, PR, D), F32),
            VMEM((NP, PR, D), F32),
            VMEM((NP, PR, D), F32),
            VMEM((NP, PR, D), BF16),
            VMEM((NP, PR, D), BF16),
            VMEM((pd, D), BF16),
            VMEM((ROWS, ROWS), BF16),
            VMEM((ROWS, ROWS), BF16),
            VMEM((ROWS, 1), F32),
            VMEM((16, D), F32),
            VMEM((1, hid_all), F32),
            VMEM((16, hid_all), F32),
            VMEM((16, D), F32),
            VMEM((16, LANE), jnp.int32),
            VMEM((16, LANE), jnp.int32),
            VMEM((16, hid_all), F32),
            VMEM((16, D), F32),
            VMEM((PR, hid_all), BF16),
            VMEM((1, hid_all), F32),
            VMEM((D, hid_all), F32),
            VMEM((pd, D), F32),
            VMEM((ROWS, ROWS), F32),
            VMEM((ROWS, D), F32),
            VMEM((16, D), F32),
        ],
        compiler_params=pltpu.CompilerParams(vmem_limit_bytes=62 << 20),
    )(labels, partner, rows, e_all, w1, w2, wc, small, mixing, class_weight)


def part_rows(DP, er):
    return -(-(D + er) // (16 * DP)) * 16


def adamw(weight, gradient, moment_one, moment_two, rate):
    mean_new = beta_one * moment_one + (1.0 - beta_one) * gradient
    square_new = beta_two * moment_two + (1.0 - beta_two) * gradient * gradient
    mean_hat = mean_new * (1.0 / (1.0 - beta_one**STEP))
    square_hat = square_new * (1.0 / (1.0 - beta_two**STEP))
    return rate * (mean_hat / (jnp.sqrt(square_hat) + adam_eps) + weight_decay * weight)


def flat(ref):
    return ref.at[:, 0, :] if len(ref.shape) == 3 else ref


def sum_kernel(G, DP, MP, big, sm, acts, fac, *refs):
    states, refs = refs[:21], refs[21:]
    (g_big, g_mix, g_shr, g_cls, g_vec, sum_a, sum_c, info), refs = refs[:8], refs[8:]
    held, refs = refs[:21], refs[21:]
    (
        ys16, yr16, zs16, zr16, zsm, zacts, zfac, ysm, yacts, yfac, nmix, nsq,
        mva, mvc, h1a, h1c, h2a, h2c,
        y_s, y_r, z_s, z_r, zf_s, zf_r, yf_s, yf_r, ag_s, ag_r, nm_s, nm_r, g_s, g_r, load,
    ) = refs
    z = lax.axis_index("mp")
    y = lax.axis_index("dp")
    g = lax.axis_index("group")
    HR = g_big.shape[0] // DP
    loads = [pltpu.make_async_copy(flat(a), b, load.at[k]) for k, (a, b) in enumerate(zip(states, held, strict=True))]
    for c in loads:
        c.start()
    zpeer = [lax.rem(z + d, MP) for d in range(1, MP)]
    ypeer = [lax.rem(y + d, DP) for d in range(1, DP)]
    gstep = []
    if G > 1:
        gstep.append(g + 1 - 2 * lax.rem(g, 2))
    if G > 2:
        gstep.append(lax.rem(g + 2, 4))
    greet([{"mp": t} for t in zpeer] + [{"dp": t} for t in ypeer] + [{"group": t} for t in gstep])

    started = []

    def go(*args):
        c = remote(*args)
        c.start()
        started.append(c)

    def arrived(dst, sem, peer):
        remote(dst, dst, sem, sem, peer).wait_recv()

    def mine(k):
        return pl.ds(pl.multiple_of(k * HR, 8), HR)

    order = zpeer + [z]
    for i, t in enumerate(order):
        for d, u in enumerate(ypeer):
            ys16[i, d] = big[t, mine(u), :].astype(BF16)
            go(ys16.at[i, d], yr16.at[t, y], y_s.at[i, d], y_r.at[t, y], {"dp": u})
        if i == 0:
            for d, v in enumerate(zpeer):
                go(acts.at[v], zacts.at[z], zf_s.at[d, 0], zf_r.at[z, 0], {"mp": v})
                go(fac.at[v], zfac.at[z], zf_s.at[d, 1], zf_r.at[z, 1], {"mp": v})
                go(sm.at[v], zsm.at[z], zf_s.at[d, 2], zf_r.at[z, 2], {"mp": v})
    zacts[z] = acts[z]
    zfac[z] = fac[z]
    zsm[z] = sm[z]
    own = None
    for i, t in enumerate(order):
        part = big[t, mine(y), :]
        for u in ypeer:
            arrived(yr16.at[t, u], y_r.at[t, u], {"dp": u})
            part = part + yr16[t, u].astype(F32)
        if i < MP - 1:
            zs16[i] = part.astype(BF16)
            go(zs16.at[i], zr16.at[z], z_s.at[i], z_r.at[z], {"mp": t})
        else:
            g_big[mine(y), :] = part

    for v in zpeer:
        arrived(zacts.at[v], zf_r.at[v, 0], {"mp": v})
        arrived(zfac.at[v], zf_r.at[v, 1], {"mp": v})
        arrived(zsm.at[v], zf_r.at[v, 2], {"mp": v})
    small = zsm[0]
    for v in range(1, MP):
        small = small + zsm[v]
    ysm[y] = small
    yacts[y] = zacts[...]
    yfac[y] = zfac[...]
    for d, u in enumerate(ypeer):
        go(ysm.at[y], ysm.at[y], yf_s.at[d, 0], yf_r.at[y, 0], {"dp": u})
        go(yacts.at[y], yacts.at[y], yf_s.at[d, 1], yf_r.at[y, 1], {"dp": u})
        go(yfac.at[y], yfac.at[y], yf_s.at[d, 2], yf_r.at[y, 2], {"dp": u})

    total = g_big[mine(y), :]
    for v in zpeer:
        arrived(zr16.at[v], z_r.at[v], {"mp": v})
        total = total + zr16[v].astype(F32)
    g_big[mine(y), :] = total
    shared = []
    for d, u in enumerate(ypeer):
        c = remote(g_big.at[mine(y), :], g_big.at[mine(y), :], ag_s.at[d], ag_r.at[y], {"dp": u})
        c.start()
        shared.append(c)

    for u in ypeer:
        arrived(ysm.at[u], yf_r.at[u, 0], {"dp": u})
    small = ysm[0]
    for u in range(1, DP):
        small = small + ysm[u]
    nmix[z] = small[0:S_VEC]
    for d, v in enumerate(zpeer):
        go(nmix.at[z], nmix.at[z], nm_s.at[d, 0], nm_r.at[z, 0], {"mp": v})
    for u in ypeer:
        arrived(yacts.at[u], yf_r.at[u, 1], {"dp": u})
        arrived(yfac.at[u], yf_r.at[u, 2], {"dp": u})

    cpad = g_cls.shape[1]
    n = 16 * MP
    grad_shr = jnp.zeros((D, D), F32)
    grad_cls = jnp.zeros((D, cpad), F32)
    cls_bias = jnp.zeros((1, cpad), F32)
    for u in range(DP):
        whole = yfac[u]
        dout = whole[:, 0:16, :].reshape(n, D)
        pooled = whole[:, 16:32, :].reshape(n, D)
        dlog = whole[:, 32:48, 0:cpad].reshape(n, cpad)
        grad_shr = grad_shr + exact(yacts[u].reshape(n, D), dout.astype(F32), ((0,), (0,)))
        grad_cls = grad_cls + dot(pooled, dlog, ((0,), (0,)))
        cls_bias = cls_bias + jnp.sum(dlog.astype(F32), axis=0, keepdims=True)
    g_shr[...] = grad_shr
    g_cls[0:D, :] = grad_cls
    g_cls[D:, :] = jnp.concatenate([cls_bias, jnp.zeros((g_cls.shape[0] - D - 1, cpad), F32)], axis=0)

    def squares(v):
        return jnp.sum(jnp.sum(v * v, axis=0, keepdims=True), axis=1, keepdims=True)

    vector = small[S_VEC:S_ROWS, 0:LANE]
    part = squares(g_shr[...]) + squares(g_cls[...]) + squares(small[0:S_VEC])
    part = part + squares(vector[0:10]) + squares(vector[11:14])
    for u in ypeer:
        arrived(g_big.at[mine(u), :], ag_r.at[u], {"dp": u})
    part = part + squares(g_big[...])
    nsq[z] = jnp.broadcast_to(part, (8, LANE))
    for d, v in enumerate(zpeer):
        go(nsq.at[z], nsq.at[z], nm_s.at[d, 1], nm_r.at[z, 1], {"mp": v})
    for c in loads:
        c.wait()
    for v in zpeer:
        arrived(nmix.at[v], nm_r.at[v, 0], {"mp": v})
        arrived(nsq.at[v], nm_r.at[v, 1], {"mp": v})
    square = nsq[0, 0:1, 0:1]
    for v in range(1, MP):
        square = square + nsq[v, 0:1, 0:1]
    loss_sum = vector[10:11, 0:1]
    weight_total = vector[10:11, 1:2]
    size = jnp.sqrt(square) / weight_total
    factor = clip_limit / jnp.maximum(size, clip_limit)
    scaled = factor / weight_total
    lane = lax.broadcasted_iota(jnp.int32, (8, LANE), 1)
    info[...] = jnp.where(lane == 0, loss_sum, jnp.where(lane == 1, weight_total, size))

    (emb, mixing, expa, shr, cls, sca, shi) = held[:7]
    (emb1, mixing1, expa1, shr1, cls1, sca1, shi1) = held[7:14]
    (emb2, mixing2, expa2, shr2, cls2, sca2, shi2) = held[14:21]
    er, ncls, wide = emb.shape[0], cls.shape[1], sca.shape[1]
    for c in shared:
        c.wait_send()
    g_big[...] = g_big[...] * scaled
    g_shr[...] = g_shr[...] * scaled
    g_cls[...] = g_cls[...] * scaled
    g_vec[...] = vector * scaled
    for t in range(MP):
        g_mix[t * S_VEC : (t + 1) * S_VEC, :] = nmix[t] * scaled
    bias = jnp.concatenate([g_vec[11 + k : 12 + k, :] for k in range(D // LANE)], axis=1)
    mva[A_EMB : A_EMB + er, :] = adamw(emb[...], g_big[D : D + er, :], emb1[...], emb2[...], matrix_rate)
    mva[A_EXP : A_EXP + D, :] = adamw(expa[0:D, :], g_big[0:D, :], expa1[0:D, :], expa2[0:D, :], matrix_rate)
    mva[A_EXP + D : A_SHR, :] = jnp.zeros((A_SHR - A_EXP - D, D), F32)
    last = slice(D, D + 1)
    mva[A_EXP + D : A_EXP + D + 1, :] = adamw(expa[last, :], bias, expa1[last, :], expa2[last, :], matrix_rate)
    mva[A_SHR : A_SHR + D, :] = adamw(shr[...], g_shr[...], shr1[...], shr2[...], matrix_rate)
    mva[A_SHR + D :, :] = jnp.zeros((A_ROWS - A_SHR - D, D), F32)
    ha, hc = A_ROWS // 2, C_ROWS // 2

    def half(ref, k, n):
        return ref.at[pl.ds(pl.multiple_of(k * n, 8), n), :]

    if G > 1:
        core, other = lax.rem(g, 2), 1 - lax.rem(g, 2)
        near = {"group": gstep[0]}
        go(half(mva, other, ha), h1a, g_s.at[0], g_r.at[0], near)
    mvc[...] = jnp.zeros_like(mvc)
    mvc[C_CLS : C_CLS + D + 1, 0:ncls] = adamw(cls[...], g_cls[0 : D + 1, 0:ncls], cls1[...], cls2[...], head_rate)
    mvc[C_MIX : C_MIX + PATCHES, 0 : PATCHES + 1] = adamw(
        mixing[...], g_mix[0:PATCHES, 0 : PATCHES + 1], mixing1[...], mixing2[...], matrix_rate
    )
    mvc[C_SCA : C_SCA + 5, 0:wide] = adamw(sca[...], g_vec[0:5, 0:wide], sca1[...], sca2[...], vector_rate)
    mvc[C_SHI : C_SHI + 5, 0:wide] = adamw(shi[...], g_vec[5:10, 0:wide], shi1[...], shi2[...], vector_rate)

    if G == 1:
        sum_a[...] = mva[...]
        sum_c[...] = mvc[...]
    else:
        go(half(mvc, other, hc), h1c, g_s.at[1], g_r.at[1], near)
        own_a = pl.ds(pl.multiple_of(core * ha, 8), ha)
        own_c = pl.ds(pl.multiple_of(core * hc, 8), hc)
        far = {"group": gstep[-1]}
        arrived(h1a, g_r.at[0], near)
        pa = mva[own_a, :] + h1a[...]
        if G > 2:
            h2a[0] = pa.astype(BF16)
            go(h2a.at[0], h2a.at[1], g_s.at[2], g_r.at[2], far)
        arrived(h1c, g_r.at[1], near)
        pc = mvc[own_c, :] + h1c[...]
        if G > 2:
            h2c[0] = pc
            go(h2c.at[0], h2c.at[1], g_s.at[3], g_r.at[3], far)
            arrived(h2a.at[1], g_r.at[2], far)
            pa = h2a[0].astype(F32) + h2a[1].astype(F32)
        sum_a[own_a, :] = pa
        go(half(sum_a, core, ha), half(sum_a, core, ha), g_s.at[4], g_r.at[4], near)
        if G > 2:
            arrived(h2c.at[1], g_r.at[3], far)
            pc = h2c[0] + h2c[1]
        sum_c[own_c, :] = pc
        go(half(sum_c, core, hc), half(sum_c, core, hc), g_s.at[5], g_r.at[5], near)
        arrived(half(sum_a, other, ha), g_r.at[4], near)
        arrived(half(sum_c, other, hc), g_r.at[5], near)

    for c in started:
        c.wait_send()


def gradient_sums(G, DP, MP, big, sm, acts, fac, shapes, states):
    dma = pltpu.SemaphoreType.DMA
    vm = pl.BlockSpec(memory_space=VMEM)
    hbm = pl.BlockSpec(memory_space=pl.ANY)
    cpad = -(-shapes[4][1] // LANE) * LANE
    s = jax.ShapeDtypeStruct
    HR = big.shape[1] // DP
    dp1 = max(DP - 1, 1)
    return pl.pallas_call(
        functools.partial(sum_kernel, G, DP, MP),
        out_shape=(
            s((DP * HR, D), F32),
            s((MP * S_VEC, 256), F32),
            s((D, D), F32),
            s((392, cpad), F32),
            s((16, LANE), F32),
            s((A_ROWS, D), F32),
            s((C_ROWS, 256), F32),
            s((8, LANE), F32),
        ),
        in_specs=[vm] * 4 + [hbm] * 21,
        out_specs=(vm,) * 8,
        scratch_shapes=[VMEM(shape, F32) for shape in shapes] * 3
        + [
            VMEM((MP, dp1, HR, D), BF16),
            VMEM((MP, DP, HR, D), BF16),
            VMEM((MP - 1, HR, D), BF16),
            VMEM((MP, HR, D), BF16),
            VMEM((MP, S_ROWS, 256), F32),
            VMEM((MP, 16, D), F32),
            VMEM((MP, 48, D), BF16),
            VMEM((DP, S_ROWS, 256), F32),
            VMEM((DP, MP, 16, D), F32),
            VMEM((DP, MP, 48, D), BF16),
            VMEM((MP, S_VEC, 256), F32),
            VMEM((MP, 8, LANE), F32),
            VMEM((A_ROWS, D), F32),
            VMEM((C_ROWS, 256), F32),
            VMEM((A_ROWS // 2, D), F32),
            VMEM((C_ROWS // 2, 256), F32),
            VMEM((2, A_ROWS // 2, D), BF16),
            VMEM((2, C_ROWS // 2, 256), F32),
            dma((MP, dp1)),
            dma((MP, DP)),
            dma((MP - 1,)),
            dma((MP,)),
            dma((MP - 1, 3)),
            dma((MP, 3)),
            dma((dp1, 3)),
            dma((DP, 3)),
            dma((dp1,)),
            dma((DP,)),
            dma((MP - 1, 2)),
            dma((MP, 2)),
            dma((6,)),
            dma((6,)),
            dma((21,)),
        ],
        compiler_params=pltpu.CompilerParams(
            collective_id=1, has_side_effects=True, vmem_limit_bytes=62 << 20
        ),
    )(big, sm, acts, fac, *states)


def finish_kernel(groups, *refs):
    (info, *grads_in), refs = refs[:8], refs[8:]
    states, refs = refs[:28], refs[28:]
    (losses, norm), refs = refs[:2], refs[2:]
    outs, refs = refs[:28], refs[28:]
    grads_held, refs = refs[:7], refs[7:]
    held, refs = refs[:28], refs[28:]
    new, (load, load_grad, save) = refs[:28], refs[28:]
    first = [pltpu.make_async_copy(a, b, load_grad.at[k]) for k, (a, b) in enumerate(zip(grads_in, grads_held, strict=True))]
    loads = [pltpu.make_async_copy(flat(a), b, load.at[k]) for k, (a, b) in enumerate(zip(states, held, strict=True))]
    saves = [pltpu.make_async_copy(a, flat(b), save.at[k]) for k, (a, b) in enumerate(zip(new, outs, strict=True))]
    for c in first:
        c.start()
    for k in (3, 2, 0, 4, 1, 5, 6):
        for j in range(4):
            loads[7 * j + k].start()
    losses[...] = info[0:1, 0:2]
    norm[...] = info[0:1, 2:3]
    g_big, g_mix, g_shr, g_cls, g_vec, sum_a, sum_c = grads_held
    for c in first:
        c.wait()
    wide = held[5].shape[1]
    ncls = held[4].shape[1]
    er = held[0].shape[0]
    all_rows = slice(None)
    bias = jnp.concatenate([g_vec[11 + k : 12 + k, :] for k in range(D // LANE)], axis=1)
    work = (
        (3, all_rows, lambda: g_shr[...], lambda: sum_a[A_SHR : A_SHR + D, :]),
        (2, slice(0, D), lambda: g_big[0:D, :], lambda: sum_a[A_EXP : A_EXP + D, :]),
        (2, slice(D, D + 1), lambda: bias, lambda: sum_a[A_EXP + D : A_EXP + D + 1, :]),
        (0, all_rows, lambda: g_big[D : D + er, :], lambda: sum_a[A_EMB : A_EMB + er, :]),
        (4, all_rows, lambda: g_cls[0 : D + 1, 0:ncls], lambda: sum_c[C_CLS : C_CLS + D + 1, 0:ncls]),
        (1, all_rows, lambda: g_mix[0:PATCHES, 0 : PATCHES + 1], lambda: sum_c[C_MIX : C_MIX + PATCHES, 0 : PATCHES + 1]),
        (5, all_rows, lambda: g_vec[0:5, 0:wide], lambda: sum_c[C_SCA : C_SCA + 5, 0:wide]),
        (6, all_rows, lambda: g_vec[5:10, 0:wide], lambda: sum_c[C_SHI : C_SHI + 5, 0:wide]),
    )
    for n, (k, r, gradient, total) in enumerate(work):
        if n == 0 or work[n - 1][0] != k:
            for j in range(4):
                loads[7 * j + k].wait()
        weight, one, two, outer = (held[7 * j + k] for j in range(4))
        update, mean, square, velocity = (new[7 * j + k] for j in range(4))
        grad = gradient()
        mean[r, :] = beta_one * one[r, :] + (1.0 - beta_one) * grad
        square[r, :] = beta_two * two[r, :] + (1.0 - beta_two) * grad * grad
        average = total() * (1.0 / groups)
        moving = outer_momentum * outer[r, :] + average
        velocity[r, :] = moving
        update[r, :] = weight[r, :] - outer_rate * (average + outer_momentum * moving)
        if n + 1 == len(work) or work[n + 1][0] != k:
            for j in range(4):
                saves[7 * j + k].start()
    for c in saves:
        c.wait()


def finish(G, info, grads, shapes, states, out_shapes):
    dma = pltpu.SemaphoreType.DMA
    vm = pl.BlockSpec(memory_space=VMEM)
    hbm = pl.BlockSpec(memory_space=pl.ANY)
    return pl.pallas_call(
        functools.partial(finish_kernel, G),
        out_shape=tuple(jax.ShapeDtypeStruct(shape, F32) for shape in ((1, 2), (1, 1), *out_shapes)),
        in_specs=[vm] + [hbm] * 35,
        out_specs=(vm,) * 2 + (hbm,) * 28,
        scratch_shapes=[VMEM(a.shape, F32) for a in grads]
        + [VMEM(shape, F32) for shape in shapes] * 8
        + [dma((28,)), dma((7,)), dma((28,))],
        compiler_params=pltpu.CompilerParams(vmem_limit_bytes=62 << 20),
    )(info, *grads, *states)


def thin(a):
    return jnp.swapaxes(a, 0, 1)


def per_device(
    G, DP, MP,
    patches, labels, partner, class_weight,
    embedding, mixing, expand, shrink, classifier, scales, shifts, *state,
):
    weights = (embedding, thin(mixing), thin(expand), shrink[0], classifier, scales, shifts)

    def moments(a):
        return (a[0][0], thin(a[1][0]), thin(a[2][0]), a[3][0, 0], thin(a[4]), thin(a[5]), thin(a[6]))

    firsts, seconds = moments(state[0:7]), moments(state[7:14])
    o = state[14:21]
    outers = (o[0], thin(o[1]), thin(o[2]), o[3][0], o[4], o[5], o[6])
    shapes = tuple((a.shape[0], a.shape[-1]) for a in weights)
    ncls = classifier.shape[1]
    cpad = -(-ncls // LANE) * LANE
    padded = jnp.pad(class_weight.reshape(MP, ncls), ((0, 0), (0, cpad - ncls))).reshape(1, MP * cpad)
    rows, e_all, w1, w2, wc, small = move(
        G, MP, partner[0], patches[0], embedding, expand[0], shrink[0], classifier, scales, shifts
    )
    big, sm, acts, fac = local_step(
        DP, MP, ncls, labels[0], partner[0], rows, e_all, w1, w2, wc, small, mixing[0], padded
    )
    *grads, info = gradient_sums(G, DP, MP, big, sm, acts, fac, shapes, (*weights, *firsts, *seconds))
    out_shapes = tuple(a.shape for a in (*weights, *firsts, *seconds, *outers))
    losses, norm, *done = finish(G, info, grads, shapes, (*weights, *firsts, *seconds, *outers), out_shapes)
    updates, means, squares, velocities = (list(done[7 * k : 7 * k + 7]) for k in range(4))

    def whole(a):
        return (a[0], thin(a[1]), thin(a[2]), a[3][None], a[4], a[5], a[6])

    def by_group(a):
        return (a[0][None], thin(a[1])[None], thin(a[2])[None], a[3][None, None], thin(a[4]), thin(a[5]), thin(a[6]))

    return (
        losses, norm[0],
        *whole(updates), *by_group(means), *by_group(squares), *whole(velocities),
    )


WEIGHT_SPECS = (
    P("mp", None),
    P(),
    P(None, None, "mp"),
    P(None, "mp", None),
    P(None, "mp"),
    P(None, "mp"),
    P(None, "mp"),
)
STATE_SPECS = (
    P("group", "mp", None),
    P("group", None, None, None),
    P("group", None, None, "mp"),
    P("group", None, "mp", None),
    P("group", None, "mp"),
    P("group", None, "mp"),
    P("group", None, "mp"),
)


def solution(mesh):
    G, DP, MP = mesh.shape["group"], mesh.shape["dp"], mesh.shape["mp"]
    return jax.shard_map(
        functools.partial(per_device, G, DP, MP),
        mesh=mesh,
        in_specs=(
            P("group", "dp", None, "mp"),
            P("group", "dp"),
            P("group", "dp"),
            P(),
            *WEIGHT_SPECS,
            *STATE_SPECS,
            *STATE_SPECS,
            *WEIGHT_SPECS,
        ),
        out_specs=(
            P("group", None),
            P("group"),
            *WEIGHT_SPECS,
            *STATE_SPECS,
            *STATE_SPECS,
            *WEIGHT_SPECS,
        ),
        check_vma=False,
    )
```

```python
import functools

import jax
import jax.numpy as jnp
from jax import lax
from jax.experimental import pallas as pl
from jax.experimental.pallas import tpu as pltpu
from jax.sharding import PartitionSpec as P

F32 = jnp.float32
BF16 = jnp.bfloat16
MESH = pl.DeviceIdType.MESH
VMEM = pltpu.VMEM
SMEM = pltpu.SMEM

D = 384
PATCHES = 196
ROWS = 208
STEP = 10
LANE = 128

mix_share = 0.7
clip_limit = 0.01
beta_one = 0.9
beta_two = 0.999
adam_eps = 1e-08
weight_decay = 0.05
matrix_rate = 0.05
head_rate = 0.5
vector_rate = 0.4
outer_rate = 0.7
outer_momentum = 0.9

GELU_A = 0.7978845608028654
GELU_B = GELU_A * 0.044715

S_VEC, S_ROWS = 56, 72
A_EMB, A_EXP, A_SHR, A_ROWS = 0, 192, 584, 992
C_CLS, C_MIX, C_SCA, C_SHI, C_ROWS = 0, 392, 592, 600, 624


def dot(a, b, dims=((1,), (0,)), precision=None):
    return lax.dot_general(
        a, b, (dims, ((), ())), preferred_element_type=F32, precision=precision
    )


def exact(a, b, dims=((1,), (0,))):
    return dot(a, b, dims, lax.Precision.HIGHEST)


def rounded(a):
    return a.astype(BF16).astype(F32)


def greet(peers):
    barrier = pltpu.get_barrier_semaphore()
    for peer in peers:
        pl.semaphore_signal(barrier, inc=1, device_id=peer, device_id_type=MESH)
    pl.semaphore_wait(barrier, len(peers))


def remote(src, dst, send_sem, recv_sem, peer):
    return pltpu.make_async_remote_copy(
        src_ref=src, dst_ref=dst, send_sem=send_sem, recv_sem=recv_sem,
        device_id=peer, device_id_type=MESH,
    )


CHUNK = 256
AHEAD = 2


def waves_of(pairs):
    cuts = [0, pairs // 2, pairs - 1, pairs] if pairs > 2 else list(range(pairs + 1))
    return list(zip(cuts[:-1], cuts[1:], strict=True))


def step_kernel(G, DP, MP, NI, ncls, *refs):
    (labels, partner, sca, shi, class_weight, patches, emb_in, exp_in, shr_in, cls_in, mix_in), refs = refs[:11], refs[11:]
    (big, sm, acts, factors), refs = refs[:4], refs[4:]
    (
        pv, emb, expa, shr, cls, mixing, stage, rows, e_all, w1, w2, wc, small,
        xs, gp, s0, s1, mx, mi, fi, ep, mm, mt, eye, mbias, vec, b1, cw, asum, s1sum, la, lb,
        dact, ds2, dh, csum, gw, ge, gm, gmb, gvec,
        load, rs_send, rs_recv, wz_send, wz_recv, wg_send, wg_recv, sm_send, sm_recv,
    ) = refs
    z = lax.axis_index("mp")
    y = lax.axis_index("dp")
    g = lax.axis_index("group")
    NP = NI // 2
    PR = 2 * ROWS
    hid = expa.shape[1]
    hid_all = hid * MP
    cpad = wc.shape[1] // MP
    er = emb.shape[0]
    NCH = hid_all // CHUNK
    pair = 2 if DP % 2 == 0 else 1

    loads = [
        pltpu.make_async_copy(flat(a), b, load.at[k])
        for k, (a, b) in enumerate(
            ((emb_in, emb), (exp_in, expa), (patches, pv), (shr_in, shr), (cls_in, cls), (mix_in, mixing))
        )
    ]
    for c in loads:
        c.start()

    zpeer = [lax.rem(z + d, MP) for d in range(1, MP)]
    half = lax.rem(y, pair)
    plane = []
    for e in range(pair):
        for d in range(G):
            if d or e:
                j = lax.rem(g + d, G)
                h = half if e == 0 else 1 - half
                plane.append((j, y if e == 0 else y + 1 - 2 * half, j * pair + h, e))
    place = g * pair + half
    parts = G * pair
    greet([{"mp": t} for t in zpeer] + [{"group": j, "dp": u} for j, u, _, _ in plane])

    def pieces(t, j):
        ee, hh, dd = er // G, hid // parts, D // parts
        return (
            e_all.at[t, pl.ds(pl.multiple_of(j // pair * ee, 16), ee), :],
            w1.at[pl.ds(pl.multiple_of(j * dd, 16), dd), pl.ds(pl.multiple_of(t * hid, LANE), hid)],
            w2.at[pl.ds(pl.multiple_of(t * hid + j * hh, 16), hh), :],
            wc.at[pl.ds(pl.multiple_of(j * dd, 16), dd), pl.ds(pl.multiple_of(t * cpad, LANE), cpad)],
        )

    started = []

    def go(*args):
        c = remote(*args)
        c.start()
        started.append(c)

    def spread(k):
        part = pieces(z, place)[k]
        for d, t in enumerate(zpeer):
            go(part, part, wz_send.at[d, k], wz_recv.at[z, k], {"mp": t})

    def pass_on(k):
        for d in range(1, MP):
            t = lax.rem(z + MP - d, MP)
            part = pieces(t, place)[k]
            remote(part, part, wz_send.at[d - 1, k], wz_recv.at[t, k], {"mp": t}).wait_recv()
            for e, (j, u, _, other) in enumerate(plane):
                if k or not other:
                    go(part, part, wg_send.at[d - 1, e, k], wg_recv.at[t, place, k], {"group": j, "dp": u})

    def gathered(k):
        for t in zpeer:
            for j, u, at, other in plane:
                if k or not other:
                    part = pieces(t, at)[k]
                    remote(part, part, wg_send.at[0, 0, k], wg_recv.at[t, at, k], {"group": j, "dp": u}).wait_recv()

    loads[0].wait()
    e_all[z] = emb[...].astype(BF16)
    spread(0)
    loads[1].wait()
    w1[:, pl.ds(pl.multiple_of(z * hid, LANE), hid)] = expa[0:D, :].astype(BF16)
    spread(1)

    row = lax.broadcasted_iota(jnp.int32, (ROWS, PATCHES), 0)
    column = lax.broadcasted_iota(jnp.int32, (ROWS, PATCHES), 1)
    eye[...] = jnp.where(row == column, 1.0, 0.0).astype(BF16)
    share = F32(mix_share)
    rest = F32(1.0 - mix_share)

    def blend(i):
        return (share * pv[i] + rest * pv[partner[i]]).astype(BF16)

    def blend_pair(t, p):
        a = blend(t * NI + 2 * p)
        b = blend(t * NI + 2 * p + 1)
        both = jnp.concatenate([a[0:LANE], b[0:LANE], a[LANE:], b[LANE:]], axis=0)
        return dot(eye[...], both, ((1,), (1,))).astype(BF16)

    def send(p, d):
        return remote(stage.at[d, p], rows.at[z, p], rs_send.at[d, p], rs_recv.at[z, p], {"mp": zpeer[d]})

    def issue(p):
        for d in range(MP - 1):
            stage[d, p] = blend_pair(zpeer[d], p)
            send(p, d).start()

    loads[2].wait()
    issue(0)

    loads[3].wait()
    w2[pl.ds(pl.multiple_of(z * hid, 16), hid), :] = shr[...].astype(BF16)
    loads[4].wait()
    head = jnp.concatenate([cls[0:D, :], jnp.zeros((D, cpad - ncls), F32)], axis=1)
    wc[:, pl.ds(pl.multiple_of(z * cpad, LANE), cpad)] = head.astype(BF16)
    spread(2)
    spread(3)
    small[z] = jnp.zeros(small.shape[1:], F32)
    small[z, 0:5, 0 : D // MP] = sca[...]
    small[z, 5:10, 0 : D // MP] = shi[...]
    small[z, 10:11, :] = rounded(expa[D : D + 1, :])
    small[z, 11:12, 0:ncls] = rounded(cls[D : D + 1, :])
    for d, t in enumerate(zpeer):
        go(small.at[z], small.at[z], sm_send.at[d], sm_recv.at[z], {"mp": t})
    for p in range(1, min(AHEAD, NP)):
        issue(p)
    pass_on(0)
    pass_on(1)

    loads[5].wait()
    wide = jnp.concatenate([mixing[...], jnp.zeros((PATCHES, 256 - PATCHES - 1), F32)], axis=1)
    wide = jnp.concatenate([wide, jnp.zeros((256 - PATCHES, 256), F32)], axis=0)
    column = lax.broadcasted_iota(jnp.int32, (256, 256), 1)
    square = jnp.where(column < PATCHES, wide, 0.0)
    mm[...] = square[0:ROWS, 0:ROWS].astype(BF16)
    mt[...] = jnp.transpose(square)[0:ROWS, 0:ROWS].astype(BF16)
    mbias[...] = rounded(jnp.sum(jnp.where(column == PATCHES, wide, 0.0), axis=1, keepdims=True)[0:ROWS])
    for t in range(MP):
        block = class_weight[:, t * ncls : (t + 1) * ncls]
        cw[:, t * cpad : (t + 1) * cpad] = jnp.concatenate([block, jnp.zeros((1, cpad - ncls), F32)], axis=1)
    asum[...] = jnp.zeros_like(asum)
    s1sum[...] = jnp.zeros_like(s1sum)
    csum[...] = jnp.zeros_like(csum)
    gw[...] = jnp.zeros_like(gw)
    ge[...] = jnp.zeros_like(ge)
    gm[...] = jnp.zeros_like(gm)
    gmb[...] = jnp.zeros_like(gmb)
    gvec[...] = jnp.zeros_like(gvec)
    la[...] = jnp.full(la.shape, -1, jnp.int32)
    lb[...] = jnp.full(lb.shape, -1, jnp.int32)
    for i in range(NI):
        own = labels[z * NI + i]
        mate = labels[partner[z * NI + i]]
        la[i : i + 1, :] = jnp.full((1, LANE), own, jnp.int32)
        lb[i : i + 1, :] = jnp.full((1, LANE), mate, jnp.int32)

    for t in zpeer:
        remote(small.at[t], small.at[t], sm_send.at[0], sm_recv.at[t], {"mp": t}).wait_recv()
    full = jnp.zeros((16, D), F32)
    for t in range(MP):
        block = small[t]
        full = full + (pltpu.roll(block, t * (D // MP), 1) if t else block)
        b1[:, t * hid : (t + 1) * hid] = small[t, 10:11, :]
    vec[...] = full
    gathered(0)
    rest_rows = er - LANE
    for t in range(MP):
        ep[t * LANE : (t + 1) * LANE, :] = e_all[t, 0:LANE, :]
        ep[MP * LANE + t * rest_rows : MP * LANE + (t + 1) * rest_rows, :] = e_all[t, LANE:er, :]
    gathered(1)
    pass_on(2)
    pass_on(3)

    def scale(k):
        return vec[k : k + 1, :]

    def shift(k):
        return vec[5 + k : 6 + k, :]

    def forward(base, p, carry):
        @pl.when(p + AHEAD < NP)
        def _():
            issue(p + AHEAD)

        q = p - base
        rows[z, p] = blend_pair(z, p)
        for t in zpeer:
            remote(stage.at[0, p], rows.at[t, p], rs_send.at[0, p], rs_recv.at[t, p], {"mp": t}).wait_recv()
        for t in range(MP):
            xs[q, 0:ROWS, t * LANE : (t + 1) * LANE] = rows[t, p, :, 0:LANE]
            xs[q, ROWS:PR, t * LANE : (t + 1) * LANE] = rows[t, p, :, LANE : 2 * LANE]
        for t in range(0, MP, 2):
            left, right = rows[t, p, :, 2 * LANE :], rows[t + 1, p, :, 2 * LANE :]
            at = MP * LANE + t * 64
            xs[q, 0:ROWS, at : at + LANE] = jnp.concatenate([left[:, 0:64], right[:, 0:64]], axis=1)
            xs[q, ROWS:PR, at : at + LANE] = jnp.concatenate([left[:, 64:], right[:, 64:]], axis=1)
        stream0 = dot(xs[q], ep[...]) + shift(3)
        s0[q] = stream0
        mi[q] = (scale(0) * stream0 + shift(0)).astype(BF16)
        for b in range(2):
            r = slice(b * ROWS, (b + 1) * ROWS)
            mixed = dot(mm[...], mi[q, r, :]) + mbias[...]
            mx[q, r, :] = mixed
            stream1 = s0[q, r, :] + scale(1) * mixed
            s1[q, r, :] = stream1
            fi[q, r, :] = (scale(2) * stream1 + shift(1)).astype(BF16)
            s1sum[pl.ds(2 * p + b, 1), :] = jnp.sum(stream1[0:PATCHES], axis=0, keepdims=True)

        def chunk(c, carry):
            cols = pl.ds(pl.multiple_of(c * CHUNK, CHUNK), CHUNK)
            for b in range(2):
                r = slice(b * ROWS, (b + 1) * ROWS)
                h = dot(fi[q, r, :], w1[:, cols]) + b1[:, cols]
                sq = h * h
                s = 0.5 * jnp.tanh(h * (GELU_A + GELU_B * sq)) + 0.5
                act = rounded(h * s)
                asum[pl.ds(2 * p + b, 1), cols] = jnp.sum(act[0:PATCHES], axis=0, keepdims=True)
                gp[q, r, cols] = s + s * (1.0 - s) * (h * (2.0 * GELU_A + 6.0 * GELU_B * sq))
                gp[q, b * ROWS + PATCHES : (b + 1) * ROWS, cols] = jnp.zeros((ROWS - PATCHES, CHUNK), F32)
            return carry

        lax.fori_loop(0, NCH, chunk, 0)
        return carry

    def class_head():
        outsum = exact(asum[...], w2[...].astype(F32)) + PATCHES * shift(2)
        stream2 = s1sum[...] + scale(3) * outsum
        pooled = (scale(4) * (stream2 * (1.0 / PATCHES)) + shift(4)).astype(BF16)
        bias = jnp.concatenate([small[t, 11:12, 0:cpad] for t in range(MP)], axis=1)
        lane = lax.broadcasted_iota(jnp.int32, (16, cpad * MP), 1)
        inside = lax.rem(lane, cpad)
        valid = inside < ncls
        class_id = (lane // cpad) * ncls + inside
        logits = jnp.where(valid, dot(pooled, wc[...]) + bias, -1e30)
        hot_a = jnp.where(valid & (class_id == la[:, 0:1]), 1.0, 0.0)
        hot_b = jnp.where(valid & (class_id == lb[:, 0:1]), 1.0, 0.0)
        weight_a = mix_share * jnp.sum(hot_a * cw[...], axis=1, keepdims=True)
        weight_b = (1.0 - mix_share) * jnp.sum(hot_b * cw[...], axis=1, keepdims=True)
        top = jnp.max(logits, axis=1, keepdims=True)
        exps = jnp.where(valid, jnp.exp(logits - top), 0.0)
        exp_sum = jnp.sum(exps, axis=1, keepdims=True)
        soft = exps / exp_sum
        dlog = ((weight_a + weight_b) * soft - weight_a * hot_a - weight_b * hot_b).astype(BF16)
        dfinal = dot(dlog, wc[...], ((1,), (1,))) * (1.0 / PATCHES)
        dstream2 = scale(4) * dfinal
        ds2[...] = dstream2
        dout = scale(3) * dstream2
        low = dout.astype(BF16)
        dact[...] = dot(low, w2[...], ((1,), (1,)))

        def last():
            log_total = top + jnp.log(exp_sum)
            target_a = jnp.sum(hot_a * logits, axis=1, keepdims=True)
            target_b = jnp.sum(hot_b * logits, axis=1, keepdims=True)
            loss = weight_a * (log_total - target_a) + weight_b * (log_total - target_b)
            loss = jnp.sum(loss, axis=0, keepdims=True)
            total = jnp.sum(weight_a + weight_b, axis=0, keepdims=True)
            factors[:, 0:16, :] = jnp.broadcast_to(low[None], (MP, 16, D))
            factors[:, 16:32, :] = jnp.broadcast_to(pooled[None], (MP, 16, D))
            for t in range(MP):
                factors[t, 32:48, 0:cpad] = dlog[:, t * cpad : (t + 1) * cpad]
                factors[t, 32:48, cpad:] = jnp.zeros((16, D - cpad), BF16)
                acts[t] = asum[:, t * hid : (t + 1) * hid]
            gvec[3:4, :] = jnp.sum(outsum * dstream2, axis=0, keepdims=True)
            gvec[4:5, :] = jnp.sum(dfinal * stream2, axis=0, keepdims=True)
            gvec[7:8, :] = PATCHES * jnp.sum(dout, axis=0, keepdims=True)
            gvec[8:9, :] = PATCHES * jnp.sum(dstream2, axis=0, keepdims=True)
            gvec[9:10, :] = PATCHES * jnp.sum(dfinal, axis=0, keepdims=True)
            lane = lax.broadcasted_iota(jnp.int32, (1, D), 1)
            gvec[10:11, :] = jnp.where(lane == 0, loss, jnp.where(lane == 1, total, 0.0))

        return last

    def backward(base, p, carry):
        q = p - base

        def chunk(c, carry):
            cols = pl.ds(pl.multiple_of(c * CHUNK, CHUNK), CHUNK)
            for b in range(2):
                r = slice(b * ROWS, (b + 1) * ROWS)
                dh[r, cols] = (gp[q, r, cols] * dact[pl.ds(2 * p + b, 1), cols]).astype(BF16)
            value = dh[:, cols]
            csum[0:1, cols] += jnp.sum(value.astype(F32), axis=0, keepdims=True)
            gw[:, cols] += dot(fi[q], value, ((0,), (0,)))
            return carry

        lax.fori_loop(0, NCH, chunk, 0)
        dffn = dot(dh[...], w1[...], ((1,), (1,)))
        gvec[2:3, :] += jnp.sum(dffn * s1[q], axis=0, keepdims=True)
        gvec[6:7, :] += jnp.sum(dffn, axis=0, keepdims=True)
        for b in range(2):
            r = slice(b * ROWS, (b + 1) * ROWS)
            d1 = ds2[pl.ds(2 * p + b, 1), :] + scale(2) * dffn[r]
            gvec[1:2, :] += jnp.sum(mx[q, r, :] * d1, axis=0, keepdims=True)
            dmixed = (scale(1) * d1).astype(BF16)
            gm[...] += dot(dmixed, mi[q, r, :], ((1,), (1,)))
            gmb[...] += dmixed.astype(F32)
            dmixer = dot(mt[...], dmixed)
            gvec[0:1, :] += jnp.sum(dmixer * s0[q, r, :], axis=0, keepdims=True)
            gvec[5:6, :] += jnp.sum(dmixer, axis=0, keepdims=True)
            d0 = (d1 + scale(0) * dmixer).astype(BF16)
            ge[...] += dot(xs[q, r, :], d0, ((0,), (0,)))
        return carry

    for n, (lo, hi) in enumerate(waves_of(NP)):
        lax.fori_loop(lo, hi, functools.partial(forward, lo), 0)
        if n == 0:
            gathered(2)
            gathered(3)
        last = class_head()
        if hi == NP:
            last()
        lax.fori_loop(lo, hi, functools.partial(backward, lo), 0)

    gvec[8:9, :] += scale(2) * gvec[6:7, :] + scale(0) * gvec[5:6, :]
    row = lax.broadcasted_iota(jnp.int32, (ROWS, 256), 0)
    column = lax.broadcasted_iota(jnp.int32, (ROWS, 256), 1)
    bias_grad = jnp.sum(gmb[...], axis=1, keepdims=True)
    grad = jnp.concatenate([gm[...], jnp.zeros((ROWS, 256 - ROWS), F32)], axis=1)
    grad = jnp.where(column < PATCHES, grad, jnp.where(column == PATCHES, bias_grad, 0.0))
    grad = jnp.where(row < PATCHES, grad, 0.0)
    own = D // MP
    lane = lax.broadcasted_iota(jnp.int32, (16, LANE), 1)
    for t in range(MP):
        big[t, 0:D, :] = gw[:, t * hid : (t + 1) * hid]
        big[t, D : D + LANE, :] = ge[t * LANE : (t + 1) * LANE, :]
        big[t, D + LANE : D + er, :] = ge[MP * LANE + t * rest_rows : MP * LANE + (t + 1) * rest_rows, :]
        if D + er < big.shape[1]:
            big[t, D + er :, :] = jnp.zeros((big.shape[1] - D - er, D), F32)
        sm[t, 0:S_VEC, :] = jnp.zeros((S_VEC, 256), F32)
        n = min(S_VEC, ROWS - t * S_VEC)
        sm[t, 0:n, :] = grad[t * S_VEC : t * S_VEC + n]
        vector = gvec[...]
        if t:
            vector = pltpu.roll(vector, D - t * own, 1)
        sm[t, S_VEC:S_ROWS, 0:LANE] = jnp.where(lane < own, vector[:, 0:LANE], 0.0)
        sm[t, S_VEC:S_ROWS, LANE:] = jnp.zeros((16, LANE), F32)
        sm[t, S_VEC + 10 : S_VEC + 11, 0:LANE] = gvec[10:11, 0:LANE]
        for k in range(hid // LANE):
            at = t * hid + k * LANE
            sm[t, S_VEC + 11 + k : S_VEC + 12 + k, 0:LANE] = csum[:, at : at + LANE]

    def drain(p, carry):
        for d in range(MP - 1):
            send(p, d).wait_send()
        return carry

    lax.fori_loop(0, NP, drain, 0)
    for c in started:
        c.wait_send()


def local_step(G, DP, MP, ncls, labels, partner, sca, shi, class_weight, patches, emb, expa, shr, cls, mixing):
    NI = patches.shape[0] // MP
    NP = NI // 2
    PR = 2 * ROWS
    hid = expa.shape[-1]
    hid_all = hid * MP
    er = emb.shape[0]
    pd = er * MP
    cpad = -(-ncls // LANE) * LANE
    wave = max(hi - lo for lo, hi in waves_of(NP))
    pair = 2 if DP % 2 == 0 else 1
    dma = pltpu.SemaphoreType.DMA
    vm = pl.BlockSpec(memory_space=VMEM)
    smem = pl.BlockSpec(memory_space=SMEM)
    hbm = pl.BlockSpec(memory_space=pl.ANY)
    return pl.pallas_call(
        functools.partial(step_kernel, G, DP, MP, NI, ncls),
        out_shape=(
            jax.ShapeDtypeStruct((MP, DP * part_rows(DP, er), D), F32),
            jax.ShapeDtypeStruct((MP, S_ROWS, 256), F32),
            jax.ShapeDtypeStruct((MP, 16, hid), F32),
            jax.ShapeDtypeStruct((MP, 48, D), BF16),
        ),
        in_specs=[smem, smem, vm, vm, vm] + [hbm] * 6,
        out_specs=(vm,) * 4,
        scratch_shapes=[
            VMEM(patches.shape, F32),
            VMEM((er, D), F32),
            VMEM((D + 1, hid), F32),
            VMEM((hid, D), F32),
            VMEM((D + 1, ncls), F32),
            VMEM((PATCHES, PATCHES + 1), F32),
            VMEM((MP - 1, NP, ROWS, 2 * er), BF16),
            VMEM((MP, NP, ROWS, 2 * er), BF16),
            VMEM((MP, er, D), BF16),
            VMEM((D, hid_all), BF16),
            VMEM((hid_all, D), BF16),
            VMEM((D, cpad * MP), BF16),
            VMEM((MP, 16, hid), F32),
            VMEM((wave, PR, pd), BF16),
            VMEM((wave, PR, hid_all), F32),
            VMEM((wave, PR, D), F32),
            VMEM((wave, PR, D), F32),
            VMEM((wave, PR, D), F32),
            VMEM((wave, PR, D), BF16),
            VMEM((wave, PR, D), BF16),
            VMEM((pd, D), BF16),
            VMEM((ROWS, ROWS), BF16),
            VMEM((ROWS, ROWS), BF16),
            VMEM((ROWS, PATCHES), BF16),
            VMEM((ROWS, 1), F32),
            VMEM((16, D), F32),
            VMEM((1, hid_all), F32),
            VMEM((1, cpad * MP), F32),
            VMEM((16, hid_all), F32),
            VMEM((16, D), F32),
            VMEM((16, LANE), jnp.int32),
            VMEM((16, LANE), jnp.int32),
            VMEM((16, hid_all), F32),
            VMEM((16, D), F32),
            VMEM((PR, hid_all), BF16),
            VMEM((1, hid_all), F32),
            VMEM((D, hid_all), F32),
            VMEM((pd, D), F32),
            VMEM((ROWS, ROWS), F32),
            VMEM((ROWS, D), F32),
            VMEM((16, D), F32),
            dma((6,)),
            dma((MP - 1, NP)),
            dma((MP, NP)),
            dma((MP - 1, 4)),
            dma((MP, 4)),
            dma((MP - 1, G * pair - 1 or 1, 4)),
            dma((MP, G * pair, 4)),
            dma((MP - 1,)),
            dma((MP,)),
        ],
        compiler_params=pltpu.CompilerParams(
            collective_id=0, has_side_effects=True, vmem_limit_bytes=63 << 20
        ),
    )(labels, partner, sca, shi, class_weight, patches, emb, expa, shr, cls, mixing)


def part_rows(DP, er):
    return -(-(D + er) // (16 * DP)) * 16


def adamw(weight, gradient, moment_one, moment_two, rate):
    mean_new = beta_one * moment_one + (1.0 - beta_one) * gradient
    square_new = beta_two * moment_two + (1.0 - beta_two) * gradient * gradient
    mean_hat = mean_new * (1.0 / (1.0 - beta_one**STEP))
    square_hat = square_new * (1.0 / (1.0 - beta_two**STEP))
    return rate * (mean_hat / (jnp.sqrt(square_hat) + adam_eps) + weight_decay * weight)


def flat(ref):
    return ref.at[:, 0, :] if len(ref.shape) == 3 and ref.shape[1] == 1 else ref


def sum_kernel(G, DP, MP, big, sm, acts, fac, *refs):
    states, refs = refs[:21], refs[21:]
    (g_big, g_mix, g_shr, g_cls, g_vec, sum_a, sum_c, info), refs = refs[:8], refs[8:]
    held, refs = refs[:21], refs[21:]
    (
        ys16, yr16, zs16, zr16, zsm, zacts, zfac, ysm, yacts, yfac, nmix, nsq,
        mva, mvc, h1a, h1c, h2a, h2c,
        y_s, y_r, z_s, z_r, zf_s, zf_r, yf_s, yf_r, ag_s, ag_r, nm_s, nm_r, g_s, g_r, load,
    ) = refs
    z = lax.axis_index("mp")
    y = lax.axis_index("dp")
    g = lax.axis_index("group")
    HR = g_big.shape[0] // DP
    loads = [pltpu.make_async_copy(flat(a), b, load.at[k]) for k, (a, b) in enumerate(zip(states, held, strict=True))]
    for c in loads:
        c.start()
    zpeer = [lax.rem(z + d, MP) for d in range(1, MP)]
    ypeer = [lax.rem(y + d, DP) for d in range(1, DP)]
    gstep = []
    if G > 1:
        gstep.append(g + 1 - 2 * lax.rem(g, 2))
    if G > 2:
        gstep.append(lax.rem(g + 2, 4))
    greet([{"mp": t} for t in zpeer] + [{"dp": t} for t in ypeer] + [{"group": t} for t in gstep])

    started = []

    def go(*args):
        c = remote(*args)
        c.start()
        started.append(c)

    def arrived(dst, sem, peer):
        remote(dst, dst, sem, sem, peer).wait_recv()

    def mine(k):
        return pl.ds(pl.multiple_of(k * HR, 8), HR)

    order = zpeer + [z]
    for i, t in enumerate(order):
        for d, u in enumerate(ypeer):
            ys16[i, d] = big[t, mine(u), :].astype(BF16)
            go(ys16.at[i, d], yr16.at[t, y], y_s.at[i, d], y_r.at[t, y], {"dp": u})
        if i == 0:
            for d, v in enumerate(zpeer):
                go(acts.at[v], zacts.at[z], zf_s.at[d, 0], zf_r.at[z, 0], {"mp": v})
                go(fac.at[v], zfac.at[z], zf_s.at[d, 1], zf_r.at[z, 1], {"mp": v})
                go(sm.at[v], zsm.at[z], zf_s.at[d, 2], zf_r.at[z, 2], {"mp": v})
    zacts[z] = acts[z]
    zfac[z] = fac[z]
    zsm[z] = sm[z]
    own = None
    for i, t in enumerate(order):
        part = big[t, mine(y), :]
        for u in ypeer:
            arrived(yr16.at[t, u], y_r.at[t, u], {"dp": u})
            part = part + yr16[t, u].astype(F32)
        if i < MP - 1:
            zs16[i] = part.astype(BF16)
            go(zs16.at[i], zr16.at[z], z_s.at[i], z_r.at[z], {"mp": t})
        else:
            g_big[mine(y), :] = part

    for v in zpeer:
        arrived(zacts.at[v], zf_r.at[v, 0], {"mp": v})
        arrived(zfac.at[v], zf_r.at[v, 1], {"mp": v})
        arrived(zsm.at[v], zf_r.at[v, 2], {"mp": v})
    small = zsm[0]
    for v in range(1, MP):
        small = small + zsm[v]
    ysm[y] = small
    yacts[y] = zacts[...]
    yfac[y] = zfac[...]
    for d, u in enumerate(ypeer):
        go(ysm.at[y], ysm.at[y], yf_s.at[d, 0], yf_r.at[y, 0], {"dp": u})
        go(yacts.at[y], yacts.at[y], yf_s.at[d, 1], yf_r.at[y, 1], {"dp": u})
        go(yfac.at[y], yfac.at[y], yf_s.at[d, 2], yf_r.at[y, 2], {"dp": u})

    total = g_big[mine(y), :]
    for v in zpeer:
        arrived(zr16.at[v], z_r.at[v], {"mp": v})
        total = total + zr16[v].astype(F32)
    g_big[mine(y), :] = total
    shared = []
    for d, u in enumerate(ypeer):
        c = remote(g_big.at[mine(y), :], g_big.at[mine(y), :], ag_s.at[d], ag_r.at[y], {"dp": u})
        c.start()
        shared.append(c)

    for u in ypeer:
        arrived(ysm.at[u], yf_r.at[u, 0], {"dp": u})
    small = ysm[0]
    for u in range(1, DP):
        small = small + ysm[u]
    nmix[z] = small[0:S_VEC]
    for d, v in enumerate(zpeer):
        go(nmix.at[z], nmix.at[z], nm_s.at[d, 0], nm_r.at[z, 0], {"mp": v})
    for u in ypeer:
        arrived(yacts.at[u], yf_r.at[u, 1], {"dp": u})
        arrived(yfac.at[u], yf_r.at[u, 2], {"dp": u})

    cpad = g_cls.shape[1]
    n = 16 * MP
    grad_shr = jnp.zeros((D, D), F32)
    grad_cls = jnp.zeros((D, cpad), F32)
    cls_bias = jnp.zeros((1, cpad), F32)
    for u in range(DP):
        whole = yfac[u]
        dout = whole[:, 0:16, :].reshape(n, D)
        pooled = whole[:, 16:32, :].reshape(n, D)
        dlog = whole[:, 32:48, 0:cpad].reshape(n, cpad)
        grad_shr = grad_shr + exact(yacts[u].reshape(n, D), dout.astype(F32), ((0,), (0,)))
        grad_cls = grad_cls + dot(pooled, dlog, ((0,), (0,)))
        cls_bias = cls_bias + jnp.sum(dlog.astype(F32), axis=0, keepdims=True)
    g_shr[...] = grad_shr
    g_cls[0:D, :] = grad_cls
    g_cls[D:, :] = jnp.concatenate([cls_bias, jnp.zeros((g_cls.shape[0] - D - 1, cpad), F32)], axis=0)

    def squares(v):
        return jnp.sum(jnp.sum(v * v, axis=0, keepdims=True), axis=1, keepdims=True)

    vector = small[S_VEC:S_ROWS, 0:LANE]
    part = squares(g_shr[...]) + squares(g_cls[...]) + squares(small[0:S_VEC])
    part = part + squares(vector[0:10]) + squares(vector[11:14])
    for u in ypeer:
        arrived(g_big.at[mine(u), :], ag_r.at[u], {"dp": u})
    part = part + squares(g_big[...])
    nsq[z] = jnp.broadcast_to(part, (8, LANE))
    for d, v in enumerate(zpeer):
        go(nsq.at[z], nsq.at[z], nm_s.at[d, 1], nm_r.at[z, 1], {"mp": v})
    for c in loads:
        c.wait()
    for v in zpeer:
        arrived(nmix.at[v], nm_r.at[v, 0], {"mp": v})
        arrived(nsq.at[v], nm_r.at[v, 1], {"mp": v})
    square = nsq[0, 0:1, 0:1]
    for v in range(1, MP):
        square = square + nsq[v, 0:1, 0:1]
    loss_sum = vector[10:11, 0:1]
    weight_total = vector[10:11, 1:2]
    size = jnp.sqrt(square) / weight_total
    factor = clip_limit / jnp.maximum(size, clip_limit)
    scaled = factor / weight_total
    lane = lax.broadcasted_iota(jnp.int32, (8, LANE), 1)
    info[...] = jnp.where(lane == 0, loss_sum, jnp.where(lane == 1, weight_total, size))

    (emb, mixing, expa, shr, cls, sca, shi) = held[:7]
    (emb1, mixing1, expa1, shr1, cls1, sca1, shi1) = held[7:14]
    (emb2, mixing2, expa2, shr2, cls2, sca2, shi2) = held[14:21]
    er, ncls, wide = emb.shape[0], cls.shape[1], sca.shape[1]
    for c in shared:
        c.wait_send()
    g_big[...] = g_big[...] * scaled
    g_shr[...] = g_shr[...] * scaled
    g_cls[...] = g_cls[...] * scaled
    g_vec[...] = vector * scaled
    for t in range(MP):
        g_mix[t * S_VEC : (t + 1) * S_VEC, :] = nmix[t] * scaled
    bias = jnp.concatenate([g_vec[11 + k : 12 + k, :] for k in range(D // LANE)], axis=1)
    mva[A_EMB : A_EMB + er, :] = adamw(emb[...], g_big[D : D + er, :], emb1[...], emb2[...], matrix_rate)
    mva[A_EXP : A_EXP + D, :] = adamw(expa[0:D, :], g_big[0:D, :], expa1[0:D, :], expa2[0:D, :], matrix_rate)
    mva[A_EXP + D : A_SHR, :] = jnp.zeros((A_SHR - A_EXP - D, D), F32)
    last = slice(D, D + 1)
    mva[A_EXP + D : A_EXP + D + 1, :] = adamw(expa[last, :], bias, expa1[last, :], expa2[last, :], matrix_rate)
    mva[A_SHR : A_SHR + D, :] = adamw(shr[...], g_shr[...], shr1[...], shr2[...], matrix_rate)
    mva[A_SHR + D :, :] = jnp.zeros((A_ROWS - A_SHR - D, D), F32)
    ha, hc = A_ROWS // 2, C_ROWS // 2

    def half(ref, k, n):
        return ref.at[pl.ds(pl.multiple_of(k * n, 8), n), :]

    if G > 1:
        core, other = lax.rem(g, 2), 1 - lax.rem(g, 2)
        near = {"group": gstep[0]}
        go(half(mva, other, ha), h1a, g_s.at[0], g_r.at[0], near)
    mvc[...] = jnp.zeros_like(mvc)
    mvc[C_CLS : C_CLS + D + 1, 0:ncls] = adamw(cls[...], g_cls[0 : D + 1, 0:ncls], cls1[...], cls2[...], head_rate)
    mvc[C_MIX : C_MIX + PATCHES, 0 : PATCHES + 1] = adamw(
        mixing[...], g_mix[0:PATCHES, 0 : PATCHES + 1], mixing1[...], mixing2[...], matrix_rate
    )
    mvc[C_SCA : C_SCA + 5, 0:wide] = adamw(sca[...], g_vec[0:5, 0:wide], sca1[...], sca2[...], vector_rate)
    mvc[C_SHI : C_SHI + 5, 0:wide] = adamw(shi[...], g_vec[5:10, 0:wide], shi1[...], shi2[...], vector_rate)

    if G == 1:
        sum_a[...] = mva[...]
        sum_c[...] = mvc[...]
    else:
        go(half(mvc, other, hc), h1c, g_s.at[1], g_r.at[1], near)
        own_a = pl.ds(pl.multiple_of(core * ha, 8), ha)
        own_c = pl.ds(pl.multiple_of(core * hc, 8), hc)
        far = {"group": gstep[-1]}
        arrived(h1a, g_r.at[0], near)
        pa = mva[own_a, :] + h1a[...]
        if G > 2:
            h2a[0] = pa.astype(BF16)
            go(h2a.at[0], h2a.at[1], g_s.at[2], g_r.at[2], far)
        arrived(h1c, g_r.at[1], near)
        pc = mvc[own_c, :] + h1c[...]
        if G > 2:
            h2c[0] = pc
            go(h2c.at[0], h2c.at[1], g_s.at[3], g_r.at[3], far)
            arrived(h2a.at[1], g_r.at[2], far)
            pa = h2a[0].astype(F32) + h2a[1].astype(F32)
        sum_a[own_a, :] = pa
        go(half(sum_a, core, ha), half(sum_a, core, ha), g_s.at[4], g_r.at[4], near)
        if G > 2:
            arrived(h2c.at[1], g_r.at[3], far)
            pc = h2c[0] + h2c[1]
        sum_c[own_c, :] = pc
        go(half(sum_c, core, hc), half(sum_c, core, hc), g_s.at[5], g_r.at[5], near)
        arrived(half(sum_a, other, ha), g_r.at[4], near)
        arrived(half(sum_c, other, hc), g_r.at[5], near)

    for c in started:
        c.wait_send()


def gradient_sums(G, DP, MP, big, sm, acts, fac, shapes, states):
    dma = pltpu.SemaphoreType.DMA
    vm = pl.BlockSpec(memory_space=VMEM)
    hbm = pl.BlockSpec(memory_space=pl.ANY)
    cpad = -(-shapes[4][1] // LANE) * LANE
    s = jax.ShapeDtypeStruct
    HR = big.shape[1] // DP
    dp1 = max(DP - 1, 1)
    return pl.pallas_call(
        functools.partial(sum_kernel, G, DP, MP),
        out_shape=(
            s((DP * HR, D), F32),
            s((MP * S_VEC, 256), F32),
            s((D, D), F32),
            s((392, cpad), F32),
            s((16, LANE), F32),
            s((A_ROWS, D), F32),
            s((C_ROWS, 256), F32),
            s((8, LANE), F32),
        ),
        in_specs=[vm] * 4 + [hbm] * 21,
        out_specs=(vm,) * 8,
        scratch_shapes=[VMEM(shape, F32) for shape in shapes] * 3
        + [
            VMEM((MP, dp1, HR, D), BF16),
            VMEM((MP, DP, HR, D), BF16),
            VMEM((MP - 1, HR, D), BF16),
            VMEM((MP, HR, D), BF16),
            VMEM((MP, S_ROWS, 256), F32),
            VMEM((MP, 16, D), F32),
            VMEM((MP, 48, D), BF16),
            VMEM((DP, S_ROWS, 256), F32),
            VMEM((DP, MP, 16, D), F32),
            VMEM((DP, MP, 48, D), BF16),
            VMEM((MP, S_VEC, 256), F32),
            VMEM((MP, 8, LANE), F32),
            VMEM((A_ROWS, D), F32),
            VMEM((C_ROWS, 256), F32),
            VMEM((A_ROWS // 2, D), F32),
            VMEM((C_ROWS // 2, 256), F32),
            VMEM((2, A_ROWS // 2, D), BF16),
            VMEM((2, C_ROWS // 2, 256), F32),
            dma((MP, dp1)),
            dma((MP, DP)),
            dma((MP - 1,)),
            dma((MP,)),
            dma((MP - 1, 3)),
            dma((MP, 3)),
            dma((dp1, 3)),
            dma((DP, 3)),
            dma((dp1,)),
            dma((DP,)),
            dma((MP - 1, 2)),
            dma((MP, 2)),
            dma((6,)),
            dma((6,)),
            dma((21,)),
        ],
        compiler_params=pltpu.CompilerParams(
            collective_id=1, has_side_effects=True, vmem_limit_bytes=62 << 20
        ),
    )(big, sm, acts, fac, *states)


def finish_kernel(groups, *refs):
    (info, *grads_in), refs = refs[:8], refs[8:]
    states, refs = refs[:28], refs[28:]
    (losses, norm), refs = refs[:2], refs[2:]
    outs, refs = refs[:28], refs[28:]
    grads_held, refs = refs[:7], refs[7:]
    held, refs = refs[:28], refs[28:]
    new, (load, load_grad, save) = refs[:28], refs[28:]
    first = [pltpu.make_async_copy(a, b, load_grad.at[k]) for k, (a, b) in enumerate(zip(grads_in, grads_held, strict=True))]
    loads = [pltpu.make_async_copy(flat(a), b, load.at[k]) for k, (a, b) in enumerate(zip(states, held, strict=True))]
    saves = [pltpu.make_async_copy(a, flat(b), save.at[k]) for k, (a, b) in enumerate(zip(new, outs, strict=True))]
    for c in first:
        c.start()
    for k in (3, 2, 0, 4, 1, 5, 6):
        for j in range(4):
            loads[7 * j + k].start()
    losses[...] = info[0:1, 0:2]
    norm[...] = info[0:1, 2:3]
    g_big, g_mix, g_shr, g_cls, g_vec, sum_a, sum_c = grads_held
    for c in first:
        c.wait()
    wide = held[5].shape[1]
    ncls = held[4].shape[1]
    er = held[0].shape[0]
    all_rows = slice(None)
    bias = jnp.concatenate([g_vec[11 + k : 12 + k, :] for k in range(D // LANE)], axis=1)
    work = (
        (3, all_rows, lambda: g_shr[...], lambda: sum_a[A_SHR : A_SHR + D, :]),
        (2, slice(0, D), lambda: g_big[0:D, :], lambda: sum_a[A_EXP : A_EXP + D, :]),
        (2, slice(D, D + 1), lambda: bias, lambda: sum_a[A_EXP + D : A_EXP + D + 1, :]),
        (0, all_rows, lambda: g_big[D : D + er, :], lambda: sum_a[A_EMB : A_EMB + er, :]),
        (4, all_rows, lambda: g_cls[0 : D + 1, 0:ncls], lambda: sum_c[C_CLS : C_CLS + D + 1, 0:ncls]),
        (1, all_rows, lambda: g_mix[0:PATCHES, 0 : PATCHES + 1], lambda: sum_c[C_MIX : C_MIX + PATCHES, 0 : PATCHES + 1]),
        (5, all_rows, lambda: g_vec[0:5, 0:wide], lambda: sum_c[C_SCA : C_SCA + 5, 0:wide]),
        (6, all_rows, lambda: g_vec[5:10, 0:wide], lambda: sum_c[C_SHI : C_SHI + 5, 0:wide]),
    )
    for n, (k, r, gradient, total) in enumerate(work):
        if n == 0 or work[n - 1][0] != k:
            for j in range(4):
                loads[7 * j + k].wait()
        weight, one, two, outer = (held[7 * j + k] for j in range(4))
        update, mean, square, velocity = (new[7 * j + k] for j in range(4))
        grad = gradient()
        mean[r, :] = beta_one * one[r, :] + (1.0 - beta_one) * grad
        square[r, :] = beta_two * two[r, :] + (1.0 - beta_two) * grad * grad
        average = total() * (1.0 / groups)
        moving = outer_momentum * outer[r, :] + average
        velocity[r, :] = moving
        update[r, :] = weight[r, :] - outer_rate * (average + outer_momentum * moving)
        if n + 1 == len(work) or work[n + 1][0] != k:
            for j in range(4):
                saves[7 * j + k].start()
    for c in saves:
        c.wait()


def finish(G, info, grads, shapes, states, out_shapes):
    dma = pltpu.SemaphoreType.DMA
    vm = pl.BlockSpec(memory_space=VMEM)
    hbm = pl.BlockSpec(memory_space=pl.ANY)
    return pl.pallas_call(
        functools.partial(finish_kernel, G),
        out_shape=tuple(jax.ShapeDtypeStruct(shape, F32) for shape in ((1, 2), (1, 1), *out_shapes)),
        in_specs=[vm] + [hbm] * 35,
        out_specs=(vm,) * 2 + (hbm,) * 28,
        scratch_shapes=[VMEM(a.shape, F32) for a in grads]
        + [VMEM(shape, F32) for shape in shapes] * 8
        + [dma((28,)), dma((7,)), dma((28,))],
        compiler_params=pltpu.CompilerParams(vmem_limit_bytes=62 << 20),
    )(info, *grads, *states)


def thin(a):
    return jnp.swapaxes(a, 0, 1)


def per_device(
    G, DP, MP,
    patches, labels, partner, class_weight,
    embedding, mixing, expand, shrink, classifier, scales, shifts, *state,
):
    weights = (embedding, thin(mixing), thin(expand), shrink[0], classifier, scales, shifts)

    def moments(a):
        return (a[0][0], thin(a[1][0]), thin(a[2][0]), a[3][0, 0], thin(a[4]), thin(a[5]), thin(a[6]))

    firsts, seconds = moments(state[0:7]), moments(state[7:14])
    o = state[14:21]
    outers = (o[0], thin(o[1]), thin(o[2]), o[3][0], o[4], o[5], o[6])
    shapes = tuple((a.shape[0], a.shape[-1]) for a in weights)
    ncls = classifier.shape[1]
    big, sm, acts, fac = local_step(
        G, DP, MP, ncls, labels[0], partner[0], scales, shifts, class_weight.reshape(1, -1),
        jnp.swapaxes(patches[0], 1, 2), embedding, weights[2], weights[3], classifier, weights[1],
    )
    *grads, info = gradient_sums(G, DP, MP, big, sm, acts, fac, shapes, (*weights, *firsts, *seconds))
    out_shapes = tuple(a.shape for a in (*weights, *firsts, *seconds, *outers))
    losses, norm, *done = finish(G, info, grads, shapes, (*weights, *firsts, *seconds, *outers), out_shapes)
    updates, means, squares, velocities = (list(done[7 * k : 7 * k + 7]) for k in range(4))

    def whole(a):
        return (a[0], thin(a[1]), thin(a[2]), a[3][None], a[4], a[5], a[6])

    def by_group(a):
        return (a[0][None], thin(a[1])[None], thin(a[2])[None], a[3][None, None], thin(a[4]), thin(a[5]), thin(a[6]))

    return (
        losses, norm[0],
        *whole(updates), *by_group(means), *by_group(squares), *whole(velocities),
    )


WEIGHT_SPECS = (
    P("mp", None),
    P(),
    P(None, None, "mp"),
    P(None, "mp", None),
    P(None, "mp"),
    P(None, "mp"),
    P(None, "mp"),
)
STATE_SPECS = (
    P("group", "mp", None),
    P("group", None, None, None),
    P("group", None, None, "mp"),
    P("group", None, "mp", None),
    P("group", None, "mp"),
    P("group", None, "mp"),
    P("group", None, "mp"),
)


def solution(mesh):
    G, DP, MP = mesh.shape["group"], mesh.shape["dp"], mesh.shape["mp"]
    return jax.shard_map(
        functools.partial(per_device, G, DP, MP),
        mesh=mesh,
        in_specs=(
            P("group", "dp", None, "mp"),
            P("group", "dp"),
            P("group", "dp"),
            P(),
            *WEIGHT_SPECS,
            *STATE_SPECS,
            *STATE_SPECS,
            *WEIGHT_SPECS,
        ),
        out_specs=(
            P("group", None),
            P("group"),
            *WEIGHT_SPECS,
            *STATE_SPECS,
            *STATE_SPECS,
            *WEIGHT_SPECS,
        ),
        check_vma=False,
    )
```

```python
import functools

import jax
import jax.numpy as jnp
from jax import lax
from jax.experimental import pallas as pl
from jax.experimental.pallas import tpu as pltpu
from jax.sharding import PartitionSpec as P

F32 = jnp.float32
BF16 = jnp.bfloat16
MESH = pl.DeviceIdType.MESH
VMEM = pltpu.VMEM
SMEM = pltpu.SMEM

D = 384
PATCHES = 196
ROWS = 208
MAIN = 192
STEP = 10
LANE = 128

mix_share = 0.7
clip_limit = 0.01
beta_one = 0.9
beta_two = 0.999
adam_eps = 1e-08
weight_decay = 0.05
matrix_rate = 0.05
head_rate = 0.5
vector_rate = 0.4
outer_rate = 0.7
outer_momentum = 0.9

GELU_A = 0.7978845608028654
GELU_B = GELU_A * 0.044715

S_VEC, S_ROWS = 56, 72
C_CLS, C_MIX, C_VEC, C_ROWS = 0, 392, 592, 608
E_EXP, E_EMB, E_ROWS = 0, 392, 608


def dot(a, b, dims=((1,), (0,)), precision=None):
    return lax.dot_general(
        a, b, (dims, ((), ())), preferred_element_type=F32, precision=precision
    )


def thirds(a, axis):
    high = a.astype(BF16)
    rest = a - high.astype(F32)
    middle = rest.astype(BF16)
    low = (rest - middle.astype(F32)).astype(BF16)
    return jnp.concatenate([high, middle, low], axis=axis)


def rounded(a):
    return a.astype(BF16).astype(F32)


def greet(peers):
    barrier = pltpu.get_barrier_semaphore()
    for peer in peers:
        pl.semaphore_signal(barrier, inc=1, device_id=peer, device_id_type=MESH)
    pl.semaphore_wait(barrier, len(peers))


def remote(src, dst, send_sem, recv_sem, peer):
    return pltpu.make_async_remote_copy(
        src_ref=src, dst_ref=dst, send_sem=send_sem, recv_sem=recv_sem,
        device_id=peer, device_id_type=MESH,
    )


CHUNK = 256
AHEAD = 2
SLOTS = AHEAD + 1


def waves_of(pairs):
    cuts = list(range(0, pairs - 1, 2)) + [pairs - 1, pairs]
    return list(zip(cuts[:-1], cuts[1:], strict=True))


def part_rows(rows, DP):
    return -(-rows // (16 * DP)) * 16


def adamw(weight, gradient, moment_one, moment_two, rate):
    mean_new = beta_one * moment_one + (1.0 - beta_one) * gradient
    square_new = beta_two * moment_two + (1.0 - beta_two) * gradient * gradient
    mean_hat = mean_new * (1.0 / (1.0 - beta_one**STEP))
    square_hat = square_new * (1.0 / (1.0 - beta_two**STEP))
    return rate * (mean_hat / (jnp.sqrt(square_hat) + adam_eps) + weight_decay * weight)


def flat(ref):
    return ref.at[:, 0, :] if len(ref.shape) == 3 and ref.shape[1] == 1 else ref


def step_kernel(G, DP, MP, NI, ncls, *refs):
    (labels, partner, sca, shi, class_weight, patches), refs = refs[:6], refs[6:]
    states, refs = refs[:21], refs[21:]
    (g_w, g_e, g_mix, g_shr, g_cls, g_vec, sum_s, sum_c, sum_e, info), refs = refs[:10], refs[10:]
    held, refs = list(refs[:17]), refs[17:]
    (
        pv, stage, rows, e_all, w1, w2, wc, small,
        xs, gp, s0, s1, mx, mi, fi, ep, mm, mt, eye, mbias, vec, b1, cw, asum, s1sum, la, lb,
        dact, ds2, dh, csum, gw, ge, gm, gmb, gvec,
        sm, fac, zsm, ysm, yacts, yfac,
        ysw, yrw, zsw, zrw, yse, yre, zse, zre, nsq,
        h2s, h2c, h2e,
        load, rs_send, rs_recv, wz_send, wz_recv, wg_send, wg_recv, sm_send, sm_recv,
        zf_s, zf_r, yf_s, yf_r, yw_s, yw_r, zw_s, zw_r, ye_s, ye_r, ze_s, ze_r, ag_s, ag_r,
        nm_s, nm_r, nq_s, nq_r, g_s, g_r,
    ) = refs
    late = {7: mx.at[0, 0 : held[0].shape[0], :], 14: mx.at[1, 0 : held[0].shape[0], :]}
    late |= {10: s1.at[0, 0:D, :], 17: s1.at[1, 0:D, :]}
    for k in sorted(late):
        held.insert(k, late[k])
    emb, mixing, expa, shr, cls = held[:5]
    z = lax.axis_index("mp")
    y = lax.axis_index("dp")
    g = lax.axis_index("group")
    NP = NI // 2
    PR = 2 * ROWS
    hid = expa.shape[1]
    hid_all = hid * MP
    cpad = wc.shape[1] // MP
    er = emb.shape[0]
    NCH = hid_all // CHUNK
    PW, PE = g_w.shape[0] // DP, g_e.shape[0] // DP
    pair = 2 if DP % 2 == 0 else 1

    loads = [pltpu.make_async_copy(flat(a), b, load.at[k]) for k, (a, b) in enumerate(zip(states, held, strict=True))]
    load_patches = pltpu.make_async_copy(patches, pv, load.at[21])
    loads[0].start()
    loads[2].start()
    load_patches.start()
    for k in range(21):
        if k not in (0, 2, *late):
            loads[k].start()

    zpeer = [lax.rem(z + d, MP) for d in range(1, MP)]
    half = lax.rem(y, pair)
    plane, plane_far = [], []
    for e in range(pair):
        for d in range(G):
            if d or e:
                j = lax.rem(g + d, G)
                h = half if e == 0 else 1 - half
                plane_far.append(d > 0)
                plane.append((j, y if e == 0 else y + 1 - 2 * half, j * pair + h, e))
    place = g * pair + half
    parts = G * pair
    ypeer = [lax.rem(y + d, DP) for d in range(1, DP)]
    others = [{"mp": lax.rem(z + c, MP), "dp": lax.rem(y + d, DP)} for d in range(DP) for c in range(MP) if c or d]
    greet(others + [{"group": j, "dp": u} for (j, u, _, _), far in zip(plane, plane_far, strict=True) if far])

    def pieces(t, j):
        ee, hh, dd = er // G, hid // parts, D // parts
        return (
            e_all.at[t, pl.ds(pl.multiple_of(j // pair * ee, 16), ee), :],
            w1.at[pl.ds(pl.multiple_of(j * dd, 16), dd), pl.ds(pl.multiple_of(t * hid, LANE), hid)],
            w2.at[pl.ds(pl.multiple_of(t * hid + j * hh, 16), hh), :],
            wc.at[pl.ds(pl.multiple_of(j * dd, 16), dd), pl.ds(pl.multiple_of(t * cpad, LANE), cpad)],
        )

    started = []

    def go(*args):
        c = remote(*args)
        c.start()
        started.append(c)

    def spread(k):
        part = pieces(z, place)[k]
        for d, t in enumerate(zpeer):
            go(part, part, wz_send.at[d, k], wz_recv.at[z, k], {"mp": t})

    def pass_on(k):
        for d in range(1, MP):
            t = lax.rem(z + MP - d, MP)
            part = pieces(t, place)[k]
            remote(part, part, wz_send.at[d - 1, k], wz_recv.at[t, k], {"mp": t}).wait_recv()
            for e, (j, u, _, other) in enumerate(plane):
                if k or not other:
                    go(part, part, wg_send.at[d - 1, e, k], wg_recv.at[t, place, k], {"group": j, "dp": u})

    def gathered(k):
        for t in zpeer:
            for j, u, at, other in plane:
                if k or not other:
                    part = pieces(t, at)[k]
                    remote(part, part, wg_send.at[0, 0, k], wg_recv.at[t, at, k], {"group": j, "dp": u}).wait_recv()

    loads[0].wait()
    e_all[z] = emb[...].astype(BF16)
    spread(0)
    loads[2].wait()
    w1[:, pl.ds(pl.multiple_of(z * hid, LANE), hid)] = expa[0:D, :].astype(BF16)
    spread(1)

    row = lax.broadcasted_iota(jnp.int32, (ROWS, PATCHES), 0)
    column = lax.broadcasted_iota(jnp.int32, (ROWS, PATCHES), 1)
    eye[...] = jnp.where(row == column, 1.0, 0.0).astype(BF16)
    share = F32(mix_share)
    rest = F32(1.0 - mix_share)

    def blend(i):
        return (share * pv[i] + rest * pv[partner[i]]).astype(BF16)

    def blend_pair(t, p, ref, lead):
        a = blend(t * NI + 2 * p)
        b = blend(t * NI + 2 * p + 1)
        both = jnp.concatenate([a[0:LANE], b[0:LANE], a[LANE:], b[LANE:]], axis=0)
        turned = dot(eye[...], both, ((1,), (1,)))
        tail = None
        for k in range(3):
            lanes = turned[:, k * LANE : (k + 1) * LANE]
            ref[lead + (slice(k * MAIN, (k + 1) * MAIN), slice(None))] = lanes[0:MAIN].astype(BF16)
            last = lanes[MAIN:ROWS]
            tail = last if k == 0 else tail + pltpu.roll(last, k * (PATCHES - MAIN), 0)
        ref[lead + (slice(3 * MAIN, 3 * MAIN + 16), slice(None))] = tail.astype(BF16)

    def slab(t, p, k):
        tail = rows[t, p, 3 * MAIN :, :].astype(F32)
        if k:
            tail = pltpu.roll(tail, 16 - k * (PATCHES - MAIN), 0)
        row = lax.broadcasted_iota(jnp.int32, (16, LANE), 0)
        tail = jnp.where(row < PATCHES - MAIN, tail, 0.0).astype(BF16)
        return rows[t, p, k * MAIN : (k + 1) * MAIN, :], tail

    def send(p, d):
        slot = lax.rem(p, SLOTS)
        return remote(stage.at[d, slot], rows.at[z, p], rs_send.at[d, slot], rs_recv.at[z, p], {"mp": zpeer[d]})

    def issue(p):
        for d in range(MP - 1):
            blend_pair(zpeer[d], p, stage, (d, lax.rem(p, SLOTS)))
            send(p, d).start()

    load_patches.wait()
    issue(0)

    loads[3].wait()
    w2[pl.ds(pl.multiple_of(z * hid, 16), hid), :] = shr[...].astype(BF16)
    loads[4].wait()
    head = jnp.concatenate([cls[0:D, :], jnp.zeros((D, cpad - ncls), F32)], axis=1)
    wc[:, pl.ds(pl.multiple_of(z * cpad, LANE), cpad)] = head.astype(BF16)
    spread(2)
    spread(3)
    small[z] = jnp.zeros(small.shape[1:], F32)
    small[z, 0:5, 0 : D // MP] = sca[...]
    small[z, 5:10, 0 : D // MP] = shi[...]
    small[z, 10:11, :] = rounded(expa[D : D + 1, :])
    small[z, 11:12, 0:ncls] = rounded(cls[D : D + 1, :])
    for d, t in enumerate(zpeer):
        go(small.at[z], small.at[z], sm_send.at[d], sm_recv.at[z], {"mp": t})
    for p in range(1, min(AHEAD, NP)):
        issue(p)
    pass_on(0)
    pass_on(1)

    loads[1].wait()
    wide = jnp.concatenate([mixing[...], jnp.zeros((PATCHES, 256 - PATCHES - 1), F32)], axis=1)
    wide = jnp.concatenate([wide, jnp.zeros((256 - PATCHES, 256), F32)], axis=0)
    column = lax.broadcasted_iota(jnp.int32, (256, 256), 1)
    square = jnp.where(column < PATCHES, wide, 0.0)
    mm[...] = square[0:ROWS, 0:ROWS].astype(BF16)
    mt[...] = jnp.transpose(square)[0:ROWS, 0:ROWS].astype(BF16)
    mbias[...] = rounded(jnp.sum(jnp.where(column == PATCHES, wide, 0.0), axis=1, keepdims=True)[0:ROWS])
    for t in range(MP):
        block = class_weight[:, t * ncls : (t + 1) * ncls]
        cw[:, t * cpad : (t + 1) * cpad] = jnp.concatenate([block, jnp.zeros((1, cpad - ncls), F32)], axis=1)
    asum[...] = jnp.zeros_like(asum)
    s1sum[...] = jnp.zeros_like(s1sum)
    csum[...] = jnp.zeros_like(csum)
    gw[...] = jnp.zeros_like(gw)
    ge[...] = jnp.zeros_like(ge)
    gm[...] = jnp.zeros_like(gm)
    gmb[...] = jnp.zeros_like(gmb)
    gvec[...] = jnp.zeros_like(gvec)
    la[...] = jnp.full(la.shape, -1, jnp.int32)
    lb[...] = jnp.full(lb.shape, -1, jnp.int32)
    for i in range(NI):
        own = labels[z * NI + i]
        mate = labels[partner[z * NI + i]]
        la[i : i + 1, :] = jnp.full((1, LANE), own, jnp.int32)
        lb[i : i + 1, :] = jnp.full((1, LANE), mate, jnp.int32)

    for t in zpeer:
        remote(small.at[t], small.at[t], sm_send.at[0], sm_recv.at[t], {"mp": t}).wait_recv()
    full = jnp.zeros((16, D), F32)
    for t in range(MP):
        block = small[t]
        full = full + (pltpu.roll(block, t * (D // MP), 1) if t else block)
        b1[:, t * hid : (t + 1) * hid] = small[t, 10:11, :]
    vec[...] = full
    gathered(0)
    rest_rows = er - LANE
    for t in range(MP):
        ep[t * LANE : (t + 1) * LANE, :] = e_all[t, 0:LANE, :]
        ep[MP * LANE + t * rest_rows : MP * LANE + (t + 1) * rest_rows, :] = e_all[t, LANE:er, :]
    gathered(1)
    pass_on(2)
    pass_on(3)

    def scale(k):
        return vec[k : k + 1, :]

    def shift(k):
        return vec[5 + k : 6 + k, :]

    def forward(base, p, carry):
        @pl.when(p + AHEAD < NP)
        def _():
            @pl.when(p + AHEAD >= SLOTS)
            def _():
                for d in range(MP - 1):
                    send(p + AHEAD - SLOTS, d).wait_send()

            issue(p + AHEAD)

        q = p - base
        blend_pair(z, p, rows, (z, p))
        for t in zpeer:
            remote(stage.at[0, 0], rows.at[t, p], rs_send.at[0, 0], rs_recv.at[t, p], {"mp": t}).wait_recv()
        for t in range(MP):
            lanes = slice(t * LANE, (t + 1) * LANE)
            for k in range(2):
                xs[q, k * ROWS : k * ROWS + MAIN, lanes], xs[q, k * ROWS + MAIN : (k + 1) * ROWS, lanes] = slab(t, p, k)
        for t in range(0, MP, 2):
            lanes = slice(MP * LANE + t * 64, MP * LANE + t * 64 + LANE)
            left, right = slab(t, p, 2), slab(t + 1, p, 2)
            for k in range(2):
                half = slice(k * 64, (k + 1) * 64)
                main, tail = (jnp.concatenate([v[:, half], w[:, half]], axis=1) for v, w in zip(left, right, strict=True))
                xs[q, k * ROWS : k * ROWS + MAIN, lanes] = main
                xs[q, k * ROWS + MAIN : (k + 1) * ROWS, lanes] = tail
        stream0 = dot(xs[q], ep[...]) + shift(3)
        s0[q] = stream0
        mi[q] = (scale(0) * stream0 + shift(0)).astype(BF16)
        for b in range(2):
            r = slice(b * ROWS, (b + 1) * ROWS)
            mixed = dot(mm[...], mi[q, r, :]) + mbias[...]
            mx[q, r, :] = mixed
            stream1 = s0[q, r, :] + scale(1) * mixed
            s1[q, r, :] = stream1
            fi[q, r, :] = (scale(2) * stream1 + shift(1)).astype(BF16)
            s1sum[pl.ds(2 * p + b, 1), :] = jnp.sum(stream1[0:PATCHES], axis=0, keepdims=True)

        def chunk(c, carry):
            cols = pl.ds(pl.multiple_of(c * CHUNK, CHUNK), CHUNK)
            for b in range(2):
                r = slice(b * ROWS, (b + 1) * ROWS)
                h = dot(fi[q, r, :], w1[:, cols]) + b1[:, cols]
                sq = h * h
                s = 0.5 * jnp.tanh(h * (GELU_A + GELU_B * sq)) + 0.5
                act = rounded(h * s)
                asum[pl.ds(2 * p + b, 1), cols] = jnp.sum(act[0:PATCHES], axis=0, keepdims=True)
                gp[q, r, cols] = s + s * (1.0 - s) * (h * (2.0 * GELU_A + 6.0 * GELU_B * sq))
                gp[q, b * ROWS + PATCHES : (b + 1) * ROWS, cols] = jnp.zeros((ROWS - PATCHES, CHUNK), F32)
            return carry

        lax.fori_loop(0, NCH, chunk, 0)
        return carry

    def class_head():
        three = dot(thirds(asum[...], 0), w2[...])
        outsum = three[0:16] + three[16:32] + three[32:48] + PATCHES * shift(2)
        stream2 = s1sum[...] + scale(3) * outsum
        pooled = (scale(4) * (stream2 * (1.0 / PATCHES)) + shift(4)).astype(BF16)
        bias = jnp.concatenate([small[t, 11:12, 0:cpad] for t in range(MP)], axis=1)
        lane = lax.broadcasted_iota(jnp.int32, (16, cpad * MP), 1)
        inside = lax.rem(lane, cpad)
        valid = inside < ncls
        class_id = (lane // cpad) * ncls + inside
        logits = jnp.where(valid, dot(pooled, wc[...]) + bias, -1e30)
        hot_a = jnp.where(valid & (class_id == la[:, 0:1]), 1.0, 0.0)
        hot_b = jnp.where(valid & (class_id == lb[:, 0:1]), 1.0, 0.0)
        weight_a = mix_share * jnp.sum(hot_a * cw[...], axis=1, keepdims=True)
        weight_b = (1.0 - mix_share) * jnp.sum(hot_b * cw[...], axis=1, keepdims=True)
        top = jnp.max(logits, axis=1, keepdims=True)
        exps = jnp.where(valid, jnp.exp(logits - top), 0.0)
        exp_sum = jnp.sum(exps, axis=1, keepdims=True)
        soft = exps / exp_sum
        dlog = ((weight_a + weight_b) * soft - weight_a * hot_a - weight_b * hot_b).astype(BF16)
        dfinal = dot(dlog, wc[...], ((1,), (1,))) * (1.0 / PATCHES)
        dstream2 = scale(4) * dfinal
        ds2[...] = dstream2
        dout = scale(3) * dstream2
        low = dout.astype(BF16)
        dact[...] = dot(low, w2[...], ((1,), (1,)))

        def last():
            log_total = top + jnp.log(exp_sum)
            target_a = jnp.sum(hot_a * logits, axis=1, keepdims=True)
            target_b = jnp.sum(hot_b * logits, axis=1, keepdims=True)
            loss = weight_a * (log_total - target_a) + weight_b * (log_total - target_b)
            loss = jnp.sum(loss, axis=0, keepdims=True)
            total = jnp.sum(weight_a + weight_b, axis=0, keepdims=True)
            fac[:, 0:16, :] = jnp.broadcast_to(low[None], (MP, 16, D))
            fac[:, 16:32, :] = jnp.broadcast_to(pooled[None], (MP, 16, D))
            for t in range(MP):
                fac[t, 32:48, 0:cpad] = dlog[:, t * cpad : (t + 1) * cpad]
                fac[t, 32:48, cpad:] = jnp.zeros((16, D - cpad), BF16)
            gvec[3:4, :] = jnp.sum(outsum * dstream2, axis=0, keepdims=True)
            gvec[4:5, :] = jnp.sum(dfinal * stream2, axis=0, keepdims=True)
            gvec[7:8, :] = PATCHES * jnp.sum(dout, axis=0, keepdims=True)
            gvec[8:9, :] = PATCHES * jnp.sum(dstream2, axis=0, keepdims=True)
            gvec[9:10, :] = PATCHES * jnp.sum(dfinal, axis=0, keepdims=True)
            lane = lax.broadcasted_iota(jnp.int32, (1, D), 1)
            gvec[10:11, :] = jnp.where(lane == 0, loss, jnp.where(lane == 1, total, 0.0))

        return last

    def backward_hidden(base, p):
        q = p - base

        def chunk(c, carry):
            cols = pl.ds(pl.multiple_of(c * CHUNK, CHUNK), CHUNK)
            for b in range(2):
                r = slice(b * ROWS, (b + 1) * ROWS)
                dh[r, cols] = (gp[q, r, cols] * dact[pl.ds(2 * p + b, 1), cols]).astype(BF16)
            value = dh[:, cols]
            csum[0:1, cols] += jnp.sum(value.astype(F32), axis=0, keepdims=True)
            gw[0:D, cols] += dot(fi[q], value, ((0,), (0,)))
            return carry

        lax.fori_loop(0, NCH, chunk, 0)

    def backward_rest(base, p):
        q = p - base
        dffn = dot(dh[...], w1[...], ((1,), (1,)))
        gvec[2:3, :] += jnp.sum(dffn * s1[q], axis=0, keepdims=True)
        gvec[6:7, :] += jnp.sum(dffn, axis=0, keepdims=True)
        for b in range(2):
            r = slice(b * ROWS, (b + 1) * ROWS)
            d1 = ds2[pl.ds(2 * p + b, 1), :] + scale(2) * dffn[r]
            gvec[1:2, :] += jnp.sum(mx[q, r, :] * d1, axis=0, keepdims=True)
            dmixed = (scale(1) * d1).astype(BF16)
            gm[...] += dot(dmixed, mi[q, r, :], ((1,), (1,)))
            gmb[...] += dmixed.astype(F32)
            dmixer = dot(mt[...], dmixed)
            gvec[0:1, :] += jnp.sum(dmixer * s0[q, r, :], axis=0, keepdims=True)
            gvec[5:6, :] += jnp.sum(dmixer, axis=0, keepdims=True)
            d0 = (d1 + scale(0) * dmixer).astype(BF16)
            grad = dot(xs[q, r, :], d0, ((0,), (0,)))
            for t in range(MP):
                ge[t, 0:LANE, :] += grad[t * LANE : (t + 1) * LANE]
                ge[t, LANE:er, :] += grad[MP * LANE + t * rest_rows : MP * LANE + (t + 1) * rest_rows]

    def backward(base, p, carry):
        backward_hidden(base, p)
        backward_rest(base, p)
        return carry

    for n, (lo, hi) in enumerate(waves_of(NP)):
        lax.fori_loop(lo, hi, functools.partial(forward, lo), 0)
        if n == 0:
            gathered(2)
            gathered(3)
        last = class_head()
        if hi < NP:
            lax.fori_loop(lo, hi, functools.partial(backward, lo), 0)

    def arrived(dst, sem, peer):
        remote(dst, dst, sem, sem, peer).wait_recv()

    def columns(t):
        return pl.ds(pl.multiple_of(t * hid, LANE), hid)

    def part(u, n):
        return pl.ds(pl.multiple_of(u * n, 8), n)

    last()
    yacts[y, z] = asum[:, columns(z)]
    yfac[y, z] = fac[z]
    for d, v in enumerate(zpeer):
        go(asum.at[:, columns(v)], yacts.at[y, z], zf_s.at[d, 0], zf_r.at[z, 0], {"mp": v})
        go(fac.at[v], yfac.at[y, z], zf_s.at[d, 1], zf_r.at[z, 1], {"mp": v})
    order = zpeer + [z]
    backward_hidden(lo, lo)
    for i, t in enumerate(order):
        for d, u in enumerate(ypeer):
            ysw[i, d] = gw[part(u, PW), columns(t)].astype(BF16)
            go(ysw.at[i, d], yrw.at[t, d], yw_s.at[i, d], yw_r.at[t, d], {"dp": u})
    backward_rest(lo, lo)
    for i, t in enumerate(order):
        for d, u in enumerate(ypeer):
            yse[i, d] = ge[t, part(u, PE), :].astype(BF16)
            go(yse.at[i, d], yre.at[t, d], ye_s.at[i, d], ye_r.at[t, d], {"dp": u})

    for k in late:
        loads[k].start()

    gvec[8:9, :] += scale(2) * gvec[6:7, :] + scale(0) * gvec[5:6, :]
    row = lax.broadcasted_iota(jnp.int32, (ROWS, 256), 0)
    column = lax.broadcasted_iota(jnp.int32, (ROWS, 256), 1)
    bias_grad = jnp.sum(gmb[...], axis=1, keepdims=True)
    grad = jnp.concatenate([gm[...], jnp.zeros((ROWS, 256 - ROWS), F32)], axis=1)
    grad = jnp.where(column < PATCHES, grad, jnp.where(column == PATCHES, bias_grad, 0.0))
    grad = jnp.where(row < PATCHES, grad, 0.0)
    own = D // MP
    lane = lax.broadcasted_iota(jnp.int32, (16, LANE), 1)
    for t in range(MP):
        n = min(S_VEC, ROWS - t * S_VEC)
        sm[t, 0:n, :] = grad[t * S_VEC : t * S_VEC + n]
        if n < S_VEC:
            sm[t, n:S_VEC, :] = jnp.zeros((S_VEC - n, 256), F32)
        vector = gvec[...]
        if t:
            vector = pltpu.roll(vector, D - t * own, 1)
        sm[t, S_VEC:S_ROWS, 0:LANE] = jnp.where(lane < own, vector[:, 0:LANE], 0.0)
        sm[t, S_VEC:S_ROWS, LANE:] = jnp.zeros((16, LANE), F32)
        sm[t, S_VEC + 10 : S_VEC + 11, 0:LANE] = gvec[10:11, 0:LANE]
        for k in range(hid // LANE):
            at = t * hid + k * LANE
            sm[t, S_VEC + 11 + k : S_VEC + 12 + k, 0:LANE] = csum[:, at : at + LANE]
    zsm[z] = sm[z]
    for d, v in enumerate(zpeer):
        go(sm.at[v], zsm.at[z], zf_s.at[d, 2], zf_r.at[z, 2], {"mp": v})

    for v in zpeer:
        arrived(yacts.at[y, v], zf_r.at[v, 0], {"mp": v})
        arrived(yfac.at[y, v], zf_r.at[v, 1], {"mp": v})
    for d, u in enumerate(ypeer):
        go(yacts.at[y], yacts.at[y], yf_s.at[d, 1], yf_r.at[y, 1], {"dp": u})
        go(yfac.at[y], yfac.at[y], yf_s.at[d, 2], yf_r.at[y, 2], {"dp": u})

    def from_dp(first, received, sems, send, out, out_sems, z_sems, n):
        for i, t in enumerate(order):
            value = first(t)
            for d in range(DP - 1):
                arrived(received.at[t, d], sems.at[t, d], {"dp": ypeer[d]})
                value = value + received[t, d].astype(F32)
            if i < MP - 1:
                send[i] = value.astype(BF16)
                go(send.at[i], out.at[i], out_sems.at[i], z_sems.at[i], {"mp": t})
        return value

    g_w[part(y, PW), :] = from_dp(lambda t: gw[part(y, PW), columns(t)], yrw, yw_r, zsw, zrw, zw_s, zw_r, PW)

    for v in zpeer:
        arrived(zsm.at[v], zf_r.at[v, 2], {"mp": v})
    summed = zsm[0]
    for v in range(1, MP):
        summed = summed + zsm[v]
    ysm[y] = summed
    for d, u in enumerate(ypeer):
        go(ysm.at[y], ysm.at[y], yf_s.at[d, 0], yf_r.at[y, 0], {"dp": u})

    g_e[part(y, PE), :] = from_dp(lambda t: ge[t, part(y, PE), :], yre, ye_r, zse, zre, ze_s, ze_r, PE)

    shared = []

    def from_mp(total, received, sems, n, k):
        value = total[part(y, n), :]
        for i in range(MP - 1):
            arrived(received.at[i], sems.at[i], {"mp": zpeer[i]})
            value = value + received[i].astype(F32)
        total[part(y, n), :] = value
        for d, u in enumerate(ypeer):
            c = remote(total.at[part(y, n), :], total.at[part(y, n), :], ag_s.at[d, k], ag_r.at[y, k], {"dp": u})
            c.start()
            shared.append(c)
        return value

    def squares(v):
        return jnp.sum(jnp.sum(v * v, axis=0, keepdims=True), axis=1, keepdims=True)

    mine = squares(from_mp(g_w, zrw, zw_r, PW, 0))

    for u in ypeer:
        arrived(ysm.at[u], yf_r.at[u, 0], {"dp": u})
    summed = ysm[0]
    for u in range(1, DP):
        summed = summed + ysm[u]
    g_mix[part(z, S_VEC), :] = summed[0:S_VEC]
    for d, v in enumerate(zpeer):
        go(g_mix.at[part(z, S_VEC), :], g_mix.at[part(z, S_VEC), :], nm_s.at[d], nm_r.at[z], {"mp": v})
    vector = summed[S_VEC:S_ROWS, 0:LANE]

    for u in ypeer:
        arrived(yacts.at[u], yf_r.at[u, 1], {"dp": u})
        arrived(yfac.at[u], yf_r.at[u, 2], {"dp": u})
    n = 16 * MP
    grad_shr = jnp.zeros((hid, D), F32)
    grad_cls = jnp.zeros((D, cpad), F32)
    cls_bias = jnp.zeros((1, cpad), F32)
    for u in range(DP):
        whole = yfac[u]
        dout = whole[:, 0:16, :].reshape(n, D)
        pooled = whole[:, 16:32, :].reshape(n, D)
        dlog = whole[:, 32:48, 0:cpad].reshape(n, cpad)
        three = thirds(yacts[u].reshape(n, hid), 0)
        grad_shr = grad_shr + dot(three, jnp.concatenate([dout] * 3, axis=0), ((0,), (0,)))
        grad_cls = grad_cls + dot(pooled, dlog, ((0,), (0,)))
        cls_bias = cls_bias + jnp.sum(dlog.astype(F32), axis=0, keepdims=True)
    g_shr[...] = grad_shr
    g_cls[0:D, :] = grad_cls
    g_cls[D:, :] = jnp.concatenate([cls_bias, jnp.zeros((g_cls.shape[0] - D - 1, cpad), F32)], axis=0)
    once = squares(grad_shr) + squares(grad_cls) + squares(cls_bias) + squares(summed[0:S_VEC])
    once = once + squares(vector[0:10]) + squares(vector[11 : 11 + hid // LANE])

    mine = mine + squares(from_mp(g_e, zre, ze_r, PE, 1))
    nsq[y, z] = jnp.broadcast_to(mine + jnp.where(y == 0, once, 0.0), (8, LANE))
    for k, peer in enumerate(others):
        go(nsq.at[y, z], nsq.at[y, z], nq_s.at[k], nq_r.at[y, z], peer)
    for k in range(4, 21):
        if k != 4:
            loads[k].wait()
    for v in zpeer:
        arrived(g_mix.at[part(v, S_VEC), :], nm_r.at[v], {"mp": v})
    for peer in others:
        arrived(nsq.at[peer["dp"], peer["mp"]], nq_r.at[peer["dp"], peer["mp"]], peer)
    square = jnp.zeros((1, 1), F32)
    for u in range(DP):
        for v in range(MP):
            square = square + nsq[u, v, 0:1, 0:1]
    loss_sum = vector[10:11, 0:1]
    weight_total = vector[10:11, 1:2]
    size = jnp.sqrt(square) / weight_total
    factor = clip_limit / jnp.maximum(size, clip_limit)
    scaled = factor / weight_total
    lane = lax.broadcasted_iota(jnp.int32, (8, LANE), 1)
    info[...] = jnp.where(
        lane == 0, loss_sum, jnp.where(lane == 1, weight_total, jnp.where(lane == 2, size, scaled))
    )

    (_, _, _, _, _, sca_w, shi_w) = held[:7]
    (emb1, mixing1, expa1, shr1, cls1, sca1, shi1) = held[7:14]
    (emb2, mixing2, expa2, shr2, cls2, sca2, shi2) = held[14:21]
    wide = sca_w.shape[1]
    gstep = [g + 1 - 2 * lax.rem(g, 2), lax.rem(g + 2, 4)]
    near, far = {"group": gstep[0]}, {"group": gstep[1]}
    core = lax.rem(g, 2)

    def halves(ref, k):
        n = ref.shape[0] // 2
        return ref.at[pl.ds(pl.multiple_of(k * n, 8), n), :]

    mvs = gp.at[0:2, 0 : hid // 2, 0:D]
    mvc = gp.at[0:2, 0 : C_ROWS // 2, D : D + 256]
    mve = gp.at[0:2, 0 : E_ROWS // 2, D + 256 : 2 * D + 256]

    def put(moved, at, value):
        n = moved.shape[1]
        rows, width = value.shape
        k = min(max(n - at, 0), rows)
        if k:
            moved[0, at : at + k, 0:width] = value[0:k]
        if k < rows:
            moved[1, at + k - n : at + rows - n, 0:width] = value[k:]

    fine = C_VEC - C_ROWS // 2

    def first_step(k, moved, out):
        go(moved.at[1 - core], halves(out, 1 - core), g_s.at[k, 0], g_r.at[k, 0], near)

    def second_step(k, moved, out, pairs):
        arrived(halves(out, core), g_r.at[k, 0], near)
        n = moved.shape[1]
        value = moved[core] + out[part(core, n), :]
        pairs[0, 0:n] = value.astype(BF16)
        if pairs.shape[1] > n:
            value = value[fine : fine + 16]
            pairs[0, n:] = (value - rounded(value)).astype(BF16)
        go(pairs.at[0], pairs.at[1], g_s.at[k, 1], g_r.at[k, 1], far)

    def third_step(k, pairs, out):
        arrived(pairs.at[1], g_r.at[k, 1], far)
        n = out.shape[0] // 2
        total = pairs[0].astype(F32) + pairs[1].astype(F32)
        out[part(core, n), :] = total[0:n]
        if pairs.shape[1] > n:
            out[pl.ds(pl.multiple_of(core * n + fine, 8), 16), :] = total[fine : fine + 16] + total[n:]
        go(halves(out, core), halves(out, core), g_s.at[k, 2], g_r.at[k, 2], near)

    put(mvs, 0, adamw(shr[...], g_shr[...] * scaled, shr1[...], shr2[...], matrix_rate))
    first_step(0, mvs, sum_s)
    mvc[...] = jnp.zeros(mvc.shape, F32)
    put(mvc, C_CLS, adamw(cls[...], g_cls[0 : D + 1, 0:ncls] * scaled, cls1[...], cls2[...], head_rate))
    put(
        mvc, C_MIX,
        adamw(mixing[...], g_mix[0:PATCHES, 0 : PATCHES + 1] * scaled, mixing1[...], mixing2[...], matrix_rate),
    )
    g_vec[...] = vector
    for k, (w, one, two) in enumerate(((sca_w, sca1, sca2), (shi_w, shi1, shi2))):
        value = adamw(w[...], g_vec[5 * k : 5 * k + 5, 0:wide] * scaled, one[...], two[...], vector_rate)
        put(mvc, C_VEC + 8 * k, value)
    first_step(1, mvc, sum_c)
    second_step(0, mvs, sum_s, h2s)
    for u in ypeer:
        arrived(g_w.at[part(u, PW), :], ag_r.at[u, 0], {"dp": u})
        arrived(g_e.at[part(u, PE), :], ag_r.at[u, 1], {"dp": u})
    bias = jnp.concatenate([g_vec[11 + k : 12 + k, :] for k in range(hid // LANE)], axis=1)
    last_row = slice(D, D + 1)
    mve[...] = jnp.zeros(mve.shape, F32)
    put(mve, E_EXP, adamw(expa[0:D, :], g_w[0:D, :] * scaled, expa1[0:D, :], expa2[0:D, :], matrix_rate))
    put(mve, E_EXP + D, adamw(expa[last_row, :], bias * scaled, expa1[last_row, :], expa2[last_row, :], matrix_rate))
    put(mve, E_EMB, adamw(emb[...], g_e[0:er, :] * scaled, emb1[...], emb2[...], matrix_rate))
    first_step(2, mve, sum_e)
    second_step(1, mvc, sum_c, h2c)
    second_step(2, mve, sum_e, h2e)
    third_step(0, h2s, sum_s)
    third_step(1, h2c, sum_c)
    third_step(2, h2e, sum_e)
    for k, out in enumerate((sum_s, sum_c, sum_e)):
        arrived(halves(out, 1 - core), g_r.at[k, 2], near)

    def drain(p, carry):
        for d in range(MP - 1):
            send(p, d).wait_send()
        return carry

    lax.fori_loop(max(NP - SLOTS, 0), NP, drain, 0)
    for c in started + shared:
        c.wait_send()


def local_step(G, DP, MP, shapes, labels, partner, sca, shi, class_weight, patches, states):
    NI = patches.shape[0] // MP
    NP = NI // 2
    PR = 2 * ROWS
    er, hid, ncls = shapes[0][0], shapes[2][1], shapes[4][1]
    hid_all = hid * MP
    pd = er * MP
    cpad = -(-ncls // LANE) * LANE
    wave = max(hi - lo for lo, hi in waves_of(NP))
    pair = 2 if DP % 2 == 0 else 1
    dp1 = max(DP - 1, 1)
    PW, PE = part_rows(D, DP), part_rows(er, DP)
    dma = pltpu.SemaphoreType.DMA
    vm = pl.BlockSpec(memory_space=VMEM)
    smem = pl.BlockSpec(memory_space=SMEM)
    hbm = pl.BlockSpec(memory_space=pl.ANY)
    s = jax.ShapeDtypeStruct
    return pl.pallas_call(
        functools.partial(step_kernel, G, DP, MP, NI, ncls),
        out_shape=(
            s((DP * PW, D), F32),
            s((DP * PE, D), F32),
            s((MP * S_VEC, 256), F32),
            s((hid, D), F32),
            s((392, cpad), F32),
            s((16, LANE), F32),
            s((hid, D), F32),
            s((C_ROWS, 256), F32),
            s((E_ROWS, D), F32),
            s((8, LANE), F32),
        ),
        in_specs=[smem, smem, vm, vm, vm] + [hbm] * 22,
        out_specs=(vm,) * 10,
        scratch_shapes=[VMEM(shape, F32) for shape in shapes + 2 * (shapes[1:3] + shapes[4:])]
        + [
            VMEM(patches.shape, F32),
            VMEM((MP - 1, SLOTS, 3 * MAIN + 16, LANE), BF16),
            VMEM((MP, NP, 3 * MAIN + 16, LANE), BF16),
            VMEM((MP, er, D), BF16),
            VMEM((D, hid_all), BF16),
            VMEM((hid_all, D), BF16),
            VMEM((D, cpad * MP), BF16),
            VMEM((MP, 16, hid), F32),
            VMEM((wave, PR, pd), BF16),
            VMEM((wave, PR, hid_all), F32),
            VMEM((wave, PR, D), F32),
            VMEM((wave, PR, D), F32),
            VMEM((wave, PR, D), F32),
            VMEM((wave, PR, D), BF16),
            VMEM((wave, PR, D), BF16),
            VMEM((pd, D), BF16),
            VMEM((ROWS, ROWS), BF16),
            VMEM((ROWS, ROWS), BF16),
            VMEM((ROWS, PATCHES), BF16),
            VMEM((ROWS, 1), F32),
            VMEM((16, D), F32),
            VMEM((1, hid_all), F32),
            VMEM((1, cpad * MP), F32),
            VMEM((16, hid_all), F32),
            VMEM((16, D), F32),
            VMEM((16, LANE), jnp.int32),
            VMEM((16, LANE), jnp.int32),
            VMEM((16, hid_all), F32),
            VMEM((16, D), F32),
            VMEM((PR, hid_all), BF16),
            VMEM((1, hid_all), F32),
            VMEM((DP * PW, hid_all), F32),
            VMEM((MP, DP * PE, D), F32),
            VMEM((ROWS, ROWS), F32),
            VMEM((ROWS, D), F32),
            VMEM((16, D), F32),
            VMEM((MP, S_ROWS, 256), F32),
            VMEM((MP, 48, D), BF16),
            VMEM((MP, S_ROWS, 256), F32),
            VMEM((DP, S_ROWS, 256), F32),
            VMEM((DP, MP, 16, hid), F32),
            VMEM((DP, MP, 48, D), BF16),
            VMEM((MP, dp1, PW, hid), BF16),
            VMEM((MP, dp1, PW, hid), BF16),
            VMEM((MP - 1, PW, hid), BF16),
            VMEM((MP - 1, PW, hid), BF16),
            VMEM((MP, dp1, PE, D), BF16),
            VMEM((MP, dp1, PE, D), BF16),
            VMEM((MP - 1, PE, D), BF16),
            VMEM((MP - 1, PE, D), BF16),
            VMEM((DP, MP, 8, LANE), F32),
            VMEM((2, hid // 2, D), BF16),
            VMEM((2, C_ROWS // 2 + 16, 256), BF16),
            VMEM((2, E_ROWS // 2, D), BF16),
            dma((22,)),
            dma((MP - 1, SLOTS)),
            dma((MP, NP)),
            dma((MP - 1, 4)),
            dma((MP, 4)),
            dma((MP - 1, G * pair - 1 or 1, 4)),
            dma((MP, G * pair, 4)),
            dma((MP - 1,)),
            dma((MP,)),
            dma((MP - 1, 3)),
            dma((MP, 3)),
            dma((dp1, 3)),
            dma((DP, 3)),
            dma((MP, dp1)),
            dma((MP, dp1)),
            dma((MP - 1,)),
            dma((MP - 1,)),
            dma((MP, dp1)),
            dma((MP, dp1)),
            dma((MP - 1,)),
            dma((MP - 1,)),
            dma((dp1, 2)),
            dma((DP, 2)),
            dma((MP - 1,)),
            dma((MP,)),
            dma((DP * MP - 1,)),
            dma((DP, MP)),
            dma((3, 3)),
            dma((3, 3)),
        ],
        compiler_params=pltpu.CompilerParams(
            collective_id=0, has_side_effects=True, vmem_limit_bytes=63 << 20
        ),
    )(labels, partner, sca, shi, class_weight, patches, *states)


def finish_kernel(groups, *refs):
    (info, *grads_in), refs = refs[:10], refs[10:]
    states, refs = refs[:28], refs[28:]
    (losses, norm), refs = refs[:2], refs[2:]
    outs, refs = refs[:28], refs[28:]
    grads_held, refs = refs[:9], refs[9:]
    held, refs = refs[:28], refs[28:]
    new, (load, load_grad, save) = refs[:28], refs[28:]
    first = [pltpu.make_async_copy(a, b, load_grad.at[k]) for k, (a, b) in enumerate(zip(grads_in, grads_held, strict=True))]
    loads = [pltpu.make_async_copy(flat(a), b, load.at[k]) for k, (a, b) in enumerate(zip(states, held, strict=True))]
    saves = [pltpu.make_async_copy(a, flat(b), save.at[k]) for k, (a, b) in enumerate(zip(new, outs, strict=True))]
    for c in first:
        c.start()
    for k in (3, 2, 0, 4, 1, 5, 6):
        for j in range(4):
            loads[7 * j + k].start()
    losses[...] = info[0:1, 0:2]
    norm[...] = info[0:1, 2:3]
    scaled = info[0:1, 3:4]
    g_w, g_e, g_mix, g_shr, g_cls, g_vec, sum_s, sum_c, sum_e = grads_held
    for c in first:
        c.wait()
    wide = held[5].shape[1]
    ncls = held[4].shape[1]
    er = held[0].shape[0]
    all_rows = slice(None)

    bias = jnp.concatenate([g_vec[11 + k : 12 + k, :] for k in range(D // LANE)], axis=1)
    work = (
        (3, all_rows, lambda: g_shr[...], lambda: sum_s[...]),
        (2, slice(0, D), lambda: g_w[0:D, :], lambda: sum_e[E_EXP : E_EXP + D, :]),
        (2, slice(D, D + 1), lambda: bias, lambda: sum_e[E_EXP + D : E_EXP + D + 1, :]),
        (0, all_rows, lambda: g_e[0:er, :], lambda: sum_e[E_EMB : E_EMB + er, :]),
        (4, all_rows, lambda: g_cls[0 : D + 1, 0:ncls], lambda: sum_c[C_CLS : C_CLS + D + 1, 0:ncls]),
        (1, all_rows, lambda: g_mix[0:PATCHES, 0 : PATCHES + 1], lambda: sum_c[C_MIX : C_MIX + PATCHES, 0 : PATCHES + 1]),
        (5, all_rows, lambda: g_vec[0:5, 0:wide], lambda: sum_c[C_VEC : C_VEC + 5, 0:wide]),
        (6, all_rows, lambda: g_vec[5:10, 0:wide], lambda: sum_c[C_VEC + 8 : C_VEC + 13, 0:wide]),
    )
    for n, (k, r, gradient, total) in enumerate(work):
        if n == 0 or work[n - 1][0] != k:
            for j in range(4):
                loads[7 * j + k].wait()
        weight, one, two, outer = (held[7 * j + k] for j in range(4))
        update, mean, square, velocity = (new[7 * j + k] for j in range(4))
        grad = gradient() * scaled
        mean[r, :] = beta_one * one[r, :] + (1.0 - beta_one) * grad
        square[r, :] = beta_two * two[r, :] + (1.0 - beta_two) * grad * grad
        average = total() * (1.0 / groups)
        moving = outer_momentum * outer[r, :] + average
        velocity[r, :] = moving
        update[r, :] = weight[r, :] - outer_rate * (average + outer_momentum * moving)
        if n + 1 == len(work) or work[n + 1][0] != k:
            for j in range(4):
                saves[7 * j + k].start()
    for c in saves:
        c.wait()


def finish(G, info, grads, shapes, states, out_shapes):
    dma = pltpu.SemaphoreType.DMA
    vm = pl.BlockSpec(memory_space=VMEM)
    hbm = pl.BlockSpec(memory_space=pl.ANY)
    return pl.pallas_call(
        functools.partial(finish_kernel, G),
        out_shape=tuple(jax.ShapeDtypeStruct(shape, F32) for shape in ((1, 2), (1, 1), *out_shapes)),
        in_specs=[vm] + [hbm] * 37,
        out_specs=(vm,) * 2 + (hbm,) * 28,
        scratch_shapes=[VMEM(a.shape, F32) for a in grads]
        + [VMEM(shape, F32) for shape in shapes] * 8
        + [dma((28,)), dma((9,)), dma((28,))],
        compiler_params=pltpu.CompilerParams(vmem_limit_bytes=62 << 20),
    )(info, *grads, *states)


def thin(a):
    return jnp.swapaxes(a, 0, 1)


def per_device(
    G, DP, MP,
    patches, labels, partner, class_weight,
    embedding, mixing, expand, shrink, classifier, scales, shifts, *state,
):
    weights = (embedding, thin(mixing), thin(expand), shrink[0], classifier, scales, shifts)

    def moments(a):
        return (a[0][0], thin(a[1][0]), thin(a[2][0]), a[3][0, 0], thin(a[4]), thin(a[5]), thin(a[6]))

    firsts, seconds = moments(state[0:7]), moments(state[7:14])
    o = state[14:21]
    outers = (o[0], thin(o[1]), thin(o[2]), o[3][0], o[4], o[5], o[6])
    shapes = tuple((a.shape[0], a.shape[-1]) for a in weights)
    *grads, info = local_step(
        G, DP, MP, shapes, labels[0], partner[0], scales, shifts, class_weight.reshape(1, -1),
        jnp.swapaxes(patches[0], 1, 2), (*weights, *firsts, *seconds),
    )
    out_shapes = tuple(a.shape for a in (*weights, *firsts, *seconds, *outers))
    losses, norm, *done = finish(G, info, grads, shapes, (*weights, *firsts, *seconds, *outers), out_shapes)
    updates, means, squares, velocities = (list(done[7 * k : 7 * k + 7]) for k in range(4))

    def whole(a):
        return (a[0], thin(a[1]), thin(a[2]), a[3][None], a[4], a[5], a[6])

    def by_group(a):
        return (a[0][None], thin(a[1])[None], thin(a[2])[None], a[3][None, None], thin(a[4]), thin(a[5]), thin(a[6]))

    return (
        losses, norm[0],
        *whole(updates), *by_group(means), *by_group(squares), *whole(velocities),
    )


WEIGHT_SPECS = (
    P("mp", None),
    P(),
    P(None, None, "mp"),
    P(None, "mp", None),
    P(None, "mp"),
    P(None, "mp"),
    P(None, "mp"),
)
STATE_SPECS = (
    P("group", "mp", None),
    P("group", None, None, None),
    P("group", None, None, "mp"),
    P("group", None, "mp", None),
    P("group", None, "mp"),
    P("group", None, "mp"),
    P("group", None, "mp"),
)


def solution(mesh):
    G, DP, MP = mesh.shape["group"], mesh.shape["dp"], mesh.shape["mp"]
    return jax.shard_map(
        functools.partial(per_device, G, DP, MP),
        mesh=mesh,
        in_specs=(
            P("group", "dp", None, "mp"),
            P("group", "dp"),
            P("group", "dp"),
            P(),
            *WEIGHT_SPECS,
            *STATE_SPECS,
            *STATE_SPECS,
            *WEIGHT_SPECS,
        ),
        out_specs=(
            P("group", None),
            P("group"),
            *WEIGHT_SPECS,
            *STATE_SPECS,
            *STATE_SPECS,
            *WEIGHT_SPECS,
        ),
        check_vma=False,
    )
```

```python
import functools

import jax
import jax.numpy as jnp
from jax import lax
from jax.experimental import pallas as pl
from jax.experimental.pallas import tpu as pltpu
from jax.sharding import PartitionSpec as P

F32 = jnp.float32
BF16 = jnp.bfloat16
MESH = pl.DeviceIdType.MESH
VMEM = pltpu.VMEM
SMEM = pltpu.SMEM

D = 384
PATCHES = 196
ROWS = 208
MAIN = 192
STEP = 10
LANE = 128

mix_share = 0.7
clip_limit = 0.01
beta_one = 0.9
beta_two = 0.999
adam_eps = 1e-08
weight_decay = 0.05
matrix_rate = 0.05
head_rate = 0.5
vector_rate = 0.4
outer_rate = 0.7
outer_momentum = 0.9

GELU_A = 0.7978845608028654
GELU_B = GELU_A * 0.044715

MIX, MIX16 = 56, 64
C_CLS, C_MIX, C_VEC, C_ROWS = 0, 392, 592, 608
E_EXP, E_EMB, E_ROWS = 0, 392, 640


def dot(a, b, dims=((1,), (0,)), precision=None):
    return lax.dot_general(
        a, b, (dims, ((), ())), preferred_element_type=F32, precision=precision
    )


def thirds(a, axis):
    high = a.astype(BF16)
    rest = a - high.astype(F32)
    middle = rest.astype(BF16)
    low = (rest - middle.astype(F32)).astype(BF16)
    return jnp.concatenate([high, middle, low], axis=axis)


def rounded(a):
    return a.astype(BF16).astype(F32)


def greet(peers):
    barrier = pltpu.get_barrier_semaphore()
    for peer in peers:
        pl.semaphore_signal(barrier, inc=1, device_id=peer, device_id_type=MESH)
    pl.semaphore_wait(barrier, len(peers))


def remote(src, dst, send_sem, recv_sem, peer):
    return pltpu.make_async_remote_copy(
        src_ref=src, dst_ref=dst, send_sem=send_sem, recv_sem=recv_sem,
        device_id=peer, device_id_type=MESH,
    )


CHUNK = 256
SLOTS = 3


def waves_of(pairs):
    return [(lo, min(lo + 2, pairs)) for lo in range(0, pairs, 2)]


def part_rows(rows, DP):
    return -(-rows // (16 * DP)) * 16


def adamw(weight, gradient, moment_one, moment_two, rate):
    mean_new = beta_one * moment_one + (1.0 - beta_one) * gradient
    square_new = beta_two * moment_two + (1.0 - beta_two) * gradient * gradient
    mean_hat = mean_new * (1.0 / (1.0 - beta_one**STEP))
    square_hat = square_new * (1.0 / (1.0 - beta_two**STEP))
    return rate * (mean_hat / (jnp.sqrt(square_hat) + adam_eps) + weight_decay * weight)


def flat(ref):
    return ref.at[:, 0, :] if len(ref.shape) == 3 and ref.shape[1] == 1 else ref


def step_kernel(G, DP, MP, NI, ncls, *refs):
    (labels, partner, sca, shi, class_weight, patches), refs = refs[:6], refs[6:]
    states, refs = refs[:21], refs[21:]
    (*results, info), refs = refs[:10], refs[10:]
    (g_w, g_e, g_mix, g_shr, g_cls, g_vec, sum_s, sum_c, sum_e), refs = refs[:9], refs[9:]
    held, refs = list(refs[:17]), refs[17:]
    (
        pv, stage, rows, e_all, w1, w2, wc, small,
        xs, gp, s0, s1, mx, mi, fi, ep, mm, mt, eye, mbias, vec, b1, cb, cw, asum, s1sum, la, lb,
        dact, ds2, dh, fit, csum, gw, ge, gm, gmb, gvec,
        gmix, sm, fac, zsm, zvec, ysm, yvec, yacts, yfac, agw, age,
        ysw, yrw, zsw, zrw, yse, yre, zse, zre, nsq,
        h2s, h2c, h2e,
        load, rs_send, rs_recv, wz_send, wz_recv, wp_send, wp_recv, wc_send, wc_recv, sm_send, sm_recv,
        zf_s, zf_r, yf_s, yf_r, yw_s, yw_r, zw_s, zw_r, ye_s, ye_r, ze_s, ze_r, ag_s, ag_r,
        nm_s, nm_r, nq_s, nq_r, g_s, g_r, out_sem,
    ) = refs
    late = {7: mx.at[0, 0 : held[0].shape[0], :], 14: mx.at[1, 0 : held[0].shape[0], :]}
    late |= {10: s1.at[0, 0:D, :], 17: s1.at[1, 0:D, :]}
    for k in sorted(late):
        held.insert(k, late[k])
    emb, mixing, expa, shr, cls = held[:5]
    z = lax.axis_index("mp")
    y = lax.axis_index("dp")
    g = lax.axis_index("group")
    NP = NI // 2
    PR = 2 * ROWS
    hid = expa.shape[1]
    hid_all = hid * MP
    cpad = wc.shape[1] // MP
    er = emb.shape[0]
    NCH = hid_all // CHUNK
    PW, PE = g_w.shape[0] // DP, g_e.shape[0] // DP

    stores = []

    def store(k, value):
        c = pltpu.make_async_copy(value, results[k], out_sem.at[k])
        c.start()
        stores.append(c)

    loads = [pltpu.make_async_copy(flat(a), b, load.at[k]) for k, (a, b) in enumerate(zip(states, held, strict=True))]
    load_patches = pltpu.make_async_copy(patches, pv, load.at[21])
    loads[0].start()
    loads[2].start()
    load_patches.start()

    zpeer = [lax.rem(z + d, MP) for d in range(1, MP)]
    ypeer = [lax.rem(y + d, DP) for d in range(1, DP)]
    others = [{"mp": lax.rem(z + c, MP), "dp": lax.rem(y + d, DP)} for d in range(DP) for c in range(MP) if c or d]
    core, beside = lax.rem(g, 2), y + 1 - 2 * lax.rem(y, 2)
    near, far = {"group": g + 1 - 2 * core}, {"group": lax.rem(g + 2, G)}
    plane = [far, {"dp": beside}, {**far, "dp": beside}]
    greet(others + [near, far, plane[2]])

    def pieces(t, k, x, h, n=1):
        if k == 0:
            size = er // 4 * (1 if n == 1 else 2)
            at = core * (er // 2) + x * (er // 4)
            return e_all.at[t, pl.ds(pl.multiple_of(at, 16), size), :]
        size = D // 8 * n
        at = core * (D // 2) + (x * 2 + h) * (D // 8)
        if k == 2:
            return w2.at[pl.ds(pl.multiple_of(t * hid + at, 16), size), :]
        ref, width = (w1, hid) if k == 1 else (wc, cpad)
        return ref.at[pl.ds(pl.multiple_of(at, 16), size), pl.ds(pl.multiple_of(t * width, LANE), width)]

    here = (g // 2, lax.rem(y, 2))

    started = []

    def go(*args):
        c = remote(*args)
        c.start()
        started.append(c)

    def spread(k):
        part = pieces(z, k, *here)
        for d, t in enumerate(zpeer):
            go(part, part, wz_send.at[d, k], wz_recv.at[z, k], {"mp": t})

    def pass_on(k):
        for d, t in enumerate(zpeer):
            part = pieces(t, k, *here)
            remote(part, part, wz_send.at[d, k], wz_recv.at[t, k], {"mp": t}).wait_recv()
            for e, peer in enumerate(plane[: 1 if k == 0 else 3]):
                go(part, part, wp_send.at[d, e, k], wp_recv.at[t, e, k], peer)

    def share_out(k):
        there = ((1 - here[0], here[1]), (here[0], 1 - here[1]), (1 - here[0], 1 - here[1]))
        for d, t in enumerate(zpeer):
            for e, peer in enumerate(plane[: 1 if k == 0 else 3]):
                part = pieces(t, k, *there[e])
                remote(part, part, wp_send.at[d, e, k], wp_recv.at[t, e, k], peer).wait_recv()
            part = pieces(t, k, 0, 0, 4)
            go(part, part, wc_send.at[d, k], wc_recv.at[t, k], near)

    def gathered(k):
        for t in zpeer:
            if k == 0:
                part = e_all.at[t, pl.ds(pl.multiple_of((1 - core) * (er // 2), 16), er // 2), :]
            elif k == 2:
                part = w2.at[pl.ds(pl.multiple_of(t * hid + (1 - core) * (D // 2), 16), D // 2), :]
            else:
                ref, width = (w1, hid) if k == 1 else (wc, cpad)
                part = ref.at[
                    pl.ds(pl.multiple_of((1 - core) * (D // 2), 16), D // 2), pl.ds(pl.multiple_of(t * width, LANE), width)
                ]
            remote(part, part, wc_send.at[0, k], wc_recv.at[t, k], near).wait_recv()

    loads[0].wait()
    e_all[z] = emb[...].astype(BF16)
    spread(0)
    loads[2].wait()
    w1[:, pl.ds(pl.multiple_of(z * hid, LANE), hid)] = expa[0:D, :].astype(BF16)
    spread(1)

    row = lax.broadcasted_iota(jnp.int32, (ROWS, PATCHES), 0)
    column = lax.broadcasted_iota(jnp.int32, (ROWS, PATCHES), 1)
    eye[...] = jnp.where(row == column, 1.0, 0.0).astype(BF16)
    share = F32(mix_share)
    rest = F32(1.0 - mix_share)

    def blend(i):
        return (share * pv[i] + rest * pv[partner[i]]).astype(BF16)

    def blend_pair(t, p, ref, lead):
        a = blend(t * NI + 2 * p)
        b = blend(t * NI + 2 * p + 1)
        both = jnp.concatenate([a[0:LANE], b[0:LANE], a[LANE:], b[LANE:]], axis=0)
        turned = dot(eye[...], both, ((1,), (1,)))
        tail = None
        for k in range(3):
            lanes = turned[:, k * LANE : (k + 1) * LANE]
            ref[lead + (slice(k * MAIN, (k + 1) * MAIN), slice(None))] = lanes[0:MAIN].astype(BF16)
            last = lanes[MAIN:ROWS]
            tail = last if k == 0 else tail + pltpu.roll(last, k * (PATCHES - MAIN), 0)
        ref[lead + (slice(3 * MAIN, 3 * MAIN + 16), slice(None))] = tail.astype(BF16)

    def slab(t, p, k):
        tail = rows[t, p, 3 * MAIN :, :].astype(F32)
        if k:
            tail = pltpu.roll(tail, 16 - k * (PATCHES - MAIN), 0)
        row = lax.broadcasted_iota(jnp.int32, (16, LANE), 0)
        tail = jnp.where(row < PATCHES - MAIN, tail, 0.0).astype(BF16)
        return rows[t, p, k * MAIN : (k + 1) * MAIN, :], tail

    def send(p, d):
        slot = lax.rem(p, SLOTS)
        return remote(stage.at[d, slot], rows.at[z, p], rs_send.at[d, slot], rs_recv.at[z, p], {"mp": zpeer[d]})

    def prepare(p):
        for d in range(MP - 1):
            blend_pair(zpeer[d], p, stage, (d, lax.rem(p, SLOTS)))

    def start(p):
        for d in range(MP - 1):
            send(p, d).start()

    for k in (3, 4, 1):
        loads[k].start()
    small[z] = jnp.zeros(small.shape[1:], F32)
    small[z, 0:5, 0 : D // MP] = sca[...]
    small[z, 5:10, 0 : D // MP] = shi[...]
    for k in range(hid // LANE):
        small[z, 10 + k : 11 + k, :] = rounded(expa[D : D + 1, k * LANE : (k + 1) * LANE])
    loads[3].wait()
    w2[pl.ds(pl.multiple_of(z * hid, 16), hid), :] = shr[...].astype(BF16)
    spread(2)
    loads[4].wait()
    head = jnp.concatenate([cls[0:D, :], jnp.zeros((D, cpad - ncls), F32)], axis=1)
    wc[:, pl.ds(pl.multiple_of(z * cpad, LANE), cpad)] = head.astype(BF16)
    spread(3)
    for k in range(cpad // LANE):
        n = min(LANE, ncls - k * LANE)
        small[z, 13 + k : 14 + k, 0:n] = rounded(cls[D : D + 1, k * LANE : k * LANE + n])
    for d, t in enumerate(zpeer):
        go(small.at[z], small.at[z], sm_send.at[d], sm_recv.at[z], {"mp": t})
    load_patches.wait()
    prepare(0)
    start(0)
    pass_on(0)
    pass_on(1)
    if NP > 1:
        prepare(1)
        start(1)
    pass_on(2)
    pass_on(3)
    for k in range(5, 21):
        if k not in late:
            loads[k].start()

    loads[1].wait()
    wide = jnp.concatenate([mixing[...], jnp.zeros((PATCHES, 256 - PATCHES - 1), F32)], axis=1)
    wide = jnp.concatenate([wide, jnp.zeros((256 - PATCHES, 256), F32)], axis=0)
    column = lax.broadcasted_iota(jnp.int32, (256, 256), 1)
    square = jnp.where(column < PATCHES, wide, 0.0)
    mm[...] = square[0:ROWS, 0:ROWS].astype(BF16)
    mt[...] = jnp.transpose(square)[0:ROWS, 0:ROWS].astype(BF16)
    mbias[...] = rounded(jnp.sum(jnp.where(column == PATCHES, wide, 0.0), axis=1, keepdims=True)[0:ROWS])
    for t in range(MP):
        block = class_weight[:, t * ncls : (t + 1) * ncls]
        cw[:, t * cpad : (t + 1) * cpad] = jnp.concatenate([block, jnp.zeros((1, cpad - ncls), F32)], axis=1)
    asum[...] = jnp.zeros_like(asum)
    s1sum[...] = jnp.zeros_like(s1sum)
    csum[...] = jnp.zeros_like(csum)
    fit[D:, :] = jnp.ones((16, PR), BF16)
    gw[...] = jnp.zeros_like(gw)
    ge[...] = jnp.zeros_like(ge)
    gm[...] = jnp.zeros_like(gm)
    gmb[...] = jnp.zeros_like(gmb)
    gvec[...] = jnp.zeros_like(gvec)
    la[...] = jnp.full(la.shape, -1, jnp.int32)
    lb[...] = jnp.full(lb.shape, -1, jnp.int32)
    for i in range(NI):
        own = labels[z * NI + i]
        mate = labels[partner[z * NI + i]]
        la[i : i + 1, :] = jnp.full((1, LANE), own, jnp.int32)
        lb[i : i + 1, :] = jnp.full((1, LANE), mate, jnp.int32)

    share_out(0)
    share_out(1)

    for t in zpeer:
        remote(small.at[t], small.at[t], sm_send.at[0], sm_recv.at[t], {"mp": t}).wait_recv()
    full = jnp.zeros((16, D), F32)
    for t in range(MP):
        block = jnp.concatenate([small[t], jnp.zeros((16, D - LANE), F32)], axis=1)
        full = full + (pltpu.roll(block, t * (D // MP), 1) if t else block)
        for k in range(hid // LANE):
            b1[:, t * hid + k * LANE : t * hid + (k + 1) * LANE] = small[t, 10 + k : 11 + k, :]
        for k in range(cpad // LANE):
            cb[:, t * cpad + k * LANE : t * cpad + (k + 1) * LANE] = small[t, 13 + k : 14 + k, :]
    vec[...] = full
    gathered(0)
    rest_rows = er - LANE
    for t in range(MP):
        ep[t * LANE : (t + 1) * LANE, :] = e_all[t, 0:LANE, :]
        ep[MP * LANE + t * rest_rows : MP * LANE + (t + 1) * rest_rows, :] = e_all[t, LANE:er, :]
    gathered(1)
    share_out(2)
    share_out(3)

    def scale(k):
        return vec[k : k + 1, :]

    def shift(k):
        return vec[5 + k : 6 + k, :]

    def forward(base, p, carry):
        @pl.when(p + 2 < NP)
        def _():
            @pl.when(p + 2 >= SLOTS)
            def _():
                for d in range(MP - 1):
                    send(p + 2 - SLOTS, d).wait_send()

            prepare(p + 2)
            start(p + 2)

        q = p - base
        blend_pair(z, p, rows, (z, p))
        for t in zpeer:
            remote(stage.at[0, 0], rows.at[t, p], rs_send.at[0, 0], rs_recv.at[t, p], {"mp": t}).wait_recv()
        for t in range(MP):
            lanes = slice(t * LANE, (t + 1) * LANE)
            for k in range(2):
                xs[q, k * ROWS : k * ROWS + MAIN, lanes], xs[q, k * ROWS + MAIN : (k + 1) * ROWS, lanes] = slab(t, p, k)
        for t in range(0, MP, 2):
            lanes = slice(MP * LANE + t * 64, MP * LANE + t * 64 + LANE)
            left, right = slab(t, p, 2), slab(t + 1, p, 2)
            for k in range(2):
                half = slice(k * 64, (k + 1) * 64)
                main, tail = (jnp.concatenate([v[:, half], w[:, half]], axis=1) for v, w in zip(left, right, strict=True))
                xs[q, k * ROWS : k * ROWS + MAIN, lanes] = main
                xs[q, k * ROWS + MAIN : (k + 1) * ROWS, lanes] = tail
        stream0 = dot(xs[q], ep[...]) + shift(3)
        s0[q] = stream0
        mi[q] = (scale(0) * stream0 + shift(0)).astype(BF16)
        for b in range(2):
            r = slice(b * ROWS, (b + 1) * ROWS)
            mixed = dot(mm[...], mi[q, r, :]) + mbias[...]
            mx[q, r, :] = mixed
            stream1 = s0[q, r, :] + scale(1) * mixed
            s1[q, r, :] = stream1
            fi[q, r, :] = (scale(2) * stream1 + shift(1)).astype(BF16)
            s1sum[pl.ds(2 * p + b, 1), :] = jnp.sum(stream1[0:PATCHES], axis=0, keepdims=True)

        def chunk(c, carry):
            cols = pl.ds(pl.multiple_of(c * CHUNK, CHUNK), CHUNK)
            for b in range(2):
                r = slice(b * ROWS, (b + 1) * ROWS)
                h = dot(fi[q, r, :], w1[:, cols]) + b1[:, cols]
                sq = h * h
                s = 0.5 * jnp.tanh(h * (GELU_A + GELU_B * sq)) + 0.5
                act = rounded(h * s)
                asum[pl.ds(2 * p + b, 1), cols] = jnp.sum(act[0:PATCHES], axis=0, keepdims=True)
                gp[q, r, cols] = s + s * (1.0 - s) * (h * (2.0 * GELU_A + 6.0 * GELU_B * sq))
                gp[q, b * ROWS + PATCHES : (b + 1) * ROWS, cols] = jnp.zeros((ROWS - PATCHES, CHUNK), F32)
            return carry

        lax.fori_loop(0, NCH, chunk, 0)

        return carry

    def class_head():
        three = dot(thirds(asum[...], 0), w2[...])
        outsum = three[0:16] + three[16:32] + three[32:48] + PATCHES * shift(2)
        stream2 = s1sum[...] + scale(3) * outsum
        pooled = (scale(4) * (stream2 * (1.0 / PATCHES)) + shift(4)).astype(BF16)
        lane = lax.broadcasted_iota(jnp.int32, (16, cpad * MP), 1)
        inside = lax.rem(lane, cpad)
        valid = inside < ncls
        class_id = (lane // cpad) * ncls + inside
        logits = jnp.where(valid, dot(pooled, wc[...]) + cb[...], -1e30)
        hot_a = jnp.where(valid & (class_id == la[:, 0:1]), 1.0, 0.0)
        hot_b = jnp.where(valid & (class_id == lb[:, 0:1]), 1.0, 0.0)
        weight_a = mix_share * jnp.sum(hot_a * cw[...], axis=1, keepdims=True)
        weight_b = (1.0 - mix_share) * jnp.sum(hot_b * cw[...], axis=1, keepdims=True)
        top = jnp.max(logits, axis=1, keepdims=True)
        exps = jnp.where(valid, jnp.exp(logits - top), 0.0)
        exp_sum = jnp.sum(exps, axis=1, keepdims=True)
        soft = exps / exp_sum
        dlog = ((weight_a + weight_b) * soft - weight_a * hot_a - weight_b * hot_b).astype(BF16)
        dfinal = dot(dlog, wc[...], ((1,), (1,))) * (1.0 / PATCHES)
        dstream2 = scale(4) * dfinal
        ds2[...] = dstream2
        dout = scale(3) * dstream2
        low = dout.astype(BF16)
        dact[...] = dot(low, w2[...], ((1,), (1,)))

        def last():
            log_total = top + jnp.log(exp_sum)
            target_a = jnp.sum(hot_a * logits, axis=1, keepdims=True)
            target_b = jnp.sum(hot_b * logits, axis=1, keepdims=True)
            loss = weight_a * (log_total - target_a) + weight_b * (log_total - target_b)
            loss = jnp.sum(loss, axis=0, keepdims=True)
            total = jnp.sum(weight_a + weight_b, axis=0, keepdims=True)
            fac[:, 0:16, :] = jnp.broadcast_to(low[None], (MP, 16, D))
            fac[:, 16:32, :] = jnp.broadcast_to(pooled[None], (MP, 16, D))
            for t in range(MP):
                fac[t, 32:48, 0:cpad] = dlog[:, t * cpad : (t + 1) * cpad]
                fac[t, 32:48, cpad:] = jnp.zeros((16, D - cpad), BF16)
            gvec[3:4, :] = jnp.sum(outsum * dstream2, axis=0, keepdims=True)
            gvec[4:5, :] = jnp.sum(dfinal * stream2, axis=0, keepdims=True)
            gvec[7:8, :] = PATCHES * jnp.sum(dout, axis=0, keepdims=True)
            gvec[8:9, :] = PATCHES * jnp.sum(dstream2, axis=0, keepdims=True)
            gvec[9:10, :] = PATCHES * jnp.sum(dfinal, axis=0, keepdims=True)
            lane = lax.broadcasted_iota(jnp.int32, (1, D), 1)
            gvec[10:11, :] = jnp.where(lane == 0, loss, jnp.where(lane == 1, total, 0.0))

        return last

    def turn_input(q):
        fit[0:D, :] = jnp.transpose(fi[q])

    def hidden_gradient(q, p, cols):
        for b in range(2):
            r = slice(b * ROWS, (b + 1) * ROWS)
            dh[r, cols] = (gp[q, r, cols] * dact[pl.ds(2 * p + b, 1), cols]).astype(BF16)

    def backward_columns(q, p, cols):
        hidden_gradient(q, p, cols)
        grad = dot(fit[...], dh[:, cols])
        gw[0:D, cols] += grad[0:D]
        csum[0:1, cols] += grad[D : D + 1]

    def backward_hidden(base, p):
        q = p - base
        turn_input(q)

        def chunk(c, carry):
            backward_columns(q, p, pl.ds(pl.multiple_of(c * CHUNK, CHUNK), CHUNK))
            return carry

        lax.fori_loop(0, NCH, chunk, 0)

    def backward_rest(base, p):
        q = p - base
        dffn = dot(dh[...], w1[...], ((1,), (1,)))
        gvec[2:3, :] += jnp.sum(dffn * s1[q], axis=0, keepdims=True)
        gvec[6:7, :] += jnp.sum(dffn, axis=0, keepdims=True)
        for b in range(2):
            r = slice(b * ROWS, (b + 1) * ROWS)
            d1 = ds2[pl.ds(2 * p + b, 1), :] + scale(2) * dffn[r]
            gvec[1:2, :] += jnp.sum(mx[q, r, :] * d1, axis=0, keepdims=True)
            dmixed = (scale(1) * d1).astype(BF16)
            gm[...] += dot(dmixed, mi[q, r, :], ((1,), (1,)))
            gmb[...] += dmixed.astype(F32)
            dmixer = dot(mt[...], dmixed)
            gvec[0:1, :] += jnp.sum(dmixer * s0[q, r, :], axis=0, keepdims=True)
            gvec[5:6, :] += jnp.sum(dmixer, axis=0, keepdims=True)
            d0 = (d1 + scale(0) * dmixer).astype(BF16)
            grad = dot(xs[q, r, :], d0, ((0,), (0,)))
            for t in range(MP):
                ge[t, 0:LANE, :] += grad[t * LANE : (t + 1) * LANE]
                ge[t, LANE:er, :] += grad[MP * LANE + t * rest_rows : MP * LANE + (t + 1) * rest_rows]

    def backward(base, p, carry):
        backward_hidden(base, p)
        backward_rest(base, p)
        return carry

    for n, (lo, hi) in enumerate(waves_of(NP)):
        lax.fori_loop(lo, hi, functools.partial(forward, lo), 0)
        if n == 0:
            gathered(2)
            gathered(3)
        last = class_head()
        if hi < NP:
            lax.fori_loop(lo, hi, functools.partial(backward, lo), 0)

    def arrived(dst, sem, peer):
        remote(dst, dst, sem, sem, peer).wait_recv()

    def columns(t):
        return pl.ds(pl.multiple_of(t * hid, LANE), hid)

    def part(u, n):
        return pl.ds(pl.multiple_of(u * n, 8), n)

    last()
    yacts[y, z] = asum[:, columns(z)]
    yfac[y, z] = fac[z]
    for d, v in enumerate(zpeer):
        go(asum.at[:, columns(v)], yacts.at[y, z], zf_s.at[d, 2], zf_r.at[z, 2], {"mp": v})
        go(fac.at[v], yfac.at[y, z], zf_s.at[d, 3], zf_r.at[z, 3], {"mp": v})
    order = zpeer + [z]
    for p in range(lo, hi - 1):
        backward_hidden(lo, p)
    turn_input(hi - 1 - lo)
    for i, t in enumerate(order):
        backward_columns(hi - 1 - lo, hi - 1, columns(t))
        for d, u in enumerate(ypeer):
            ysw[i, d] = gw[part(u, PW), columns(t)].astype(BF16)
            go(ysw.at[i, d], yrw.at[t, d], yw_s.at[i, d], yw_r.at[t, d], {"dp": u})
    backward_rest(lo, hi - 1)
    for p in range(lo, hi - 1):
        for t in range(MP):
            hidden_gradient(p - lo, p, columns(t))
        backward_rest(lo, p)
    for i, t in enumerate(order):
        for d, u in enumerate(ypeer):
            yse[i, d] = ge[t, part(u, PE), :].astype(BF16)
            go(yse.at[i, d], yre.at[t, d], ye_s.at[i, d], ye_r.at[t, d], {"dp": u})

    for k in late:
        loads[k].start()

    gvec[8:9, :] += scale(2) * gvec[6:7, :] + scale(0) * gvec[5:6, :]
    row = lax.broadcasted_iota(jnp.int32, (ROWS, 256), 0)
    column = lax.broadcasted_iota(jnp.int32, (ROWS, 256), 1)
    bias_grad = jnp.sum(gmb[...], axis=1, keepdims=True)
    grad = jnp.concatenate([gm[...], jnp.zeros((ROWS, 256 - ROWS), F32)], axis=1)
    grad = jnp.where(column < PATCHES, grad, jnp.where(column == PATCHES, bias_grad, 0.0))
    grad = jnp.where(row < PATCHES, grad, 0.0)
    own = D // MP
    lane = lax.broadcasted_iota(jnp.int32, (16, LANE), 1)
    for t in range(MP):
        n = min(MIX, ROWS - t * MIX)
        gmix[t, 0:n, :] = grad[t * MIX : t * MIX + n]
        gmix[t, n:, :] = jnp.zeros((MIX16 - n, 256), F32)
        sm[t] = gmix[t].astype(BF16)
        vector = gvec[...]
        if t:
            vector = pltpu.roll(vector, D - t * own, 1)
        zvec[z, t] = jnp.where(lane < own, vector[:, 0:LANE], 0.0)
        zvec[z, t, 10:11, :] = gvec[10:11, 0:LANE]
        for k in range(hid // LANE):
            at = t * hid + k * LANE
            zvec[z, t, 11 + k : 12 + k, :] = csum[:, at : at + LANE]
    for d, v in enumerate(zpeer):
        go(sm.at[v], zsm.at[z], zf_s.at[d, 0], zf_r.at[z, 0], {"mp": v})
        go(zvec.at[z, v], zvec.at[z, v], zf_s.at[d, 1], zf_r.at[z, 1], {"mp": v})

    for v in zpeer:
        arrived(yacts.at[y, v], zf_r.at[v, 2], {"mp": v})
        arrived(yfac.at[y, v], zf_r.at[v, 3], {"mp": v})
    for d, u in enumerate(ypeer):
        go(yacts.at[y], yacts.at[y], yf_s.at[d, 2], yf_r.at[y, 2], {"dp": u})
        go(yfac.at[y], yfac.at[y], yf_s.at[d, 3], yf_r.at[y, 3], {"dp": u})

    def from_dp(first, received, sems, send, out, out_sems, z_sems, n):
        for i, t in enumerate(order):
            value = first(t)
            for d in range(DP - 1):
                arrived(received.at[t, d], sems.at[t, d], {"dp": ypeer[d]})
                value = value + received[t, d].astype(F32)
            if i < MP - 1:
                send[i] = value.astype(BF16)
                go(send.at[i], out.at[i], out_sems.at[i], z_sems.at[i], {"mp": t})
        return value

    own_w = from_dp(lambda t: gw[part(y, PW), columns(t)], yrw, yw_r, zsw, zrw, zw_s, zw_r, PW)

    mixed = gmix[z, 0:MIX, :]
    for v in zpeer:
        arrived(zsm.at[v], zf_r.at[v, 0], {"mp": v})
        arrived(zvec.at[v, z], zf_r.at[v, 1], {"mp": v})
        mixed = mixed + zsm[v, 0:MIX, :].astype(F32)
    vector = zvec[0, z]
    for v in range(1, MP):
        vector = vector + zvec[v, z]
    ysm[y] = mixed
    yvec[y] = vector
    for d, u in enumerate(ypeer):
        go(ysm.at[y], ysm.at[y], yf_s.at[d, 0], yf_r.at[y, 0], {"dp": u})
        go(yvec.at[y], yvec.at[y], yf_s.at[d, 1], yf_r.at[y, 1], {"dp": u})

    own_e = from_dp(lambda t: ge[t, part(y, PE), :], yre, ye_r, zse, zre, ze_s, ze_r, PE)

    def from_mp(own_sum, received, sems, gathered, k):
        value = own_sum
        for i in range(MP - 1):
            arrived(received.at[i], sems.at[i], {"mp": zpeer[i]})
            value = value + received[i].astype(F32)
        gathered[y] = value.astype(BF16)
        for d, u in enumerate(ypeer):
            go(gathered.at[y], gathered.at[y], ag_s.at[d, k], ag_r.at[y, k], {"dp": u})
        return rounded(value)

    def squares(v):
        return jnp.sum(jnp.sum(v * v, axis=0, keepdims=True), axis=1, keepdims=True)

    mine = squares(from_mp(own_w, zrw, zw_r, agw, 0))

    for u in ypeer:
        arrived(ysm.at[u], yf_r.at[u, 0], {"dp": u})
        arrived(yvec.at[u], yf_r.at[u, 1], {"dp": u})
    mixed, vector = ysm[0], yvec[0]
    for u in range(1, DP):
        mixed, vector = mixed + ysm[u], vector + yvec[u]
    g_mix[part(z, MIX), :] = mixed

    for u in ypeer:
        arrived(yacts.at[u], yf_r.at[u, 2], {"dp": u})
        arrived(yfac.at[u], yf_r.at[u, 3], {"dp": u})
    n = 16 * MP
    grad_shr = jnp.zeros((hid, D), F32)
    grad_cls = jnp.zeros((D, cpad), F32)
    cls_bias = jnp.zeros((1, cpad), F32)
    for u in range(DP):
        whole = yfac[u]
        dout = whole[:, 0:16, :].reshape(n, D)
        pooled = whole[:, 16:32, :].reshape(n, D)
        dlog = whole[:, 32:48, 0:cpad].reshape(n, cpad)
        three = thirds(yacts[u].reshape(n, hid), 0)
        grad_shr = grad_shr + dot(three, jnp.concatenate([dout] * 3, axis=0), ((0,), (0,)))
        grad_cls = grad_cls + dot(pooled, dlog, ((0,), (0,)))
        cls_bias = cls_bias + jnp.sum(dlog.astype(F32), axis=0, keepdims=True)
    g_shr[...] = grad_shr
    g_cls[0:D, :] = grad_cls
    g_cls[D:, :] = jnp.concatenate([cls_bias, jnp.zeros((g_cls.shape[0] - D - 1, cpad), F32)], axis=0)
    once = squares(grad_shr) + squares(grad_cls) + squares(cls_bias) + squares(mixed)
    once = once + squares(vector[0:10]) + squares(vector[11 : 11 + hid // LANE])

    mine = mine + squares(from_mp(own_e, zre, ze_r, age, 1))
    nsq[y, z] = jnp.broadcast_to(mine + jnp.where(y == 0, once, 0.0), (8, LANE))
    for k, peer in enumerate(others):
        go(nsq.at[y, z], nsq.at[y, z], nq_s.at[k], nq_r.at[y, z], peer)
    for d, v in enumerate(zpeer):
        go(g_mix.at[part(z, MIX), :], g_mix.at[part(z, MIX), :], nm_s.at[d], nm_r.at[z], {"mp": v})
    store(3, g_shr)
    store(4, g_cls)
    g_vec[...] = vector
    store(5, g_vec)
    for k in range(4, 21):
        if k != 4:
            loads[k].wait()
    for peer in others:
        arrived(nsq.at[peer["dp"], peer["mp"]], nq_r.at[peer["dp"], peer["mp"]], peer)
    square = jnp.zeros((1, 1), F32)
    for u in range(DP):
        for v in range(MP):
            square = square + nsq[u, v, 0:1, 0:1]
    loss_sum = vector[10:11, 0:1]
    weight_total = vector[10:11, 1:2]
    size = jnp.sqrt(square) / weight_total
    factor = clip_limit / jnp.maximum(size, clip_limit)
    scaled = factor / weight_total
    lane = lax.broadcasted_iota(jnp.int32, (8, LANE), 1)
    info[...] = jnp.where(
        lane == 0, loss_sum, jnp.where(lane == 1, weight_total, jnp.where(lane == 2, size, scaled))
    )

    (_, _, _, _, _, sca_w, shi_w) = held[:7]
    (emb1, mixing1, expa1, shr1, cls1, sca1, shi1) = held[7:14]
    (emb2, mixing2, expa2, shr2, cls2, sca2, shi2) = held[14:21]
    wide = sca_w.shape[1]
    def halves(ref, k):
        n = ref.shape[0] // 2
        return ref.at[pl.ds(pl.multiple_of(k * n, 8), n), :]

    mvs = gp.at[0:2, 0 : hid // 2, 0:D]
    mvc = gp.at[0:2, 0 : C_ROWS // 2, D : D + 256]
    mve = gp.at[0:2, 0 : E_ROWS // 2, D + 256 : 2 * D + 256]

    def put(moved, at, value):
        n = moved.shape[1]
        rows, width = value.shape
        k = min(max(n - at, 0), rows)
        if k:
            moved[0, at : at + k, 0:width] = value[0:k]
        if k < rows:
            moved[1, at + k - n : at + rows - n, 0:width] = value[k:]

    fine = C_VEC - C_ROWS // 2

    def first_step(k, moved, out):
        go(moved.at[1 - core], halves(out, 1 - core), g_s.at[k, 0], g_r.at[k, 0], near)

    side = lax.rem(y, 2)

    def some(ref, k, which):
        n = ref.shape[1] // 2
        return ref.at[k, pl.ds(pl.multiple_of(which * n, 16), n), :]

    def second_step(k, moved, out, pairs):
        arrived(halves(out, core), g_r.at[k, 0], near)
        n = moved.shape[1]
        value = moved[core] + out[part(core, n), :]
        pairs[0, 0:n] = value.astype(BF16)
        if pairs.shape[1] > n:
            value = value[fine : fine + 16]
            pairs[0, n:] = (value - rounded(value)).astype(BF16)
        go(some(pairs, 0, side), some(pairs, 1, side), g_s.at[k, 1], g_r.at[k, 1], far)

    def hand_on(k, pairs):
        arrived(some(pairs, 1, side), g_r.at[k, 1], far)
        go(some(pairs, 1, side), some(pairs, 1, side), g_s.at[k, 2], g_r.at[k, 2], {"dp": beside})

    def third_step(k, pairs, out):
        arrived(some(pairs, 1, 1 - side), g_r.at[k, 2], {"dp": beside})
        n = out.shape[0] // 2
        total = pairs[0].astype(F32) + pairs[1].astype(F32)
        out[part(core, n), :] = total[0:n]
        if pairs.shape[1] > n:
            out[pl.ds(pl.multiple_of(core * n + fine, 8), 16), :] = total[fine : fine + 16] + total[n:]
        go(halves(out, core), halves(out, core), g_s.at[k, 3], g_r.at[k, 3], near)

    put(mvs, 0, adamw(shr[...], g_shr[...] * scaled, shr1[...], shr2[...], matrix_rate))
    first_step(0, mvs, sum_s)
    for u in ypeer:
        arrived(agw.at[u], ag_r.at[u, 0], {"dp": u})
        arrived(age.at[u], ag_r.at[u, 1], {"dp": u})
    for u in range(DP):
        g_w[u * PW : (u + 1) * PW, :] = agw[u].astype(F32)
        g_e[u * PE : (u + 1) * PE, :] = age[u].astype(F32)
    store(0, g_w)
    store(1, g_e)
    bias = jnp.concatenate([g_vec[11 + k : 12 + k, :] for k in range(hid // LANE)], axis=1)
    last_row = slice(D, D + 1)
    mve[...] = jnp.zeros(mve.shape, F32)
    put(mve, E_EXP, adamw(expa[0:D, :], g_w[0:D, :] * scaled, expa1[0:D, :], expa2[0:D, :], matrix_rate))
    put(mve, E_EXP + D, adamw(expa[last_row, :], bias * scaled, expa1[last_row, :], expa2[last_row, :], matrix_rate))
    put(mve, E_EMB, adamw(emb[...], g_e[0:er, :] * scaled, emb1[...], emb2[...], matrix_rate))
    first_step(2, mve, sum_e)
    second_step(0, mvs, sum_s, h2s)
    for v in zpeer:
        arrived(g_mix.at[part(v, MIX), :], nm_r.at[v], {"mp": v})
    store(2, g_mix)
    mvc[...] = jnp.zeros(mvc.shape, F32)
    put(mvc, C_CLS, adamw(cls[...], g_cls[0 : D + 1, 0:ncls] * scaled, cls1[...], cls2[...], head_rate))
    put(
        mvc, C_MIX,
        adamw(mixing[...], g_mix[0:PATCHES, 0 : PATCHES + 1] * scaled, mixing1[...], mixing2[...], matrix_rate),
    )
    for k, (w, one, two) in enumerate(((sca_w, sca1, sca2), (shi_w, shi1, shi2))):
        value = adamw(w[...], g_vec[5 * k : 5 * k + 5, 0:wide] * scaled, one[...], two[...], vector_rate)
        put(mvc, C_VEC + 8 * k, value)
    first_step(1, mvc, sum_c)
    second_step(2, mve, sum_e, h2e)
    hand_on(0, h2s)
    second_step(1, mvc, sum_c, h2c)
    hand_on(2, h2e)
    third_step(0, h2s, sum_s)
    hand_on(1, h2c)
    third_step(2, h2e, sum_e)
    arrived(halves(sum_s, 1 - core), g_r.at[0, 3], near)
    store(6, sum_s)
    third_step(1, h2c, sum_c)
    arrived(halves(sum_e, 1 - core), g_r.at[2, 3], near)
    store(8, sum_e)
    arrived(halves(sum_c, 1 - core), g_r.at[1, 3], near)
    store(7, sum_c)

    def drain(p, carry):
        for d in range(MP - 1):
            send(p, d).wait_send()
        return carry

    lax.fori_loop(max(NP - SLOTS, 0), NP, drain, 0)
    for c in started:
        c.wait_send()
    for c in stores:
        c.wait()


def local_step(G, DP, MP, shapes, labels, partner, sca, shi, class_weight, patches, states):
    NI = patches.shape[0] // MP
    NP = NI // 2
    PR = 2 * ROWS
    er, hid, ncls = shapes[0][0], shapes[2][1], shapes[4][1]
    hid_all = hid * MP
    pd = er * MP
    cpad = -(-ncls // LANE) * LANE
    wave = max(hi - lo for lo, hi in waves_of(NP))
    dp1 = max(DP - 1, 1)
    PW, PE = part_rows(D, DP), part_rows(er, DP)
    dma = pltpu.SemaphoreType.DMA
    vm = pl.BlockSpec(memory_space=VMEM)
    smem = pl.BlockSpec(memory_space=SMEM)
    hbm = pl.BlockSpec(memory_space=pl.ANY)
    s = jax.ShapeDtypeStruct
    results = (
        (DP * PW, D), (DP * PE, D), (MP * MIX, 256), (hid, D), (392, cpad), (16, LANE),
        (hid, D), (C_ROWS, 256), (E_ROWS, D),
    )
    return pl.pallas_call(
        functools.partial(step_kernel, G, DP, MP, NI, ncls),
        out_shape=(*(s(shape, F32) for shape in results), s((8, LANE), F32)),
        in_specs=[smem, smem, vm, vm, vm] + [hbm] * 22,
        out_specs=(hbm,) * 9 + (vm,),
        scratch_shapes=[VMEM(shape, F32) for shape in results]
        + [VMEM(shape, F32) for shape in shapes + 2 * (shapes[1:3] + shapes[4:])]
        + [
            VMEM(patches.shape, F32),
            VMEM((MP - 1, SLOTS, 3 * MAIN + 16, LANE), BF16),
            VMEM((MP, NP, 3 * MAIN + 16, LANE), BF16),
            VMEM((MP, er, D), BF16),
            VMEM((D, hid_all), BF16),
            VMEM((hid_all, D), BF16),
            VMEM((D, cpad * MP), BF16),
            VMEM((MP, 16, LANE), F32),
            VMEM((wave, PR, pd), BF16),
            VMEM((wave, PR, hid_all), F32),
            VMEM((wave, PR, D), F32),
            VMEM((wave, PR, D), F32),
            VMEM((wave, PR, D), F32),
            VMEM((wave, PR, D), BF16),
            VMEM((wave, PR, D), BF16),
            VMEM((pd, D), BF16),
            VMEM((ROWS, ROWS), BF16),
            VMEM((ROWS, ROWS), BF16),
            VMEM((ROWS, PATCHES), BF16),
            VMEM((ROWS, 1), F32),
            VMEM((16, D), F32),
            VMEM((1, hid_all), F32),
            VMEM((1, cpad * MP), F32),
            VMEM((1, cpad * MP), F32),
            VMEM((16, hid_all), F32),
            VMEM((16, D), F32),
            VMEM((16, LANE), jnp.int32),
            VMEM((16, LANE), jnp.int32),
            VMEM((16, hid_all), F32),
            VMEM((16, D), F32),
            VMEM((PR, hid_all), BF16),
            VMEM((D + 16, PR), BF16),
            VMEM((1, hid_all), F32),
            VMEM((DP * PW, hid_all), F32),
            VMEM((MP, DP * PE, D), F32),
            VMEM((ROWS, ROWS), F32),
            VMEM((ROWS, D), F32),
            VMEM((16, D), F32),
            VMEM((MP, MIX16, 256), F32),
            VMEM((MP, MIX16, 256), BF16),
            VMEM((MP, 48, D), BF16),
            VMEM((MP, MIX16, 256), BF16),
            VMEM((MP, MP, 16, LANE), F32),
            VMEM((DP, MIX, 256), F32),
            VMEM((DP, 16, LANE), F32),
            VMEM((DP, MP, 16, hid), F32),
            VMEM((DP, MP, 48, D), BF16),
            VMEM((DP, PW, hid), BF16),
            VMEM((DP, PE, D), BF16),
            VMEM((MP, dp1, PW, hid), BF16),
            VMEM((MP, dp1, PW, hid), BF16),
            VMEM((MP - 1, PW, hid), BF16),
            VMEM((MP - 1, PW, hid), BF16),
            VMEM((MP, dp1, PE, D), BF16),
            VMEM((MP, dp1, PE, D), BF16),
            VMEM((MP - 1, PE, D), BF16),
            VMEM((MP - 1, PE, D), BF16),
            VMEM((DP, MP, 8, LANE), F32),
            VMEM((2, hid // 2, D), BF16),
            VMEM((2, C_ROWS // 2 + 16, 256), BF16),
            VMEM((2, E_ROWS // 2, D), BF16),
            dma((22,)),
            dma((MP - 1, SLOTS)),
            dma((MP, NP)),
            dma((MP - 1, 4)),
            dma((MP, 4)),
            dma((MP - 1, 3, 4)),
            dma((MP, 3, 4)),
            dma((MP - 1, 4)),
            dma((MP, 4)),
            dma((MP - 1,)),
            dma((MP,)),
            dma((MP - 1, 4)),
            dma((MP, 4)),
            dma((dp1, 4)),
            dma((DP, 4)),
            dma((MP, dp1)),
            dma((MP, dp1)),
            dma((MP - 1,)),
            dma((MP - 1,)),
            dma((MP, dp1)),
            dma((MP, dp1)),
            dma((MP - 1,)),
            dma((MP - 1,)),
            dma((dp1, 2)),
            dma((DP, 2)),
            dma((MP - 1,)),
            dma((MP,)),
            dma((DP * MP - 1,)),
            dma((DP, MP)),
            dma((3, 4)),
            dma((3, 4)),
            dma((9,)),
        ],
        compiler_params=pltpu.CompilerParams(
            collective_id=0, has_side_effects=True, vmem_limit_bytes=63 << 20
        ),
    )(labels, partner, sca, shi, class_weight, patches, *states)


def finish_kernel(groups, *refs):
    (info, *grads_in), refs = refs[:10], refs[10:]
    states, refs = refs[:28], refs[28:]
    (losses, norm), refs = refs[:2], refs[2:]
    outs, refs = refs[:28], refs[28:]
    grads_held, refs = refs[:9], refs[9:]
    held, refs = refs[:28], refs[28:]
    new, (load, load_grad, save) = refs[:28], refs[28:]
    first = [pltpu.make_async_copy(a, b, load_grad.at[k]) for k, (a, b) in enumerate(zip(grads_in, grads_held, strict=True))]
    loads = [pltpu.make_async_copy(flat(a), b, load.at[k]) for k, (a, b) in enumerate(zip(states, held, strict=True))]
    saves = [pltpu.make_async_copy(a, flat(b), save.at[k]) for k, (a, b) in enumerate(zip(new, outs, strict=True))]
    for c in first:
        c.start()
    for k in (3, 2, 0, 4, 1, 5, 6):
        for j in range(4):
            loads[7 * j + k].start()
    losses[...] = info[0:1, 0:2]
    norm[...] = info[0:1, 2:3]
    scaled = info[0:1, 3:4]
    g_w, g_e, g_mix, g_shr, g_cls, g_vec, sum_s, sum_c, sum_e = grads_held
    for c in first:
        c.wait()
    wide = held[5].shape[1]
    ncls = held[4].shape[1]
    er = held[0].shape[0]
    all_rows = slice(None)

    bias = jnp.concatenate([g_vec[11 + k : 12 + k, :] for k in range(D // LANE)], axis=1)
    work = (
        (3, all_rows, lambda: g_shr[...], lambda: sum_s[...]),
        (2, slice(0, D), lambda: g_w[0:D, :], lambda: sum_e[E_EXP : E_EXP + D, :]),
        (2, slice(D, D + 1), lambda: bias, lambda: sum_e[E_EXP + D : E_EXP + D + 1, :]),
        (0, all_rows, lambda: g_e[0:er, :], lambda: sum_e[E_EMB : E_EMB + er, :]),
        (4, all_rows, lambda: g_cls[0 : D + 1, 0:ncls], lambda: sum_c[C_CLS : C_CLS + D + 1, 0:ncls]),
        (1, all_rows, lambda: g_mix[0:PATCHES, 0 : PATCHES + 1], lambda: sum_c[C_MIX : C_MIX + PATCHES, 0 : PATCHES + 1]),
        (5, all_rows, lambda: g_vec[0:5, 0:wide], lambda: sum_c[C_VEC : C_VEC + 5, 0:wide]),
        (6, all_rows, lambda: g_vec[5:10, 0:wide], lambda: sum_c[C_VEC + 8 : C_VEC + 13, 0:wide]),
    )
    for n, (k, r, gradient, total) in enumerate(work):
        if n == 0 or work[n - 1][0] != k:
            for j in range(4):
                loads[7 * j + k].wait()
        weight, one, two, outer = (held[7 * j + k] for j in range(4))
        update, mean, square, velocity = (new[7 * j + k] for j in range(4))
        grad = gradient() * scaled
        mean[r, :] = beta_one * one[r, :] + (1.0 - beta_one) * grad
        square[r, :] = beta_two * two[r, :] + (1.0 - beta_two) * grad * grad
        average = total() * (1.0 / groups)
        moving = outer_momentum * outer[r, :] + average
        velocity[r, :] = moving
        update[r, :] = weight[r, :] - outer_rate * (average + outer_momentum * moving)
        if n + 1 == len(work) or work[n + 1][0] != k:
            for j in range(4):
                saves[7 * j + k].start()
    for c in saves:
        c.wait()


def finish(G, info, grads, shapes, states, out_shapes):
    dma = pltpu.SemaphoreType.DMA
    vm = pl.BlockSpec(memory_space=VMEM)
    hbm = pl.BlockSpec(memory_space=pl.ANY)
    return pl.pallas_call(
        functools.partial(finish_kernel, G),
        out_shape=tuple(jax.ShapeDtypeStruct(shape, F32) for shape in ((1, 2), (1, 1), *out_shapes)),
        in_specs=[vm] + [hbm] * 37,
        out_specs=(vm,) * 2 + (hbm,) * 28,
        scratch_shapes=[VMEM(a.shape, F32) for a in grads]
        + [VMEM(shape, F32) for shape in shapes] * 8
        + [dma((28,)), dma((9,)), dma((28,))],
        compiler_params=pltpu.CompilerParams(vmem_limit_bytes=62 << 20),
    )(info, *grads, *states)


def thin(a):
    return jnp.swapaxes(a, 0, 1)


def per_device(
    G, DP, MP,
    patches, labels, partner, class_weight,
    embedding, mixing, expand, shrink, classifier, scales, shifts, *state,
):
    weights = (embedding, thin(mixing), thin(expand), shrink[0], classifier, scales, shifts)

    def moments(a):
        return (a[0][0], thin(a[1][0]), thin(a[2][0]), a[3][0, 0], thin(a[4]), thin(a[5]), thin(a[6]))

    firsts, seconds = moments(state[0:7]), moments(state[7:14])
    o = state[14:21]
    outers = (o[0], thin(o[1]), thin(o[2]), o[3][0], o[4], o[5], o[6])
    shapes = tuple((a.shape[0], a.shape[-1]) for a in weights)
    *grads, info = local_step(
        G, DP, MP, shapes, labels[0], partner[0], scales, shifts, class_weight.reshape(1, -1),
        jnp.swapaxes(patches[0], 1, 2), (*weights, *firsts, *seconds),
    )
    out_shapes = tuple(a.shape for a in (*weights, *firsts, *seconds, *outers))
    losses, norm, *done = finish(G, info, grads, shapes, (*weights, *firsts, *seconds, *outers), out_shapes)
    updates, means, squares, velocities = (list(done[7 * k : 7 * k + 7]) for k in range(4))

    def whole(a):
        return (a[0], thin(a[1]), thin(a[2]), a[3][None], a[4], a[5], a[6])

    def by_group(a):
        return (a[0][None], thin(a[1])[None], thin(a[2])[None], a[3][None, None], thin(a[4]), thin(a[5]), thin(a[6]))

    return (
        losses, norm[0],
        *whole(updates), *by_group(means), *by_group(squares), *whole(velocities),
    )


WEIGHT_SPECS = (
    P("mp", None),
    P(),
    P(None, None, "mp"),
    P(None, "mp", None),
    P(None, "mp"),
    P(None, "mp"),
    P(None, "mp"),
)
STATE_SPECS = (
    P("group", "mp", None),
    P("group", None, None, None),
    P("group", None, None, "mp"),
    P("group", None, "mp", None),
    P("group", None, "mp"),
    P("group", None, "mp"),
    P("group", None, "mp"),
)


def solution(mesh):
    G, DP, MP = mesh.shape["group"], mesh.shape["dp"], mesh.shape["mp"]
    return jax.shard_map(
        functools.partial(per_device, G, DP, MP),
        mesh=mesh,
        in_specs=(
            P("group", "dp", None, "mp"),
            P("group", "dp"),
            P("group", "dp"),
            P(),
            *WEIGHT_SPECS,
            *STATE_SPECS,
            *STATE_SPECS,
            *WEIGHT_SPECS,
        ),
        out_specs=(
            P("group", None),
            P("group"),
            *WEIGHT_SPECS,
            *STATE_SPECS,
            *STATE_SPECS,
            *WEIGHT_SPECS,
        ),
        check_vma=False,
    )
```

```python
import functools

import jax
import jax.numpy as jnp
from jax import lax
from jax.experimental import pallas as pl
from jax.experimental.pallas import tpu as pltpu
from jax.sharding import PartitionSpec as P

F32 = jnp.float32
BF16 = jnp.bfloat16
MESH = pl.DeviceIdType.MESH
VMEM = pltpu.VMEM
SMEM = pltpu.SMEM

D = 384
PATCHES = 196
ROWS = 208
MAIN = 192
STEP = 10
LANE = 128

mix_share = 0.7
clip_limit = 0.01
beta_one = 0.9
beta_two = 0.999
adam_eps = 1e-08
weight_decay = 0.05
matrix_rate = 0.05
head_rate = 0.5
vector_rate = 0.4
outer_rate = 0.7
outer_momentum = 0.9

GELU_A = 0.7978845608028654
GELU_B = GELU_A * 0.044715

MIX, MIX16 = 56, 64
C_CLS, C_MIX, C_VEC, C_ROWS = 0, 392, 592, 608
E_EXP, E_EMB, E_ROWS = 0, 392, 640


def dot(a, b, dims=((1,), (0,)), precision=None):
    return lax.dot_general(
        a, b, (dims, ((), ())), preferred_element_type=F32, precision=precision
    )


def thirds(a, axis):
    high = a.astype(BF16)
    rest = a - high.astype(F32)
    middle = rest.astype(BF16)
    low = (rest - middle.astype(F32)).astype(BF16)
    return jnp.concatenate([high, middle, low], axis=axis)


def rounded(a):
    return a.astype(BF16).astype(F32)


def greet(peers):
    barrier = pltpu.get_barrier_semaphore()
    for peer in peers:
        pl.semaphore_signal(barrier, inc=1, device_id=peer, device_id_type=MESH)
    pl.semaphore_wait(barrier, len(peers))


def remote(src, dst, send_sem, recv_sem, peer):
    return pltpu.make_async_remote_copy(
        src_ref=src, dst_ref=dst, send_sem=send_sem, recv_sem=recv_sem,
        device_id=peer, device_id_type=MESH,
    )


CHUNK = 256
SLOTS = 3


def waves_of(pairs):
    return [(lo, min(lo + 2, pairs)) for lo in range(0, pairs, 2)]


def part_rows(rows, DP):
    return -(-rows // (16 * DP)) * 16


def adamw(weight, gradient, moment_one, moment_two, rate):
    mean_new = beta_one * moment_one + (1.0 - beta_one) * gradient
    square_new = beta_two * moment_two + (1.0 - beta_two) * gradient * gradient
    mean_hat = mean_new * (1.0 / (1.0 - beta_one**STEP))
    square_hat = square_new * (1.0 / (1.0 - beta_two**STEP))
    return rate * (mean_hat / (jnp.sqrt(square_hat) + adam_eps) + weight_decay * weight)


def flat(ref):
    return ref.at[:, 0, :] if len(ref.shape) == 3 and ref.shape[1] == 1 else ref


def step_kernel(G, DP, MP, NI, ncls, *refs):
    (labels, partner, sca, shi, class_weight, patches), refs = refs[:6], refs[6:]
    states, refs = refs[:21], refs[21:]
    (*results, info), refs = refs[:10], refs[10:]
    (g_w, g_e, g_mix, g_shr, g_cls, g_vec, sum_s, sum_c, sum_e), refs = refs[:9], refs[9:]
    held, refs = list(refs[:17]), refs[17:]
    (
        pv, stage, rows, e_all, w1, w2, wc, small,
        xs, gp, s0, s1, mx, mi, fi, ep, mm, mt, eye, mbias, vec, b1, cb, cw, asum, s1sum, la, lb,
        dact, ds2, dh, fit, csum, gw, ge, gm, gmb, gvec,
        gmix, sm, fac, zsm, zvec, ysm, yvec, yacts, yfac, agw, age,
        ysw, yrw, zsw, zrw, yse, yre, zse, zre, nsq,
        h2s, h2c, h2e,
        load, rs_send, rs_recv, wz_send, wz_recv, wp_send, wp_recv, wc_send, wc_recv, sm_send, sm_recv,
        zf_s, zf_r, yf_s, yf_r, yw_s, yw_r, zw_s, zw_r, ye_s, ye_r, ze_s, ze_r, ag_s, ag_r,
        nm_s, nm_r, nq_s, nq_r, g_s, g_r, out_sem,
    ) = refs
    late = {7: mx.at[0, 0 : held[0].shape[0], :], 14: mx.at[1, 0 : held[0].shape[0], :]}
    late |= {10: s1.at[0, 0:D, :], 17: s1.at[1, 0:D, :]}
    for k in sorted(late):
        held.insert(k, late[k])
    emb, mixing, expa, shr, cls = held[:5]
    z = lax.axis_index("mp")
    y = lax.axis_index("dp")
    g = lax.axis_index("group")
    NP = NI // 2
    PR = 2 * ROWS
    hid = expa.shape[1]
    hid_all = hid * MP
    cpad = wc.shape[1] // MP
    er = emb.shape[0]
    NCH = hid_all // CHUNK
    PW, PE = g_w.shape[0] // DP, g_e.shape[0] // DP

    stores = []

    def store(k, value):
        c = pltpu.make_async_copy(value, results[k], out_sem.at[k])
        c.start()
        stores.append(c)

    loads = [pltpu.make_async_copy(flat(a), b, load.at[k]) for k, (a, b) in enumerate(zip(states, held, strict=True))]
    load_patches = pltpu.make_async_copy(patches, pv, load.at[21])
    loads[0].start()
    loads[2].start()
    load_patches.start()

    zpeer = [lax.rem(z + d, MP) for d in range(1, MP)]
    ypeer = [lax.rem(y + d, DP) for d in range(1, DP)]
    others = [{"mp": lax.rem(z + c, MP), "dp": lax.rem(y + d, DP)} for d in range(DP) for c in range(MP) if c or d]
    core, beside = lax.rem(g, 2), y + 1 - 2 * lax.rem(y, 2)
    near, far = {"group": g + 1 - 2 * core}, {"group": lax.rem(g + 2, G)}
    plane = [far, {"dp": beside}, {**far, "dp": beside}]
    greet(others + [near, far, plane[2]])

    def pieces(t, k, x, h, n=1):
        if k == 0:
            size = er // 4 * (1 if n == 1 else 2)
            at = core * (er // 2) + x * (er // 4)
            return e_all.at[t, pl.ds(pl.multiple_of(at, 16), size), :]
        size = D // 8 * n
        at = core * (D // 2) + (x * 2 + h) * (D // 8)
        if k == 2:
            return w2.at[pl.ds(pl.multiple_of(t * hid + at, 16), size), :]
        ref, width = (w1, hid) if k == 1 else (wc, cpad)
        return ref.at[pl.ds(pl.multiple_of(at, 16), size), pl.ds(pl.multiple_of(t * width, LANE), width)]

    here = (g // 2, lax.rem(y, 2))

    started = []

    def go(*args):
        c = remote(*args)
        c.start()
        started.append(c)

    def spread(k):
        part = pieces(z, k, *here)
        for d, t in enumerate(zpeer):
            go(part, part, wz_send.at[d, k], wz_recv.at[z, k], {"mp": t})

    def pass_on(k):
        for d, t in enumerate(zpeer):
            part = pieces(t, k, *here)
            remote(part, part, wz_send.at[d, k], wz_recv.at[t, k], {"mp": t}).wait_recv()
            for e, peer in enumerate(plane[: 1 if k == 0 else 3]):
                go(part, part, wp_send.at[d, e, k], wp_recv.at[t, e, k], peer)

    def share_out(k):
        there = ((1 - here[0], here[1]), (here[0], 1 - here[1]), (1 - here[0], 1 - here[1]))
        for d, t in enumerate(zpeer):
            for e, peer in enumerate(plane[: 1 if k == 0 else 3]):
                part = pieces(t, k, *there[e])
                remote(part, part, wp_send.at[d, e, k], wp_recv.at[t, e, k], peer).wait_recv()
            part = pieces(t, k, 0, 0, 4)
            go(part, part, wc_send.at[d, k], wc_recv.at[t, k], near)

    def gathered(k):
        for t in zpeer:
            if k == 0:
                part = e_all.at[t, pl.ds(pl.multiple_of((1 - core) * (er // 2), 16), er // 2), :]
            elif k == 2:
                part = w2.at[pl.ds(pl.multiple_of(t * hid + (1 - core) * (D // 2), 16), D // 2), :]
            else:
                ref, width = (w1, hid) if k == 1 else (wc, cpad)
                part = ref.at[
                    pl.ds(pl.multiple_of((1 - core) * (D // 2), 16), D // 2), pl.ds(pl.multiple_of(t * width, LANE), width)
                ]
            remote(part, part, wc_send.at[0, k], wc_recv.at[t, k], near).wait_recv()

    loads[0].wait()
    e_all[z] = emb[...].astype(BF16)
    spread(0)
    loads[2].wait()
    w1[:, pl.ds(pl.multiple_of(z * hid, LANE), hid)] = expa[0:D, :].astype(BF16)
    spread(1)

    row = lax.broadcasted_iota(jnp.int32, (ROWS, PATCHES), 0)
    column = lax.broadcasted_iota(jnp.int32, (ROWS, PATCHES), 1)
    eye[...] = jnp.where(row == column, 1.0, 0.0).astype(BF16)
    share = F32(mix_share)
    rest = F32(1.0 - mix_share)

    def blend(i):
        return (share * pv[i] + rest * pv[partner[i]]).astype(BF16)

    def blend_pair(t, p, ref, lead):
        a = blend(t * NI + 2 * p)
        b = blend(t * NI + 2 * p + 1)
        both = jnp.concatenate([a[0:LANE], b[0:LANE], a[LANE:], b[LANE:]], axis=0)
        turned = dot(eye[...], both, ((1,), (1,)))
        tail = None
        for k in range(3):
            lanes = turned[:, k * LANE : (k + 1) * LANE]
            ref[lead + (slice(k * MAIN, (k + 1) * MAIN), slice(None))] = lanes[0:MAIN].astype(BF16)
            last = lanes[MAIN:ROWS]
            tail = last if k == 0 else tail + pltpu.roll(last, k * (PATCHES - MAIN), 0)
        ref[lead + (slice(3 * MAIN, 3 * MAIN + 16), slice(None))] = tail.astype(BF16)

    def slab(t, p, k):
        tail = rows[t, p, 3 * MAIN :, :].astype(F32)
        if k:
            tail = pltpu.roll(tail, 16 - k * (PATCHES - MAIN), 0)
        row = lax.broadcasted_iota(jnp.int32, (16, LANE), 0)
        tail = jnp.where(row < PATCHES - MAIN, tail, 0.0).astype(BF16)
        return rows[t, p, k * MAIN : (k + 1) * MAIN, :], tail

    def send(p, d):
        slot = lax.rem(p, SLOTS)
        return remote(stage.at[d, slot], rows.at[z, p], rs_send.at[d, slot], rs_recv.at[z, p], {"mp": zpeer[d]})

    def prepare(p):
        for d in range(MP - 1):
            blend_pair(zpeer[d], p, stage, (d, lax.rem(p, SLOTS)))

    def start(p):
        for d in range(MP - 1):
            send(p, d).start()

    for k in (3, 4, 1):
        loads[k].start()
    small[z] = jnp.zeros(small.shape[1:], F32)
    small[z, 0:5, 0 : D // MP] = sca[...]
    small[z, 5:10, 0 : D // MP] = shi[...]
    for k in range(hid // LANE):
        small[z, 10 + k : 11 + k, :] = rounded(expa[D : D + 1, k * LANE : (k + 1) * LANE])
    loads[3].wait()
    w2[pl.ds(pl.multiple_of(z * hid, 16), hid), :] = shr[...].astype(BF16)
    spread(2)
    loads[4].wait()
    head = jnp.concatenate([cls[0:D, :], jnp.zeros((D, cpad - ncls), F32)], axis=1)
    wc[:, pl.ds(pl.multiple_of(z * cpad, LANE), cpad)] = head.astype(BF16)
    spread(3)
    for k in range(cpad // LANE):
        n = min(LANE, ncls - k * LANE)
        small[z, 13 + k : 14 + k, 0:n] = rounded(cls[D : D + 1, k * LANE : k * LANE + n])
    for d, t in enumerate(zpeer):
        go(small.at[z], small.at[z], sm_send.at[d], sm_recv.at[z], {"mp": t})
    load_patches.wait()
    prepare(0)
    start(0)
    pass_on(0)
    pass_on(1)
    if NP > 1:
        prepare(1)
        start(1)
    pass_on(2)
    pass_on(3)
    for k in range(5, 21):
        if k not in late:
            loads[k].start()

    loads[1].wait()
    wide = jnp.concatenate([mixing[...], jnp.zeros((PATCHES, 256 - PATCHES - 1), F32)], axis=1)
    wide = jnp.concatenate([wide, jnp.zeros((256 - PATCHES, 256), F32)], axis=0)
    column = lax.broadcasted_iota(jnp.int32, (256, 256), 1)
    square = jnp.where(column < PATCHES, wide, 0.0)
    mm[...] = square[0:ROWS, 0:ROWS].astype(BF16)
    mt[...] = jnp.transpose(square)[0:ROWS, 0:ROWS].astype(BF16)
    mbias[...] = rounded(jnp.sum(jnp.where(column == PATCHES, wide, 0.0), axis=1, keepdims=True)[0:ROWS])
    for t in range(MP):
        block = class_weight[:, t * ncls : (t + 1) * ncls]
        cw[:, t * cpad : (t + 1) * cpad] = jnp.concatenate([block, jnp.zeros((1, cpad - ncls), F32)], axis=1)
    asum[...] = jnp.zeros_like(asum)
    s1sum[...] = jnp.zeros_like(s1sum)
    csum[...] = jnp.zeros_like(csum)
    fit[:, D:, :] = jnp.ones((fit.shape[0], 16, PR), BF16)
    gw[...] = jnp.zeros_like(gw)
    ge[...] = jnp.zeros_like(ge)
    gm[...] = jnp.zeros_like(gm)
    gmb[...] = jnp.zeros_like(gmb)
    gvec[...] = jnp.zeros_like(gvec)
    la[...] = jnp.full(la.shape, -1, jnp.int32)
    lb[...] = jnp.full(lb.shape, -1, jnp.int32)
    for i in range(NI):
        own = labels[z * NI + i]
        mate = labels[partner[z * NI + i]]
        la[i : i + 1, :] = jnp.full((1, LANE), own, jnp.int32)
        lb[i : i + 1, :] = jnp.full((1, LANE), mate, jnp.int32)

    share_out(0)
    share_out(1)

    for t in zpeer:
        remote(small.at[t], small.at[t], sm_send.at[0], sm_recv.at[t], {"mp": t}).wait_recv()
    full = jnp.zeros((16, D), F32)
    for t in range(MP):
        block = jnp.concatenate([small[t], jnp.zeros((16, D - LANE), F32)], axis=1)
        full = full + (pltpu.roll(block, t * (D // MP), 1) if t else block)
        for k in range(hid // LANE):
            b1[:, t * hid + k * LANE : t * hid + (k + 1) * LANE] = small[t, 10 + k : 11 + k, :]
        for k in range(cpad // LANE):
            cb[:, t * cpad + k * LANE : t * cpad + (k + 1) * LANE] = small[t, 13 + k : 14 + k, :]
    vec[...] = full
    gathered(0)
    rest_rows = er - LANE
    for t in range(MP):
        ep[t * LANE : (t + 1) * LANE, :] = e_all[t, 0:LANE, :]
        ep[MP * LANE + t * rest_rows : MP * LANE + (t + 1) * rest_rows, :] = e_all[t, LANE:er, :]
    gathered(1)
    share_out(2)
    share_out(3)

    def scale(k):
        return vec[k : k + 1, :]

    def shift(k):
        return vec[5 + k : 6 + k, :]

    def forward(base, p, carry):
        @pl.when(p + 2 < NP)
        def _():
            @pl.when(p + 2 >= SLOTS)
            def _():
                for d in range(MP - 1):
                    send(p + 2 - SLOTS, d).wait_send()

            prepare(p + 2)
            start(p + 2)

        q = p - base
        blend_pair(z, p, rows, (z, p))
        for t in zpeer:
            remote(stage.at[0, 0], rows.at[t, p], rs_send.at[0, 0], rs_recv.at[t, p], {"mp": t}).wait_recv()
        for t in range(MP):
            lanes = slice(t * LANE, (t + 1) * LANE)
            for k in range(2):
                xs[q, k * ROWS : k * ROWS + MAIN, lanes], xs[q, k * ROWS + MAIN : (k + 1) * ROWS, lanes] = slab(t, p, k)
        for t in range(0, MP, 2):
            lanes = slice(MP * LANE + t * 64, MP * LANE + t * 64 + LANE)
            left, right = slab(t, p, 2), slab(t + 1, p, 2)
            for k in range(2):
                half = slice(k * 64, (k + 1) * 64)
                main, tail = (jnp.concatenate([v[:, half], w[:, half]], axis=1) for v, w in zip(left, right, strict=True))
                xs[q, k * ROWS : k * ROWS + MAIN, lanes] = main
                xs[q, k * ROWS + MAIN : (k + 1) * ROWS, lanes] = tail
        stream0 = dot(xs[q], ep[...]) + shift(3)
        s0[q] = stream0
        mi[q] = (scale(0) * stream0 + shift(0)).astype(BF16)
        for b in range(2):
            r = slice(b * ROWS, (b + 1) * ROWS)
            mixed = dot(mm[...], mi[q, r, :]) + mbias[...]
            mx[q, r, :] = mixed
            stream1 = s0[q, r, :] + scale(1) * mixed
            s1[q, r, :] = stream1
            fi[q, r, :] = (scale(2) * stream1 + shift(1)).astype(BF16)
            s1sum[pl.ds(2 * p + b, 1), :] = jnp.sum(stream1[0:PATCHES], axis=0, keepdims=True)

        def chunk(c, carry):
            cols = pl.ds(pl.multiple_of(c * CHUNK, CHUNK), CHUNK)
            for b in range(2):
                r = slice(b * ROWS, (b + 1) * ROWS)
                h = dot(fi[q, r, :], w1[:, cols]) + b1[:, cols]
                sq = h * h
                s = 0.5 * jnp.tanh(h * (GELU_A + GELU_B * sq)) + 0.5
                act = rounded(h * s)
                asum[pl.ds(2 * p + b, 1), cols] = jnp.sum(act[0:PATCHES], axis=0, keepdims=True)
                gp[q, r, cols] = s + s * (1.0 - s) * (h * (2.0 * GELU_A + 6.0 * GELU_B * sq))
                gp[q, b * ROWS + PATCHES : (b + 1) * ROWS, cols] = jnp.zeros((ROWS - PATCHES, CHUNK), F32)
            return carry

        lax.fori_loop(0, NCH, chunk, 0)

        return carry

    def class_head():
        three = dot(thirds(asum[...], 0), w2[...])
        outsum = three[0:16] + three[16:32] + three[32:48] + PATCHES * shift(2)
        stream2 = s1sum[...] + scale(3) * outsum
        pooled = (scale(4) * (stream2 * (1.0 / PATCHES)) + shift(4)).astype(BF16)
        lane = lax.broadcasted_iota(jnp.int32, (16, cpad * MP), 1)
        inside = lax.rem(lane, cpad)
        valid = inside < ncls
        class_id = (lane // cpad) * ncls + inside
        logits = jnp.where(valid, dot(pooled, wc[...]) + cb[...], -1e30)
        hot_a = jnp.where(valid & (class_id == la[:, 0:1]), 1.0, 0.0)
        hot_b = jnp.where(valid & (class_id == lb[:, 0:1]), 1.0, 0.0)
        weight_a = mix_share * jnp.sum(hot_a * cw[...], axis=1, keepdims=True)
        weight_b = (1.0 - mix_share) * jnp.sum(hot_b * cw[...], axis=1, keepdims=True)
        top = jnp.max(logits, axis=1, keepdims=True)
        exps = jnp.where(valid, jnp.exp(logits - top), 0.0)
        exp_sum = jnp.sum(exps, axis=1, keepdims=True)
        soft = exps / exp_sum
        dlog = ((weight_a + weight_b) * soft - weight_a * hot_a - weight_b * hot_b).astype(BF16)
        dfinal = dot(dlog, wc[...], ((1,), (1,))) * (1.0 / PATCHES)
        dstream2 = scale(4) * dfinal
        ds2[...] = dstream2
        dout = scale(3) * dstream2
        low = dout.astype(BF16)
        dact[...] = dot(low, w2[...], ((1,), (1,)))

        def last():
            log_total = top + jnp.log(exp_sum)
            target_a = jnp.sum(hot_a * logits, axis=1, keepdims=True)
            target_b = jnp.sum(hot_b * logits, axis=1, keepdims=True)
            loss = weight_a * (log_total - target_a) + weight_b * (log_total - target_b)
            loss = jnp.sum(loss, axis=0, keepdims=True)
            total = jnp.sum(weight_a + weight_b, axis=0, keepdims=True)
            fac[:, 0:16, :] = jnp.broadcast_to(low[None], (MP, 16, D))
            fac[:, 16:32, :] = jnp.broadcast_to(pooled[None], (MP, 16, D))
            for t in range(MP):
                fac[t, 32:48, 0:cpad] = dlog[:, t * cpad : (t + 1) * cpad]
                fac[t, 32:48, cpad:] = jnp.zeros((16, D - cpad), BF16)
            gvec[3:4, :] = jnp.sum(outsum * dstream2, axis=0, keepdims=True)
            gvec[4:5, :] = jnp.sum(dfinal * stream2, axis=0, keepdims=True)
            gvec[7:8, :] = PATCHES * jnp.sum(dout, axis=0, keepdims=True)
            gvec[8:9, :] = PATCHES * jnp.sum(dstream2, axis=0, keepdims=True)
            gvec[9:10, :] = PATCHES * jnp.sum(dfinal, axis=0, keepdims=True)
            lane = lax.broadcasted_iota(jnp.int32, (1, D), 1)
            gvec[10:11, :] = jnp.where(lane == 0, loss, jnp.where(lane == 1, total, 0.0))

        return last

    def turn_input(q):
        fit[q, 0:D, :] = jnp.transpose(fi[q])

    def hidden_gradient(q, p, cols):
        for b in range(2):
            r = slice(b * ROWS, (b + 1) * ROWS)
            dh[r, cols] = (gp[q, r, cols] * dact[pl.ds(2 * p + b, 1), cols]).astype(BF16)

    def backward_columns(q, p, cols):
        hidden_gradient(q, p, cols)
        grad = dot(fit[q], dh[:, cols])
        gw[0:D, cols] += grad[0:D]
        csum[0:1, cols] += grad[D : D + 1]

    def backward_hidden(base, p):
        q = p - base
        turn_input(q)

        def chunk(c, carry):
            backward_columns(q, p, pl.ds(pl.multiple_of(c * CHUNK, CHUNK), CHUNK))
            return carry

        lax.fori_loop(0, NCH, chunk, 0)

    def backward_rest(base, p):
        q = p - base
        dffn = dot(dh[...], w1[...], ((1,), (1,)))
        gvec[2:3, :] += jnp.sum(dffn * s1[q], axis=0, keepdims=True)
        gvec[6:7, :] += jnp.sum(dffn, axis=0, keepdims=True)
        for b in range(2):
            r = slice(b * ROWS, (b + 1) * ROWS)
            d1 = ds2[pl.ds(2 * p + b, 1), :] + scale(2) * dffn[r]
            gvec[1:2, :] += jnp.sum(mx[q, r, :] * d1, axis=0, keepdims=True)
            dmixed = (scale(1) * d1).astype(BF16)
            gm[...] += dot(dmixed, mi[q, r, :], ((1,), (1,)))
            gmb[...] += dmixed.astype(F32)
            dmixer = dot(mt[...], dmixed)
            gvec[0:1, :] += jnp.sum(dmixer * s0[q, r, :], axis=0, keepdims=True)
            gvec[5:6, :] += jnp.sum(dmixer, axis=0, keepdims=True)
            d0 = (d1 + scale(0) * dmixer).astype(BF16)
            grad = dot(xs[q, r, :], d0, ((0,), (0,)))
            for t in range(MP):
                ge[t, 0:LANE, :] += grad[t * LANE : (t + 1) * LANE]
                ge[t, LANE:er, :] += grad[MP * LANE + t * rest_rows : MP * LANE + (t + 1) * rest_rows]

    def backward(base, p, carry):
        backward_hidden(base, p)
        backward_rest(base, p)
        return carry

    for n, (lo, hi) in enumerate(waves_of(NP)):
        lax.fori_loop(lo, hi, functools.partial(forward, lo), 0)
        if n == 0:
            gathered(2)
            gathered(3)
        last = class_head()
        if hi < NP:
            lax.fori_loop(lo, hi, functools.partial(backward, lo), 0)

    def arrived(dst, sem, peer):
        remote(dst, dst, sem, sem, peer).wait_recv()

    def columns(t):
        return pl.ds(pl.multiple_of(t * hid, LANE), hid)

    def part(u, n):
        return pl.ds(pl.multiple_of(u * n, 8), n)

    last()
    yacts[y, z] = asum[:, columns(z)]
    yfac[y, z] = fac[z]
    for d, v in enumerate(zpeer):
        go(asum.at[:, columns(v)], yacts.at[y, z], zf_s.at[d, 2], zf_r.at[z, 2], {"mp": v})
        go(fac.at[v], yfac.at[y, z], zf_s.at[d, 3], zf_r.at[z, 3], {"mp": v})
    order = zpeer + [z]
    for p in range(lo, hi):
        turn_input(p - lo)
    for i, t in enumerate(order):
        for p in range(lo, hi):
            backward_columns(p - lo, p, columns(t))
        for d, u in enumerate(ypeer):
            ysw[i, d] = gw[part(u, PW), columns(t)].astype(BF16)
            go(ysw.at[i, d], yrw.at[t, d], yw_s.at[i, d], yw_r.at[t, d], {"dp": u})
    backward_rest(lo, hi - 1)
    for p in range(lo, hi - 1):
        for t in range(MP):
            hidden_gradient(p - lo, p, columns(t))
        backward_rest(lo, p)
    for i, t in enumerate(order):
        for d, u in enumerate(ypeer):
            yse[i, d] = ge[t, part(u, PE), :].astype(BF16)
            go(yse.at[i, d], yre.at[t, d], ye_s.at[i, d], ye_r.at[t, d], {"dp": u})

    for k in late:
        loads[k].start()

    gvec[8:9, :] += scale(2) * gvec[6:7, :] + scale(0) * gvec[5:6, :]
    row = lax.broadcasted_iota(jnp.int32, (ROWS, 256), 0)
    column = lax.broadcasted_iota(jnp.int32, (ROWS, 256), 1)
    bias_grad = jnp.sum(gmb[...], axis=1, keepdims=True)
    grad = jnp.concatenate([gm[...], jnp.zeros((ROWS, 256 - ROWS), F32)], axis=1)
    grad = jnp.where(column < PATCHES, grad, jnp.where(column == PATCHES, bias_grad, 0.0))
    grad = jnp.where(row < PATCHES, grad, 0.0)
    own = D // MP
    lane = lax.broadcasted_iota(jnp.int32, (16, LANE), 1)
    for t in range(MP):
        n = min(MIX, ROWS - t * MIX)
        gmix[t, 0:n, :] = grad[t * MIX : t * MIX + n]
        gmix[t, n:, :] = jnp.zeros((MIX16 - n, 256), F32)
        sm[t] = gmix[t].astype(BF16)
        vector = gvec[...]
        if t:
            vector = pltpu.roll(vector, D - t * own, 1)
        zvec[z, t] = jnp.where(lane < own, vector[:, 0:LANE], 0.0)
        zvec[z, t, 10:11, :] = gvec[10:11, 0:LANE]
        for k in range(hid // LANE):
            at = t * hid + k * LANE
            zvec[z, t, 11 + k : 12 + k, :] = csum[:, at : at + LANE]
    for d, v in enumerate(zpeer):
        go(sm.at[v], zsm.at[z], zf_s.at[d, 0], zf_r.at[z, 0], {"mp": v})
        go(zvec.at[z, v], zvec.at[z, v], zf_s.at[d, 1], zf_r.at[z, 1], {"mp": v})

    for v in zpeer:
        arrived(yacts.at[y, v], zf_r.at[v, 2], {"mp": v})
        arrived(yfac.at[y, v], zf_r.at[v, 3], {"mp": v})
    for d, u in enumerate(ypeer):
        go(yacts.at[y], yacts.at[y], yf_s.at[d, 2], yf_r.at[y, 2], {"dp": u})
        go(yfac.at[y], yfac.at[y], yf_s.at[d, 3], yf_r.at[y, 3], {"dp": u})

    def from_dp(first, received, sems, send, out, out_sems, z_sems, n):
        for i, t in enumerate(order):
            value = first(t)
            for d in range(DP - 1):
                arrived(received.at[t, d], sems.at[t, d], {"dp": ypeer[d]})
                value = value + received[t, d].astype(F32)
            if i < MP - 1:
                send[i] = value.astype(BF16)
                go(send.at[i], out.at[i], out_sems.at[i], z_sems.at[i], {"mp": t})
        return value

    own_w = from_dp(lambda t: gw[part(y, PW), columns(t)], yrw, yw_r, zsw, zrw, zw_s, zw_r, PW)

    mixed = gmix[z, 0:MIX, :]
    for v in zpeer:
        arrived(zsm.at[v], zf_r.at[v, 0], {"mp": v})
        arrived(zvec.at[v, z], zf_r.at[v, 1], {"mp": v})
        mixed = mixed + zsm[v, 0:MIX, :].astype(F32)
    vector = zvec[0, z]
    for v in range(1, MP):
        vector = vector + zvec[v, z]
    ysm[y] = mixed
    yvec[y] = vector
    for d, u in enumerate(ypeer):
        go(ysm.at[y], ysm.at[y], yf_s.at[d, 0], yf_r.at[y, 0], {"dp": u})
        go(yvec.at[y], yvec.at[y], yf_s.at[d, 1], yf_r.at[y, 1], {"dp": u})

    own_e = from_dp(lambda t: ge[t, part(y, PE), :], yre, ye_r, zse, zre, ze_s, ze_r, PE)

    def from_mp(own_sum, received, sems, gathered, k):
        value = own_sum
        for i in range(MP - 1):
            arrived(received.at[i], sems.at[i], {"mp": zpeer[i]})
            value = value + received[i].astype(F32)
        gathered[y] = value.astype(BF16)
        for d, u in enumerate(ypeer):
            go(gathered.at[y], gathered.at[y], ag_s.at[d, k], ag_r.at[y, k], {"dp": u})
        return rounded(value)

    def squares(v):
        return jnp.sum(jnp.sum(v * v, axis=0, keepdims=True), axis=1, keepdims=True)

    mine = squares(from_mp(own_w, zrw, zw_r, agw, 0))

    for u in ypeer:
        arrived(ysm.at[u], yf_r.at[u, 0], {"dp": u})
        arrived(yvec.at[u], yf_r.at[u, 1], {"dp": u})
    mixed, vector = ysm[0], yvec[0]
    for u in range(1, DP):
        mixed, vector = mixed + ysm[u], vector + yvec[u]
    g_mix[part(z, MIX), :] = mixed

    for u in ypeer:
        arrived(yacts.at[u], yf_r.at[u, 2], {"dp": u})
        arrived(yfac.at[u], yf_r.at[u, 3], {"dp": u})
    n = 16 * MP
    grad_shr = jnp.zeros((hid, D), F32)
    grad_cls = jnp.zeros((D, cpad), F32)
    cls_bias = jnp.zeros((1, cpad), F32)
    for u in range(DP):
        whole = yfac[u]
        dout = whole[:, 0:16, :].reshape(n, D)
        pooled = whole[:, 16:32, :].reshape(n, D)
        dlog = whole[:, 32:48, 0:cpad].reshape(n, cpad)
        three = thirds(yacts[u].reshape(n, hid), 0)
        grad_shr = grad_shr + dot(three, jnp.concatenate([dout] * 3, axis=0), ((0,), (0,)))
        grad_cls = grad_cls + dot(pooled, dlog, ((0,), (0,)))
        cls_bias = cls_bias + jnp.sum(dlog.astype(F32), axis=0, keepdims=True)
    g_shr[...] = grad_shr
    g_cls[0:D, :] = grad_cls
    g_cls[D:, :] = jnp.concatenate([cls_bias, jnp.zeros((g_cls.shape[0] - D - 1, cpad), F32)], axis=0)
    once = squares(grad_shr) + squares(grad_cls) + squares(cls_bias) + squares(mixed)
    once = once + squares(vector[0:10]) + squares(vector[11 : 11 + hid // LANE])

    mine = mine + squares(from_mp(own_e, zre, ze_r, age, 1))
    nsq[y, z] = jnp.broadcast_to(mine + jnp.where(y == 0, once, 0.0), (8, LANE))
    for k, peer in enumerate(others):
        go(nsq.at[y, z], nsq.at[y, z], nq_s.at[k], nq_r.at[y, z], peer)
    for d, v in enumerate(zpeer):
        go(g_mix.at[part(z, MIX), :], g_mix.at[part(z, MIX), :], nm_s.at[d], nm_r.at[z], {"mp": v})
    store(3, g_shr)
    store(4, g_cls)
    g_vec[...] = vector
    store(5, g_vec)
    for k in range(4, 21):
        if k != 4:
            loads[k].wait()
    for peer in others:
        arrived(nsq.at[peer["dp"], peer["mp"]], nq_r.at[peer["dp"], peer["mp"]], peer)
    square = jnp.zeros((1, 1), F32)
    for u in range(DP):
        for v in range(MP):
            square = square + nsq[u, v, 0:1, 0:1]
    loss_sum = vector[10:11, 0:1]
    weight_total = vector[10:11, 1:2]
    size = jnp.sqrt(square) / weight_total
    factor = clip_limit / jnp.maximum(size, clip_limit)
    scaled = factor / weight_total
    lane = lax.broadcasted_iota(jnp.int32, (8, LANE), 1)
    info[...] = jnp.where(
        lane == 0, loss_sum, jnp.where(lane == 1, weight_total, jnp.where(lane == 2, size, scaled))
    )

    (_, _, _, _, _, sca_w, shi_w) = held[:7]
    (emb1, mixing1, expa1, shr1, cls1, sca1, shi1) = held[7:14]
    (emb2, mixing2, expa2, shr2, cls2, sca2, shi2) = held[14:21]
    wide = sca_w.shape[1]
    def halves(ref, k):
        n = ref.shape[0] // 2
        return ref.at[pl.ds(pl.multiple_of(k * n, 8), n), :]

    mvs = gp.at[0:2, 0 : hid // 2, 0:D]
    mvc = gp.at[0:2, 0 : C_ROWS // 2, D : D + 256]
    mve = gp.at[0:2, 0 : E_ROWS // 2, D + 256 : 2 * D + 256]

    def put(moved, at, value):
        n = moved.shape[1]
        rows, width = value.shape
        k = min(max(n - at, 0), rows)
        if k:
            moved[0, at : at + k, 0:width] = value[0:k]
        if k < rows:
            moved[1, at + k - n : at + rows - n, 0:width] = value[k:]

    fine = C_VEC - C_ROWS // 2

    def first_step(k, moved, out):
        go(moved.at[1 - core], halves(out, 1 - core), g_s.at[k, 0], g_r.at[k, 0], near)

    split = (True, False, True)
    side = lax.rem(y, 2)

    def some(ref, k, which):
        n = ref.shape[1] // 2
        return ref.at[k, pl.ds(pl.multiple_of(which * n, 16), n), :]

    def second_step(k, moved, out, pairs):
        arrived(halves(out, core), g_r.at[k, 0], near)
        n = moved.shape[1]
        value = moved[core] + out[part(core, n), :]
        pairs[0, 0:n] = value.astype(BF16)
        if pairs.shape[1] > n:
            value = value[fine : fine + 16]
            pairs[0, n:] = (value - rounded(value)).astype(BF16)
        if split[k]:
            go(some(pairs, 0, side), some(pairs, 1, side), g_s.at[k, 1], g_r.at[k, 1], far)
        else:
            go(pairs.at[0], pairs.at[1], g_s.at[k, 1], g_r.at[k, 1], far)

    def hand_on(k, pairs):
        if not split[k]:
            return
        arrived(some(pairs, 1, side), g_r.at[k, 1], far)
        go(some(pairs, 1, side), some(pairs, 1, side), g_s.at[k, 2], g_r.at[k, 2], {"dp": beside})

    def third_step(k, pairs, out):
        if split[k]:
            arrived(some(pairs, 1, 1 - side), g_r.at[k, 2], {"dp": beside})
        else:
            arrived(pairs.at[1], g_r.at[k, 1], far)
        n = out.shape[0] // 2
        total = pairs[0].astype(F32) + pairs[1].astype(F32)
        out[part(core, n), :] = total[0:n]
        if pairs.shape[1] > n:
            out[pl.ds(pl.multiple_of(core * n + fine, 8), 16), :] = total[fine : fine + 16] + total[n:]
        go(halves(out, core), halves(out, core), g_s.at[k, 3], g_r.at[k, 3], near)

    put(mvs, 0, adamw(shr[...], g_shr[...] * scaled, shr1[...], shr2[...], matrix_rate))
    first_step(0, mvs, sum_s)
    for u in ypeer:
        arrived(agw.at[u], ag_r.at[u, 0], {"dp": u})
        arrived(age.at[u], ag_r.at[u, 1], {"dp": u})
    for u in range(DP):
        g_w[u * PW : (u + 1) * PW, :] = agw[u].astype(F32)
        g_e[u * PE : (u + 1) * PE, :] = age[u].astype(F32)
    store(0, g_w)
    store(1, g_e)
    bias = jnp.concatenate([g_vec[11 + k : 12 + k, :] for k in range(hid // LANE)], axis=1)
    last_row = slice(D, D + 1)
    mve[...] = jnp.zeros(mve.shape, F32)
    put(mve, E_EXP, adamw(expa[0:D, :], g_w[0:D, :] * scaled, expa1[0:D, :], expa2[0:D, :], matrix_rate))
    put(mve, E_EXP + D, adamw(expa[last_row, :], bias * scaled, expa1[last_row, :], expa2[last_row, :], matrix_rate))
    put(mve, E_EMB, adamw(emb[...], g_e[0:er, :] * scaled, emb1[...], emb2[...], matrix_rate))
    first_step(2, mve, sum_e)
    second_step(0, mvs, sum_s, h2s)
    for v in zpeer:
        arrived(g_mix.at[part(v, MIX), :], nm_r.at[v], {"mp": v})
    store(2, g_mix)
    mvc[...] = jnp.zeros(mvc.shape, F32)
    put(mvc, C_CLS, adamw(cls[...], g_cls[0 : D + 1, 0:ncls] * scaled, cls1[...], cls2[...], head_rate))
    put(
        mvc, C_MIX,
        adamw(mixing[...], g_mix[0:PATCHES, 0 : PATCHES + 1] * scaled, mixing1[...], mixing2[...], matrix_rate),
    )
    for k, (w, one, two) in enumerate(((sca_w, sca1, sca2), (shi_w, shi1, shi2))):
        value = adamw(w[...], g_vec[5 * k : 5 * k + 5, 0:wide] * scaled, one[...], two[...], vector_rate)
        put(mvc, C_VEC + 8 * k, value)
    first_step(1, mvc, sum_c)
    second_step(2, mve, sum_e, h2e)
    hand_on(0, h2s)
    second_step(1, mvc, sum_c, h2c)
    hand_on(2, h2e)
    third_step(0, h2s, sum_s)
    hand_on(1, h2c)
    third_step(2, h2e, sum_e)
    arrived(halves(sum_s, 1 - core), g_r.at[0, 3], near)
    store(6, sum_s)
    third_step(1, h2c, sum_c)
    arrived(halves(sum_e, 1 - core), g_r.at[2, 3], near)
    store(8, sum_e)
    arrived(halves(sum_c, 1 - core), g_r.at[1, 3], near)
    store(7, sum_c)

    def drain(p, carry):
        for d in range(MP - 1):
            send(p, d).wait_send()
        return carry

    lax.fori_loop(max(NP - SLOTS, 0), NP, drain, 0)
    for c in started:
        c.wait_send()
    for c in stores:
        c.wait()


def local_step(G, DP, MP, shapes, labels, partner, sca, shi, class_weight, patches, states):
    NI = patches.shape[0] // MP
    NP = NI // 2
    PR = 2 * ROWS
    er, hid, ncls = shapes[0][0], shapes[2][1], shapes[4][1]
    hid_all = hid * MP
    pd = er * MP
    cpad = -(-ncls // LANE) * LANE
    wave = max(hi - lo for lo, hi in waves_of(NP))
    dp1 = max(DP - 1, 1)
    PW, PE = part_rows(D, DP), part_rows(er, DP)
    dma = pltpu.SemaphoreType.DMA
    vm = pl.BlockSpec(memory_space=VMEM)
    smem = pl.BlockSpec(memory_space=SMEM)
    hbm = pl.BlockSpec(memory_space=pl.ANY)
    s = jax.ShapeDtypeStruct
    results = (
        (DP * PW, D), (DP * PE, D), (MP * MIX, 256), (hid, D), (392, cpad), (16, LANE),
        (hid, D), (C_ROWS, 256), (E_ROWS, D),
    )
    return pl.pallas_call(
        functools.partial(step_kernel, G, DP, MP, NI, ncls),
        out_shape=(*(s(shape, F32) for shape in results), s((8, LANE), F32)),
        in_specs=[smem, smem, vm, vm, vm] + [hbm] * 22,
        out_specs=(hbm,) * 9 + (vm,),
        scratch_shapes=[VMEM(shape, F32) for shape in results]
        + [VMEM(shape, F32) for shape in shapes + 2 * (shapes[1:3] + shapes[4:])]
        + [
            VMEM(patches.shape, F32),
            VMEM((MP - 1, SLOTS, 3 * MAIN + 16, LANE), BF16),
            VMEM((MP, NP, 3 * MAIN + 16, LANE), BF16),
            VMEM((MP, er, D), BF16),
            VMEM((D, hid_all), BF16),
            VMEM((hid_all, D), BF16),
            VMEM((D, cpad * MP), BF16),
            VMEM((MP, 16, LANE), F32),
            VMEM((wave, PR, pd), BF16),
            VMEM((wave, PR, hid_all), F32),
            VMEM((wave, PR, D), F32),
            VMEM((wave, PR, D), F32),
            VMEM((wave, PR, D), F32),
            VMEM((wave, PR, D), BF16),
            VMEM((wave, PR, D), BF16),
            VMEM((pd, D), BF16),
            VMEM((ROWS, ROWS), BF16),
            VMEM((ROWS, ROWS), BF16),
            VMEM((ROWS, PATCHES), BF16),
            VMEM((ROWS, 1), F32),
            VMEM((16, D), F32),
            VMEM((1, hid_all), F32),
            VMEM((1, cpad * MP), F32),
            VMEM((1, cpad * MP), F32),
            VMEM((16, hid_all), F32),
            VMEM((16, D), F32),
            VMEM((16, LANE), jnp.int32),
            VMEM((16, LANE), jnp.int32),
            VMEM((16, hid_all), F32),
            VMEM((16, D), F32),
            VMEM((PR, hid_all), BF16),
            VMEM((wave, D + 16, PR), BF16),
            VMEM((1, hid_all), F32),
            VMEM((DP * PW, hid_all), F32),
            VMEM((MP, DP * PE, D), F32),
            VMEM((ROWS, ROWS), F32),
            VMEM((ROWS, D), F32),
            VMEM((16, D), F32),
            VMEM((MP, MIX16, 256), F32),
            VMEM((MP, MIX16, 256), BF16),
            VMEM((MP, 48, D), BF16),
            VMEM((MP, MIX16, 256), BF16),
            VMEM((MP, MP, 16, LANE), F32),
            VMEM((DP, MIX, 256), F32),
            VMEM((DP, 16, LANE), F32),
            VMEM((DP, MP, 16, hid), F32),
            VMEM((DP, MP, 48, D), BF16),
            VMEM((DP, PW, hid), BF16),
            VMEM((DP, PE, D), BF16),
            VMEM((MP, dp1, PW, hid), BF16),
            VMEM((MP, dp1, PW, hid), BF16),
            VMEM((MP - 1, PW, hid), BF16),
            VMEM((MP - 1, PW, hid), BF16),
            VMEM((MP, dp1, PE, D), BF16),
            VMEM((MP, dp1, PE, D), BF16),
            VMEM((MP - 1, PE, D), BF16),
            VMEM((MP - 1, PE, D), BF16),
            VMEM((DP, MP, 8, LANE), F32),
            VMEM((2, hid // 2, D), BF16),
            VMEM((2, C_ROWS // 2 + 16, 256), BF16),
            VMEM((2, E_ROWS // 2, D), BF16),
            dma((22,)),
            dma((MP - 1, SLOTS)),
            dma((MP, NP)),
            dma((MP - 1, 4)),
            dma((MP, 4)),
            dma((MP - 1, 3, 4)),
            dma((MP, 3, 4)),
            dma((MP - 1, 4)),
            dma((MP, 4)),
            dma((MP - 1,)),
            dma((MP,)),
            dma((MP - 1, 4)),
            dma((MP, 4)),
            dma((dp1, 4)),
            dma((DP, 4)),
            dma((MP, dp1)),
            dma((MP, dp1)),
            dma((MP - 1,)),
            dma((MP - 1,)),
            dma((MP, dp1)),
            dma((MP, dp1)),
            dma((MP - 1,)),
            dma((MP - 1,)),
            dma((dp1, 2)),
            dma((DP, 2)),
            dma((MP - 1,)),
            dma((MP,)),
            dma((DP * MP - 1,)),
            dma((DP, MP)),
            dma((3, 4)),
            dma((3, 4)),
            dma((9,)),
        ],
        compiler_params=pltpu.CompilerParams(
            collective_id=0, has_side_effects=True, vmem_limit_bytes=63 << 20
        ),
    )(labels, partner, sca, shi, class_weight, patches, *states)


def finish_kernel(groups, *refs):
    (info, *grads_in), refs = refs[:10], refs[10:]
    states, refs = refs[:28], refs[28:]
    (losses, norm), refs = refs[:2], refs[2:]
    outs, refs = refs[:28], refs[28:]
    grads_held, refs = refs[:9], refs[9:]
    held, refs = refs[:28], refs[28:]
    new, (load, load_grad, save) = refs[:28], refs[28:]
    first = [pltpu.make_async_copy(a, b, load_grad.at[k]) for k, (a, b) in enumerate(zip(grads_in, grads_held, strict=True))]
    loads = [pltpu.make_async_copy(flat(a), b, load.at[k]) for k, (a, b) in enumerate(zip(states, held, strict=True))]
    saves = [pltpu.make_async_copy(a, flat(b), save.at[k]) for k, (a, b) in enumerate(zip(new, outs, strict=True))]
    for c in first:
        c.start()
    for k in (3, 2, 0, 4, 1, 5, 6):
        for j in range(4):
            loads[7 * j + k].start()
    losses[...] = info[0:1, 0:2]
    norm[...] = info[0:1, 2:3]
    scaled = info[0:1, 3:4]
    g_w, g_e, g_mix, g_shr, g_cls, g_vec, sum_s, sum_c, sum_e = grads_held
    for c in first:
        c.wait()
    wide = held[5].shape[1]
    ncls = held[4].shape[1]
    er = held[0].shape[0]
    all_rows = slice(None)

    bias = jnp.concatenate([g_vec[11 + k : 12 + k, :] for k in range(D // LANE)], axis=1)
    work = (
        (3, all_rows, lambda: g_shr[...], lambda: sum_s[...]),
        (2, slice(0, D), lambda: g_w[0:D, :], lambda: sum_e[E_EXP : E_EXP + D, :]),
        (2, slice(D, D + 1), lambda: bias, lambda: sum_e[E_EXP + D : E_EXP + D + 1, :]),
        (0, all_rows, lambda: g_e[0:er, :], lambda: sum_e[E_EMB : E_EMB + er, :]),
        (4, all_rows, lambda: g_cls[0 : D + 1, 0:ncls], lambda: sum_c[C_CLS : C_CLS + D + 1, 0:ncls]),
        (1, all_rows, lambda: g_mix[0:PATCHES, 0 : PATCHES + 1], lambda: sum_c[C_MIX : C_MIX + PATCHES, 0 : PATCHES + 1]),
        (5, all_rows, lambda: g_vec[0:5, 0:wide], lambda: sum_c[C_VEC : C_VEC + 5, 0:wide]),
        (6, all_rows, lambda: g_vec[5:10, 0:wide], lambda: sum_c[C_VEC + 8 : C_VEC + 13, 0:wide]),
    )
    for n, (k, r, gradient, total) in enumerate(work):
        if n == 0 or work[n - 1][0] != k:
            for j in range(4):
                loads[7 * j + k].wait()
        weight, one, two, outer = (held[7 * j + k] for j in range(4))
        update, mean, square, velocity = (new[7 * j + k] for j in range(4))
        grad = gradient() * scaled
        mean[r, :] = beta_one * one[r, :] + (1.0 - beta_one) * grad
        square[r, :] = beta_two * two[r, :] + (1.0 - beta_two) * grad * grad
        average = total() * (1.0 / groups)
        moving = outer_momentum * outer[r, :] + average
        velocity[r, :] = moving
        update[r, :] = weight[r, :] - outer_rate * (average + outer_momentum * moving)
        if n + 1 == len(work) or work[n + 1][0] != k:
            for j in range(4):
                saves[7 * j + k].start()
    for c in saves:
        c.wait()


def finish(G, info, grads, shapes, states, out_shapes):
    dma = pltpu.SemaphoreType.DMA
    vm = pl.BlockSpec(memory_space=VMEM)
    hbm = pl.BlockSpec(memory_space=pl.ANY)
    return pl.pallas_call(
        functools.partial(finish_kernel, G),
        out_shape=tuple(jax.ShapeDtypeStruct(shape, F32) for shape in ((1, 2), (1, 1), *out_shapes)),
        in_specs=[vm] + [hbm] * 37,
        out_specs=(vm,) * 2 + (hbm,) * 28,
        scratch_shapes=[VMEM(a.shape, F32) for a in grads]
        + [VMEM(shape, F32) for shape in shapes] * 8
        + [dma((28,)), dma((9,)), dma((28,))],
        compiler_params=pltpu.CompilerParams(vmem_limit_bytes=62 << 20),
    )(info, *grads, *states)


def thin(a):
    return jnp.swapaxes(a, 0, 1)


def per_device(
    G, DP, MP,
    patches, labels, partner, class_weight,
    embedding, mixing, expand, shrink, classifier, scales, shifts, *state,
):
    weights = (embedding, thin(mixing), thin(expand), shrink[0], classifier, scales, shifts)

    def moments(a):
        return (a[0][0], thin(a[1][0]), thin(a[2][0]), a[3][0, 0], thin(a[4]), thin(a[5]), thin(a[6]))

    firsts, seconds = moments(state[0:7]), moments(state[7:14])
    o = state[14:21]
    outers = (o[0], thin(o[1]), thin(o[2]), o[3][0], o[4], o[5], o[6])
    shapes = tuple((a.shape[0], a.shape[-1]) for a in weights)
    *grads, info = local_step(
        G, DP, MP, shapes, labels[0], partner[0], scales, shifts, class_weight.reshape(1, -1),
        jnp.swapaxes(patches[0], 1, 2), (*weights, *firsts, *seconds),
    )
    out_shapes = tuple(a.shape for a in (*weights, *firsts, *seconds, *outers))
    losses, norm, *done = finish(G, info, grads, shapes, (*weights, *firsts, *seconds, *outers), out_shapes)
    updates, means, squares, velocities = (list(done[7 * k : 7 * k + 7]) for k in range(4))

    def whole(a):
        return (a[0], thin(a[1]), thin(a[2]), a[3][None], a[4], a[5], a[6])

    def by_group(a):
        return (a[0][None], thin(a[1])[None], thin(a[2])[None], a[3][None, None], thin(a[4]), thin(a[5]), thin(a[6]))

    return (
        losses, norm[0],
        *whole(updates), *by_group(means), *by_group(squares), *whole(velocities),
    )


WEIGHT_SPECS = (
    P("mp", None),
    P(),
    P(None, None, "mp"),
    P(None, "mp", None),
    P(None, "mp"),
    P(None, "mp"),
    P(None, "mp"),
)
STATE_SPECS = (
    P("group", "mp", None),
    P("group", None, None, None),
    P("group", None, None, "mp"),
    P("group", None, "mp", None),
    P("group", None, "mp"),
    P("group", None, "mp"),
    P("group", None, "mp"),
)


def solution(mesh):
    G, DP, MP = mesh.shape["group"], mesh.shape["dp"], mesh.shape["mp"]
    return jax.shard_map(
        functools.partial(per_device, G, DP, MP),
        mesh=mesh,
        in_specs=(
            P("group", "dp", None, "mp"),
            P("group", "dp"),
            P("group", "dp"),
            P(),
            *WEIGHT_SPECS,
            *STATE_SPECS,
            *STATE_SPECS,
            *WEIGHT_SPECS,
        ),
        out_specs=(
            P("group", None),
            P("group"),
            *WEIGHT_SPECS,
            *STATE_SPECS,
            *STATE_SPECS,
            *WEIGHT_SPECS,
        ),
        check_vma=False,
    )
```

```python
import functools

import jax
import jax.numpy as jnp
from jax import lax
from jax.experimental import pallas as pl
from jax.experimental.pallas import tpu as pltpu
from jax.sharding import PartitionSpec as P

F32 = jnp.float32
BF16 = jnp.bfloat16
MESH = pl.DeviceIdType.MESH
VMEM = pltpu.VMEM
SMEM = pltpu.SMEM

D = 384
PATCHES = 196
ROWS = 208
MAIN = 192
STEP = 10
LANE = 128

mix_share = 0.7
clip_limit = 0.01
beta_one = 0.9
beta_two = 0.999
adam_eps = 1e-08
weight_decay = 0.05
matrix_rate = 0.05
head_rate = 0.5
vector_rate = 0.4
outer_rate = 0.7
outer_momentum = 0.9

GELU_A = 0.7978845608028654
GELU_B = GELU_A * 0.044715

MIX, MIX16 = 56, 64
C_CLS, C_MIX, C_VEC, C_ROWS = 0, 392, 592, 608
E_EXP, E_EMB, E_ROWS = 0, 392, 640


def dot(a, b, dims=((1,), (0,)), precision=None):
    return lax.dot_general(
        a, b, (dims, ((), ())), preferred_element_type=F32, precision=precision
    )


def thirds(a, axis):
    high = a.astype(BF16)
    rest = a - high.astype(F32)
    middle = rest.astype(BF16)
    low = (rest - middle.astype(F32)).astype(BF16)
    return jnp.concatenate([high, middle, low], axis=axis)


def rounded(a):
    return a.astype(BF16).astype(F32)


def greet(peers):
    barrier = pltpu.get_barrier_semaphore()
    for peer in peers:
        pl.semaphore_signal(barrier, inc=1, device_id=peer, device_id_type=MESH)
    pl.semaphore_wait(barrier, len(peers))


def remote(src, dst, send_sem, recv_sem, peer):
    return pltpu.make_async_remote_copy(
        src_ref=src, dst_ref=dst, send_sem=send_sem, recv_sem=recv_sem,
        device_id=peer, device_id_type=MESH,
    )


CHUNK = 256
SLOTS = 3


def waves_of(pairs):
    return [(lo, min(lo + 2, pairs)) for lo in range(0, pairs, 2)]


def part_rows(rows, DP):
    return -(-rows // (16 * DP)) * 16


def adamw(weight, gradient, moment_one, moment_two, rate):
    mean_new = beta_one * moment_one + (1.0 - beta_one) * gradient
    square_new = beta_two * moment_two + (1.0 - beta_two) * gradient * gradient
    mean_hat = mean_new * (1.0 / (1.0 - beta_one**STEP))
    square_hat = square_new * (1.0 / (1.0 - beta_two**STEP))
    return rate * (mean_hat / (jnp.sqrt(square_hat) + adam_eps) + weight_decay * weight)


def flat(ref):
    return ref.at[:, 0, :] if len(ref.shape) == 3 and ref.shape[1] == 1 else ref


def step_kernel(G, DP, MP, NI, ncls, *refs):
    (labels, partner, sca, shi, class_weight, patches), refs = refs[:6], refs[6:]
    states, refs = refs[:21], refs[21:]
    (*results, info), refs = refs[:10], refs[10:]
    (g_w, g_e, g_mix, g_shr, g_cls, g_vec, sum_s, sum_c, sum_e), refs = refs[:9], refs[9:]
    held, refs = list(refs[:17]), refs[17:]
    (
        pv, stage, rows, e_all, w1, w2, wc, small,
        xs, gp, s0, s1, mx, mi, fi, ep, mm, mt, eye, mbias, vec, b1, cb, cw, asum, s1sum, la, lb,
        dact, ds2, dh, fit, csum, gw, ge, gm, gmb, gvec,
        gmix, sm, fac, zsm, zvec, ysm, yvec, yacts, yfac, agw, age,
        ysw, yrw, zsw, zrw, yse, yre, zse, zre, nsq,
        h2s, h2c, h2e,
        load, rs_send, rs_recv, wz_send, wz_recv, wp_send, wp_recv, wc_send, wc_recv, sm_send, sm_recv,
        zf_s, zf_r, yf_s, yf_r, yw_s, yw_r, zw_s, zw_r, ye_s, ye_r, ze_s, ze_r, ag_s, ag_r,
        nm_s, nm_r, nq_s, nq_r, g_s, g_r, out_sem,
    ) = refs
    late = {7: mx.at[0, 0 : held[0].shape[0], :], 14: mx.at[1, 0 : held[0].shape[0], :]}
    late |= {10: s1.at[0, 0:D, :], 17: s1.at[1, 0:D, :]}
    for k in sorted(late):
        held.insert(k, late[k])
    emb, mixing, expa, shr, cls = held[:5]
    z = lax.axis_index("mp")
    y = lax.axis_index("dp")
    g = lax.axis_index("group")
    NP = NI // 2
    PR = 2 * ROWS
    hid = expa.shape[1]
    hid_all = hid * MP
    cpad = wc.shape[1] // MP
    er = emb.shape[0]
    NCH = hid_all // CHUNK
    PW, PE = g_w.shape[0] // DP, g_e.shape[0] // DP

    stores = []

    def store(k, value):
        c = pltpu.make_async_copy(value, results[k], out_sem.at[k])
        c.start()
        stores.append(c)

    loads = [pltpu.make_async_copy(flat(a), b, load.at[k]) for k, (a, b) in enumerate(zip(states, held, strict=True))]
    load_patches = pltpu.make_async_copy(patches, pv, load.at[21])
    loads[0].start()
    loads[2].start()
    load_patches.start()

    zpeer = [lax.rem(z + d, MP) for d in range(1, MP)]
    ypeer = [lax.rem(y + d, DP) for d in range(1, DP)]
    others = [{"mp": lax.rem(z + c, MP), "dp": lax.rem(y + d, DP)} for d in range(DP) for c in range(MP) if c or d]
    core, beside = lax.rem(g, 2), y + 1 - 2 * lax.rem(y, 2)
    near, far = {"group": g + 1 - 2 * core}, {"group": lax.rem(g + 2, G)}
    plane = [far, {"dp": beside}, {**far, "dp": beside}]
    greet(others + [near, far, plane[2]])

    def pieces(t, k, x, h, n=1):
        if k == 0:
            size = er // 4 * (1 if n == 1 else 2)
            at = core * (er // 2) + x * (er // 4)
            return e_all.at[t, pl.ds(pl.multiple_of(at, 16), size), :]
        size = D // 8 * n
        at = core * (D // 2) + (x * 2 + h) * (D // 8)
        if k == 2:
            return w2.at[pl.ds(pl.multiple_of(t * hid + at, 16), size), :]
        ref, width = (w1, hid) if k == 1 else (wc, cpad)
        return ref.at[pl.ds(pl.multiple_of(at, 16), size), pl.ds(pl.multiple_of(t * width, LANE), width)]

    here = (g // 2, lax.rem(y, 2))

    started = []

    def go(*args):
        c = remote(*args)
        c.start()
        started.append(c)

    def spread(k):
        part = pieces(z, k, *here)
        for d, t in enumerate(zpeer):
            go(part, part, wz_send.at[d, k], wz_recv.at[z, k], {"mp": t})

    def pass_on(k):
        for d, t in enumerate(zpeer):
            part = pieces(t, k, *here)
            remote(part, part, wz_send.at[d, k], wz_recv.at[t, k], {"mp": t}).wait_recv()
            for e, peer in enumerate(plane[: 1 if k == 0 else 3]):
                go(part, part, wp_send.at[d, e, k], wp_recv.at[t, e, k], peer)

    def share_out(k):
        there = ((1 - here[0], here[1]), (here[0], 1 - here[1]), (1 - here[0], 1 - here[1]))
        for d, t in enumerate(zpeer):
            for e, peer in enumerate(plane[: 1 if k == 0 else 3]):
                part = pieces(t, k, *there[e])
                remote(part, part, wp_send.at[d, e, k], wp_recv.at[t, e, k], peer).wait_recv()
            part = pieces(t, k, 0, 0, 4)
            go(part, part, wc_send.at[d, k], wc_recv.at[t, k], near)

    def gathered(k):
        for t in zpeer:
            if k == 0:
                part = e_all.at[t, pl.ds(pl.multiple_of((1 - core) * (er // 2), 16), er // 2), :]
            elif k == 2:
                part = w2.at[pl.ds(pl.multiple_of(t * hid + (1 - core) * (D // 2), 16), D // 2), :]
            else:
                ref, width = (w1, hid) if k == 1 else (wc, cpad)
                part = ref.at[
                    pl.ds(pl.multiple_of((1 - core) * (D // 2), 16), D // 2), pl.ds(pl.multiple_of(t * width, LANE), width)
                ]
            remote(part, part, wc_send.at[0, k], wc_recv.at[t, k], near).wait_recv()

    loads[0].wait()
    e_all[z] = emb[...].astype(BF16)
    spread(0)
    loads[2].wait()
    w1[:, pl.ds(pl.multiple_of(z * hid, LANE), hid)] = expa[0:D, :].astype(BF16)
    spread(1)

    row = lax.broadcasted_iota(jnp.int32, (ROWS, PATCHES), 0)
    column = lax.broadcasted_iota(jnp.int32, (ROWS, PATCHES), 1)
    eye[...] = jnp.where(row == column, 1.0, 0.0).astype(BF16)
    share = F32(mix_share)
    rest = F32(1.0 - mix_share)

    def blend(i):
        return (share * pv[i] + rest * pv[partner[i]]).astype(BF16)

    def blend_pair(t, p, ref, lead):
        a = blend(t * NI + 2 * p)
        b = blend(t * NI + 2 * p + 1)
        both = jnp.concatenate([a[0:LANE], b[0:LANE], a[LANE:], b[LANE:]], axis=0)
        turned = dot(eye[...], both, ((1,), (1,)))
        tail = None
        for k in range(3):
            lanes = turned[:, k * LANE : (k + 1) * LANE]
            ref[lead + (slice(k * MAIN, (k + 1) * MAIN), slice(None))] = lanes[0:MAIN].astype(BF16)
            last = lanes[MAIN:ROWS]
            tail = last if k == 0 else tail + pltpu.roll(last, k * (PATCHES - MAIN), 0)
        ref[lead + (slice(3 * MAIN, 3 * MAIN + 16), slice(None))] = tail.astype(BF16)

    def slab(t, p, k):
        tail = rows[t, p, 3 * MAIN :, :].astype(F32)
        if k:
            tail = pltpu.roll(tail, 16 - k * (PATCHES - MAIN), 0)
        row = lax.broadcasted_iota(jnp.int32, (16, LANE), 0)
        tail = jnp.where(row < PATCHES - MAIN, tail, 0.0).astype(BF16)
        return rows[t, p, k * MAIN : (k + 1) * MAIN, :], tail

    def send(p, d):
        slot = lax.rem(p, SLOTS)
        return remote(stage.at[d, slot], rows.at[z, p], rs_send.at[d, slot], rs_recv.at[z, p], {"mp": zpeer[d]})

    def prepare(p):
        for d in range(MP - 1):
            blend_pair(zpeer[d], p, stage, (d, lax.rem(p, SLOTS)))

    def start(p):
        for d in reversed(range(MP - 1)):
            send(p, d).start()

    for k in (3, 4, 1):
        loads[k].start()
    small[z] = jnp.zeros(small.shape[1:], F32)
    small[z, 0:5, 0 : D // MP] = sca[...]
    small[z, 5:10, 0 : D // MP] = shi[...]
    for k in range(hid // LANE):
        small[z, 10 + k : 11 + k, :] = rounded(expa[D : D + 1, k * LANE : (k + 1) * LANE])
    loads[3].wait()
    w2[pl.ds(pl.multiple_of(z * hid, 16), hid), :] = shr[...].astype(BF16)
    spread(2)
    loads[4].wait()
    head = jnp.concatenate([cls[0:D, :], jnp.zeros((D, cpad - ncls), F32)], axis=1)
    wc[:, pl.ds(pl.multiple_of(z * cpad, LANE), cpad)] = head.astype(BF16)
    spread(3)
    for k in range(cpad // LANE):
        n = min(LANE, ncls - k * LANE)
        small[z, 13 + k : 14 + k, 0:n] = rounded(cls[D : D + 1, k * LANE : k * LANE + n])
    for d, t in enumerate(zpeer):
        go(small.at[z], small.at[z], sm_send.at[d], sm_recv.at[z], {"mp": t})
    load_patches.wait()
    prepare(0)
    start(0)
    pass_on(0)
    pass_on(1)
    if NP > 1:
        prepare(1)
        start(1)
    pass_on(2)
    pass_on(3)
    for k in range(5, 21):
        if k not in late:
            loads[k].start()

    loads[1].wait()
    wide = jnp.concatenate([mixing[...], jnp.zeros((PATCHES, 256 - PATCHES - 1), F32)], axis=1)
    wide = jnp.concatenate([wide, jnp.zeros((256 - PATCHES, 256), F32)], axis=0)
    column = lax.broadcasted_iota(jnp.int32, (256, 256), 1)
    square = jnp.where(column < PATCHES, wide, 0.0)
    mm[...] = square[0:ROWS, 0:ROWS].astype(BF16)
    mt[...] = jnp.transpose(square)[0:ROWS, 0:ROWS].astype(BF16)
    mbias[...] = rounded(jnp.sum(jnp.where(column == PATCHES, wide, 0.0), axis=1, keepdims=True)[0:ROWS])
    for t in range(MP):
        block = class_weight[:, t * ncls : (t + 1) * ncls]
        cw[:, t * cpad : (t + 1) * cpad] = jnp.concatenate([block, jnp.zeros((1, cpad - ncls), F32)], axis=1)
    asum[...] = jnp.zeros_like(asum)
    s1sum[...] = jnp.zeros_like(s1sum)
    csum[...] = jnp.zeros_like(csum)
    fit[:, D:, :] = jnp.ones((fit.shape[0], 16, PR), BF16)
    gw[...] = jnp.zeros_like(gw)
    ge[...] = jnp.zeros_like(ge)
    gm[...] = jnp.zeros_like(gm)
    gmb[...] = jnp.zeros_like(gmb)
    gvec[...] = jnp.zeros_like(gvec)
    la[...] = jnp.full(la.shape, -1, jnp.int32)
    lb[...] = jnp.full(lb.shape, -1, jnp.int32)
    for i in range(NI):
        own = labels[z * NI + i]
        mate = labels[partner[z * NI + i]]
        la[i : i + 1, :] = jnp.full((1, LANE), own, jnp.int32)
        lb[i : i + 1, :] = jnp.full((1, LANE), mate, jnp.int32)

    share_out(0)
    share_out(1)

    for t in zpeer:
        remote(small.at[t], small.at[t], sm_send.at[0], sm_recv.at[t], {"mp": t}).wait_recv()
    full = jnp.zeros((16, D), F32)
    for t in range(MP):
        block = jnp.concatenate([small[t], jnp.zeros((16, D - LANE), F32)], axis=1)
        full = full + (pltpu.roll(block, t * (D // MP), 1) if t else block)
        for k in range(hid // LANE):
            b1[:, t * hid + k * LANE : t * hid + (k + 1) * LANE] = small[t, 10 + k : 11 + k, :]
        for k in range(cpad // LANE):
            cb[:, t * cpad + k * LANE : t * cpad + (k + 1) * LANE] = small[t, 13 + k : 14 + k, :]
    vec[...] = full
    gathered(0)
    rest_rows = er - LANE
    for t in range(MP):
        ep[t * LANE : (t + 1) * LANE, :] = e_all[t, 0:LANE, :]
        ep[MP * LANE + t * rest_rows : MP * LANE + (t + 1) * rest_rows, :] = e_all[t, LANE:er, :]
    gathered(1)
    share_out(2)
    share_out(3)

    def scale(k):
        return vec[k : k + 1, :]

    def shift(k):
        return vec[5 + k : 6 + k, :]

    def forward(base, p, carry):
        @pl.when(p + 2 < NP)
        def _():
            @pl.when(p + 2 >= SLOTS)
            def _():
                for d in range(MP - 1):
                    send(p + 2 - SLOTS, d).wait_send()

            prepare(p + 2)
            start(p + 2)

        q = p - base
        blend_pair(z, p, rows, (z, p))
        for t in zpeer:
            remote(stage.at[0, 0], rows.at[t, p], rs_send.at[0, 0], rs_recv.at[t, p], {"mp": t}).wait_recv()
        for t in range(MP):
            lanes = slice(t * LANE, (t + 1) * LANE)
            for k in range(2):
                xs[q, k * ROWS : k * ROWS + MAIN, lanes], xs[q, k * ROWS + MAIN : (k + 1) * ROWS, lanes] = slab(t, p, k)
        for t in range(0, MP, 2):
            lanes = slice(MP * LANE + t * 64, MP * LANE + t * 64 + LANE)
            left, right = slab(t, p, 2), slab(t + 1, p, 2)
            for k in range(2):
                half = slice(k * 64, (k + 1) * 64)
                main, tail = (jnp.concatenate([v[:, half], w[:, half]], axis=1) for v, w in zip(left, right, strict=True))
                xs[q, k * ROWS : k * ROWS + MAIN, lanes] = main
                xs[q, k * ROWS + MAIN : (k + 1) * ROWS, lanes] = tail
        stream0 = dot(xs[q], ep[...]) + shift(3)
        s0[q] = stream0
        mi[q] = (scale(0) * stream0 + shift(0)).astype(BF16)
        for b in range(2):
            r = slice(b * ROWS, (b + 1) * ROWS)
            mixed = dot(mm[...], mi[q, r, :]) + mbias[...]
            mx[q, r, :] = mixed
            stream1 = s0[q, r, :] + scale(1) * mixed
            s1[q, r, :] = stream1
            fi[q, r, :] = (scale(2) * stream1 + shift(1)).astype(BF16)
            s1sum[pl.ds(2 * p + b, 1), :] = jnp.sum(stream1[0:PATCHES], axis=0, keepdims=True)

        def chunk(c, carry):
            cols = pl.ds(pl.multiple_of(c * CHUNK, CHUNK), CHUNK)
            for b in range(2):
                r = slice(b * ROWS, (b + 1) * ROWS)
                h = dot(fi[q, r, :], w1[:, cols]) + b1[:, cols]
                sq = h * h
                s = 0.5 * jnp.tanh(h * (GELU_A + GELU_B * sq)) + 0.5
                act = rounded(h * s)
                asum[pl.ds(2 * p + b, 1), cols] = jnp.sum(act[0:PATCHES], axis=0, keepdims=True)
                gp[q, r, cols] = s + s * (1.0 - s) * (h * (2.0 * GELU_A + 6.0 * GELU_B * sq))
                gp[q, b * ROWS + PATCHES : (b + 1) * ROWS, cols] = jnp.zeros((ROWS - PATCHES, CHUNK), F32)
            return carry

        lax.fori_loop(0, NCH, chunk, 0)

        return carry

    def class_head():
        three = dot(thirds(asum[...], 0), w2[...])
        outsum = three[0:16] + three[16:32] + three[32:48] + PATCHES * shift(2)
        stream2 = s1sum[...] + scale(3) * outsum
        pooled = (scale(4) * (stream2 * (1.0 / PATCHES)) + shift(4)).astype(BF16)
        lane = lax.broadcasted_iota(jnp.int32, (16, cpad * MP), 1)
        inside = lax.rem(lane, cpad)
        valid = inside < ncls
        class_id = (lane // cpad) * ncls + inside
        logits = jnp.where(valid, dot(pooled, wc[...]) + cb[...], -1e30)
        hot_a = jnp.where(valid & (class_id == la[:, 0:1]), 1.0, 0.0)
        hot_b = jnp.where(valid & (class_id == lb[:, 0:1]), 1.0, 0.0)
        weight_a = mix_share * jnp.sum(hot_a * cw[...], axis=1, keepdims=True)
        weight_b = (1.0 - mix_share) * jnp.sum(hot_b * cw[...], axis=1, keepdims=True)
        top = jnp.max(logits, axis=1, keepdims=True)
        exps = jnp.where(valid, jnp.exp(logits - top), 0.0)
        exp_sum = jnp.sum(exps, axis=1, keepdims=True)
        soft = exps / exp_sum
        dlog = ((weight_a + weight_b) * soft - weight_a * hot_a - weight_b * hot_b).astype(BF16)
        dfinal = dot(dlog, wc[...], ((1,), (1,))) * (1.0 / PATCHES)
        dstream2 = scale(4) * dfinal
        ds2[...] = dstream2
        dout = scale(3) * dstream2
        low = dout.astype(BF16)
        dact[...] = dot(low, w2[...], ((1,), (1,)))

        def last():
            log_total = top + jnp.log(exp_sum)
            target_a = jnp.sum(hot_a * logits, axis=1, keepdims=True)
            target_b = jnp.sum(hot_b * logits, axis=1, keepdims=True)
            loss = weight_a * (log_total - target_a) + weight_b * (log_total - target_b)
            loss = jnp.sum(loss, axis=0, keepdims=True)
            total = jnp.sum(weight_a + weight_b, axis=0, keepdims=True)
            fac[:, 0:16, :] = jnp.broadcast_to(low[None], (MP, 16, D))
            fac[:, 16:32, :] = jnp.broadcast_to(pooled[None], (MP, 16, D))
            for t in range(MP):
                fac[t, 32:48, 0:cpad] = dlog[:, t * cpad : (t + 1) * cpad]
                fac[t, 32:48, cpad:] = jnp.zeros((16, D - cpad), BF16)
            gvec[3:4, :] = jnp.sum(outsum * dstream2, axis=0, keepdims=True)
            gvec[4:5, :] = jnp.sum(dfinal * stream2, axis=0, keepdims=True)
            gvec[7:8, :] = PATCHES * jnp.sum(dout, axis=0, keepdims=True)
            gvec[8:9, :] = PATCHES * jnp.sum(dstream2, axis=0, keepdims=True)
            gvec[9:10, :] = PATCHES * jnp.sum(dfinal, axis=0, keepdims=True)
            lane = lax.broadcasted_iota(jnp.int32, (1, D), 1)
            gvec[10:11, :] = jnp.where(lane == 0, loss, jnp.where(lane == 1, total, 0.0))

        return last

    def turn_input(q):
        fit[q, 0:D, :] = jnp.transpose(fi[q])

    def hidden_gradient(q, p, cols):
        for b in range(2):
            r = slice(b * ROWS, (b + 1) * ROWS)
            dh[r, cols] = (gp[q, r, cols] * dact[pl.ds(2 * p + b, 1), cols]).astype(BF16)

    def backward_columns(q, p, cols):
        hidden_gradient(q, p, cols)
        grad = dot(fit[q], dh[:, cols])
        gw[0:D, cols] += grad[0:D]
        csum[0:1, cols] += grad[D : D + 1]

    def backward_hidden(base, p):
        q = p - base
        turn_input(q)

        def chunk(c, carry):
            backward_columns(q, p, pl.ds(pl.multiple_of(c * CHUNK, CHUNK), CHUNK))
            return carry

        lax.fori_loop(0, NCH, chunk, 0)

    def backward_rest(base, p):
        q = p - base
        dffn = dot(dh[...], w1[...], ((1,), (1,)))
        gvec[2:3, :] += jnp.sum(dffn * s1[q], axis=0, keepdims=True)
        gvec[6:7, :] += jnp.sum(dffn, axis=0, keepdims=True)
        for b in range(2):
            r = slice(b * ROWS, (b + 1) * ROWS)
            d1 = ds2[pl.ds(2 * p + b, 1), :] + scale(2) * dffn[r]
            gvec[1:2, :] += jnp.sum(mx[q, r, :] * d1, axis=0, keepdims=True)
            dmixed = (scale(1) * d1).astype(BF16)
            gm[...] += dot(dmixed, mi[q, r, :], ((1,), (1,)))
            gmb[...] += dmixed.astype(F32)
            dmixer = dot(mt[...], dmixed)
            gvec[0:1, :] += jnp.sum(dmixer * s0[q, r, :], axis=0, keepdims=True)
            gvec[5:6, :] += jnp.sum(dmixer, axis=0, keepdims=True)
            d0 = (d1 + scale(0) * dmixer).astype(BF16)
            grad = dot(xs[q, r, :], d0, ((0,), (0,)))
            for t in range(MP):
                ge[t, 0:LANE, :] += grad[t * LANE : (t + 1) * LANE]
                ge[t, LANE:er, :] += grad[MP * LANE + t * rest_rows : MP * LANE + (t + 1) * rest_rows]

    def backward(base, p, carry):
        backward_hidden(base, p)
        backward_rest(base, p)
        return carry

    for n, (lo, hi) in enumerate(waves_of(NP)):
        lax.fori_loop(lo, hi, functools.partial(forward, lo), 0)
        if n == 0:
            gathered(2)
            gathered(3)
        last = class_head()
        if hi < NP:
            lax.fori_loop(lo, hi, functools.partial(backward, lo), 0)

    def arrived(dst, sem, peer):
        remote(dst, dst, sem, sem, peer).wait_recv()

    def columns(t):
        return pl.ds(pl.multiple_of(t * hid, LANE), hid)

    def part(u, n):
        return pl.ds(pl.multiple_of(u * n, 8), n)

    last()
    yacts[y, z] = asum[:, columns(z)]
    yfac[y, z] = fac[z]
    for d, v in enumerate(zpeer):
        go(asum.at[:, columns(v)], yacts.at[y, z], zf_s.at[d, 2], zf_r.at[z, 2], {"mp": v})
        go(fac.at[v], yfac.at[y, z], zf_s.at[d, 3], zf_r.at[z, 3], {"mp": v})
    order = zpeer[::-1] + [z]
    for p in range(lo, hi):
        turn_input(p - lo)
    for i, t in enumerate(order):
        for p in range(lo, hi):
            backward_columns(p - lo, p, columns(t))
        for d, u in enumerate(ypeer):
            ysw[i, d] = gw[part(u, PW), columns(t)].astype(BF16)
            go(ysw.at[i, d], yrw.at[t, d], yw_s.at[i, d], yw_r.at[t, d], {"dp": u})
    backward_rest(lo, hi - 1)
    for p in range(lo, hi - 1):
        for t in range(MP):
            hidden_gradient(p - lo, p, columns(t))
        backward_rest(lo, p)
    for i, t in enumerate(order):
        for d, u in enumerate(ypeer):
            yse[i, d] = ge[t, part(u, PE), :].astype(BF16)
            go(yse.at[i, d], yre.at[t, d], ye_s.at[i, d], ye_r.at[t, d], {"dp": u})

    for k in late:
        loads[k].start()

    gvec[8:9, :] += scale(2) * gvec[6:7, :] + scale(0) * gvec[5:6, :]
    row = lax.broadcasted_iota(jnp.int32, (ROWS, 256), 0)
    column = lax.broadcasted_iota(jnp.int32, (ROWS, 256), 1)
    bias_grad = jnp.sum(gmb[...], axis=1, keepdims=True)
    grad = jnp.concatenate([gm[...], jnp.zeros((ROWS, 256 - ROWS), F32)], axis=1)
    grad = jnp.where(column < PATCHES, grad, jnp.where(column == PATCHES, bias_grad, 0.0))
    grad = jnp.where(row < PATCHES, grad, 0.0)
    own = D // MP
    lane = lax.broadcasted_iota(jnp.int32, (16, LANE), 1)
    for t in range(MP):
        n = min(MIX, ROWS - t * MIX)
        gmix[t, 0:n, :] = grad[t * MIX : t * MIX + n]
        gmix[t, n:, :] = jnp.zeros((MIX16 - n, 256), F32)
        sm[t] = gmix[t].astype(BF16)
        vector = gvec[...]
        if t:
            vector = pltpu.roll(vector, D - t * own, 1)
        zvec[z, t] = jnp.where(lane < own, vector[:, 0:LANE], 0.0)
        zvec[z, t, 10:11, :] = gvec[10:11, 0:LANE]
        for k in range(hid // LANE):
            at = t * hid + k * LANE
            zvec[z, t, 11 + k : 12 + k, :] = csum[:, at : at + LANE]
    for d, v in enumerate(zpeer):
        go(sm.at[v], zsm.at[z], zf_s.at[d, 0], zf_r.at[z, 0], {"mp": v})
        go(zvec.at[z, v], zvec.at[z, v], zf_s.at[d, 1], zf_r.at[z, 1], {"mp": v})

    for v in zpeer:
        arrived(yacts.at[y, v], zf_r.at[v, 2], {"mp": v})
        arrived(yfac.at[y, v], zf_r.at[v, 3], {"mp": v})
    for d, u in enumerate(ypeer):
        go(yacts.at[y], yacts.at[y], yf_s.at[d, 2], yf_r.at[y, 2], {"dp": u})
        go(yfac.at[y], yfac.at[y], yf_s.at[d, 3], yf_r.at[y, 3], {"dp": u})

    def from_dp(first, received, sems, send, out, out_sems, z_sems, n):
        for i, t in enumerate(order):
            value = first(t)
            for d in range(DP - 1):
                arrived(received.at[t, d], sems.at[t, d], {"dp": ypeer[d]})
                value = value + received[t, d].astype(F32)
            if i < MP - 1:
                send[i] = value.astype(BF16)
                go(send.at[i], out.at[i], out_sems.at[i], z_sems.at[i], {"mp": t})
        return value

    own_w = from_dp(lambda t: gw[part(y, PW), columns(t)], yrw, yw_r, zsw, zrw, zw_s, zw_r, PW)

    mixed = gmix[z, 0:MIX, :]
    for v in zpeer:
        arrived(zsm.at[v], zf_r.at[v, 0], {"mp": v})
        arrived(zvec.at[v, z], zf_r.at[v, 1], {"mp": v})
        mixed = mixed + zsm[v, 0:MIX, :].astype(F32)
    vector = zvec[0, z]
    for v in range(1, MP):
        vector = vector + zvec[v, z]
    ysm[y] = mixed
    yvec[y] = vector
    for d, u in enumerate(ypeer):
        go(ysm.at[y], ysm.at[y], yf_s.at[d, 0], yf_r.at[y, 0], {"dp": u})
        go(yvec.at[y], yvec.at[y], yf_s.at[d, 1], yf_r.at[y, 1], {"dp": u})

    own_e = from_dp(lambda t: ge[t, part(y, PE), :], yre, ye_r, zse, zre, ze_s, ze_r, PE)

    def from_mp(own_sum, received, sems, gathered, k):
        value = own_sum
        for i in range(MP - 1):
            arrived(received.at[i], sems.at[i], {"mp": order[i]})
            value = value + received[i].astype(F32)
        gathered[y] = value.astype(BF16)
        for d, u in enumerate(ypeer):
            go(gathered.at[y], gathered.at[y], ag_s.at[d, k], ag_r.at[y, k], {"dp": u})
        return rounded(value)

    def squares(v):
        return jnp.sum(jnp.sum(v * v, axis=0, keepdims=True), axis=1, keepdims=True)

    mine = squares(from_mp(own_w, zrw, zw_r, agw, 0))

    for u in ypeer:
        arrived(ysm.at[u], yf_r.at[u, 0], {"dp": u})
        arrived(yvec.at[u], yf_r.at[u, 1], {"dp": u})
    mixed, vector = ysm[0], yvec[0]
    for u in range(1, DP):
        mixed, vector = mixed + ysm[u], vector + yvec[u]
    g_mix[part(z, MIX), :] = mixed

    for u in ypeer:
        arrived(yacts.at[u], yf_r.at[u, 2], {"dp": u})
        arrived(yfac.at[u], yf_r.at[u, 3], {"dp": u})
    n = 16 * MP
    grad_shr = jnp.zeros((hid, D), F32)
    grad_cls = jnp.zeros((D, cpad), F32)
    cls_bias = jnp.zeros((1, cpad), F32)
    for u in range(DP):
        whole = yfac[u]
        dout = whole[:, 0:16, :].reshape(n, D)
        pooled = whole[:, 16:32, :].reshape(n, D)
        dlog = whole[:, 32:48, 0:cpad].reshape(n, cpad)
        three = thirds(yacts[u].reshape(n, hid), 0)
        grad_shr = grad_shr + dot(three, jnp.concatenate([dout] * 3, axis=0), ((0,), (0,)))
        grad_cls = grad_cls + dot(pooled, dlog, ((0,), (0,)))
        cls_bias = cls_bias + jnp.sum(dlog.astype(F32), axis=0, keepdims=True)
    g_shr[...] = grad_shr
    g_cls[0:D, :] = grad_cls
    g_cls[D:, :] = jnp.concatenate([cls_bias, jnp.zeros((g_cls.shape[0] - D - 1, cpad), F32)], axis=0)
    once = squares(grad_shr) + squares(grad_cls) + squares(cls_bias) + squares(mixed)
    once = once + squares(vector[0:10]) + squares(vector[11 : 11 + hid // LANE])

    mine = mine + squares(from_mp(own_e, zre, ze_r, age, 1))
    nsq[y, z] = jnp.broadcast_to(mine + jnp.where(y == 0, once, 0.0), (8, LANE))
    for k, peer in enumerate(others):
        go(nsq.at[y, z], nsq.at[y, z], nq_s.at[k], nq_r.at[y, z], peer)
    for d, v in enumerate(zpeer):
        go(g_mix.at[part(z, MIX), :], g_mix.at[part(z, MIX), :], nm_s.at[d], nm_r.at[z], {"mp": v})
    store(3, g_shr)
    store(4, g_cls)
    g_vec[...] = vector
    store(5, g_vec)
    for k in range(4, 21):
        if k != 4:
            loads[k].wait()
    for peer in others:
        arrived(nsq.at[peer["dp"], peer["mp"]], nq_r.at[peer["dp"], peer["mp"]], peer)
    square = jnp.zeros((1, 1), F32)
    for u in range(DP):
        for v in range(MP):
            square = square + nsq[u, v, 0:1, 0:1]
    loss_sum = vector[10:11, 0:1]
    weight_total = vector[10:11, 1:2]
    size = jnp.sqrt(square) / weight_total
    factor = clip_limit / jnp.maximum(size, clip_limit)
    scaled = factor / weight_total
    lane = lax.broadcasted_iota(jnp.int32, (8, LANE), 1)
    info[...] = jnp.where(
        lane == 0, loss_sum, jnp.where(lane == 1, weight_total, jnp.where(lane == 2, size, scaled))
    )

    (_, _, _, _, _, sca_w, shi_w) = held[:7]
    (emb1, mixing1, expa1, shr1, cls1, sca1, shi1) = held[7:14]
    (emb2, mixing2, expa2, shr2, cls2, sca2, shi2) = held[14:21]
    wide = sca_w.shape[1]
    def halves(ref, k):
        n = ref.shape[0] // 2
        return ref.at[pl.ds(pl.multiple_of(k * n, 8), n), :]

    mvs = gp.at[0:2, 0 : hid // 2, 0:D]
    mvc = gp.at[0:2, 0 : C_ROWS // 2, D : D + 256]
    mve = gp.at[0:2, 0 : E_ROWS // 2, D + 256 : 2 * D + 256]

    def put(moved, at, value):
        n = moved.shape[1]
        rows, width = value.shape
        k = min(max(n - at, 0), rows)
        if k:
            moved[0, at : at + k, 0:width] = value[0:k]
        if k < rows:
            moved[1, at + k - n : at + rows - n, 0:width] = value[k:]

    fine = C_VEC - C_ROWS // 2

    def first_step(k, moved, out):
        go(moved.at[1 - core], halves(out, 1 - core), g_s.at[k, 0], g_r.at[k, 0], near)

    split = (True, False, True)
    side = lax.rem(y, 2)

    def some(ref, k, which):
        n = ref.shape[1] // 2
        return ref.at[k, pl.ds(pl.multiple_of(which * n, 16), n), :]

    def second_step(k, moved, out, pairs):
        arrived(halves(out, core), g_r.at[k, 0], near)
        n = moved.shape[1]
        value = moved[core] + out[part(core, n), :]
        pairs[0, 0:n] = value.astype(BF16)
        if pairs.shape[1] > n:
            value = value[fine : fine + 16]
            pairs[0, n:] = (value - rounded(value)).astype(BF16)
        if split[k]:
            go(some(pairs, 0, side), some(pairs, 1, side), g_s.at[k, 1], g_r.at[k, 1], far)
        else:
            go(pairs.at[0], pairs.at[1], g_s.at[k, 1], g_r.at[k, 1], far)

    def hand_on(k, pairs):
        if not split[k]:
            return
        arrived(some(pairs, 1, side), g_r.at[k, 1], far)
        go(some(pairs, 1, side), some(pairs, 1, side), g_s.at[k, 2], g_r.at[k, 2], {"dp": beside})

    def third_step(k, pairs, out):
        if split[k]:
            arrived(some(pairs, 1, 1 - side), g_r.at[k, 2], {"dp": beside})
        else:
            arrived(pairs.at[1], g_r.at[k, 1], far)
        n = out.shape[0] // 2
        total = pairs[0].astype(F32) + pairs[1].astype(F32)
        out[part(core, n), :] = total[0:n]
        if pairs.shape[1] > n:
            out[pl.ds(pl.multiple_of(core * n + fine, 8), 16), :] = total[fine : fine + 16] + total[n:]
        go(halves(out, core), halves(out, core), g_s.at[k, 3], g_r.at[k, 3], near)

    put(mvs, 0, adamw(shr[...], g_shr[...] * scaled, shr1[...], shr2[...], matrix_rate))
    first_step(0, mvs, sum_s)
    for u in ypeer:
        arrived(agw.at[u], ag_r.at[u, 0], {"dp": u})
        arrived(age.at[u], ag_r.at[u, 1], {"dp": u})
    for u in range(DP):
        g_w[u * PW : (u + 1) * PW, :] = agw[u].astype(F32)
        g_e[u * PE : (u + 1) * PE, :] = age[u].astype(F32)
    store(0, g_w)
    store(1, g_e)
    bias = jnp.concatenate([g_vec[11 + k : 12 + k, :] for k in range(hid // LANE)], axis=1)
    last_row = slice(D, D + 1)
    mve[...] = jnp.zeros(mve.shape, F32)
    put(mve, E_EXP, adamw(expa[0:D, :], g_w[0:D, :] * scaled, expa1[0:D, :], expa2[0:D, :], matrix_rate))
    put(mve, E_EXP + D, adamw(expa[last_row, :], bias * scaled, expa1[last_row, :], expa2[last_row, :], matrix_rate))
    put(mve, E_EMB, adamw(emb[...], g_e[0:er, :] * scaled, emb1[...], emb2[...], matrix_rate))
    first_step(2, mve, sum_e)
    second_step(0, mvs, sum_s, h2s)
    for v in zpeer:
        arrived(g_mix.at[part(v, MIX), :], nm_r.at[v], {"mp": v})
    store(2, g_mix)
    mvc[...] = jnp.zeros(mvc.shape, F32)
    put(mvc, C_CLS, adamw(cls[...], g_cls[0 : D + 1, 0:ncls] * scaled, cls1[...], cls2[...], head_rate))
    put(
        mvc, C_MIX,
        adamw(mixing[...], g_mix[0:PATCHES, 0 : PATCHES + 1] * scaled, mixing1[...], mixing2[...], matrix_rate),
    )
    for k, (w, one, two) in enumerate(((sca_w, sca1, sca2), (shi_w, shi1, shi2))):
        value = adamw(w[...], g_vec[5 * k : 5 * k + 5, 0:wide] * scaled, one[...], two[...], vector_rate)
        put(mvc, C_VEC + 8 * k, value)
    first_step(1, mvc, sum_c)
    second_step(2, mve, sum_e, h2e)
    hand_on(0, h2s)
    second_step(1, mvc, sum_c, h2c)
    hand_on(2, h2e)
    third_step(0, h2s, sum_s)
    hand_on(1, h2c)
    third_step(2, h2e, sum_e)
    arrived(halves(sum_s, 1 - core), g_r.at[0, 3], near)
    store(6, sum_s)
    third_step(1, h2c, sum_c)
    arrived(halves(sum_e, 1 - core), g_r.at[2, 3], near)
    store(8, sum_e)
    arrived(halves(sum_c, 1 - core), g_r.at[1, 3], near)
    store(7, sum_c)

    def drain(p, carry):
        for d in range(MP - 1):
            send(p, d).wait_send()
        return carry

    lax.fori_loop(max(NP - SLOTS, 0), NP, drain, 0)
    for c in started:
        c.wait_send()
    for c in stores:
        c.wait()


def local_step(G, DP, MP, shapes, labels, partner, sca, shi, class_weight, patches, states):
    NI = patches.shape[0] // MP
    NP = NI // 2
    PR = 2 * ROWS
    er, hid, ncls = shapes[0][0], shapes[2][1], shapes[4][1]
    hid_all = hid * MP
    pd = er * MP
    cpad = -(-ncls // LANE) * LANE
    wave = max(hi - lo for lo, hi in waves_of(NP))
    dp1 = max(DP - 1, 1)
    PW, PE = part_rows(D, DP), part_rows(er, DP)
    dma = pltpu.SemaphoreType.DMA
    vm = pl.BlockSpec(memory_space=VMEM)
    smem = pl.BlockSpec(memory_space=SMEM)
    hbm = pl.BlockSpec(memory_space=pl.ANY)
    s = jax.ShapeDtypeStruct
    results = (
        (DP * PW, D), (DP * PE, D), (MP * MIX, 256), (hid, D), (392, cpad), (16, LANE),
        (hid, D), (C_ROWS, 256), (E_ROWS, D),
    )
    return pl.pallas_call(
        functools.partial(step_kernel, G, DP, MP, NI, ncls),
        out_shape=(*(s(shape, F32) for shape in results), s((8, LANE), F32)),
        in_specs=[smem, smem, vm, vm, vm] + [hbm] * 22,
        out_specs=(hbm,) * 9 + (vm,),
        scratch_shapes=[VMEM(shape, F32) for shape in results]
        + [VMEM(shape, F32) for shape in shapes + 2 * (shapes[1:3] + shapes[4:])]
        + [
            VMEM(patches.shape, F32),
            VMEM((MP - 1, SLOTS, 3 * MAIN + 16, LANE), BF16),
            VMEM((MP, NP, 3 * MAIN + 16, LANE), BF16),
            VMEM((MP, er, D), BF16),
            VMEM((D, hid_all), BF16),
            VMEM((hid_all, D), BF16),
            VMEM((D, cpad * MP), BF16),
            VMEM((MP, 16, LANE), F32),
            VMEM((wave, PR, pd), BF16),
            VMEM((wave, PR, hid_all), F32),
            VMEM((wave, PR, D), F32),
            VMEM((wave, PR, D), F32),
            VMEM((wave, PR, D), F32),
            VMEM((wave, PR, D), BF16),
            VMEM((wave, PR, D), BF16),
            VMEM((pd, D), BF16),
            VMEM((ROWS, ROWS), BF16),
            VMEM((ROWS, ROWS), BF16),
            VMEM((ROWS, PATCHES), BF16),
            VMEM((ROWS, 1), F32),
            VMEM((16, D), F32),
            VMEM((1, hid_all), F32),
            VMEM((1, cpad * MP), F32),
            VMEM((1, cpad * MP), F32),
            VMEM((16, hid_all), F32),
            VMEM((16, D), F32),
            VMEM((16, LANE), jnp.int32),
            VMEM((16, LANE), jnp.int32),
            VMEM((16, hid_all), F32),
            VMEM((16, D), F32),
            VMEM((PR, hid_all), BF16),
            VMEM((wave, D + 16, PR), BF16),
            VMEM((1, hid_all), F32),
            VMEM((DP * PW, hid_all), F32),
            VMEM((MP, DP * PE, D), F32),
            VMEM((ROWS, ROWS), F32),
            VMEM((ROWS, D), F32),
            VMEM((16, D), F32),
            VMEM((MP, MIX16, 256), F32),
            VMEM((MP, MIX16, 256), BF16),
            VMEM((MP, 48, D), BF16),
            VMEM((MP, MIX16, 256), BF16),
            VMEM((MP, MP, 16, LANE), F32),
            VMEM((DP, MIX, 256), F32),
            VMEM((DP, 16, LANE), F32),
            VMEM((DP, MP, 16, hid), F32),
            VMEM((DP, MP, 48, D), BF16),
            VMEM((DP, PW, hid), BF16),
            VMEM((DP, PE, D), BF16),
            VMEM((MP, dp1, PW, hid), BF16),
            VMEM((MP, dp1, PW, hid), BF16),
            VMEM((MP - 1, PW, hid), BF16),
            VMEM((MP - 1, PW, hid), BF16),
            VMEM((MP, dp1, PE, D), BF16),
            VMEM((MP, dp1, PE, D), BF16),
            VMEM((MP - 1, PE, D), BF16),
            VMEM((MP - 1, PE, D), BF16),
            VMEM((DP, MP, 8, LANE), F32),
            VMEM((2, hid // 2, D), BF16),
            VMEM((2, C_ROWS // 2 + 16, 256), BF16),
            VMEM((2, E_ROWS // 2, D), BF16),
            dma((22,)),
            dma((MP - 1, SLOTS)),
            dma((MP, NP)),
            dma((MP - 1, 4)),
            dma((MP, 4)),
            dma((MP - 1, 3, 4)),
            dma((MP, 3, 4)),
            dma((MP - 1, 4)),
            dma((MP, 4)),
            dma((MP - 1,)),
            dma((MP,)),
            dma((MP - 1, 4)),
            dma((MP, 4)),
            dma((dp1, 4)),
            dma((DP, 4)),
            dma((MP, dp1)),
            dma((MP, dp1)),
            dma((MP - 1,)),
            dma((MP - 1,)),
            dma((MP, dp1)),
            dma((MP, dp1)),
            dma((MP - 1,)),
            dma((MP - 1,)),
            dma((dp1, 2)),
            dma((DP, 2)),
            dma((MP - 1,)),
            dma((MP,)),
            dma((DP * MP - 1,)),
            dma((DP, MP)),
            dma((3, 4)),
            dma((3, 4)),
            dma((9,)),
        ],
        compiler_params=pltpu.CompilerParams(
            collective_id=0, has_side_effects=True, vmem_limit_bytes=63 << 20
        ),
    )(labels, partner, sca, shi, class_weight, patches, *states)


def finish_kernel(groups, *refs):
    (info, *grads_in), refs = refs[:10], refs[10:]
    states, refs = refs[:28], refs[28:]
    (losses, norm), refs = refs[:2], refs[2:]
    outs, refs = refs[:28], refs[28:]
    grads_held, refs = refs[:9], refs[9:]
    held, refs = refs[:28], refs[28:]
    new, (load, load_grad, save) = refs[:28], refs[28:]
    first = [pltpu.make_async_copy(a, b, load_grad.at[k]) for k, (a, b) in enumerate(zip(grads_in, grads_held, strict=True))]
    loads = [pltpu.make_async_copy(flat(a), b, load.at[k]) for k, (a, b) in enumerate(zip(states, held, strict=True))]
    saves = [pltpu.make_async_copy(a, flat(b), save.at[k]) for k, (a, b) in enumerate(zip(new, outs, strict=True))]
    for c in first:
        c.start()
    for k in (3, 2, 0, 4, 1, 5, 6):
        for j in range(4):
            loads[7 * j + k].start()
    losses[...] = info[0:1, 0:2]
    norm[...] = info[0:1, 2:3]
    scaled = info[0:1, 3:4]
    g_w, g_e, g_mix, g_shr, g_cls, g_vec, sum_s, sum_c, sum_e = grads_held
    for c in first:
        c.wait()
    wide = held[5].shape[1]
    ncls = held[4].shape[1]
    er = held[0].shape[0]
    all_rows = slice(None)

    bias = jnp.concatenate([g_vec[11 + k : 12 + k, :] for k in range(D // LANE)], axis=1)
    work = (
        (3, all_rows, lambda: g_shr[...], lambda: sum_s[...]),
        (2, slice(0, D), lambda: g_w[0:D, :], lambda: sum_e[E_EXP : E_EXP + D, :]),
        (2, slice(D, D + 1), lambda: bias, lambda: sum_e[E_EXP + D : E_EXP + D + 1, :]),
        (0, all_rows, lambda: g_e[0:er, :], lambda: sum_e[E_EMB : E_EMB + er, :]),
        (4, all_rows, lambda: g_cls[0 : D + 1, 0:ncls], lambda: sum_c[C_CLS : C_CLS + D + 1, 0:ncls]),
        (1, all_rows, lambda: g_mix[0:PATCHES, 0 : PATCHES + 1], lambda: sum_c[C_MIX : C_MIX + PATCHES, 0 : PATCHES + 1]),
        (5, all_rows, lambda: g_vec[0:5, 0:wide], lambda: sum_c[C_VEC : C_VEC + 5, 0:wide]),
        (6, all_rows, lambda: g_vec[5:10, 0:wide], lambda: sum_c[C_VEC + 8 : C_VEC + 13, 0:wide]),
    )
    for n, (k, r, gradient, total) in enumerate(work):
        if n == 0 or work[n - 1][0] != k:
            for j in range(4):
                loads[7 * j + k].wait()
        weight, one, two, outer = (held[7 * j + k] for j in range(4))
        update, mean, square, velocity = (new[7 * j + k] for j in range(4))
        grad = gradient() * scaled
        mean[r, :] = beta_one * one[r, :] + (1.0 - beta_one) * grad
        square[r, :] = beta_two * two[r, :] + (1.0 - beta_two) * grad * grad
        average = total() * (1.0 / groups)
        moving = outer_momentum * outer[r, :] + average
        velocity[r, :] = moving
        update[r, :] = weight[r, :] - outer_rate * (average + outer_momentum * moving)
        if n + 1 == len(work) or work[n + 1][0] != k:
            for j in range(4):
                saves[7 * j + k].start()
    for c in saves:
        c.wait()


def finish(G, info, grads, shapes, states, out_shapes):
    dma = pltpu.SemaphoreType.DMA
    vm = pl.BlockSpec(memory_space=VMEM)
    hbm = pl.BlockSpec(memory_space=pl.ANY)
    return pl.pallas_call(
        functools.partial(finish_kernel, G),
        out_shape=tuple(jax.ShapeDtypeStruct(shape, F32) for shape in ((1, 2), (1, 1), *out_shapes)),
        in_specs=[vm] + [hbm] * 37,
        out_specs=(vm,) * 2 + (hbm,) * 28,
        scratch_shapes=[VMEM(a.shape, F32) for a in grads]
        + [VMEM(shape, F32) for shape in shapes] * 8
        + [dma((28,)), dma((9,)), dma((28,))],
        compiler_params=pltpu.CompilerParams(vmem_limit_bytes=62 << 20),
    )(info, *grads, *states)


def thin(a):
    return jnp.swapaxes(a, 0, 1)


def per_device(
    G, DP, MP,
    patches, labels, partner, class_weight,
    embedding, mixing, expand, shrink, classifier, scales, shifts, *state,
):
    weights = (embedding, thin(mixing), thin(expand), shrink[0], classifier, scales, shifts)

    def moments(a):
        return (a[0][0], thin(a[1][0]), thin(a[2][0]), a[3][0, 0], thin(a[4]), thin(a[5]), thin(a[6]))

    firsts, seconds = moments(state[0:7]), moments(state[7:14])
    o = state[14:21]
    outers = (o[0], thin(o[1]), thin(o[2]), o[3][0], o[4], o[5], o[6])
    shapes = tuple((a.shape[0], a.shape[-1]) for a in weights)
    *grads, info = local_step(
        G, DP, MP, shapes, labels[0], partner[0], scales, shifts, class_weight.reshape(1, -1),
        jnp.swapaxes(patches[0], 1, 2), (*weights, *firsts, *seconds),
    )
    out_shapes = tuple(a.shape for a in (*weights, *firsts, *seconds, *outers))
    losses, norm, *done = finish(G, info, grads, shapes, (*weights, *firsts, *seconds, *outers), out_shapes)
    updates, means, squares, velocities = (list(done[7 * k : 7 * k + 7]) for k in range(4))

    def whole(a):
        return (a[0], thin(a[1]), thin(a[2]), a[3][None], a[4], a[5], a[6])

    def by_group(a):
        return (a[0][None], thin(a[1])[None], thin(a[2])[None], a[3][None, None], thin(a[4]), thin(a[5]), thin(a[6]))

    return (
        losses, norm[0],
        *whole(updates), *by_group(means), *by_group(squares), *whole(velocities),
    )


WEIGHT_SPECS = (
    P("mp", None),
    P(),
    P(None, None, "mp"),
    P(None, "mp", None),
    P(None, "mp"),
    P(None, "mp"),
    P(None, "mp"),
)
STATE_SPECS = (
    P("group", "mp", None),
    P("group", None, None, None),
    P("group", None, None, "mp"),
    P("group", None, "mp", None),
    P("group", None, "mp"),
    P("group", None, "mp"),
    P("group", None, "mp"),
)


def solution(mesh):
    G, DP, MP = mesh.shape["group"], mesh.shape["dp"], mesh.shape["mp"]
    return jax.shard_map(
        functools.partial(per_device, G, DP, MP),
        mesh=mesh,
        in_specs=(
            P("group", "dp", None, "mp"),
            P("group", "dp"),
            P("group", "dp"),
            P(),
            *WEIGHT_SPECS,
            *STATE_SPECS,
            *STATE_SPECS,
            *WEIGHT_SPECS,
        ),
        out_specs=(
            P("group", None),
            P("group"),
            *WEIGHT_SPECS,
            *STATE_SPECS,
            *STATE_SPECS,
            *WEIGHT_SPECS,
        ),
        check_vma=False,
    )
```

```python
import functools

import jax
import jax.numpy as jnp
from jax import lax
from jax.experimental import pallas as pl
from jax.experimental.pallas import tpu as pltpu
from jax.sharding import PartitionSpec as P

F32 = jnp.float32
BF16 = jnp.bfloat16
MESH = pl.DeviceIdType.MESH
VMEM = pltpu.VMEM
SMEM = pltpu.SMEM

D = 384
PATCHES = 196
ROWS = 208
MAIN = 192
STEP = 10
LANE = 128

mix_share = 0.7
clip_limit = 0.01
beta_one = 0.9
beta_two = 0.999
adam_eps = 1e-08
weight_decay = 0.05
matrix_rate = 0.05
head_rate = 0.5
vector_rate = 0.4
outer_rate = 0.7
outer_momentum = 0.9

GELU_A = 0.7978845608028654
GELU_B = GELU_A * 0.044715

MIX, MIX16 = 56, 64
C_CLS, C_MIX, C_VEC, C_ROWS = 0, 392, 592, 608
E_EXP, E_EMB, E_ROWS = 0, 392, 640


def dot(a, b, dims=((1,), (0,)), precision=None):
    return lax.dot_general(
        a, b, (dims, ((), ())), preferred_element_type=F32, precision=precision
    )


def thirds(a, axis):
    high = a.astype(BF16)
    rest = a - high.astype(F32)
    middle = rest.astype(BF16)
    low = (rest - middle.astype(F32)).astype(BF16)
    return jnp.concatenate([high, middle, low], axis=axis)


def rounded(a):
    return a.astype(BF16).astype(F32)


def greet(peers):
    barrier = pltpu.get_barrier_semaphore()
    for peer in peers:
        pl.semaphore_signal(barrier, inc=1, device_id=peer, device_id_type=MESH)
    pl.semaphore_wait(barrier, len(peers))


def remote(src, dst, send_sem, recv_sem, peer):
    return pltpu.make_async_remote_copy(
        src_ref=src, dst_ref=dst, send_sem=send_sem, recv_sem=recv_sem,
        device_id=peer, device_id_type=MESH,
    )


CHUNK = 256
SLOTS = 3


def waves_of(pairs):
    return [(lo, min(lo + 2, pairs)) for lo in range(0, pairs, 2)]


def part_rows(rows, DP):
    return -(-rows // (16 * DP)) * 16


def adamw(weight, gradient, moment_one, moment_two, rate):
    mean_new = beta_one * moment_one + (1.0 - beta_one) * gradient
    square_new = beta_two * moment_two + (1.0 - beta_two) * gradient * gradient
    mean_hat = mean_new * (1.0 / (1.0 - beta_one**STEP))
    square_hat = square_new * (1.0 / (1.0 - beta_two**STEP))
    return rate * (mean_hat / (jnp.sqrt(square_hat) + adam_eps) + weight_decay * weight)


def flat(ref):
    return ref.at[:, 0, :] if len(ref.shape) == 3 and ref.shape[1] == 1 else ref


def step_kernel(G, DP, MP, NI, ncls, *refs):
    (labels, partner, sca, shi, class_weight, patches), refs = refs[:6], refs[6:]
    states, refs = refs[:21], refs[21:]
    (*results, info), refs = refs[:10], refs[10:]
    (g_w, g_e, g_mix, g_shr, g_cls, g_vec, sum_s, sum_c, sum_e), refs = refs[:9], refs[9:]
    held, refs = list(refs[:17]), refs[17:]
    (
        pv, stage, rows, e_all, w1, w2, wc, small,
        xs, gp, s0, s1, mx, mi, fi, ep, mm, mt, eye, mbias, vec, b1, cb, cw, asum, s1sum, la, lb,
        dact, ds2, dh, fit, csum, gw, ge, gm, gmb, gvec,
        gmix, sm, fac, zsm, zvec, ysm, yvec, yacts, yfac, agw, age,
        ysw, yrw, zsw, zrw, yse, yre, zse, zre, nsq,
        h2s, h2c, h2e,
        load, rs_send, rs_recv, wz_send, wz_recv, wp_send, wp_recv, wc_send, wc_recv, sm_send, sm_recv,
        zf_s, zf_r, yf_s, yf_r, yw_s, yw_r, zw_s, zw_r, ye_s, ye_r, ze_s, ze_r, ag_s, ag_r,
        nm_s, nm_r, nq_s, nq_r, g_s, g_r, out_sem,
    ) = refs
    late = {7: mx.at[0, 0 : held[0].shape[0], :], 14: mx.at[1, 0 : held[0].shape[0], :]}
    late |= {10: s1.at[0, 0:D, :], 17: s1.at[1, 0:D, :]}
    for k in sorted(late):
        held.insert(k, late[k])
    emb, mixing, expa, shr, cls = held[:5]
    z = lax.axis_index("mp")
    y = lax.axis_index("dp")
    g = lax.axis_index("group")
    NP = NI // 2
    PR = 2 * ROWS
    hid = expa.shape[1]
    hid_all = hid * MP
    cpad = wc.shape[1] // MP
    er = emb.shape[0]
    NCH = hid_all // CHUNK
    PW, PE = g_w.shape[0] // DP, g_e.shape[0] // DP

    stores = []

    def store(k, value):
        c = pltpu.make_async_copy(value, results[k], out_sem.at[k])
        c.start()
        stores.append(c)

    loads = [pltpu.make_async_copy(flat(a), b, load.at[k]) for k, (a, b) in enumerate(zip(states, held, strict=True))]
    load_patches = pltpu.make_async_copy(patches, pv, load.at[21])
    loads[0].start()
    loads[2].start()
    load_patches.start()

    zpeer = [lax.rem(z + d, MP) for d in range(1, MP)]
    ypeer = [lax.rem(y + d, DP) for d in range(1, DP)]
    others = [{"mp": lax.rem(z + c, MP), "dp": lax.rem(y + d, DP)} for d in range(DP) for c in range(MP) if c or d]
    core, beside = lax.rem(g, 2), y + 1 - 2 * lax.rem(y, 2)
    near, far = {"group": g + 1 - 2 * core}, {"group": lax.rem(g + 2, G)}
    plane = [far, {"dp": beside}, {**far, "dp": beside}]
    greet(others + [near, far, plane[2]])

    def pieces(t, k, x, h, n=1):
        if k == 0:
            size = er // 4 * (1 if n == 1 else 2)
            at = core * (er // 2) + x * (er // 4)
            return e_all.at[t, pl.ds(pl.multiple_of(at, 16), size), :]
        size = D // 8 * n
        at = core * (D // 2) + (x * 2 + h) * (D // 8)
        if k == 2:
            return w2.at[pl.ds(pl.multiple_of(t * hid + at, 16), size), :]
        ref, width = (w1, hid) if k == 1 else (wc, cpad)
        return ref.at[pl.ds(pl.multiple_of(at, 16), size), pl.ds(pl.multiple_of(t * width, LANE), width)]

    here = (g // 2, lax.rem(y, 2))

    started = []

    def go(*args):
        c = remote(*args)
        c.start()
        started.append(c)

    def spread(k):
        part = pieces(z, k, *here)
        for d, t in enumerate(zpeer):
            go(part, part, wz_send.at[d, k], wz_recv.at[z, k], {"mp": t})

    def pass_on(k):
        for d, t in enumerate(zpeer):
            part = pieces(t, k, *here)
            remote(part, part, wz_send.at[d, k], wz_recv.at[t, k], {"mp": t}).wait_recv()
            for e, peer in enumerate(plane[: 1 if k == 0 else 3]):
                go(part, part, wp_send.at[d, e, k], wp_recv.at[t, e, k], peer)

    def share_out(k):
        there = ((1 - here[0], here[1]), (here[0], 1 - here[1]), (1 - here[0], 1 - here[1]))
        for d, t in enumerate(zpeer):
            for e, peer in enumerate(plane[: 1 if k == 0 else 3]):
                part = pieces(t, k, *there[e])
                remote(part, part, wp_send.at[d, e, k], wp_recv.at[t, e, k], peer).wait_recv()
            part = pieces(t, k, 0, 0, 4)
            go(part, part, wc_send.at[d, k], wc_recv.at[t, k], near)

    def gathered(k):
        for t in zpeer:
            if k == 0:
                part = e_all.at[t, pl.ds(pl.multiple_of((1 - core) * (er // 2), 16), er // 2), :]
            elif k == 2:
                part = w2.at[pl.ds(pl.multiple_of(t * hid + (1 - core) * (D // 2), 16), D // 2), :]
            else:
                ref, width = (w1, hid) if k == 1 else (wc, cpad)
                part = ref.at[
                    pl.ds(pl.multiple_of((1 - core) * (D // 2), 16), D // 2), pl.ds(pl.multiple_of(t * width, LANE), width)
                ]
            remote(part, part, wc_send.at[0, k], wc_recv.at[t, k], near).wait_recv()

    loads[0].wait()
    e_all[z] = emb[...].astype(BF16)
    spread(0)
    loads[2].wait()
    w1[:, pl.ds(pl.multiple_of(z * hid, LANE), hid)] = expa[0:D, :].astype(BF16)
    spread(1)

    row = lax.broadcasted_iota(jnp.int32, (ROWS, PATCHES), 0)
    column = lax.broadcasted_iota(jnp.int32, (ROWS, PATCHES), 1)
    eye[...] = jnp.where(row == column, 1.0, 0.0).astype(BF16)
    share = F32(mix_share)
    rest = F32(1.0 - mix_share)

    def blend(i):
        return (share * pv[i] + rest * pv[partner[i]]).astype(BF16)

    def blend_pair(t, p, ref, lead):
        a = blend(t * NI + 2 * p)
        b = blend(t * NI + 2 * p + 1)
        both = jnp.concatenate([a[0:LANE], b[0:LANE], a[LANE:], b[LANE:]], axis=0)
        turned = dot(eye[...], both, ((1,), (1,)))
        tail = None
        for k in range(3):
            lanes = turned[:, k * LANE : (k + 1) * LANE]
            ref[lead + (slice(k * MAIN, (k + 1) * MAIN), slice(None))] = lanes[0:MAIN].astype(BF16)
            last = lanes[MAIN:ROWS]
            tail = last if k == 0 else tail + pltpu.roll(last, k * (PATCHES - MAIN), 0)
        ref[lead + (slice(3 * MAIN, 3 * MAIN + 16), slice(None))] = tail.astype(BF16)

    def slab(t, p, k):
        tail = rows[t, p, 3 * MAIN :, :].astype(F32)
        if k:
            tail = pltpu.roll(tail, 16 - k * (PATCHES - MAIN), 0)
        row = lax.broadcasted_iota(jnp.int32, (16, LANE), 0)
        tail = jnp.where(row < PATCHES - MAIN, tail, 0.0).astype(BF16)
        return rows[t, p, k * MAIN : (k + 1) * MAIN, :], tail

    def send(p, d):
        slot = lax.rem(p, SLOTS)
        return remote(stage.at[d, slot], rows.at[z, p], rs_send.at[d, slot], rs_recv.at[z, p], {"mp": zpeer[d]})

    def prepare(p):
        for d in range(MP - 1):
            blend_pair(zpeer[d], p, stage, (d, lax.rem(p, SLOTS)))

    def start(p):
        for d in reversed(range(MP - 1)):
            send(p, d).start()

    for k in (3, 4, 1):
        loads[k].start()
    small[z] = jnp.zeros(small.shape[1:], F32)
    small[z, 0:5, 0 : D // MP] = sca[...]
    small[z, 5:10, 0 : D // MP] = shi[...]
    for k in range(hid // LANE):
        small[z, 10 + k : 11 + k, :] = rounded(expa[D : D + 1, k * LANE : (k + 1) * LANE])
    loads[3].wait()
    w2[pl.ds(pl.multiple_of(z * hid, 16), hid), :] = shr[...].astype(BF16)
    spread(2)
    loads[4].wait()
    head = jnp.concatenate([cls[0:D, :], jnp.zeros((D, cpad - ncls), F32)], axis=1)
    wc[:, pl.ds(pl.multiple_of(z * cpad, LANE), cpad)] = head.astype(BF16)
    spread(3)
    for k in range(cpad // LANE):
        n = min(LANE, ncls - k * LANE)
        small[z, 13 + k : 14 + k, 0:n] = rounded(cls[D : D + 1, k * LANE : k * LANE + n])
    for d, t in enumerate(zpeer):
        go(small.at[z], small.at[z], sm_send.at[d], sm_recv.at[z], {"mp": t})
    load_patches.wait()
    prepare(0)
    start(0)
    pass_on(0)
    pass_on(1)
    if NP > 1:
        prepare(1)
        start(1)
    pass_on(2)
    pass_on(3)
    for k in range(5, 21):
        if k not in late:
            loads[k].start()

    loads[1].wait()
    wide = jnp.concatenate([mixing[...], jnp.zeros((PATCHES, 256 - PATCHES - 1), F32)], axis=1)
    wide = jnp.concatenate([wide, jnp.zeros((256 - PATCHES, 256), F32)], axis=0)
    column = lax.broadcasted_iota(jnp.int32, (256, 256), 1)
    square = jnp.where(column < PATCHES, wide, 0.0)
    mm[...] = square[0:ROWS, 0:ROWS].astype(BF16)
    mt[...] = jnp.transpose(square)[0:ROWS, 0:ROWS].astype(BF16)
    mbias[...] = rounded(jnp.sum(jnp.where(column == PATCHES, wide, 0.0), axis=1, keepdims=True)[0:ROWS])
    for t in range(MP):
        block = class_weight[:, t * ncls : (t + 1) * ncls]
        cw[:, t * cpad : (t + 1) * cpad] = jnp.concatenate([block, jnp.zeros((1, cpad - ncls), F32)], axis=1)
    asum[...] = jnp.zeros_like(asum)
    s1sum[...] = jnp.zeros_like(s1sum)
    csum[...] = jnp.zeros_like(csum)
    fit[:, D:, :] = jnp.ones((fit.shape[0], 16, PR), BF16)
    gw[...] = jnp.zeros_like(gw)
    ge[...] = jnp.zeros_like(ge)
    gm[...] = jnp.zeros_like(gm)
    gmb[...] = jnp.zeros_like(gmb)
    gvec[...] = jnp.zeros_like(gvec)
    la[...] = jnp.full(la.shape, -1, jnp.int32)
    lb[...] = jnp.full(lb.shape, -1, jnp.int32)
    for i in range(NI):
        own = labels[z * NI + i]
        mate = labels[partner[z * NI + i]]
        la[i : i + 1, :] = jnp.full((1, LANE), own, jnp.int32)
        lb[i : i + 1, :] = jnp.full((1, LANE), mate, jnp.int32)

    share_out(0)
    share_out(1)

    for t in zpeer:
        remote(small.at[t], small.at[t], sm_send.at[0], sm_recv.at[t], {"mp": t}).wait_recv()
    full = jnp.zeros((16, D), F32)
    for t in range(MP):
        block = jnp.concatenate([small[t], jnp.zeros((16, D - LANE), F32)], axis=1)
        full = full + (pltpu.roll(block, t * (D // MP), 1) if t else block)
        for k in range(hid // LANE):
            b1[:, t * hid + k * LANE : t * hid + (k + 1) * LANE] = small[t, 10 + k : 11 + k, :]
        for k in range(cpad // LANE):
            cb[:, t * cpad + k * LANE : t * cpad + (k + 1) * LANE] = small[t, 13 + k : 14 + k, :]
    vec[...] = full
    gathered(0)
    rest_rows = er - LANE
    for t in range(MP):
        ep[t * LANE : (t + 1) * LANE, :] = e_all[t, 0:LANE, :]
        ep[MP * LANE + t * rest_rows : MP * LANE + (t + 1) * rest_rows, :] = e_all[t, LANE:er, :]
    gathered(1)
    share_out(2)
    share_out(3)

    def scale(k):
        return vec[k : k + 1, :]

    def shift(k):
        return vec[5 + k : 6 + k, :]

    def forward(base, p, carry):
        @pl.when(p + 2 < NP)
        def _():
            @pl.when(p + 2 >= SLOTS)
            def _():
                for d in range(MP - 1):
                    send(p + 2 - SLOTS, d).wait_send()

            prepare(p + 2)
            start(p + 2)

        q = p - base
        blend_pair(z, p, rows, (z, p))
        for t in zpeer:
            remote(stage.at[0, 0], rows.at[t, p], rs_send.at[0, 0], rs_recv.at[t, p], {"mp": t}).wait_recv()
        for t in range(MP):
            lanes = slice(t * LANE, (t + 1) * LANE)
            for k in range(2):
                xs[q, k * ROWS : k * ROWS + MAIN, lanes], xs[q, k * ROWS + MAIN : (k + 1) * ROWS, lanes] = slab(t, p, k)
        for t in range(0, MP, 2):
            lanes = slice(MP * LANE + t * 64, MP * LANE + t * 64 + LANE)
            left, right = slab(t, p, 2), slab(t + 1, p, 2)
            for k in range(2):
                half = slice(k * 64, (k + 1) * 64)
                main, tail = (jnp.concatenate([v[:, half], w[:, half]], axis=1) for v, w in zip(left, right, strict=True))
                xs[q, k * ROWS : k * ROWS + MAIN, lanes] = main
                xs[q, k * ROWS + MAIN : (k + 1) * ROWS, lanes] = tail
        stream0 = dot(xs[q], ep[...]) + shift(3)
        s0[q] = stream0
        mi[q] = (scale(0) * stream0 + shift(0)).astype(BF16)
        for b in range(2):
            r = slice(b * ROWS, (b + 1) * ROWS)
            mixed = dot(mm[...], mi[q, r, :]) + mbias[...]
            mx[q, r, :] = mixed
            stream1 = s0[q, r, :] + scale(1) * mixed
            s1[q, r, :] = stream1
            fi[q, r, :] = (scale(2) * stream1 + shift(1)).astype(BF16)
            s1sum[pl.ds(2 * p + b, 1), :] = jnp.sum(stream1[0:PATCHES], axis=0, keepdims=True)

        def chunk(c, carry):
            cols = pl.ds(pl.multiple_of(c * CHUNK, CHUNK), CHUNK)
            for b in range(2):
                r = slice(b * ROWS, (b + 1) * ROWS)
                h = dot(fi[q, r, :], w1[:, cols]) + b1[:, cols]
                sq = h * h
                s = 0.5 * jnp.tanh(h * (GELU_A + GELU_B * sq)) + 0.5
                act = rounded(h * s)
                asum[pl.ds(2 * p + b, 1), cols] = jnp.sum(act[0:PATCHES], axis=0, keepdims=True)
                gp[q, r, cols] = s + s * (1.0 - s) * (h * (2.0 * GELU_A + 6.0 * GELU_B * sq))
                gp[q, b * ROWS + PATCHES : (b + 1) * ROWS, cols] = jnp.zeros((ROWS - PATCHES, CHUNK), F32)
            return carry

        lax.fori_loop(0, NCH, chunk, 0)

        return carry

    def class_head():
        three = dot(thirds(asum[...], 0), w2[...])
        outsum = three[0:16] + three[16:32] + three[32:48] + PATCHES * shift(2)
        stream2 = s1sum[...] + scale(3) * outsum
        pooled = (scale(4) * (stream2 * (1.0 / PATCHES)) + shift(4)).astype(BF16)
        lane = lax.broadcasted_iota(jnp.int32, (16, cpad * MP), 1)
        inside = lax.rem(lane, cpad)
        valid = inside < ncls
        class_id = (lane // cpad) * ncls + inside
        logits = jnp.where(valid, dot(pooled, wc[...]) + cb[...], -1e30)
        hot_a = jnp.where(valid & (class_id == la[:, 0:1]), 1.0, 0.0)
        hot_b = jnp.where(valid & (class_id == lb[:, 0:1]), 1.0, 0.0)
        weight_a = mix_share * jnp.sum(hot_a * cw[...], axis=1, keepdims=True)
        weight_b = (1.0 - mix_share) * jnp.sum(hot_b * cw[...], axis=1, keepdims=True)
        top = jnp.max(logits, axis=1, keepdims=True)
        exps = jnp.where(valid, jnp.exp(logits - top), 0.0)
        exp_sum = jnp.sum(exps, axis=1, keepdims=True)
        soft = exps / exp_sum
        dlog = ((weight_a + weight_b) * soft - weight_a * hot_a - weight_b * hot_b).astype(BF16)
        dfinal = dot(dlog, wc[...], ((1,), (1,))) * (1.0 / PATCHES)
        dstream2 = scale(4) * dfinal
        ds2[...] = dstream2
        dout = scale(3) * dstream2
        low = dout.astype(BF16)
        dact[...] = dot(low, w2[...], ((1,), (1,)))

        def last():
            log_total = top + jnp.log(exp_sum)
            target_a = jnp.sum(hot_a * logits, axis=1, keepdims=True)
            target_b = jnp.sum(hot_b * logits, axis=1, keepdims=True)
            loss = weight_a * (log_total - target_a) + weight_b * (log_total - target_b)
            loss = jnp.sum(loss, axis=0, keepdims=True)
            total = jnp.sum(weight_a + weight_b, axis=0, keepdims=True)
            fac[:, 0:16, :] = jnp.broadcast_to(low[None], (MP, 16, D))
            fac[:, 16:32, :] = jnp.broadcast_to(pooled[None], (MP, 16, D))
            for t in range(MP):
                fac[t, 32:48, 0:cpad] = dlog[:, t * cpad : (t + 1) * cpad]
                fac[t, 32:48, cpad:] = jnp.zeros((16, D - cpad), BF16)
            gvec[3:4, :] = jnp.sum(outsum * dstream2, axis=0, keepdims=True)
            gvec[4:5, :] = jnp.sum(dfinal * stream2, axis=0, keepdims=True)
            gvec[7:8, :] = PATCHES * jnp.sum(dout, axis=0, keepdims=True)
            gvec[8:9, :] = PATCHES * jnp.sum(dstream2, axis=0, keepdims=True)
            gvec[9:10, :] = PATCHES * jnp.sum(dfinal, axis=0, keepdims=True)
            lane = lax.broadcasted_iota(jnp.int32, (1, D), 1)
            gvec[10:11, :] = jnp.where(lane == 0, loss, jnp.where(lane == 1, total, 0.0))

        return last

    def turn_input(q):
        fit[q, 0:D, :] = jnp.transpose(fi[q])

    def hidden_gradient(q, p, cols):
        for b in range(2):
            r = slice(b * ROWS, (b + 1) * ROWS)
            dh[r, cols] = (gp[q, r, cols] * dact[pl.ds(2 * p + b, 1), cols]).astype(BF16)

    def backward_columns(q, p, cols):
        hidden_gradient(q, p, cols)
        grad = dot(fit[q], dh[:, cols])
        gw[0:D, cols] += grad[0:D]
        csum[0:1, cols] += grad[D : D + 1]

    def backward_hidden(base, p):
        q = p - base
        turn_input(q)

        def chunk(c, carry):
            backward_columns(q, p, pl.ds(pl.multiple_of(c * CHUNK, CHUNK), CHUNK))
            return carry

        lax.fori_loop(0, NCH, chunk, 0)

    def backward_rest(base, p):
        q = p - base
        dffn = dot(dh[...], w1[...], ((1,), (1,)))
        gvec[2:3, :] += jnp.sum(dffn * s1[q], axis=0, keepdims=True)
        gvec[6:7, :] += jnp.sum(dffn, axis=0, keepdims=True)
        for b in range(2):
            r = slice(b * ROWS, (b + 1) * ROWS)
            d1 = ds2[pl.ds(2 * p + b, 1), :] + scale(2) * dffn[r]
            gvec[1:2, :] += jnp.sum(mx[q, r, :] * d1, axis=0, keepdims=True)
            dmixed = (scale(1) * d1).astype(BF16)
            gm[...] += dot(dmixed, mi[q, r, :], ((1,), (1,)))
            gmb[...] += dmixed.astype(F32)
            dmixer = dot(mt[...], dmixed)
            gvec[0:1, :] += jnp.sum(dmixer * s0[q, r, :], axis=0, keepdims=True)
            gvec[5:6, :] += jnp.sum(dmixer, axis=0, keepdims=True)
            d0 = (d1 + scale(0) * dmixer).astype(BF16)
            grad = dot(xs[q, r, :], d0, ((0,), (0,)))
            for t in range(MP):
                ge[t, 0:LANE, :] += grad[t * LANE : (t + 1) * LANE]
                ge[t, LANE:er, :] += grad[MP * LANE + t * rest_rows : MP * LANE + (t + 1) * rest_rows]

    def backward(base, p, carry):
        backward_hidden(base, p)
        backward_rest(base, p)
        return carry

    for n, (lo, hi) in enumerate(waves_of(NP)):
        lax.fori_loop(lo, hi, functools.partial(forward, lo), 0)
        if n == 0:
            gathered(2)
            gathered(3)
        last = class_head()
        if hi < NP:
            lax.fori_loop(lo, hi, functools.partial(backward, lo), 0)

    def arrived(dst, sem, peer):
        remote(dst, dst, sem, sem, peer).wait_recv()

    def columns(t):
        return pl.ds(pl.multiple_of(t * hid, LANE), hid)

    def part(u, n):
        return pl.ds(pl.multiple_of(u * n, 8), n)

    last()
    yacts[y, z] = asum[:, columns(z)]
    yfac[y, z] = fac[z]
    for d, v in enumerate(zpeer):
        go(asum.at[:, columns(v)], yacts.at[y, z], zf_s.at[d, 2], zf_r.at[z, 2], {"mp": v})
        go(fac.at[v], yfac.at[y, z], zf_s.at[d, 3], zf_r.at[z, 3], {"mp": v})
    order = zpeer + [z]
    for p in range(lo, hi):
        turn_input(p - lo)
    for i, t in enumerate(order):
        for p in range(lo, hi):
            backward_columns(p - lo, p, columns(t))
        for d, u in enumerate(ypeer):
            ysw[i, d] = gw[part(u, PW), columns(t)].astype(BF16)
            go(ysw.at[i, d], yrw.at[t, d], yw_s.at[i, d], yw_r.at[t, d], {"dp": u})
    backward_rest(lo, hi - 1)
    for p in range(lo, hi - 1):
        for t in range(MP):
            hidden_gradient(p - lo, p, columns(t))
        backward_rest(lo, p)
    for i, t in enumerate(order):
        for d, u in enumerate(ypeer):
            yse[i, d] = ge[t, part(u, PE), :].astype(BF16)
            go(yse.at[i, d], yre.at[t, d], ye_s.at[i, d], ye_r.at[t, d], {"dp": u})

    for k in late:
        loads[k].start()

    gvec[8:9, :] += scale(2) * gvec[6:7, :] + scale(0) * gvec[5:6, :]
    row = lax.broadcasted_iota(jnp.int32, (ROWS, 256), 0)
    column = lax.broadcasted_iota(jnp.int32, (ROWS, 256), 1)
    bias_grad = jnp.sum(gmb[...], axis=1, keepdims=True)
    grad = jnp.concatenate([gm[...], jnp.zeros((ROWS, 256 - ROWS), F32)], axis=1)
    grad = jnp.where(column < PATCHES, grad, jnp.where(column == PATCHES, bias_grad, 0.0))
    grad = jnp.where(row < PATCHES, grad, 0.0)
    own = D // MP
    lane = lax.broadcasted_iota(jnp.int32, (16, LANE), 1)
    for t in range(MP):
        n = min(MIX, ROWS - t * MIX)
        gmix[t, 0:n, :] = grad[t * MIX : t * MIX + n]
        gmix[t, n:, :] = jnp.zeros((MIX16 - n, 256), F32)
        sm[t] = gmix[t].astype(BF16)
        vector = gvec[...]
        if t:
            vector = pltpu.roll(vector, D - t * own, 1)
        zvec[z, t] = jnp.where(lane < own, vector[:, 0:LANE], 0.0)
        zvec[z, t, 10:11, :] = gvec[10:11, 0:LANE]
        for k in range(hid // LANE):
            at = t * hid + k * LANE
            zvec[z, t, 11 + k : 12 + k, :] = csum[:, at : at + LANE]
    for d, v in enumerate(zpeer):
        go(sm.at[v], zsm.at[z], zf_s.at[d, 0], zf_r.at[z, 0], {"mp": v})
        go(zvec.at[z, v], zvec.at[z, v], zf_s.at[d, 1], zf_r.at[z, 1], {"mp": v})

    for v in zpeer:
        arrived(yacts.at[y, v], zf_r.at[v, 2], {"mp": v})
        arrived(yfac.at[y, v], zf_r.at[v, 3], {"mp": v})
    for d, u in enumerate(ypeer):
        go(yacts.at[y], yacts.at[y], yf_s.at[d, 2], yf_r.at[y, 2], {"dp": u})
        go(yfac.at[y], yfac.at[y], yf_s.at[d, 3], yf_r.at[y, 3], {"dp": u})

    def from_dp(first, received, sems, send, out, out_sems, z_sems, n):
        for i, t in enumerate(order):
            value = first(t)
            for d in range(DP - 1):
                arrived(received.at[t, d], sems.at[t, d], {"dp": ypeer[d]})
                value = value + received[t, d].astype(F32)
            if i < MP - 1:
                send[i] = value.astype(BF16)
                go(send.at[i], out.at[i], out_sems.at[i], z_sems.at[i], {"mp": t})
        return value

    own_w = from_dp(lambda t: gw[part(y, PW), columns(t)], yrw, yw_r, zsw, zrw, zw_s, zw_r, PW)

    mixed = gmix[z, 0:MIX, :]
    for v in zpeer:
        arrived(zsm.at[v], zf_r.at[v, 0], {"mp": v})
        arrived(zvec.at[v, z], zf_r.at[v, 1], {"mp": v})
        mixed = mixed + zsm[v, 0:MIX, :].astype(F32)
    vector = zvec[0, z]
    for v in range(1, MP):
        vector = vector + zvec[v, z]
    ysm[y] = mixed
    yvec[y] = vector
    for d, u in enumerate(ypeer):
        go(ysm.at[y], ysm.at[y], yf_s.at[d, 0], yf_r.at[y, 0], {"dp": u})
        go(yvec.at[y], yvec.at[y], yf_s.at[d, 1], yf_r.at[y, 1], {"dp": u})

    own_e = from_dp(lambda t: ge[t, part(y, PE), :], yre, ye_r, zse, zre, ze_s, ze_r, PE)

    def from_mp(own_sum, received, sems, gathered, k):
        value = own_sum
        for i in range(MP - 1):
            arrived(received.at[i], sems.at[i], {"mp": zpeer[i]})
            value = value + received[i].astype(F32)
        gathered[y] = value.astype(BF16)
        for d, u in enumerate(ypeer):
            go(gathered.at[y], gathered.at[y], ag_s.at[d, k], ag_r.at[y, k], {"dp": u})
        return rounded(value)

    def squares(v):
        return jnp.sum(jnp.sum(v * v, axis=0, keepdims=True), axis=1, keepdims=True)

    mine = squares(from_mp(own_w, zrw, zw_r, agw, 0))

    for u in ypeer:
        arrived(ysm.at[u], yf_r.at[u, 0], {"dp": u})
        arrived(yvec.at[u], yf_r.at[u, 1], {"dp": u})
    mixed, vector = ysm[0], yvec[0]
    for u in range(1, DP):
        mixed, vector = mixed + ysm[u], vector + yvec[u]
    g_mix[part(z, MIX), :] = mixed

    for u in ypeer:
        arrived(yacts.at[u], yf_r.at[u, 2], {"dp": u})
        arrived(yfac.at[u], yf_r.at[u, 3], {"dp": u})
    n = 16 * MP
    grad_shr = jnp.zeros((hid, D), F32)
    grad_cls = jnp.zeros((D, cpad), F32)
    cls_bias = jnp.zeros((1, cpad), F32)
    for u in range(DP):
        whole = yfac[u]
        dout = whole[:, 0:16, :].reshape(n, D)
        pooled = whole[:, 16:32, :].reshape(n, D)
        dlog = whole[:, 32:48, 0:cpad].reshape(n, cpad)
        three = thirds(yacts[u].reshape(n, hid), 0)
        grad_shr = grad_shr + dot(three, jnp.concatenate([dout] * 3, axis=0), ((0,), (0,)))
        grad_cls = grad_cls + dot(pooled, dlog, ((0,), (0,)))
        cls_bias = cls_bias + jnp.sum(dlog.astype(F32), axis=0, keepdims=True)
    g_shr[...] = grad_shr
    g_cls[0:D, :] = grad_cls
    g_cls[D:, :] = jnp.concatenate([cls_bias, jnp.zeros((g_cls.shape[0] - D - 1, cpad), F32)], axis=0)
    once = squares(grad_shr) + squares(grad_cls) + squares(cls_bias) + squares(mixed)
    once = once + squares(vector[0:10]) + squares(vector[11 : 11 + hid // LANE])

    mine = mine + squares(from_mp(own_e, zre, ze_r, age, 1))
    nsq[y, z] = jnp.broadcast_to(mine + jnp.where(y == 0, once, 0.0), (8, LANE))
    for k, peer in enumerate(others):
        go(nsq.at[y, z], nsq.at[y, z], nq_s.at[k], nq_r.at[y, z], peer)
    for d, v in enumerate(zpeer):
        go(g_mix.at[part(z, MIX), :], g_mix.at[part(z, MIX), :], nm_s.at[d], nm_r.at[z], {"mp": v})
    store(3, g_shr)
    store(4, g_cls)
    g_vec[...] = vector
    store(5, g_vec)
    for k in range(4, 21):
        if k != 4:
            loads[k].wait()
    for peer in others:
        arrived(nsq.at[peer["dp"], peer["mp"]], nq_r.at[peer["dp"], peer["mp"]], peer)
    square = jnp.zeros((1, 1), F32)
    for u in range(DP):
        for v in range(MP):
            square = square + nsq[u, v, 0:1, 0:1]
    loss_sum = vector[10:11, 0:1]
    weight_total = vector[10:11, 1:2]
    size = jnp.sqrt(square) / weight_total
    factor = clip_limit / jnp.maximum(size, clip_limit)
    scaled = factor / weight_total
    lane = lax.broadcasted_iota(jnp.int32, (8, LANE), 1)
    info[...] = jnp.where(
        lane == 0, loss_sum, jnp.where(lane == 1, weight_total, jnp.where(lane == 2, size, scaled))
    )

    (_, _, _, _, _, sca_w, shi_w) = held[:7]
    (emb1, mixing1, expa1, shr1, cls1, sca1, shi1) = held[7:14]
    (emb2, mixing2, expa2, shr2, cls2, sca2, shi2) = held[14:21]
    wide = sca_w.shape[1]
    def halves(ref, k):
        n = ref.shape[0] // 2
        return ref.at[pl.ds(pl.multiple_of(k * n, 8), n), :]

    mvs = gp.at[0:2, 0 : hid // 2, 0:D]
    mvc = gp.at[0:2, 0 : C_ROWS // 2, D : D + 256]
    mve = gp.at[0:2, 0 : E_ROWS // 2, D + 256 : 2 * D + 256]

    def put(moved, at, value):
        n = moved.shape[1]
        rows, width = value.shape
        k = min(max(n - at, 0), rows)
        if k:
            moved[0, at : at + k, 0:width] = value[0:k]
        if k < rows:
            moved[1, at + k - n : at + rows - n, 0:width] = value[k:]

    fine = C_VEC - C_ROWS // 2

    def first_step(k, moved, out):
        go(moved.at[1 - core], halves(out, 1 - core), g_s.at[k, 0], g_r.at[k, 0], near)

    split = (True, False, True)
    side = lax.rem(y, 2)

    def some(ref, k, which):
        n = ref.shape[1] // 2
        return ref.at[k, pl.ds(pl.multiple_of(which * n, 16), n), :]

    def second_step(k, moved, out, pairs):
        arrived(halves(out, core), g_r.at[k, 0], near)
        n = moved.shape[1]
        value = moved[core] + out[part(core, n), :]
        pairs[0, 0:n] = value.astype(BF16)
        if pairs.shape[1] > n:
            value = value[fine : fine + 16]
            pairs[0, n:] = (value - rounded(value)).astype(BF16)
        if split[k]:
            go(some(pairs, 0, side), some(pairs, 1, side), g_s.at[k, 1], g_r.at[k, 1], far)
        else:
            go(pairs.at[0], pairs.at[1], g_s.at[k, 1], g_r.at[k, 1], far)

    def hand_on(k, pairs):
        if not split[k]:
            return
        arrived(some(pairs, 1, side), g_r.at[k, 1], far)
        go(some(pairs, 1, side), some(pairs, 1, side), g_s.at[k, 2], g_r.at[k, 2], {"dp": beside})

    def third_step(k, pairs, out):
        if split[k]:
            arrived(some(pairs, 1, 1 - side), g_r.at[k, 2], {"dp": beside})
        else:
            arrived(pairs.at[1], g_r.at[k, 1], far)
        n = out.shape[0] // 2
        total = pairs[0].astype(F32) + pairs[1].astype(F32)
        out[part(core, n), :] = total[0:n]
        if pairs.shape[1] > n:
            out[pl.ds(pl.multiple_of(core * n + fine, 8), 16), :] = total[fine : fine + 16] + total[n:]
        go(halves(out, core), halves(out, core), g_s.at[k, 3], g_r.at[k, 3], near)

    put(mvs, 0, adamw(shr[...], g_shr[...] * scaled, shr1[...], shr2[...], matrix_rate))
    first_step(0, mvs, sum_s)
    for u in ypeer:
        arrived(agw.at[u], ag_r.at[u, 0], {"dp": u})
        arrived(age.at[u], ag_r.at[u, 1], {"dp": u})
    for u in range(DP):
        g_w[u * PW : (u + 1) * PW, :] = agw[u].astype(F32)
        g_e[u * PE : (u + 1) * PE, :] = age[u].astype(F32)
    store(0, g_w)
    store(1, g_e)
    bias = jnp.concatenate([g_vec[11 + k : 12 + k, :] for k in range(hid // LANE)], axis=1)
    last_row = slice(D, D + 1)
    mve[...] = jnp.zeros(mve.shape, F32)
    put(mve, E_EXP, adamw(expa[0:D, :], g_w[0:D, :] * scaled, expa1[0:D, :], expa2[0:D, :], matrix_rate))
    put(mve, E_EXP + D, adamw(expa[last_row, :], bias * scaled, expa1[last_row, :], expa2[last_row, :], matrix_rate))
    put(mve, E_EMB, adamw(emb[...], g_e[0:er, :] * scaled, emb1[...], emb2[...], matrix_rate))
    first_step(2, mve, sum_e)
    second_step(0, mvs, sum_s, h2s)
    for v in zpeer:
        arrived(g_mix.at[part(v, MIX), :], nm_r.at[v], {"mp": v})
    store(2, g_mix)
    mvc[...] = jnp.zeros(mvc.shape, F32)
    put(mvc, C_CLS, adamw(cls[...], g_cls[0 : D + 1, 0:ncls] * scaled, cls1[...], cls2[...], head_rate))
    put(
        mvc, C_MIX,
        adamw(mixing[...], g_mix[0:PATCHES, 0 : PATCHES + 1] * scaled, mixing1[...], mixing2[...], matrix_rate),
    )
    for k, (w, one, two) in enumerate(((sca_w, sca1, sca2), (shi_w, shi1, shi2))):
        value = adamw(w[...], g_vec[5 * k : 5 * k + 5, 0:wide] * scaled, one[...], two[...], vector_rate)
        put(mvc, C_VEC + 8 * k, value)
    first_step(1, mvc, sum_c)
    second_step(2, mve, sum_e, h2e)
    hand_on(0, h2s)
    second_step(1, mvc, sum_c, h2c)
    hand_on(2, h2e)
    third_step(0, h2s, sum_s)
    hand_on(1, h2c)
    third_step(2, h2e, sum_e)
    arrived(halves(sum_s, 1 - core), g_r.at[0, 3], near)
    store(6, sum_s)
    third_step(1, h2c, sum_c)
    arrived(halves(sum_e, 1 - core), g_r.at[2, 3], near)
    store(8, sum_e)
    arrived(halves(sum_c, 1 - core), g_r.at[1, 3], near)
    store(7, sum_c)

    def drain(p, carry):
        for d in range(MP - 1):
            send(p, d).wait_send()
        return carry

    lax.fori_loop(max(NP - SLOTS, 0), NP, drain, 0)
    for c in started:
        c.wait_send()
    for c in stores:
        c.wait()


def local_step(G, DP, MP, shapes, labels, partner, sca, shi, class_weight, patches, states):
    NI = patches.shape[0] // MP
    NP = NI // 2
    PR = 2 * ROWS
    er, hid, ncls = shapes[0][0], shapes[2][1], shapes[4][1]
    hid_all = hid * MP
    pd = er * MP
    cpad = -(-ncls // LANE) * LANE
    wave = max(hi - lo for lo, hi in waves_of(NP))
    dp1 = max(DP - 1, 1)
    PW, PE = part_rows(D, DP), part_rows(er, DP)
    dma = pltpu.SemaphoreType.DMA
    vm = pl.BlockSpec(memory_space=VMEM)
    smem = pl.BlockSpec(memory_space=SMEM)
    hbm = pl.BlockSpec(memory_space=pl.ANY)
    s = jax.ShapeDtypeStruct
    results = (
        (DP * PW, D), (DP * PE, D), (MP * MIX, 256), (hid, D), (392, cpad), (16, LANE),
        (hid, D), (C_ROWS, 256), (E_ROWS, D),
    )
    return pl.pallas_call(
        functools.partial(step_kernel, G, DP, MP, NI, ncls),
        out_shape=(*(s(shape, F32) for shape in results), s((8, LANE), F32)),
        in_specs=[smem, smem, vm, vm, vm] + [hbm] * 22,
        out_specs=(hbm,) * 9 + (vm,),
        scratch_shapes=[VMEM(shape, F32) for shape in results]
        + [VMEM(shape, F32) for shape in shapes + 2 * (shapes[1:3] + shapes[4:])]
        + [
            VMEM(patches.shape, F32),
            VMEM((MP - 1, SLOTS, 3 * MAIN + 16, LANE), BF16),
            VMEM((MP, NP, 3 * MAIN + 16, LANE), BF16),
            VMEM((MP, er, D), BF16),
            VMEM((D, hid_all), BF16),
            VMEM((hid_all, D), BF16),
            VMEM((D, cpad * MP), BF16),
            VMEM((MP, 16, LANE), F32),
            VMEM((wave, PR, pd), BF16),
            VMEM((wave, PR, hid_all), F32),
            VMEM((wave, PR, D), F32),
            VMEM((wave, PR, D), F32),
            VMEM((wave, PR, D), F32),
            VMEM((wave, PR, D), BF16),
            VMEM((wave, PR, D), BF16),
            VMEM((pd, D), BF16),
            VMEM((ROWS, ROWS), BF16),
            VMEM((ROWS, ROWS), BF16),
            VMEM((ROWS, PATCHES), BF16),
            VMEM((ROWS, 1), F32),
            VMEM((16, D), F32),
            VMEM((1, hid_all), F32),
            VMEM((1, cpad * MP), F32),
            VMEM((1, cpad * MP), F32),
            VMEM((16, hid_all), F32),
            VMEM((16, D), F32),
            VMEM((16, LANE), jnp.int32),
            VMEM((16, LANE), jnp.int32),
            VMEM((16, hid_all), F32),
            VMEM((16, D), F32),
            VMEM((PR, hid_all), BF16),
            VMEM((wave, D + 16, PR), BF16),
            VMEM((1, hid_all), F32),
            VMEM((DP * PW, hid_all), F32),
            VMEM((MP, DP * PE, D), F32),
            VMEM((ROWS, ROWS), F32),
            VMEM((ROWS, D), F32),
            VMEM((16, D), F32),
            VMEM((MP, MIX16, 256), F32),
            VMEM((MP, MIX16, 256), BF16),
            VMEM((MP, 48, D), BF16),
            VMEM((MP, MIX16, 256), BF16),
            VMEM((MP, MP, 16, LANE), F32),
            VMEM((DP, MIX, 256), F32),
            VMEM((DP, 16, LANE), F32),
            VMEM((DP, MP, 16, hid), F32),
            VMEM((DP, MP, 48, D), BF16),
            VMEM((DP, PW, hid), BF16),
            VMEM((DP, PE, D), BF16),
            VMEM((MP, dp1, PW, hid), BF16),
            VMEM((MP, dp1, PW, hid), BF16),
            VMEM((MP - 1, PW, hid), BF16),
            VMEM((MP - 1, PW, hid), BF16),
            VMEM((MP, dp1, PE, D), BF16),
            VMEM((MP, dp1, PE, D), BF16),
            VMEM((MP - 1, PE, D), BF16),
            VMEM((MP - 1, PE, D), BF16),
            VMEM((DP, MP, 8, LANE), F32),
            VMEM((2, hid // 2, D), BF16),
            VMEM((2, C_ROWS // 2 + 16, 256), BF16),
            VMEM((2, E_ROWS // 2, D), BF16),
            dma((22,)),
            dma((MP - 1, SLOTS)),
            dma((MP, NP)),
            dma((MP - 1, 4)),
            dma((MP, 4)),
            dma((MP - 1, 3, 4)),
            dma((MP, 3, 4)),
            dma((MP - 1, 4)),
            dma((MP, 4)),
            dma((MP - 1,)),
            dma((MP,)),
            dma((MP - 1, 4)),
            dma((MP, 4)),
            dma((dp1, 4)),
            dma((DP, 4)),
            dma((MP, dp1)),
            dma((MP, dp1)),
            dma((MP - 1,)),
            dma((MP - 1,)),
            dma((MP, dp1)),
            dma((MP, dp1)),
            dma((MP - 1,)),
            dma((MP - 1,)),
            dma((dp1, 2)),
            dma((DP, 2)),
            dma((MP - 1,)),
            dma((MP,)),
            dma((DP * MP - 1,)),
            dma((DP, MP)),
            dma((3, 4)),
            dma((3, 4)),
            dma((9,)),
        ],
        compiler_params=pltpu.CompilerParams(
            collective_id=0, has_side_effects=True, vmem_limit_bytes=63 << 20
        ),
    )(labels, partner, sca, shi, class_weight, patches, *states)


def finish_kernel(groups, *refs):
    (info, *grads_in), refs = refs[:10], refs[10:]
    states, refs = refs[:28], refs[28:]
    (losses, norm), refs = refs[:2], refs[2:]
    outs, refs = refs[:28], refs[28:]
    grads_held, refs = refs[:9], refs[9:]
    held, refs = refs[:28], refs[28:]
    new, (load, load_grad, save) = refs[:28], refs[28:]
    first = [pltpu.make_async_copy(a, b, load_grad.at[k]) for k, (a, b) in enumerate(zip(grads_in, grads_held, strict=True))]
    loads = [pltpu.make_async_copy(flat(a), b, load.at[k]) for k, (a, b) in enumerate(zip(states, held, strict=True))]
    saves = [pltpu.make_async_copy(a, flat(b), save.at[k]) for k, (a, b) in enumerate(zip(new, outs, strict=True))]
    for c in first:
        c.start()
    for k in (3, 2, 0, 4, 1, 5, 6):
        for j in range(4):
            loads[7 * j + k].start()
    losses[...] = info[0:1, 0:2]
    norm[...] = info[0:1, 2:3]
    scaled = info[0:1, 3:4]
    g_w, g_e, g_mix, g_shr, g_cls, g_vec, sum_s, sum_c, sum_e = grads_held
    for c in first:
        c.wait()
    wide = held[5].shape[1]
    ncls = held[4].shape[1]
    er = held[0].shape[0]
    all_rows = slice(None)

    bias = jnp.concatenate([g_vec[11 + k : 12 + k, :] for k in range(D // LANE)], axis=1)
    work = (
        (3, all_rows, lambda: g_shr[...], lambda: sum_s[...]),
        (2, slice(0, D), lambda: g_w[0:D, :], lambda: sum_e[E_EXP : E_EXP + D, :]),
        (2, slice(D, D + 1), lambda: bias, lambda: sum_e[E_EXP + D : E_EXP + D + 1, :]),
        (0, all_rows, lambda: g_e[0:er, :], lambda: sum_e[E_EMB : E_EMB + er, :]),
        (4, all_rows, lambda: g_cls[0 : D + 1, 0:ncls], lambda: sum_c[C_CLS : C_CLS + D + 1, 0:ncls]),
        (1, all_rows, lambda: g_mix[0:PATCHES, 0 : PATCHES + 1], lambda: sum_c[C_MIX : C_MIX + PATCHES, 0 : PATCHES + 1]),
        (5, all_rows, lambda: g_vec[0:5, 0:wide], lambda: sum_c[C_VEC : C_VEC + 5, 0:wide]),
        (6, all_rows, lambda: g_vec[5:10, 0:wide], lambda: sum_c[C_VEC + 8 : C_VEC + 13, 0:wide]),
    )
    for n, (k, r, gradient, total) in enumerate(work):
        if n == 0 or work[n - 1][0] != k:
            for j in range(4):
                loads[7 * j + k].wait()
        weight, one, two, outer = (held[7 * j + k] for j in range(4))
        update, mean, square, velocity = (new[7 * j + k] for j in range(4))
        grad = gradient() * scaled
        mean[r, :] = beta_one * one[r, :] + (1.0 - beta_one) * grad
        square[r, :] = beta_two * two[r, :] + (1.0 - beta_two) * grad * grad
        average = total() * (1.0 / groups)
        moving = outer_momentum * outer[r, :] + average
        velocity[r, :] = moving
        update[r, :] = weight[r, :] - outer_rate * (average + outer_momentum * moving)
        if n + 1 == len(work) or work[n + 1][0] != k:
            for j in range(4):
                saves[7 * j + k].start()
    for c in saves:
        c.wait()


def finish(G, info, grads, shapes, states, out_shapes):
    dma = pltpu.SemaphoreType.DMA
    vm = pl.BlockSpec(memory_space=VMEM)
    hbm = pl.BlockSpec(memory_space=pl.ANY)
    return pl.pallas_call(
        functools.partial(finish_kernel, G),
        out_shape=tuple(jax.ShapeDtypeStruct(shape, F32) for shape in ((1, 2), (1, 1), *out_shapes)),
        in_specs=[vm] + [hbm] * 37,
        out_specs=(vm,) * 2 + (hbm,) * 28,
        scratch_shapes=[VMEM(a.shape, F32) for a in grads]
        + [VMEM(shape, F32) for shape in shapes] * 8
        + [dma((28,)), dma((9,)), dma((28,))],
        compiler_params=pltpu.CompilerParams(vmem_limit_bytes=62 << 20),
    )(info, *grads, *states)


def thin(a):
    return jnp.swapaxes(a, 0, 1)


def per_device(
    G, DP, MP,
    patches, labels, partner, class_weight,
    embedding, mixing, expand, shrink, classifier, scales, shifts, *state,
):
    weights = (embedding, thin(mixing), thin(expand), shrink[0], classifier, scales, shifts)

    def moments(a):
        return (a[0][0], thin(a[1][0]), thin(a[2][0]), a[3][0, 0], thin(a[4]), thin(a[5]), thin(a[6]))

    firsts, seconds = moments(state[0:7]), moments(state[7:14])
    o = state[14:21]
    outers = (o[0], thin(o[1]), thin(o[2]), o[3][0], o[4], o[5], o[6])
    shapes = tuple((a.shape[0], a.shape[-1]) for a in weights)
    *grads, info = local_step(
        G, DP, MP, shapes, labels[0], partner[0], scales, shifts, class_weight.reshape(1, -1),
        jnp.swapaxes(patches[0], 1, 2), (*weights, *firsts, *seconds),
    )
    out_shapes = tuple(a.shape for a in (*weights, *firsts, *seconds, *outers))
    losses, norm, *done = finish(G, info, grads, shapes, (*weights, *firsts, *seconds, *outers), out_shapes)
    updates, means, squares, velocities = (list(done[7 * k : 7 * k + 7]) for k in range(4))

    def whole(a):
        return (a[0], thin(a[1]), thin(a[2]), a[3][None], a[4], a[5], a[6])

    def by_group(a):
        return (a[0][None], thin(a[1])[None], thin(a[2])[None], a[3][None, None], thin(a[4]), thin(a[5]), thin(a[6]))

    return (
        losses, norm[0],
        *whole(updates), *by_group(means), *by_group(squares), *whole(velocities),
    )


WEIGHT_SPECS = (
    P("mp", None),
    P(),
    P(None, None, "mp"),
    P(None, "mp", None),
    P(None, "mp"),
    P(None, "mp"),
    P(None, "mp"),
)
STATE_SPECS = (
    P("group", "mp", None),
    P("group", None, None, None),
    P("group", None, None, "mp"),
    P("group", None, "mp", None),
    P("group", None, "mp"),
    P("group", None, "mp"),
    P("group", None, "mp"),
)


def solution(mesh):
    G, DP, MP = mesh.shape["group"], mesh.shape["dp"], mesh.shape["mp"]
    return jax.shard_map(
        functools.partial(per_device, G, DP, MP),
        mesh=mesh,
        in_specs=(
            P("group", "dp", None, "mp"),
            P("group", "dp"),
            P("group", "dp"),
            P(),
            *WEIGHT_SPECS,
            *STATE_SPECS,
            *STATE_SPECS,
            *WEIGHT_SPECS,
        ),
        out_specs=(
            P("group", None),
            P("group"),
            *WEIGHT_SPECS,
            *STATE_SPECS,
            *STATE_SPECS,
            *WEIGHT_SPECS,
        ),
        check_vma=False,
    )
```
